32 devices in a mesh: case: 2 (over y), strip: 8 (over z, x), clus: 2 (over core).
Axes of the slice: x: 2, y: 2, z: 4, core: 2. Of those that a mesh axis runs over, the one named last changes fastest.
Arguments:
- loads: float32 [4, 32768], P(None, ('case', 'strip', 'clus')), parts along dimension 1, may hold values from -60 to 60, as said below
- self_term: float32 [32768], P(('case', 'strip', 'clus')), parts along dimension 0, may hold values from 1 to 4
- near_tiles: bfloat16 [2560, 128, 128], P(('case', 'strip', 'clus')), parts along dimension 0, may hold values from -0.083496094 to 0.083496094
- near_list: int32 [2560, 2], P(('case', 'strip', 'clus')), parts along dimension 0, may hold values from 0 to 47, as said below
- far_rows: float32 [32, 32768], P(None, ('case', 'strip', 'clus')), parts along dimension 1, may hold values from -1 to 1
- far_cols: float32 [32, 32768], P(None, ('case', 'strip', 'clus')), parts along dimension 1, may hold values from -0.1875 to 0.1875
- coupling: float32 [16, 16, 32, 32], P(None, ('strip', 'clus')), may hold values from -0.375 to 0.375
- ranks: int32 [16, 16], P(None, ('strip', 'clus')), may hold values from 0 to 32, as said below
Outputs:
- solution: float32 [4, 32768], P(None, ('case', 'strip', 'clus')), parts along dimension 1
The draws below stay inside these ranges and needn't reach their ends.
There are 2 independent parts, one for each index of `case`. The reference program is written for one: setup_inputs(seed, part) draws one part's arguments, and reference() takes and returns one part's arrays. A program takes and returns all parts, laid end to end along the dimension named above; an argument that names none is the same for every part. Nothing has to cross between parts.
Inputs may be any that keep to these rules, and one draw needn't show every extreme that they name: `loads`: rises about threefold in scale from the first panel to the last. `near_list`: column 0 is a target block row of the group, 0 to 7, each of which has at least one block; column 1 is a source block of the window, 0 to 47; the same pair may repeat. `ranks`: zero exactly where the two groups' strips are less than two apart, otherwise 32 // 4 to 32.
All inputs are finite; a program needn't handle non-finite values.
Results may differ from the reference program's by a relative error of at most 0.00044.
Values may be sent and summed in bfloat16 or wider, within the bound.
No kernel may reach another device: no remote copies, remote signals or barrier semaphores. Data moves between devices by JAX's collectives and lax.ppermute only.
A program may use at most 64 MiB of HBM per device.

```python
import math
import jax
import jax.numpy as jnp
from jax import lax

P_DEV = 1024
NRHS = 4
BLK = 128
R = 32
BLK_ROW = 10
ITERS = 2
NCLUS = 2
NDEV = 16
PANELS = 16384
NBR = 8
NBD = 80
NWIN = 48


def draw_loads(key, part):
    key = jax.random.fold_in(key, 11)
    position = jnp.arange(PANELS, dtype=jnp.float32) / PANELS
    ramp = 1.0 + 2.0 * position
    return jax.random.normal(key, (NRHS, PANELS), jnp.float32) * ramp[None, :]


def draw_near_list(key, part):
    key = jax.random.fold_in(key, 23)
    first, second = jax.random.split(key)
    slot = jnp.arange(NDEV * NBD, dtype=jnp.int32) % NBD
    picked = jax.random.randint(first, (NDEV * NBD,), 0, NBR, dtype=jnp.int32)
    target = jnp.where(slot < NBR, slot, picked)
    source = jax.random.randint(second, (NDEV * NBD,), 0, NWIN, dtype=jnp.int32)
    return jnp.stack([target, source], axis=1).astype(jnp.int32)


def draw_ranks(key, part):
    key = jax.random.fold_in(key, 37)
    strip_of = jnp.arange(NDEV, dtype=jnp.int32) // NCLUS
    apart = jnp.abs(strip_of[:, None] - strip_of[None, :]) >= 2
    level = jax.random.randint(key, (NDEV, NDEV), R // 4, R + 1, dtype=jnp.int32)
    return jnp.where(apart, level, 0).astype(jnp.int32)


def strengthened(array, key, source, target, parts, factor):
    owner, partner = [(jnp.arange(array.shape[dim]) // (array.shape[dim] // parts)).reshape([-1 if axis == dim else 1 for axis in range(array.ndim)]) for dim in (source, target)]
    chosen = jax.random.permutation(key, parts)[partner]
    strong = (owner == chosen) | (owner == (partner + parts // 2) % parts)
    return jnp.where(strong, factor * array, array)


def shard_levels(key, extent, cuts, smallest, top_value):
    factor_of = 1.0
    for dim, shards_of in cuts:
        steps = jax.random.uniform(jax.random.fold_in(jax.random.fold_in(key, 6), dim), (shards_of,), jnp.float32, smallest / len(cuts), top_value / len(cuts))
        factor_of = factor_of * jnp.repeat(jnp.exp(steps), extent[dim] // shards_of).reshape((-1,) + (1,) * (len(extent) - 1 - dim))
    return factor_of


def scatter_about(stream_key, extent, width, limit, cuts=(), held_as=jnp.bfloat16):
    values = jax.random.normal(stream_key, extent, jnp.float32) * width
    if len(cuts) > 0:
        values = shard_levels(stream_key, extent, cuts, -0.22, 0.18) * values
    return jnp.clip(values, min=-limit, max=limit).astype(held_as)


def bell_draw_with(own_key, extent, width, bound, cuts, heavy, held_as=jnp.bfloat16):
    values = width * jax.random.normal(own_key, extent, jnp.float32)
    if cuts:
        values = values * shard_levels(own_key, extent, cuts, -0.22, 0.18)
    return jnp.clip(strengthened(values, jax.random.fold_in(own_key, 3), *heavy), -bound, bound).astype(held_as)


def setup_inputs(seed: int = 0, part: int = 0) -> dict:
    seeds = jax.random.split(jax.random.key(seed), 9)
    own_keys = jax.random.split(jax.random.fold_in(seeds[8], part), 9)
    return {
        "loads": draw_loads(jax.random.fold_in(jax.random.fold_in(seeds[8], part), 71), part),
        "self_term": jnp.clip(jnp.exp(math.log(4.0) - 1.3862944 * jax.random.uniform(own_keys[1], (PANELS,), jnp.float32) ** shard_levels(own_keys[1], (PANELS,), ((0, 16),), -0.2, 0.2)), 1.0, 4.0),
        "near_tiles": scatter_about(own_keys[2], (NDEV * NBD, BLK, BLK), (0.5 / (BLK_ROW * BLK) ** 0.5), 0.083496094, ((0, 16),)),
        "near_list": draw_near_list(jax.random.fold_in(jax.random.fold_in(seeds[8], part), 71), part),
        "far_rows": scatter_about(own_keys[4], (R, PANELS), R ** -0.5, 1.0, ((1, 16),), jnp.float32),
        "far_cols": scatter_about(own_keys[5], (R, PANELS), P_DEV ** -0.5, 0.1875, ((1, 16),), jnp.float32),
        "coupling": bell_draw_with(seeds[6], (NDEV, NDEV, R, R), (NDEV * R) ** -0.5, 0.375, ((1, 16),), (1, 0, 16, 2.0), jnp.float32),
        "ranks": draw_ranks(jax.random.fold_in(seeds[8], 71), part),
    }


HIGH = lax.Precision.HIGHEST

def apply_operator(field, self_term, near_tiles, near_list, far_rows, far_cols, coupling, ranks):
    rounded = field.astype(jnp.bfloat16)
    padded = jnp.pad(rounded, ((0, 0), (NCLUS * P_DEV, NCLUS * P_DEV)))
    tiles = near_tiles.reshape(NDEV, NBD, BLK, BLK)
    lists = near_list.reshape(NDEV, NBD, 2)

    def one_group(items):
        index, group_tiles, group_list = items
        strip_no = (index // NCLUS).astype(jnp.int32)
        window = lax.dynamic_slice_in_dim(padded, strip_no * (NCLUS * P_DEV), NWIN * BLK, 1)
        window = window.reshape(NRHS, NWIN, BLK)
        sources = jnp.take(window, group_list[:, 1], axis=1)
        product = jnp.einsum('rnk,nkt->rnt', sources.astype(jnp.float32), group_tiles.astype(jnp.float32), precision=HIGH)
        onehot = (group_list[:, 0][:, None] == jnp.arange(NBR, dtype=jnp.int32)[None, :]).astype(jnp.float32)
        blocks = jnp.einsum('rnt,nb->rbt', product, onehot, precision=HIGH)
        return blocks.reshape(NRHS, P_DEV)
    near = lax.map(one_group, (jnp.arange(NDEV, dtype=jnp.int32), tiles, lists))
    near = near.transpose(1, 0, 2).reshape(NRHS, PANELS)
    proj = jnp.einsum('rdp,adp->dra', field.reshape(NRHS, NDEV, P_DEV), far_cols.reshape(R, NDEV, P_DEV), precision=HIGH)
    masks = (jnp.arange(R, dtype=jnp.int32)[None, None, :] < ranks[:, :, None]).astype(jnp.float32)

    def one_target(items):
        couple_row, mask_row = items
        return jnp.einsum('jra,jab->rb', proj * mask_row[:, None, :], couple_row, precision=HIGH)
    far_sum = lax.map(one_target, (coupling, masks))
    far = jnp.einsum('irb,bip->rip', far_sum, far_rows.reshape(R, NDEV, P_DEV), precision=HIGH).reshape(NRHS, PANELS)
    return self_term[None, :] * field + near + far

def small_solve(hess, beta):
    gram = [[sum((hess[j][k] * hess[j][l] for j in range(ITERS + 1))) for l in range(ITERS)] for k in range(ITERS)]
    target = [beta * hess[0][k] for k in range(ITERS)]
    lower = [[None] * ITERS for k in range(ITERS)]
    for i in range(ITERS):
        for j in range(i + 1):
            total = gram[i][j]
            for m in range(j):
                total = total - lower[i][m] * lower[j][m]
            if i == j:
                lower[i][j] = jnp.sqrt(total)
            else:
                lower[i][j] = total / lower[j][j]
    middle = []
    for i in range(ITERS):
        total = target[i]
        for m in range(i):
            total = total - lower[i][m] * middle[m]
        middle.append(total / lower[i][i])
    coeffs = [None] * ITERS
    for i in reversed(range(ITERS)):
        total = middle[i]
        for m in range(i + 1, ITERS):
            total = total - lower[m][i] * coeffs[m]
        coeffs[i] = total / lower[i][i]
    return coeffs

def reference(loads, self_term, near_tiles, near_list, far_rows, far_cols, coupling, ranks):
    beta = jnp.sqrt(lax.optimization_barrier(jnp.sum(loads * loads, axis=1)))
    basis = [loads / beta[:, None]]
    zeros = jnp.zeros((NRHS,), jnp.float32)
    hess = [[zeros for k in range(ITERS)] for j in range(ITERS + 1)]
    for k in range(ITERS):
        image = apply_operator(basis[k], self_term, near_tiles, near_list, far_rows, far_cols, coupling, ranks)
        stacked = jnp.stack(basis)
        inner = lax.optimization_barrier(jnp.sum(stacked * image[None], axis=2))
        image = image - lax.optimization_barrier(jnp.sum(inner[:, :, None] * stacked, axis=0))
        height = jnp.sqrt(lax.optimization_barrier(jnp.sum(image * image, axis=1)))
        for j in range(k + 1):
            hess[j][k] = inner[j]
        hess[k + 1][k] = height
        basis.append(image / height[:, None])
    coeffs = small_solve(hess, beta)
    solution = coeffs[0][:, None] * basis[0]
    for k in range(1, ITERS):
        solution = solution + coeffs[k][:, None] * basis[k]
    return solution
```

```python
import jax
import jax.numpy as jnp
from jax import lax
from jax.sharding import PartitionSpec as P

HIGH = lax.Precision.HIGHEST
GROUP = ("strip", "clus")


def window_of(field):
    paired = lax.all_gather(field, "clus", axis=1, tiled=True)
    devices = lax.axis_size("strip")
    up = [(i, i + 1) for i in range(devices - 1)]
    down = [(j, i) for i, j in up]
    before = lax.ppermute(paired, "strip", up)
    after = lax.ppermute(paired, "strip", down)
    return jnp.concatenate([before, paired, after], axis=1)


def near_field(window, near_tiles, near_list, block_rows):
    nrhs = window.shape[0]
    tile = near_tiles.shape[1]
    blocks = window.astype(jnp.bfloat16).reshape(nrhs, -1, tile)
    sources = jnp.take(blocks, near_list[:, 1], axis=1)
    product = jnp.einsum("rnk,nkt->rnt", sources, near_tiles, preferred_element_type=jnp.float32)
    onehot = (near_list[:, 0][:, None] == jnp.arange(block_rows, dtype=jnp.int32)[None, :]).astype(
        jnp.float32
    )
    summed = jnp.einsum("rnt,nb->rbt", product, onehot, precision=HIGH)
    return summed.reshape(nrhs, -1)


def far_terms(field, far_cols, couple, masks):
    proj = jnp.einsum("rp,ap->ra", field, far_cols, precision=HIGH)
    return jnp.einsum("ira,iab->irb", masks[:, None, :] * proj[None], couple, precision=HIGH)


def exchange(terms, stats):
    groups, nrhs, rank = terms.shape
    kinds = stats.shape[0]
    flat = terms.reshape(groups, nrhs * rank)
    every = jnp.broadcast_to(stats.reshape(1, kinds * nrhs), (groups, kinds * nrhs))
    sent = jnp.concatenate([flat, every], axis=1)
    got = lax.all_to_all(sent, GROUP, 0, 0, tiled=True)
    far_sum = jnp.sum(got[:, : nrhs * rank], axis=0).reshape(nrhs, rank)
    return far_sum, got[:, nrhs * rank :].reshape(groups, kinds, nrhs)


def exchange_stats(stats):
    kinds, nrhs = stats.shape
    groups = lax.axis_size("strip") * lax.axis_size("clus")
    every = jnp.broadcast_to(stats.reshape(1, kinds * nrhs), (groups, kinds * nrhs))
    got = lax.all_to_all(every, GROUP, 0, 0, tiled=True)
    return got.reshape(groups, kinds, nrhs)


def body(loads, self_term, near_tiles, near_list, far_rows, far_cols, coupling, ranks):
    nrhs, panels = loads.shape
    rank = far_cols.shape[0]
    block_rows = panels // near_tiles.shape[1]
    masks = (jnp.arange(rank, dtype=jnp.int32)[None, :] < ranks[:, 0][:, None]).astype(jnp.float32)
    couple = coupling[:, 0]

    def image_of(field, window, far_sum):
        near = near_field(window, near_tiles, near_list, block_rows)
        far = jnp.einsum("rb,bp->rp", far_sum, far_rows, precision=HIGH)
        return self_term[None, :] * field + near + far

    loads_window = window_of(loads)
    far_loads, got = exchange(
        far_terms(loads, far_cols, couple, masks), jnp.sum(loads * loads, axis=1)[None]
    )
    beta = jnp.sqrt(jnp.sum(got[:, 0], axis=0))
    basis0 = loads / beta[:, None]
    window0 = loads_window / beta[:, None]
    far0 = far_loads / beta[:, None]
    image0 = image_of(basis0, window0, far0)

    norm = jnp.sum(basis0 * basis0, axis=1)
    dot = jnp.sum(basis0 * image0, axis=1)
    share = jnp.where(norm > 0, dot / jnp.where(norm > 0, norm, 1.0), 0.0)
    rest = image0 - share[:, None] * basis0
    stats = jnp.stack([norm, dot, share, jnp.sum(rest * rest, axis=1)])
    image_window = window_of(image0)
    far_image, got = exchange(far_terms(image0, far_cols, couple, masks), stats)
    h00 = jnp.sum(got[:, 1], axis=0)
    h10 = jnp.sqrt(jnp.sum(got[:, 3] + got[:, 0] * (got[:, 2] - h00[None]) ** 2, axis=0))
    basis1 = (image0 - h00[:, None] * basis0) / h10[:, None]
    window1 = (image_window - h00[:, None] * window0) / h10[:, None]
    far1 = (far_image - h00[:, None] * far0) / h10[:, None]
    image1 = image_of(basis1, window1, far1)

    stats = jnp.stack(
        [
            jnp.sum(basis0 * image1, axis=1),
            jnp.sum(basis1 * image1, axis=1),
            jnp.sum(image1 * image1, axis=1),
        ]
    )
    h01, h11, gram11 = jnp.sum(exchange_stats(stats), axis=0)
    gram00 = h00 * h00 + h10 * h10
    gram01 = h00 * h01 + h10 * h11
    lower00 = jnp.sqrt(gram00)
    lower10 = gram01 / lower00
    lower11 = jnp.sqrt(gram11 - lower10 * lower10)
    middle0 = beta * h00 / lower00
    middle1 = (beta * h01 - lower10 * middle0) / lower11
    y1 = middle1 / lower11
    y0 = (middle0 - lower10 * y1) / lower00
    return y0[:, None] * basis0 + y1[:, None] * basis1


def solution(mesh):
    in_specs = (
        P(None, ("case", "strip", "clus")),
        P(("case", "strip", "clus")),
        P(("case", "strip", "clus"), None, None),
        P(("case", "strip", "clus"), None),
        P(None, ("case", "strip", "clus")),
        P(None, ("case", "strip", "clus")),
        P(None, ("strip", "clus"), None, None),
        P(None, ("strip", "clus")),
    )
    out_specs = P(None, ("case", "strip", "clus"))
    return jax.shard_map(body, mesh=mesh, in_specs=in_specs, out_specs=out_specs, check_vma=False)
```

```python
import jax
import jax.numpy as jnp
from jax import lax
from jax.sharding import Mesh
from jax.sharding import PartitionSpec as P

HIGH = lax.Precision.HIGHEST
LAYER = ("lo", "clus")
GROUP = ("hi", "lo", "clus")


def near_field(blocks, near_tiles, target, source, block_rows):
    sources = jnp.take(blocks, source, axis=0)
    product = jnp.einsum("nrk,nkt->nrt", sources, near_tiles, preferred_element_type=jnp.float32)
    onehot = (target[:, None] == jnp.arange(block_rows, dtype=jnp.int32)[None, :]).astype(jnp.float32)
    summed = jnp.einsum("nrt,nb->rbt", product, onehot, precision=HIGH)
    return summed.reshape(summed.shape[0], -1)


def far_terms(field, far_cols, couple, masks):
    proj = jnp.einsum("rp,ap->ra", field, far_cols, precision=HIGH)
    return jnp.einsum("ira,iab->irb", masks[:, None, :] * proj[None], couple, precision=HIGH)


def packed(field, terms, stats):
    width = field.shape[1]
    rows = -(-terms.size // width)
    flat = jnp.pad(terms.reshape(-1), (0, rows * width - terms.size)).reshape(rows, width)
    last = jnp.pad(stats.reshape(-1), (0, width - stats.size)).reshape(1, width)
    return jnp.concatenate([field, flat, last], axis=0)


def combine(stats):
    norm = jnp.sum(stats[:, 0], axis=0)
    dot = jnp.sum(stats[:, 1], axis=0)
    share = jnp.where(norm > 0, dot / jnp.where(norm > 0, norm, 1.0), 0.0)
    rest = jnp.sum(stats[:, 3] + stats[:, 0] * (stats[:, 2] - share[None]) ** 2, axis=0)
    return jnp.stack([norm, dot, share, rest])


def body(loads, self_term, near_tiles, near_list, far_rows, far_cols, coupling, ranks):
    nrhs, panels = loads.shape
    rank = far_cols.shape[0]
    tile = near_tiles.shape[1]
    block_rows = panels // tile
    layers, lows, cores = (lax.axis_size(axis) for axis in GROUP)
    groups = layers * lows * cores
    layer, low, core = (lax.axis_index(axis) for axis in GROUP)
    me = (layer * lows + low) * cores + core
    masks = (jnp.arange(rank, dtype=jnp.int32)[None, :] < ranks[:, 0][:, None]).astype(jnp.float32)
    couple = coupling[:, 0]
    target = near_list[:, 0]
    source = near_list[:, 1] + low * (cores * block_rows)
    term_size = groups * nrhs * rank

    def split(gathered):
        count = gathered.shape[0]
        field = gathered[:, :nrhs]
        terms = gathered[:, nrhs:-1].reshape(count, -1)[:, :term_size].reshape(count, groups, nrhs, rank)
        stats = gathered[:, -1]
        return field, terms, stats

    def first_round(field, terms, stats):
        kinds = stats.shape[0]
        got = lax.all_gather(packed(field, terms, stats), "hi", axis=0)
        fields, terms, stats = split(got)
        stats = stats[:, : kinds * nrhs].reshape(layers, kinds, nrhs)
        wanted = layer + 1 - 2 * low
        beside = lax.dynamic_index_in_dim(fields, jnp.clip(wanted, 0, layers - 1), 0, keepdims=False)
        beside = jnp.where((wanted >= 0) & (wanted < layers), beside, 0.0)
        both = jnp.concatenate([field, beside], axis=0)
        stats = combine(stats) if kinds == 4 else jnp.sum(stats, axis=0)
        got = lax.all_gather(packed(both, jnp.sum(terms, axis=0), stats), LAYER, axis=0)
        own = got[:, :nrhs].reshape(lows, cores, nrhs, panels)
        beside = got[:, nrhs : 2 * nrhs].reshape(lows, cores, nrhs, panels)
        window = jnp.concatenate([beside[1], own[0], own[1], beside[0]], axis=0)
        _, terms, stats = split(got[:, nrhs:])
        far = jnp.sum(lax.dynamic_index_in_dim(terms, me, 1, keepdims=False), axis=0)
        return window, far, stats[:, : kinds * nrhs].reshape(-1, kinds, nrhs)

    def second_round(field, terms, stats):
        if groups > 64:
            return first_round(field, terms, stats)
        kinds = stats.shape[0]
        got = lax.all_gather(packed(field, terms, stats), GROUP, axis=0)
        fields, terms, stats = split(got)
        far = jnp.sum(lax.dynamic_index_in_dim(terms, me, 1, keepdims=False), axis=0)
        edge = jnp.zeros((cores,) + fields.shape[1:], fields.dtype)
        fields = jnp.concatenate([edge, fields, edge], axis=0)
        window = lax.dynamic_slice_in_dim(fields, layer * lows * cores, (lows + 2) * cores, 0)
        return window, far, stats[:, : kinds * nrhs].reshape(-1, kinds, nrhs)

    def image_of(field, window, far_sum):
        blocks = window.astype(jnp.bfloat16).reshape(-1, nrhs, block_rows, tile)
        blocks = blocks.transpose(0, 2, 1, 3).reshape(-1, nrhs, tile)
        near = near_field(blocks, near_tiles, target, source, block_rows)
        far = jnp.einsum("rb,bp->rp", far_sum, far_rows, precision=HIGH)
        return self_term[None, :] * field + near + far

    square = jnp.sum(loads * loads, axis=1)[None]
    window, far, stats = first_round(loads, far_terms(loads, far_cols, couple, masks), square)
    beta = jnp.sqrt(jnp.sum(stats[:, 0], axis=0))
    basis0 = loads / beta[:, None]
    window0 = window / beta[None, :, None]
    far0 = far / beta[:, None]
    image0 = image_of(basis0, window0, far0)

    norm = jnp.sum(basis0 * basis0, axis=1)
    dot = jnp.sum(basis0 * image0, axis=1)
    share = jnp.where(norm > 0, dot / jnp.where(norm > 0, norm, 1.0), 0.0)
    rest = image0 - share[:, None] * basis0
    stats = jnp.stack([norm, dot, share, jnp.sum(rest * rest, axis=1)])
    window, far, stats = second_round(image0, far_terms(image0, far_cols, couple, masks), stats)
    _, h00, _, square = combine(stats)
    h10 = jnp.sqrt(square)
    basis1 = (image0 - h00[:, None] * basis0) / h10[:, None]
    window1 = (window - h00[None, :, None] * window0) / h10[None, :, None]
    far1 = (far - h00[:, None] * far0) / h10[:, None]
    image1 = image_of(basis1, window1, far1)

    stats = jnp.stack(
        [
            jnp.sum(basis0 * image1, axis=1),
            jnp.sum(basis1 * image1, axis=1),
            jnp.sum(image1 * image1, axis=1),
        ]
    )
    stats = lax.all_gather(lax.all_gather(stats, LAYER, axis=0), "hi", axis=0)
    h01, h11, gram11 = jnp.sum(stats, axis=(0, 1))
    gram00 = h00 * h00 + h10 * h10
    gram01 = h00 * h01 + h10 * h11
    lower00 = jnp.sqrt(gram00)
    lower10 = gram01 / lower00
    lower11 = jnp.sqrt(gram11 - lower10 * lower10)
    middle0 = beta * h00 / lower00
    middle1 = (beta * h01 - lower10 * middle0) / lower11
    y1 = middle1 / lower11
    y0 = (middle0 - lower10 * y1) / lower00
    return y0[:, None] * basis0 + y1[:, None] * basis1


def solution(mesh):
    cases, strips, cores = (mesh.shape[axis] for axis in ("case", "strip", "clus"))
    fine = Mesh(mesh.devices.reshape(cases, strips // 2, 2, cores), ("case",) + GROUP)
    every = ("case",) + GROUP
    in_specs = (
        P(None, every),
        P(every),
        P(every, None, None),
        P(every, None),
        P(None, every),
        P(None, every),
        P(None, GROUP, None, None),
        P(None, GROUP),
    )
    return jax.shard_map(body, mesh=fine, in_specs=in_specs, out_specs=P(None, every), check_vma=False)
```

```python
import functools

import jax
import jax.numpy as jnp
from jax import lax
from jax.experimental import pallas as pl
from jax.experimental.pallas import tpu as pltpu
from jax.sharding import PartitionSpec as P

HIGH = lax.Precision.HIGHEST
GROUP = ("strip", "clus")
LANES = 128
CHUNK = 16
F32 = jnp.float32


def lanes_of(shape):
    return lax.broadcasted_iota(jnp.int32, shape, 1)


def rows_of(shape):
    return lax.broadcasted_iota(jnp.int32, shape, 0)


def stats_row(columns, rank):
    shape = (columns[0].shape[0], LANES)
    first = lanes_of(shape) - rank * rows_of(shape)
    spread = sum(jnp.where(first == k, column, 0.0) for k, column in enumerate(columns))
    return jnp.sum(spread, axis=0, keepdims=True)


def stat_column(row, k, nrhs, rank):
    shape = (nrhs, LANES)
    first = lanes_of(shape) - rank * rows_of(shape)
    return jnp.sum(jnp.where(first == k, row, 0.0), axis=1, keepdims=True)


def shifted(value, k):
    return pltpu.roll(value, LANES - k, 1)


def far_sum_of(got_ref, nrhs, rank):
    row = jnp.sum(got_ref[:, 0, :LANES], axis=0, keepdims=True)
    shape = (nrhs, LANES)
    first = lanes_of(shape) - rank * rows_of(shape)
    own = jnp.where((first >= 0) & (first < rank), row, 0.0)
    return sum((pltpu.roll(own, k * rank, 1) for k in range(1, LANES // rank)), own)


def put_message(field, columns, far_cols_ref, couple_ref, ranks_ref, sent_ref):
    nrhs, rank = field.shape[0], far_cols_ref.shape[0]
    groups = sent_ref.shape[0]
    proj = lax.dot_general(
        field, far_cols_ref[...], (((1,), (1,)), ((), ())), precision=HIGH, preferred_element_type=F32
    )
    wide = jnp.concatenate([proj] * CHUNK, axis=1)
    shape = (CHUNK, CHUNK * rank)
    owner = lax.div(lanes_of(shape), rank)
    inner = lax.rem(lanes_of(shape), rank)
    row = stats_row(columns, rank)
    for start in range(0, groups, CHUNK):
        limit = jnp.zeros(shape, jnp.int32)
        for i in range(CHUNK):
            limit = jnp.where(owner == i, ranks_ref[0, start + i], limit)
        keep = (owner == rows_of(shape)) & (inner < limit)
        spread = jnp.concatenate([jnp.where(keep, wide[r : r + 1], 0.0) for r in range(nrhs)], axis=0)
        couple = couple_ref[pl.ds(start * rank, CHUNK * rank), :]
        terms = jnp.dot(spread, couple, precision=HIGH, preferred_element_type=F32)
        terms = jnp.concatenate([terms[r * CHUNK : (r + 1) * CHUNK] for r in range(nrhs)], axis=1)
        sent_ref[pl.ds(start, CHUNK), 0, :LANES] = terms
        sent_ref[pl.ds(start, CHUNK), 0, LANES:] = jnp.broadcast_to(row, (CHUNK, LANES))


def put_blocks(part, first, window):
    part = part.astype(jnp.bfloat16).astype(F32)
    part = jnp.concatenate([part, jnp.zeros_like(part)], axis=0)
    for c in range(part.shape[1] // LANES):
        window[first + c] = part[:, c * LANES : (c + 1) * LANES]


def near_field(window, tiles_ref, list_ref, sums):
    for total in sums:
        total[...] = jnp.zeros_like(total)
    for n in range(tiles_ref.shape[0]):
        total = sums[n % len(sums)]
        source = window[list_ref[1, n]].astype(jnp.bfloat16)
        product = jnp.dot(source, tiles_ref[n], preferred_element_type=F32)
        total[list_ref[0, n]] += product
    whole = sum((total[...] for total in sums[1:]), sums[0][...])
    return jnp.concatenate([whole[b] for b in range(whole.shape[0])], axis=1)


def start_kernel(loads_ref, far_cols_ref, couple_ref, ranks_ref, sent_ref, field_ref):
    loads = loads_ref[...]
    field_ref[...] = loads
    square = jnp.sum(loads * loads, axis=1, keepdims=True)
    put_message(loads, [square], far_cols_ref, couple_ref, ranks_ref, sent_ref)


def image_of(field, far, self_ref, far_rows_ref, near):
    rank = far_rows_ref.shape[0]
    far = jnp.dot(far[:, :rank], far_rows_ref[...], precision=HIGH, preferred_element_type=F32)
    return self_ref[...] * field + near[: field.shape[0]] + far


def step0_kernel(
    loads_ref, before_ref, pair_ref, after_ref, got_ref, self_ref, tiles_ref, list_ref, far_rows_ref,
    far_cols_ref, couple_ref, ranks_ref, sent_ref, image_ref, state_ref, window, *sums,
):
    nrhs, rank = loads_ref.shape[0], far_rows_ref.shape[0]
    row = jnp.sum(got_ref[:, 0, LANES:], axis=0, keepdims=True)
    beta = jnp.sqrt(stat_column(row, 0, nrhs, rank))
    basis = loads_ref[...] / beta
    first = 0
    for part in (before_ref, pair_ref, after_ref):
        put_blocks(part[...] / beta, first, window)
        first += part.shape[1] // LANES
    far = far_sum_of(got_ref, nrhs, rank) / beta
    near = near_field(window, tiles_ref, list_ref, sums)
    image = image_of(basis, far, self_ref, far_rows_ref, near)
    image_ref[...] = image
    state_ref[...] = jnp.concatenate([far, jnp.broadcast_to(beta, far.shape)], axis=0)
    norm = jnp.sum(basis * basis, axis=1, keepdims=True)
    dot = jnp.sum(basis * image, axis=1, keepdims=True)
    share = jnp.where(norm > 0, dot / jnp.where(norm > 0, norm, 1.0), 0.0)
    rest = image - share * basis
    rest = jnp.sum(rest * rest, axis=1, keepdims=True)
    put_message(image, [norm, dot, share, rest], far_cols_ref, couple_ref, ranks_ref, sent_ref)


def step1_kernel(
    loads_ref, before_ref, pair_ref, after_ref, image_ref, image_before_ref, image_pair_ref, image_after_ref,
    got_ref, state_ref, self_ref, tiles_ref, list_ref, far_rows_ref, sent_ref, basis_ref, coeff_ref, window, *sums,
):
    nrhs, rank = loads_ref.shape[0], far_rows_ref.shape[0]
    beta = state_ref[nrhs:, :1]
    far0 = state_ref[:nrhs, :]
    stats = got_ref[:, 0, LANES:]
    row = jnp.sum(stats, axis=0, keepdims=True)
    h00 = stat_column(row, 1, nrhs, rank)
    away = shifted(stats, 2) - shifted(row, 1)
    rest = jnp.sum(shifted(stats, 3) + stats * away * away, axis=0, keepdims=True)
    h10 = jnp.sqrt(stat_column(rest, 0, nrhs, rank))
    basis0 = loads_ref[...] / beta
    basis1 = (image_ref[...] - h00 * basis0) / h10
    first = 0
    for part, image_part in (
        (before_ref, image_before_ref), (pair_ref, image_pair_ref), (after_ref, image_after_ref)
    ):
        put_blocks((image_part[...] - h00 * (part[...] / beta)) / h10, first, window)
        first += part.shape[1] // LANES
    far = (far_sum_of(got_ref, nrhs, rank) - h00 * far0) / h10
    near = near_field(window, tiles_ref, list_ref, sums)
    image = image_of(basis1, far, self_ref, far_rows_ref, near)
    columns = [jnp.sum(a * image, axis=1, keepdims=True) for a in (basis0, basis1, image)]
    row = stats_row(columns, rank)
    sent_ref[:, 0, :] = jnp.broadcast_to(row, (sent_ref.shape[0], LANES))
    basis_ref[...] = jnp.concatenate([basis0, basis1], axis=0)
    coeff_ref[...] = jnp.concatenate([jnp.broadcast_to(v, (nrhs, LANES)) for v in (beta, h00, h10)], axis=0)


def finish_kernel(rank, got_ref, basis_ref, coeff_ref, out_ref):
    nrhs = out_ref.shape[0]
    row = jnp.sum(got_ref[:, 0, :], axis=0, keepdims=True)
    h01, h11, gram11 = (stat_column(row, k, nrhs, rank) for k in range(3))
    beta, h00, h10 = (coeff_ref[k * nrhs : (k + 1) * nrhs, :1] for k in range(3))
    gram00 = h00 * h00 + h10 * h10
    gram01 = h00 * h01 + h10 * h11
    lower00 = jnp.sqrt(gram00)
    lower10 = gram01 / lower00
    lower11 = jnp.sqrt(gram11 - lower10 * lower10)
    middle0 = beta * h00 / lower00
    middle1 = (beta * h01 - lower10 * middle0) / lower11
    y1 = middle1 / lower11
    y0 = (middle0 - lower10 * y1) / lower00
    out_ref[...] = y0 * basis_ref[:nrhs, :] + y1 * basis_ref[nrhs:, :]


def call(kernel, args, outs, scratch=(), smem=()):
    in_specs = [
        pl.BlockSpec(memory_space=pltpu.SMEM if i in smem else pltpu.VMEM) for i in range(len(args))
    ]
    return pl.pallas_call(
        kernel,
        out_shape=[jax.ShapeDtypeStruct(shape, F32) for shape in outs],
        in_specs=in_specs,
        out_specs=[pl.BlockSpec(memory_space=pltpu.VMEM)] * len(outs),
        scratch_shapes=list(scratch),
        compiler_params=pltpu.CompilerParams(vmem_limit_bytes=32 * 2**20),
    )(*args)


def window_of(field):
    pair = lax.all_gather(field, "clus", axis=1, tiled=True)
    devices = lax.axis_size("strip")
    up = [(i, i + 1) for i in range(devices - 1)]
    down = [(j, i) for i, j in up]
    return lax.ppermute(pair, "strip", up), pair, lax.ppermute(pair, "strip", down)


def exchanged(message):
    return lax.all_to_all(message, GROUP, 0, 0, tiled=True)


def body(loads, self_term, near_tiles, near_list, far_rows, far_cols, coupling, ranks):
    nrhs, panels = loads.shape
    rank = far_cols.shape[0]
    tile = near_tiles.shape[1]
    rows = panels // tile
    cores = lax.axis_size("clus")
    groups = lax.axis_size("strip") * cores
    couple = coupling.reshape(groups * rank, rank)
    near_list = near_list.T
    ranks = ranks.reshape(1, groups)
    self_term = self_term.reshape(1, panels)
    message = (groups, 1, 2 * LANES)
    scratch = [pltpu.VMEM((3 * cores * rows, 2 * nrhs, tile), F32)]
    scratch += [pltpu.VMEM((rows, 2 * nrhs, tile), F32)] * 4

    sent, field = call(start_kernel, (loads, far_cols, couple, ranks), [message, loads.shape], smem=(3,))
    got = exchanged(sent)
    before, pair, after = window_of(field)
    sent, image, state = call(
        step0_kernel,
        (loads, before, pair, after, got, self_term, near_tiles, near_list, far_rows, far_cols, couple, ranks),
        [message, loads.shape, (2 * nrhs, LANES)],
        scratch,
        smem=(7, 11),
    )
    got = exchanged(sent)
    image_before, image_pair, image_after = window_of(image)
    sent, basis, coeff = call(
        step1_kernel,
        (
            loads, before, pair, after, image, image_before, image_pair, image_after, got, state, self_term,
            near_tiles, near_list, far_rows,
        ),
        [(groups, 1, LANES), (2 * nrhs, panels), (3 * nrhs, LANES)],
        scratch,
        smem=(12,),
    )
    got = exchanged(sent)
    return call(functools.partial(finish_kernel, rank), (got, basis, coeff), [loads.shape])[0]


def solution(mesh):
    every = ("case",) + GROUP
    in_specs = (
        P(None, every),
        P(every),
        P(every, None, None),
        P(every, None),
        P(None, every),
        P(None, every),
        P(None, GROUP, None, None),
        P(None, GROUP),
    )
    return jax.shard_map(body, mesh=mesh, in_specs=in_specs, out_specs=P(None, every), check_vma=False)
```

```python
import functools

import jax
import jax.numpy as jnp
from jax import lax
from jax.experimental import pallas as pl
from jax.experimental.pallas import tpu as pltpu
from jax.sharding import Mesh
from jax.sharding import PartitionSpec as P

HIGH = lax.Precision.HIGHEST
GROUP = ("hi", "lo", "clus")
LANES = 128
CHUNK = 16
F32 = jnp.float32


def lanes_of(shape):
    return lax.broadcasted_iota(jnp.int32, shape, 1)


def rows_of(shape):
    return lax.broadcasted_iota(jnp.int32, shape, 0)


def stats_row(columns, rank):
    shape = (columns[0].shape[0], LANES)
    first = lanes_of(shape) - rank * rows_of(shape)
    spread = sum(jnp.where(first == k, column, 0.0) for k, column in enumerate(columns))
    return jnp.sum(spread, axis=0, keepdims=True)


def stat_column(row, k, nrhs, rank):
    shape = (nrhs, LANES)
    first = lanes_of(shape) - rank * rows_of(shape)
    return jnp.sum(jnp.where(first == k, row, 0.0), axis=1, keepdims=True)


def shifted(value, k):
    return pltpu.roll(value, LANES - k, 1)


def far_sum_of(row, nrhs, rank):
    shape = (nrhs, LANES)
    first = lanes_of(shape) - rank * rows_of(shape)
    own = jnp.where((first >= 0) & (first < rank), row, 0.0)
    return sum((pltpu.roll(own, k * rank, 1) for k in range(1, LANES // rank)), own)


def total(rows):
    return jnp.sum(rows, axis=0, keepdims=True)


def put_message(field, columns, far_cols, couple_ref, ranks_ref, groups, put):
    nrhs, rank = field.shape[0], far_cols.shape[0]
    proj = lax.dot_general(
        field, far_cols, (((1,), (1,)), ((), ())), precision=HIGH, preferred_element_type=F32
    )
    wide = jnp.concatenate([proj] * CHUNK, axis=1)
    shape = (CHUNK, CHUNK * rank)
    owner = lax.div(lanes_of(shape), rank)
    inner = lax.rem(lanes_of(shape), rank)
    row = stats_row(columns, rank)
    for start in range(0, groups, CHUNK):
        limit = jnp.zeros(shape, jnp.int32)
        for i in range(CHUNK):
            limit = jnp.where(owner == i, ranks_ref[0, start + i], limit)
        keep = (owner == rows_of(shape)) & (inner < limit)
        spread = jnp.concatenate([jnp.where(keep, wide[r : r + 1], 0.0) for r in range(nrhs)], axis=0)
        couple = couple_ref[pl.ds(start * rank, CHUNK * rank), :]
        terms = jnp.dot(spread, couple, precision=HIGH, preferred_element_type=F32)
        terms = jnp.concatenate([terms[r * CHUNK : (r + 1) * CHUNK] for r in range(nrhs)], axis=1)
        put(start, terms, row)


def put_blocks(part, first, window):
    part = part.astype(jnp.bfloat16).astype(F32)
    part = jnp.concatenate([part, jnp.zeros_like(part)], axis=0)
    for c in range(part.shape[1] // LANES):
        window[first + c] = part[:, c * LANES : (c + 1) * LANES]


def near_field(window, tiles_ref, list_ref, sums):
    for held in sums:
        held[...] = jnp.zeros_like(held)
    for n in range(tiles_ref.shape[0]):
        held = sums[n % len(sums)]
        source = window[list_ref[1, n]].astype(jnp.bfloat16)
        product = jnp.dot(source, tiles_ref[n], preferred_element_type=F32)
        held[list_ref[0, n]] += product
    whole = sum((held[...] for held in sums[1:]), sums[0][...])
    return jnp.concatenate([whole[b] for b in range(whole.shape[0])], axis=1)


def start_kernel(loads_ref, ranks_ref, *refs):
    count = 5
    sources, (sent_ref, field_ref), held, sems = refs[:count], refs[count : count + 2], refs[count + 2 : -1], refs[-1]
    copies = [pltpu.make_async_copy(a, b, sems.at[i]) for i, (a, b) in enumerate(zip(sources, held))]
    for copy in copies:
        copy.start()
    loads = loads_ref[...]
    field_ref[...] = loads
    square = jnp.sum(loads * loads, axis=1, keepdims=True)
    copies[0].wait()
    copies[1].wait()

    def put(start, terms, row):
        sent_ref[pl.ds(start, CHUNK), 0, :LANES] = terms
        sent_ref[pl.ds(start, CHUNK), 0, LANES:] = jnp.broadcast_to(row, terms.shape)

    put_message(loads, [square], held[0][...], held[1], ranks_ref, sent_ref.shape[0], put)
    for copy in copies[2:]:
        copy.wait()


def image_of(field, far, self_ref, far_rows_ref, near):
    rank = far_rows_ref.shape[0]
    far = jnp.dot(far[:, :rank], far_rows_ref[...], precision=HIGH, preferred_element_type=F32)
    return self_ref[...] * field + near[: field.shape[0]] + far


def step0_kernel(
    loads_ref, pair_ref, even_ref, odd_ref, got_ref, far_cols_ref, couple_ref, tiles_ref, far_rows_ref, self_ref,
    list_ref, ranks_ref, sent_ref, window0_ref, state_ref, window, *sums,
):
    nrhs, rank = loads_ref.shape[0], far_rows_ref.shape[0]
    span = pair_ref.shape[1] // LANES
    low, core = lax.axis_index("lo"), lax.axis_index("clus")
    mine = lax.rem(rows_of((got_ref.shape[1], LANES)), 2) == core
    got = [jnp.where(mine, got_ref[0, :, 0, k : k + LANES], 0.0) + jnp.where(mine, got_ref[1, :, 0, k : k + LANES], 0.0) for k in (0, LANES)]
    beta = jnp.sqrt(stat_column(total(got[1]), 0, nrhs, rank))
    basis = loads_ref[...] / beta
    for part_ref, place in ((pair_ref, 1), (even_ref, 2 * (1 - low)), (odd_ref, 2 * low)):
        part = part_ref[...] / beta
        window0_ref[place] = part
        put_blocks(part, place * span, window)
    far = far_sum_of(total(got[0]), nrhs, rank) / beta
    near = near_field(window, tiles_ref, list_ref, sums)
    image = image_of(basis, far, self_ref, far_rows_ref, near)
    state_ref[...] = jnp.concatenate([far, jnp.broadcast_to(beta, far.shape)], axis=0)
    norm = jnp.sum(basis * basis, axis=1, keepdims=True)
    dot = jnp.sum(basis * image, axis=1, keepdims=True)
    share = jnp.where(norm > 0, dot / jnp.where(norm > 0, norm, 1.0), 0.0)
    rest = image - share * basis
    rest = jnp.sum(rest * rest, axis=1, keepdims=True)

    def put(start, terms, row):
        blank = jnp.zeros((nrhs - 2, LANES), F32)
        for i in range(CHUNK):
            tail = jnp.concatenate([terms[i : i + 1], row, blank], axis=0)
            sent_ref[start + i] = jnp.concatenate([image, tail], axis=1)

    put_message(image, [norm, dot, share, rest], far_cols_ref[...], couple_ref, ranks_ref, sent_ref.shape[0], put)


def step1_kernel(
    loads_ref, window0_ref, got_ref, state_ref, tiles_ref, far_rows_ref, self_ref, list_ref,
    sent_ref, basis_ref, coeff_ref, window, *sums,
):
    nrhs, rank = loads_ref.shape[0], far_rows_ref.shape[0]
    panels = loads_ref.shape[1]
    groups = got_ref.shape[0]
    beta = state_ref[nrhs:, :1]
    far0 = state_ref[:nrhs, :]
    tail = got_ref[:, :, panels:]
    summed = jnp.sum(tail, axis=0)
    h00 = stat_column(summed[1:2], 1, nrhs, rank)
    stats = tail[:, 1]
    away = shifted(stats, 2) - shifted(summed[1:2], 1)
    rest = total(shifted(stats, 3) + stats * away * away)
    h10 = jnp.sqrt(stat_column(rest, 0, nrhs, rank))
    basis0 = loads_ref[...] / beta
    strip = lax.axis_index("hi") * 2 + lax.axis_index("lo")
    core = lax.axis_index("clus")
    cores = lax.axis_size("clus")
    image0 = got_ref[strip * cores + core, :, :panels]
    basis1 = (image0 - h00 * basis0) / h10
    span = panels // LANES
    for i in range(3 * cores):
        owner = (strip - 1) * cores + i
        inside = (owner >= 0) & (owner < groups)
        owner = jnp.clip(owner, 0, groups - 1)
        field = jnp.where(inside, got_ref[owner, :, :panels], 0.0)
        field0 = window0_ref[i // cores, :, (i % cores) * panels : (i % cores + 1) * panels]
        put_blocks((field - h00 * field0) / h10, i * span, window)
    far = (far_sum_of(summed[0:1], nrhs, rank) - h00 * far0) / h10
    near = near_field(window, tiles_ref, list_ref, sums)
    image = image_of(basis1, far, self_ref, far_rows_ref, near)
    columns = [jnp.sum(a * image, axis=1, keepdims=True) for a in (basis0, basis1, image)]
    row = stats_row(columns, rank)
    sent_ref[:, 0, :] = jnp.broadcast_to(row, (sent_ref.shape[0], LANES))
    basis_ref[...] = jnp.concatenate([basis0, basis1], axis=0)
    coeff_ref[...] = jnp.concatenate([jnp.broadcast_to(v, (nrhs, LANES)) for v in (beta, h00, h10)], axis=0)


def relay_kernel(got_ref, sent_ref):
    row = total(got_ref[:, 0, :])
    sent_ref[:, 0, :] = jnp.broadcast_to(row, (sent_ref.shape[0], LANES))


def finish_kernel(rank, got_ref, basis_ref, coeff_ref, out_ref):
    nrhs = out_ref.shape[0]
    row = total(got_ref[:, 0, :])
    h01, h11, gram11 = (stat_column(row, k, nrhs, rank) for k in range(3))
    beta, h00, h10 = (coeff_ref[k * nrhs : (k + 1) * nrhs, :1] for k in range(3))
    gram00 = h00 * h00 + h10 * h10
    gram01 = h00 * h01 + h10 * h11
    lower00 = jnp.sqrt(gram00)
    lower10 = gram01 / lower00
    lower11 = jnp.sqrt(gram11 - lower10 * lower10)
    middle0 = beta * h00 / lower00
    middle1 = (beta * h01 - lower10 * middle0) / lower11
    y1 = middle1 / lower11
    y0 = (middle0 - lower10 * y1) / lower00
    out_ref[...] = y0 * basis_ref[:nrhs, :] + y1 * basis_ref[nrhs:, :]


def call(kernel, args, outs, scratch=(), smem=(), held=()):
    space = {i: pltpu.SMEM for i in smem} | {i: pl.ANY for i in held}
    args = [pltpu.with_memory_space_constraint(a, pltpu.HBM) if i in held else a for i, a in enumerate(args)]
    return pl.pallas_call(
        kernel,
        out_shape=[
            in_vmem_like(out) if hasattr(out, "dtype") else jax.ShapeDtypeStruct(out, F32) for out in outs
        ],
        in_specs=[pl.BlockSpec(memory_space=space.get(i, pltpu.VMEM)) for i in range(len(args))],
        out_specs=[pl.BlockSpec(memory_space=pltpu.VMEM)] * len(outs),
        scratch_shapes=list(scratch),
        compiler_params=pltpu.CompilerParams(vmem_limit_bytes=24 * 2**20),
    )(*args)


def in_vmem_like(array):
    return pltpu.VMEM(array.shape, array.dtype)


def in_vmem(arrays):
    return [pltpu.with_memory_space_constraint(a, pltpu.VMEM) for a in arrays]


def body(loads, self_term, near_tiles, near_list, far_rows, far_cols, coupling, ranks):
    nrhs, panels = loads.shape
    rank = far_cols.shape[0]
    tile = near_tiles.shape[1]
    rows = panels // tile
    layers, lows, cores = (lax.axis_size(axis) for axis in GROUP)
    strips = layers * lows
    groups = strips * cores
    couple = coupling.reshape(groups * rank, rank)
    near_list = near_list.T
    ranks = ranks.reshape(1, groups)
    self_term = self_term.reshape(1, panels)
    scratch = [pltpu.VMEM((3 * cores * rows, 2 * nrhs, tile), F32)]
    scratch += [pltpu.VMEM((rows, 2 * nrhs, tile), F32)] * 4

    constants = (far_cols, couple, near_tiles, far_rows, self_term)
    sent, field, *constants = call(
        start_kernel,
        (loads, ranks) + constants,
        [(groups, 1, 2 * LANES), loads.shape] + list(constants),
        [pltpu.SemaphoreType.DMA((5,))],
        smem=(1,),
        held=range(2, 7),
    )
    far_cols, couple, near_tiles, far_rows, self_term = constants = in_vmem(constants)
    even = [(i, i ^ 1) for i in range(strips)]
    odd = [(i, j) for i in range(1, strips - 1, 2) for i, j in ((i, i + 1), (i + 1, i))]
    even, odd = (lax.ppermute(field, ("hi", "lo"), pairs) for pairs in (even, odd))
    got = lax.all_to_all(sent, ("hi", "lo"), 0, 0, tiled=True)
    pair, even, odd = (lax.all_gather(a, "clus", axis=1, tiled=True) for a in (field, even, odd))
    got = lax.all_gather(got, "clus", axis=0)
    sent, window0, state = call(
        step0_kernel,
        (loads, pair, even, odd, got, *constants, near_list, ranks),
        [(groups, nrhs, panels + LANES), (3, nrhs, cores * panels), (2 * nrhs, LANES)],
        scratch,
        smem=(10, 11),
    )
    got = lax.all_to_all(sent, GROUP, 0, 0, tiled=True)
    sent, basis, coeff = call(
        step1_kernel,
        (loads, window0, got, state, near_tiles, far_rows, self_term, near_list),
        [(layers, 1, LANES), (2 * nrhs, panels), (3 * nrhs, LANES)],
        scratch,
        smem=(7,),
    )
    got = lax.all_to_all(sent, "hi", 0, 0, tiled=True)
    (sent,) = call(relay_kernel, (got,), [(lows * cores, 1, LANES)])
    got = lax.all_to_all(sent, ("lo", "clus"), 0, 0, tiled=True)
    return call(functools.partial(finish_kernel, rank), (got, basis, coeff), [loads.shape])[0]


def solution(mesh):
    cases, strips, cores = (mesh.shape[axis] for axis in ("case", "strip", "clus"))
    fine = Mesh(mesh.devices.reshape(cases, strips // 2, 2, cores), ("case",) + GROUP)
    every = ("case",) + GROUP
    in_specs = (
        P(None, every),
        P(every),
        P(every, None, None),
        P(every, None),
        P(None, every),
        P(None, every),
        P(None, GROUP, None, None),
        P(None, GROUP),
    )
    return jax.shard_map(body, mesh=fine, in_specs=in_specs, out_specs=P(None, every), check_vma=False)
```

```python
import functools

import jax
import jax.numpy as jnp
from jax import lax
from jax.experimental import pallas as pl
from jax.experimental.pallas import tpu as pltpu
from jax.sharding import Mesh
from jax.sharding import PartitionSpec as P

HIGH = lax.Precision.HIGHEST
STRIP = ("high", "mid", "low")
GROUP = STRIP + ("clus",)
LANES = 128
CHUNK = 16
PIECES = 8
F32 = jnp.float32


def fold_of(strips, field):
    return max(LANES, field.size // strips)


def lanes_of(shape):
    return lax.broadcasted_iota(jnp.int32, shape, 1)


def rows_of(shape):
    return lax.broadcasted_iota(jnp.int32, shape, 0)


def stats_row(columns, rank):
    shape = (columns[0].shape[0], LANES)
    first = lanes_of(shape) - rank * rows_of(shape)
    spread = sum(jnp.where(first == k, column, 0.0) for k, column in enumerate(columns))
    return jnp.sum(spread, axis=0, keepdims=True)


def stat_column(row, k, nrhs, rank):
    shape = (nrhs, LANES)
    first = lanes_of(shape) - rank * rows_of(shape)
    return jnp.sum(jnp.where(first == k, row, 0.0), axis=1, keepdims=True)


def shifted(value, k):
    return pltpu.roll(value, LANES - k, 1)


def far_sum_of(row, nrhs, rank):
    shape = (nrhs, LANES)
    first = lanes_of(shape) - rank * rows_of(shape)
    own = jnp.where((first >= 0) & (first < rank), row, 0.0)
    return sum((pltpu.roll(own, k * rank, 1) for k in range(1, LANES // rank)), own)


def total(rows):
    return jnp.sum(rows, axis=0, keepdims=True)


def put_message(field, columns, far_cols, couple_ref, ranks_ref, sent_ref):
    nrhs, rank = field.shape[0], far_cols.shape[0]
    strips, fold = sent_ref.shape[0], fold_of(sent_ref.shape[0], field)
    for part in range(field.shape[1] // fold):
        sent_ref[pl.ds(part * nrhs, nrhs), 0, :fold] = field[:, part * fold : (part + 1) * fold]
    proj = lax.dot_general(
        field, far_cols, (((1,), (1,)), ((), ())), precision=HIGH, preferred_element_type=F32
    )
    wide = jnp.concatenate([proj] * CHUNK, axis=1)
    shape = (CHUNK, CHUNK * rank)
    owner = lax.div(lanes_of(shape), rank)
    inner = lax.rem(lanes_of(shape), rank)
    row = stats_row(columns, rank)
    half = CHUNK // 2
    number = rows_of(shape)
    number = jnp.where(number < half, 2 * number, 2 * (number - half) + 1)
    for start in range(0, strips, half):
        limit = jnp.zeros(shape, jnp.int32)
        for i in range(CHUNK):
            limit = jnp.where(owner == i, ranks_ref[0, 2 * start + i], limit)
        keep = (owner == number) & (inner < limit)
        spread = jnp.concatenate([jnp.where(keep, wide[r : r + 1], 0.0) for r in range(nrhs)], axis=0)
        couple = couple_ref[pl.ds(2 * start * rank, CHUNK * rank), :]
        terms = jnp.dot(spread, couple, precision=HIGH, preferred_element_type=F32)
        terms = jnp.concatenate([terms[r * CHUNK : (r + 1) * CHUNK] for r in range(nrhs)], axis=1)
        here = pl.ds(start, half)
        sent_ref[here, 0, fold : fold + LANES] = terms[:half]
        sent_ref[here, 0, fold + LANES : fold + 2 * LANES] = terms[half:]
        sent_ref[here, 0, fold + 2 * LANES :] = jnp.broadcast_to(row, (half, LANES))


def message_parts(got_ref, core, fold):
    whole = got_ref.shape[2] // 2
    near = [k * whole + fold for k in (0, 1)]
    terms = [
        jnp.where(core == 0, got_ref[:, 0, k : k + LANES], got_ref[:, 0, k + LANES : k + 2 * LANES]) for k in near
    ]
    stats = [got_ref[:, 0, k + 2 * LANES : k + 3 * LANES] for k in near]
    return jnp.concatenate(terms, axis=0), jnp.concatenate(stats, axis=0)


def field_of(pair_ref, core, nrhs, panels, fold):
    base = core * (pair_ref.shape[2] // 2)
    return jnp.concatenate(
        [pair_ref[pl.ds(part * nrhs, nrhs), 0, base : base + fold] for part in range(panels // fold)], axis=1
    )


def put_blocks(part, first, window):
    part = part.astype(jnp.bfloat16).astype(F32)
    part = jnp.concatenate([part, jnp.zeros_like(part)], axis=0)
    for c in range(part.shape[1] // LANES):
        window[first + c] = part[:, c * LANES : (c + 1) * LANES]


def near_field(window, tiles_ref, list_ref, sums, copies=()):
    every = tiles_ref.shape[0] // max(len(copies), 1)
    for held in sums:
        held[...] = jnp.zeros_like(held)
    for n in range(tiles_ref.shape[0]):
        if copies and n % every == 0:
            copies[n // every].wait()
        held = sums[n % len(sums)]
        source = window[list_ref[1, n]].astype(jnp.bfloat16)
        product = jnp.dot(source, tiles_ref[n], preferred_element_type=F32)
        held[list_ref[0, n]] += product
    whole = sum((held[...] for held in sums[1:]), sums[0][...])
    return jnp.concatenate([whole[b] for b in range(whole.shape[0])], axis=1)


def start_kernel(*refs):
    count = 5
    ranks_hbm, sources = refs[0], refs[1 : 1 + count]
    sent_ref, held = refs[1 + count], refs[2 + count : 2 + 2 * count]
    ranks_ref, sems = refs[2 + 2 * count :]
    pairs = [(ranks_hbm, ranks_ref)] + list(zip(sources, held))
    copies = [pltpu.make_async_copy(a, b, sems.at[i]) for i, (a, b) in enumerate(pairs)]
    for copy in copies:
        copy.start()
    for copy in copies:
        copy.wait()
    loads_ref, far_cols_ref, couple_ref = held[:3]
    loads = loads_ref[...]
    square = jnp.sum(loads * loads, axis=1, keepdims=True)
    put_message(loads, [square], far_cols_ref[...], couple_ref, ranks_ref, sent_ref)


def image_of(field, far, self_ref, far_rows_ref, near):
    rank = far_rows_ref.shape[0]
    far = jnp.dot(far[:, :rank], far_rows_ref[...], precision=HIGH, preferred_element_type=F32)
    return self_ref[...] * field + near[: field.shape[0]] + far


def places():
    low = lax.axis_index("low")
    return 1, 2 * (1 - low), 2 * low


def step0_kernel(
    loads_ref, pair_ref, even_ref, odd_ref, got_ref, far_cols_ref, couple_ref, far_rows_ref, self_ref, tiles_hbm,
    list_ref, ranks_ref, sent_ref, state_ref, tiles_ref, sems, window, *sums,
):
    (nrhs, panels), rank = loads_ref.shape, far_rows_ref.shape[0]
    every = tiles_ref.shape[0] // PIECES
    pieces = [pl.ds(i * every, every) for i in range(PIECES)]
    copies = [pltpu.make_async_copy(tiles_hbm.at[p], tiles_ref.at[p], sems.at[i]) for i, p in enumerate(pieces)]
    for copy in copies:
        copy.start()
    span = panels // LANES
    fold = fold_of(sent_ref.shape[0], loads_ref)
    terms, stats = message_parts(got_ref, lax.axis_index("clus"), fold)
    beta = jnp.sqrt(stat_column(total(stats), 0, nrhs, rank))
    basis = loads_ref[...] / beta
    for part_ref, place in zip((pair_ref, even_ref, odd_ref), places()):
        for core in range(2):
            put_blocks(field_of(part_ref, core, nrhs, panels, fold) / beta, (2 * place + core) * span, window)
    far = far_sum_of(total(terms), nrhs, rank) / beta
    near = near_field(window, tiles_ref, list_ref, sums, copies)
    image = image_of(basis, far, self_ref, far_rows_ref, near)
    state_ref[...] = jnp.concatenate([far, jnp.broadcast_to(beta, far.shape)], axis=0)
    norm = jnp.sum(basis * basis, axis=1, keepdims=True)
    dot = jnp.sum(basis * image, axis=1, keepdims=True)
    share = jnp.where(norm > 0, dot / jnp.where(norm > 0, norm, 1.0), 0.0)
    rest = image - share * basis
    rest = jnp.sum(rest * rest, axis=1, keepdims=True)
    put_message(image, [norm, dot, share, rest], far_cols_ref[...], couple_ref, ranks_ref, sent_ref)


def step1_kernel(
    loads_ref, pair_ref, even_ref, odd_ref, sent_image_ref, image_pair_ref, image_even_ref, image_odd_ref, got_ref,
    state_ref, far_rows_ref, self_ref, tiles_ref, list_ref, sent_ref, basis_ref, coeff_ref, window, *sums,
):
    (nrhs, panels), rank = loads_ref.shape, far_rows_ref.shape[0]
    span = panels // LANES
    fold = fold_of(got_ref.shape[0], loads_ref)
    beta = state_ref[nrhs:, :1]
    far0 = state_ref[:nrhs, :]
    terms, stats = message_parts(got_ref, lax.axis_index("clus"), fold)
    summed = total(stats)
    h00 = stat_column(summed, 1, nrhs, rank)
    away = shifted(stats, 2) - shifted(summed, 1)
    rest = total(shifted(stats, 3) + stats * away * away)
    h10 = jnp.sqrt(stat_column(rest, 0, nrhs, rank))
    basis0 = loads_ref[...] / beta
    basis1 = (field_of(sent_image_ref, 0, nrhs, panels, fold) - h00 * basis0) / h10
    refs = zip((pair_ref, even_ref, odd_ref), (image_pair_ref, image_even_ref, image_odd_ref), places())
    for part_ref, image_ref, place in refs:
        for core in range(2):
            part = field_of(part_ref, core, nrhs, panels, fold) / beta
            part = (field_of(image_ref, core, nrhs, panels, fold) - h00 * part) / h10
            put_blocks(part, (2 * place + core) * span, window)
    far = (far_sum_of(total(terms), nrhs, rank) - h00 * far0) / h10
    near = near_field(window, tiles_ref, list_ref, sums)
    image = image_of(basis1, far, self_ref, far_rows_ref, near)
    columns = [jnp.sum(a * image, axis=1, keepdims=True) for a in (basis0, basis1, image)]
    sent_ref[0] = stats_row(columns, rank)
    basis_ref[...] = jnp.concatenate([basis0, basis1], axis=0)
    coeff_ref[...] = jnp.concatenate([jnp.broadcast_to(v, (nrhs, LANES)) for v in (beta, h00, h10)], axis=0)


def finish_kernel(rank, got_ref, basis_ref, coeff_ref, out_ref):
    nrhs = out_ref.shape[0]
    row = total(got_ref[:, 0, :])
    h01, h11, gram11 = (stat_column(row, k, nrhs, rank) for k in range(3))
    beta, h00, h10 = (coeff_ref[k * nrhs : (k + 1) * nrhs, :1] for k in range(3))
    gram00 = h00 * h00 + h10 * h10
    gram01 = h00 * h01 + h10 * h11
    lower00 = jnp.sqrt(gram00)
    lower10 = gram01 / lower00
    lower11 = jnp.sqrt(gram11 - lower10 * lower10)
    middle0 = beta * h00 / lower00
    middle1 = (beta * h01 - lower10 * middle0) / lower11
    y1 = middle1 / lower11
    y0 = (middle0 - lower10 * y1) / lower00
    out_ref[...] = y0 * basis_ref[:nrhs, :] + y1 * basis_ref[nrhs:, :]


def call(kernel, args, outs, scratch=(), smem=(), held=()):
    space = {i: pltpu.SMEM for i in smem} | {i: pl.ANY for i in held}
    args = [pltpu.with_memory_space_constraint(a, pltpu.HBM) if i in held else a for i, a in enumerate(args)]
    return pl.pallas_call(
        kernel,
        out_shape=[
            in_vmem_like(out) if hasattr(out, "dtype") else jax.ShapeDtypeStruct(out, F32) for out in outs
        ],
        in_specs=[pl.BlockSpec(memory_space=space.get(i, pltpu.VMEM)) for i in range(len(args))],
        out_specs=[pl.BlockSpec(memory_space=pltpu.VMEM)] * len(outs),
        scratch_shapes=list(scratch),
        compiler_params=pltpu.CompilerParams(vmem_limit_bytes=24 * 2**20),
    )(*args)


def in_vmem_like(array):
    return pltpu.VMEM(array.shape, array.dtype)


def in_vmem(arrays):
    return [pltpu.with_memory_space_constraint(a, pltpu.VMEM) for a in arrays]


def exchanged(sent):
    strips = sent.shape[0]
    even = [(i, i ^ 1) for i in range(strips)]
    odd = [(i, j) for i in range(1, strips - 1, 2) for i, j in ((i, i + 1), (i + 1, i))]
    pair = lax.all_gather(sent, "clus", axis=2, tiled=True)
    even, odd = (lax.ppermute(pair, STRIP, pairs) for pairs in (even, odd))
    return pair, even, odd, lax.all_to_all(pair, STRIP, 0, 0, tiled=True)


def body(loads, self_term, near_tiles, near_list, far_rows, far_cols, coupling, ranks):
    nrhs, panels = loads.shape
    rank = far_cols.shape[0]
    tile = near_tiles.shape[1]
    rows = panels // tile
    strips = coupling.shape[0] // 2
    couple = coupling.reshape(2 * strips * rank, rank)
    near_list = near_list.T
    ranks = ranks.reshape(1, 2 * strips)
    self_term = self_term.reshape(1, panels)
    scratch = [pltpu.VMEM((6 * rows, 2 * nrhs, tile), F32)]
    scratch += [pltpu.VMEM((rows, 2 * nrhs, tile), F32)] * 4
    message = (strips, 1, fold_of(strips, loads) + 3 * LANES)

    held = (loads, far_cols, couple, far_rows, self_term)
    sent, *held = call(
        start_kernel,
        (ranks,) + held,
        [message] + list(held),
        [pltpu.SMEM(ranks.shape, jnp.int32), pltpu.SemaphoreType.DMA((6,))],
        held=range(6),
    )
    loads, far_cols, couple, far_rows, self_term = in_vmem(held)
    first = exchanged(sent)
    sent, state, near_tiles = call(
        step0_kernel,
        (loads, *first, far_cols, couple, far_rows, self_term, near_tiles, near_list, ranks),
        [message, (2 * nrhs, LANES), near_tiles],
        [pltpu.SemaphoreType.DMA((PIECES,))] + scratch,
        smem=(10, 11),
        held=(9,),
    )
    (near_tiles,) = in_vmem([near_tiles])
    second = exchanged(sent)
    sent, basis, coeff = call(
        step1_kernel,
        (loads, *first[:3], sent, *second, state, far_rows, self_term, near_tiles, near_list),
        [(1, 1, LANES), (2 * nrhs, panels), (3 * nrhs, LANES)],
        scratch,
        smem=(13,),
    )
    for axis in reversed(GROUP):
        sent = lax.all_gather(sent, axis, axis=0, tiled=True)
    return call(functools.partial(finish_kernel, rank), (sent, basis, coeff), [loads.shape])[0]


def solution(mesh):
    cases, strips, cores = (mesh.shape[axis] for axis in ("case", "strip", "clus"))
    fine = Mesh(mesh.devices.reshape(cases, strips // 4, 2, 2, cores), ("case",) + GROUP)
    every = ("case",) + GROUP
    in_specs = (
        P(None, every),
        P(every),
        P(every, None, None),
        P(every, None),
        P(None, every),
        P(None, every),
        P(None, GROUP, None, None),
        P(None, GROUP),
    )
    return jax.shard_map(body, mesh=fine, in_specs=in_specs, out_specs=P(None, every), check_vma=False)
```

```python
import functools

import jax
import jax.numpy as jnp
from jax import lax
from jax.experimental import pallas as pl
from jax.experimental.pallas import tpu as pltpu
from jax.sharding import PartitionSpec as P

HIGH = lax.Precision.HIGHEST
GROUP = ("strip", "clus")
LANES = 128
CHUNK = 16
PIECES = 8
F32 = jnp.float32


CORES = 2


def lanes_of(shape):
    return lax.broadcasted_iota(jnp.int32, shape, 1)


def rows_of(shape):
    return lax.broadcasted_iota(jnp.int32, shape, 0)


def stats_row(columns, rank):
    shape = (columns[0].shape[0], LANES)
    first = lanes_of(shape) - rank * rows_of(shape)
    spread = sum(jnp.where(first == k, column, 0.0) for k, column in enumerate(columns))
    return jnp.sum(spread, axis=0, keepdims=True)


def stat_column(row, k, nrhs, rank):
    shape = (nrhs, LANES)
    first = lanes_of(shape) - rank * rows_of(shape)
    return jnp.sum(jnp.where(first == k, row, 0.0), axis=1, keepdims=True)


def shifted(value, k):
    return pltpu.roll(value, LANES - k, 1)


def far_sum_of(row, nrhs, rank):
    shape = (nrhs, LANES)
    first = lanes_of(shape) - rank * rows_of(shape)
    own = jnp.where((first >= 0) & (first < rank), row, 0.0)
    return sum((pltpu.roll(own, k * rank, 1) for k in range(1, LANES // rank)), own)


def total(rows):
    return jnp.sum(rows, axis=0, keepdims=True)


def put_message(field, columns, far_cols, couple_ref, ranks_ref, sent_ref):
    (nrhs, panels), rank = field.shape, far_cols.shape[0]
    strips = sent_ref.shape[0]
    proj = lax.dot_general(
        field, far_cols, (((1,), (1,)), ((), ())), precision=HIGH, preferred_element_type=F32
    )
    wide = jnp.concatenate([proj] * CHUNK, axis=1)
    shape = (CHUNK, CHUNK * rank)
    owner = lax.div(lanes_of(shape), rank)
    inner = lax.rem(lanes_of(shape), rank)
    row = stats_row(columns, rank)
    half = CHUNK // 2
    number = rows_of(shape)
    number = jnp.where(number < half, 2 * number, 2 * (number - half) + 1)
    for start in range(0, strips, half):
        limit = jnp.zeros(shape, jnp.int32)
        for i in range(CHUNK):
            limit = jnp.where(owner == i, ranks_ref[0, 2 * start + i], limit)
        keep = (owner == number) & (inner < limit)
        spread = jnp.concatenate([jnp.where(keep, wide[r : r + 1], 0.0) for r in range(nrhs)], axis=0)
        couple = couple_ref[pl.ds(2 * start * rank, CHUNK * rank), :]
        terms = jnp.dot(spread, couple, precision=HIGH, preferred_element_type=F32)
        terms = jnp.concatenate([terms[r * CHUNK : (r + 1) * CHUNK] for r in range(nrhs)], axis=1)
        blank = jnp.zeros((nrhs - 3, LANES), F32)
        for i in range(half):
            tail = [terms[i : i + 1], terms[half + i : half + i + 1], row, blank]
            sent_ref[start + i, :, :panels] = field
            sent_ref[start + i, :, panels:] = jnp.concatenate(tail, axis=0)


def message_parts(got_ref, panels):
    terms = jnp.sum(got_ref[:, :, panels:], axis=0)
    terms = jnp.where(lax.axis_index("clus") == 0, terms[0:1], terms[1:2])
    return terms, got_ref[:, 2, panels:]


def window_fields(strips):
    strip = lax.axis_index("strip")
    for place in range(3):
        owner = strip + (place - 1)
        inside = (owner >= 0) & (owner < strips)
        for core in range(CORES):
            yield inside, core * strips + jnp.clip(owner, 0, strips - 1)


def own_place(strips):
    return lax.axis_index("clus") * strips + lax.axis_index("strip")


def fetch(pairs, sems):
    copies = [pltpu.make_async_copy(a, b, sems.at[i]) for i, (a, b) in enumerate(pairs)]
    for copy in copies:
        copy.start()
    return copies


def put_blocks(part, first, window):
    part = part.astype(jnp.bfloat16).astype(F32)
    part = jnp.concatenate([part, jnp.zeros_like(part)], axis=0)
    for c in range(part.shape[1] // LANES):
        window[first + c] = part[:, c * LANES : (c + 1) * LANES]


def near_field(window, tiles_ref, list_ref, sums):
    for held in sums:
        held[...] = jnp.zeros_like(held)
    for n in range(tiles_ref.shape[0]):
        held = sums[n % len(sums)]
        source = window[list_ref[1, n]].astype(jnp.bfloat16)
        product = jnp.dot(source, tiles_ref[n], preferred_element_type=F32)
        held[list_ref[0, n]] += product
    whole = sum((held[...] for held in sums[1:]), sums[0][...])
    return jnp.concatenate([whole[b] for b in range(whole.shape[0])], axis=1)


def start_kernel(
    loads_hbm, cols_hbm, couple_hbm, ranks_hbm, sent_ref, cols_ref, couple_ref, done_ref, loads_ref, ranks_ref, sems
):
    pairs = ((loads_hbm, loads_ref), (cols_hbm, cols_ref), (couple_hbm, couple_ref), (ranks_hbm, ranks_ref))
    for copy in fetch(pairs, sems):
        copy.wait()
    loads = loads_ref[...]
    square = jnp.sum(loads * loads, axis=1, keepdims=True)
    put_message(loads, [square], cols_ref[...], couple_ref, ranks_ref, sent_ref)
    done_ref[...] = jnp.zeros_like(done_ref)


def fetch_kernel(done_ref, tiles_hbm, rows_hbm, self_hbm, tiles_ref, rows_ref, self_ref, sems):
    del done_ref
    every = tiles_hbm.shape[0] // PIECES
    pieces = [pl.ds(i * every, every) for i in range(PIECES)]
    pairs = [(tiles_hbm.at[p], tiles_ref.at[p]) for p in pieces]
    for copy in fetch(pairs + [(rows_hbm, rows_ref), (self_hbm, self_ref)], sems):
        copy.wait()


def image_of(field, far, self_ref, far_rows_ref, near):
    rank = far_rows_ref.shape[0]
    far = jnp.dot(far[:, :rank], far_rows_ref[...], precision=HIGH, preferred_element_type=F32)
    return self_ref[...] * field + near[: field.shape[0]] + far


def step0_kernel(
    got_ref, cols_ref, couple_ref, rows_ref, self_ref, tiles_ref, list_hbm, ranks_hbm,
    sent_ref, state_ref, list_ref, ranks_ref, sems, window, *sums,
):
    panels, rank = cols_ref.shape[1], cols_ref.shape[0]
    nrhs, strips = got_ref.shape[1], got_ref.shape[0] // CORES
    span = panels // LANES
    copies = fetch(((list_hbm, list_ref), (ranks_hbm, ranks_ref)), sems)
    terms, stats = message_parts(got_ref, panels)
    beta = jnp.sqrt(stat_column(total(stats), 0, nrhs, rank))
    basis = got_ref[own_place(strips), :, :panels] / beta
    for i, (inside, place) in enumerate(window_fields(strips)):
        field = jnp.where(inside, got_ref[place, :, :panels], 0.0)
        put_blocks(field / beta, i * span, window)
    far = far_sum_of(terms, nrhs, rank) / beta
    for copy in copies:
        copy.wait()
    near = near_field(window, tiles_ref, list_ref, sums)
    image = image_of(basis, far, self_ref, rows_ref, near)
    state_ref[...] = jnp.concatenate([far, jnp.broadcast_to(beta, far.shape)], axis=0)
    norm = jnp.sum(basis * basis, axis=1, keepdims=True)
    dot = jnp.sum(basis * image, axis=1, keepdims=True)
    share = jnp.where(norm > 0, dot / jnp.where(norm > 0, norm, 1.0), 0.0)
    rest = image - share * basis
    rest = jnp.sum(rest * rest, axis=1, keepdims=True)
    put_message(image, [norm, dot, share, rest], cols_ref[...], couple_ref, ranks_ref, sent_ref)


def step1_kernel(
    got0_ref, got_ref, state_ref, rows_ref, self_ref, tiles_ref, list_hbm,
    sent_ref, basis_ref, coeff_ref, list_ref, sems, window, *sums,
):
    panels, rank = rows_ref.shape[1], rows_ref.shape[0]
    nrhs, strips = got_ref.shape[1], got_ref.shape[0] // CORES
    span = panels // LANES
    (copy,) = fetch(((list_hbm, list_ref),), sems)
    beta = state_ref[nrhs:, :1]
    far0 = state_ref[:nrhs, :]
    terms, stats = message_parts(got_ref, panels)
    summed = total(stats)
    h00 = stat_column(summed, 1, nrhs, rank)
    away = shifted(stats, 2) - shifted(summed, 1)
    rest = total(shifted(stats, 3) + stats * away * away)
    h10 = jnp.sqrt(stat_column(rest, 0, nrhs, rank))
    mine = own_place(strips)
    basis0 = got0_ref[mine, :, :panels] / beta
    basis1 = (got_ref[mine, :, :panels] - h00 * basis0) / h10
    for i, (inside, place) in enumerate(window_fields(strips)):
        field = (got_ref[place, :, :panels] - h00 * (got0_ref[place, :, :panels] / beta)) / h10
        put_blocks(jnp.where(inside, field, 0.0), i * span, window)
    far = (far_sum_of(terms, nrhs, rank) - h00 * far0) / h10
    copy.wait()
    near = near_field(window, tiles_ref, list_ref, sums)
    image = image_of(basis1, far, self_ref, rows_ref, near)
    columns = [jnp.sum(a * image, axis=1, keepdims=True) for a in (basis0, basis1, image)]
    sent_ref[:, 0, :] = jnp.broadcast_to(stats_row(columns, rank), (strips, LANES))
    basis_ref[...] = jnp.concatenate([basis0, basis1], axis=0)
    coeff_ref[...] = jnp.concatenate([jnp.broadcast_to(v, (nrhs, LANES)) for v in (beta, h00, h10)], axis=0)


def finish_kernel(rank, got_ref, basis_ref, coeff_ref, out_ref):
    nrhs = out_ref.shape[0]
    row = total(got_ref[:, 0, :])
    h01, h11, gram11 = (stat_column(row, k, nrhs, rank) for k in range(3))
    beta, h00, h10 = (coeff_ref[k * nrhs : (k + 1) * nrhs, :1] for k in range(3))
    gram00 = h00 * h00 + h10 * h10
    gram01 = h00 * h01 + h10 * h11
    lower00 = jnp.sqrt(gram00)
    lower10 = gram01 / lower00
    lower11 = jnp.sqrt(gram11 - lower10 * lower10)
    middle0 = beta * h00 / lower00
    middle1 = (beta * h01 - lower10 * middle0) / lower11
    y1 = middle1 / lower11
    y0 = (middle0 - lower10 * y1) / lower00
    out_ref[...] = y0 * basis_ref[:nrhs, :] + y1 * basis_ref[nrhs:, :]


def call(kernel, args, outs, scratch=(), held=()):
    args = [pltpu.with_memory_space_constraint(a, pltpu.HBM) if i in held else a for i, a in enumerate(args)]
    return pl.pallas_call(
        kernel,
        out_shape=[
            in_vmem_like(out) if hasattr(out, "dtype") else jax.ShapeDtypeStruct(out, F32) for out in outs
        ],
        in_specs=[pl.BlockSpec(memory_space=pl.ANY if i in held else pltpu.VMEM) for i in range(len(args))],
        out_specs=[pl.BlockSpec(memory_space=pltpu.VMEM)] * len(outs),
        scratch_shapes=list(scratch),
        compiler_params=pltpu.CompilerParams(vmem_limit_bytes=24 * 2**20),
    )(*args)


def in_vmem_like(array):
    return pltpu.VMEM(array.shape, array.dtype)


def in_vmem(arrays):
    return [pltpu.with_memory_space_constraint(a, pltpu.VMEM) for a in arrays]


def exchanged(sent):
    return lax.all_gather(lax.all_to_all(sent, "strip", 0, 0, tiled=True), "clus", axis=0, tiled=True)


def body(loads, self_term, near_tiles, near_list, far_rows, far_cols, coupling, ranks):
    nrhs, panels = loads.shape
    rank = far_cols.shape[0]
    tile = near_tiles.shape[1]
    rows = panels // tile
    strips = coupling.shape[0] // CORES
    couple = coupling.reshape(CORES * strips * rank, rank)
    near_list = near_list.T
    ranks = ranks.reshape(1, CORES * strips)
    self_term = self_term.reshape(1, panels)
    indices = [pltpu.SMEM(near_list.shape, jnp.int32), pltpu.SMEM(ranks.shape, jnp.int32)]
    scratch = [pltpu.VMEM((3 * CORES * rows, 2 * nrhs, tile), F32)]
    scratch += [pltpu.VMEM((rows, 2 * nrhs, tile), F32)] * 4
    message = (strips, nrhs, panels + LANES)

    sent, far_cols, couple, done = call(
        start_kernel,
        (loads, far_cols, couple, ranks),
        [message, far_cols, couple, (8, LANES)],
        [pltpu.VMEM(loads.shape, F32), indices[1], pltpu.SemaphoreType.DMA((4,))],
        held=range(4),
    )
    near_tiles, far_rows, self_term = call(
        fetch_kernel,
        (done, near_tiles, far_rows, self_term),
        [near_tiles, far_rows, self_term],
        [pltpu.SemaphoreType.DMA((PIECES + 2,))],
        held=range(1, 4),
    )
    far_cols, couple, near_tiles, far_rows, self_term = in_vmem((far_cols, couple, near_tiles, far_rows, self_term))
    got0 = exchanged(sent)
    sent, state = call(
        step0_kernel,
        (got0, far_cols, couple, far_rows, self_term, near_tiles, near_list, ranks),
        [message, (2 * nrhs, LANES)],
        indices + [pltpu.SemaphoreType.DMA((2,))] + scratch,
        held=(6, 7),
    )
    got1 = exchanged(sent)
    sent, basis, coeff = call(
        step1_kernel,
        (got0, got1, state, far_rows, self_term, near_tiles, near_list),
        [(strips, 1, LANES), (2 * nrhs, panels), (3 * nrhs, LANES)],
        indices[:1] + [pltpu.SemaphoreType.DMA((1,))] + scratch,
        held=(6,),
    )
    return call(functools.partial(finish_kernel, rank), (exchanged(sent), basis, coeff), [loads.shape])[0]


def solution(mesh):
    every = ("case",) + GROUP
    in_specs = (
        P(None, every),
        P(every),
        P(every, None, None),
        P(every, None),
        P(None, every),
        P(None, every),
        P(None, GROUP, None, None),
        P(None, GROUP),
    )
    return jax.shard_map(body, mesh=mesh, in_specs=in_specs, out_specs=P(None, every), check_vma=False)
```

```python
import functools

import jax
import jax.numpy as jnp
from jax import lax
from jax.experimental import pallas as pl
from jax.experimental.pallas import tpu as pltpu
from jax.sharding import PartitionSpec as P

HIGH = lax.Precision.HIGHEST
GROUP = ("strip", "clus")
LANES = 128
CHUNK = 16
PIECES = 8
F32 = jnp.float32


CORES = 2


def lanes_of(shape):
    return lax.broadcasted_iota(jnp.int32, shape, 1)


def rows_of(shape):
    return lax.broadcasted_iota(jnp.int32, shape, 0)


def stats_row(columns, rank):
    shape = (columns[0].shape[0], LANES)
    first = lanes_of(shape) - rank * rows_of(shape)
    spread = sum(jnp.where(first == k, column, 0.0) for k, column in enumerate(columns))
    return jnp.sum(spread, axis=0, keepdims=True)


def stat_column(row, k, nrhs, rank):
    shape = (nrhs, LANES)
    first = lanes_of(shape) - rank * rows_of(shape)
    return jnp.sum(jnp.where(first == k, row, 0.0), axis=1, keepdims=True)


def shifted(value, k):
    return pltpu.roll(value, LANES - k, 1)


def far_sum_of(row, nrhs, rank):
    shape = (nrhs, LANES)
    first = lanes_of(shape) - rank * rows_of(shape)
    own = jnp.where((first >= 0) & (first < rank), row, 0.0)
    return sum((pltpu.roll(own, k * rank, 1) for k in range(1, LANES // rank)), own)


def total(rows):
    return jnp.sum(rows, axis=0, keepdims=True)


def put_message(field, columns, cols_ref, couple_ref, ranks_ref, sent_ref, copies=()):
    (nrhs, panels), rank = field.shape, cols_ref.shape[0]
    strips = sent_ref.shape[0]
    row = stats_row(columns, rank)
    for i in range(strips):
        sent_ref[i, :, :panels] = field
    for copy in copies[:1]:
        copy.wait()
    proj = lax.dot_general(
        field, cols_ref[...], (((1,), (1,)), ((), ())), precision=HIGH, preferred_element_type=F32
    )
    wide = jnp.concatenate([proj] * CHUNK, axis=1)
    shape = (CHUNK, CHUNK * rank)
    owner = lax.div(lanes_of(shape), rank)
    inner = lax.rem(lanes_of(shape), rank)
    for copy in copies[1:]:
        copy.wait()
    half = CHUNK // 2
    number = rows_of(shape)
    number = jnp.where(number < half, 2 * number, 2 * (number - half) + 1)
    for start in range(0, strips, half):
        limit = jnp.zeros(shape, jnp.int32)
        for i in range(CHUNK):
            limit = jnp.where(owner == i, ranks_ref[0, 2 * start + i], limit)
        keep = (owner == number) & (inner < limit)
        spread = jnp.concatenate([jnp.where(keep, wide[r : r + 1], 0.0) for r in range(nrhs)], axis=0)
        couple = couple_ref[pl.ds(2 * start * rank, CHUNK * rank), :]
        terms = jnp.dot(spread, couple, precision=HIGH, preferred_element_type=F32)
        terms = jnp.concatenate([terms[r * CHUNK : (r + 1) * CHUNK] for r in range(nrhs)], axis=1)
        blank = jnp.zeros((nrhs - 3, LANES), F32)
        for i in range(half):
            tail = [terms[i : i + 1], terms[half + i : half + i + 1], row, blank]
            sent_ref[start + i, :, panels:] = jnp.concatenate(tail, axis=0)


def message_parts(got, panels):
    terms = sum(jnp.sum(ref[:, :, panels:], axis=0) for ref in got)
    terms = jnp.where(lax.axis_index("clus") == 0, terms[0:1], terms[1:2])
    return terms, jnp.concatenate([ref[:, 2, panels:] for ref in got], axis=0)


def window_places(strips):
    strip, core = lax.axis_index("strip"), lax.axis_index("clus")
    for step in range(3):
        owner = strip + (step - 1)
        inside = (owner >= 0) & (owner < strips)
        for other in range(CORES):
            place = CORES * step + (core if other == 0 else 1 - core)
            yield inside, jnp.clip(owner, 0, strips - 1), other, place


def fetch(pairs, sems):
    copies = [pltpu.make_async_copy(a, b, sems.at[i]) for i, (a, b) in enumerate(pairs)]
    for copy in copies:
        copy.start()
    return copies


def put_blocks(part, first, window):
    part = part.astype(jnp.bfloat16).astype(F32)
    part = jnp.concatenate([part, jnp.zeros_like(part)], axis=0)
    for c in range(part.shape[1] // LANES):
        window[first + c] = part[:, c * LANES : (c + 1) * LANES]


def near_field(window, tiles_ref, list_ref, sums):
    for held in sums:
        held[...] = jnp.zeros_like(held)
    for n in range(tiles_ref.shape[0]):
        held = sums[n % len(sums)]
        source = window[list_ref[1, n]].astype(jnp.bfloat16)
        product = jnp.dot(source, tiles_ref[n], preferred_element_type=F32)
        held[list_ref[0, n]] += product
    whole = sum((held[...] for held in sums[1:]), sums[0][...])
    return jnp.concatenate([whole[b] for b in range(whole.shape[0])], axis=1)


def start_kernel(
    loads_hbm, cols_hbm, couple_hbm, ranks_hbm, sent_ref, cols_ref, couple_ref, done_ref, loads_ref, ranks_ref, sems
):
    pairs = ((loads_hbm, loads_ref), (cols_hbm, cols_ref), (couple_hbm, couple_ref), (ranks_hbm, ranks_ref))
    copies = fetch(pairs, sems)
    copies[0].wait()
    loads = loads_ref[...]
    square = jnp.sum(loads * loads, axis=1, keepdims=True)
    done_ref[...] = jnp.zeros_like(done_ref)
    put_message(loads, [square], cols_ref, couple_ref, ranks_ref, sent_ref, copies[1:])


def fetch_kernel(done_ref, tiles_hbm, rows_hbm, self_hbm, tiles_ref, rows_ref, self_ref, sems):
    del done_ref
    every = tiles_hbm.shape[0] // PIECES
    pieces = [pl.ds(i * every, every) for i in range(PIECES)]
    pairs = [(tiles_hbm.at[p], tiles_ref.at[p]) for p in pieces]
    for copy in fetch(pairs + [(rows_hbm, rows_ref), (self_hbm, self_ref)], sems):
        copy.wait()


def image_of(field, far, self_ref, far_rows_ref, near):
    rank = far_rows_ref.shape[0]
    far = jnp.dot(far[:, :rank], far_rows_ref[...], precision=HIGH, preferred_element_type=F32)
    return self_ref[...] * field + near[: field.shape[0]] + far


def step0_kernel(
    own_ref, other_ref, cols_ref, couple_ref, rows_ref, self_ref, tiles_ref, list_hbm, ranks_hbm,
    sent_ref, state_ref, list_ref, ranks_ref, sems, window, *sums,
):
    panels, rank = cols_ref.shape[1], cols_ref.shape[0]
    got = (own_ref, other_ref)
    strips, nrhs = own_ref.shape[:2]
    span = panels // LANES
    copies = fetch(((list_hbm, list_ref), (ranks_hbm, ranks_ref)), sems)
    terms, stats = message_parts(got, panels)
    beta = jnp.sqrt(stat_column(total(stats), 0, nrhs, rank))
    basis = own_ref[lax.axis_index("strip"), :, :panels] / beta
    for inside, strip, other, place in window_places(strips):
        field = jnp.where(inside, got[other][strip, :, :panels], 0.0)
        put_blocks(field / beta, place * span, window)
    far = far_sum_of(terms, nrhs, rank) / beta
    for copy in copies:
        copy.wait()
    near = near_field(window, tiles_ref, list_ref, sums)
    image = image_of(basis, far, self_ref, rows_ref, near)
    state_ref[...] = jnp.concatenate([far, jnp.broadcast_to(beta, far.shape)], axis=0)
    norm = jnp.sum(basis * basis, axis=1, keepdims=True)
    dot = jnp.sum(basis * image, axis=1, keepdims=True)
    share = jnp.where(norm > 0, dot / jnp.where(norm > 0, norm, 1.0), 0.0)
    rest = image - share * basis
    rest = jnp.sum(rest * rest, axis=1, keepdims=True)
    put_message(image, [norm, dot, share, rest], cols_ref, couple_ref, ranks_ref, sent_ref)


def step1_kernel(
    own0_ref, other0_ref, own_ref, other_ref, state_ref, rows_ref, self_ref, tiles_ref, list_hbm,
    sent_ref, basis_ref, coeff_ref, list_ref, sems, window, *sums,
):
    panels, rank = rows_ref.shape[1], rows_ref.shape[0]
    got0, got = (own0_ref, other0_ref), (own_ref, other_ref)
    strips, nrhs = own_ref.shape[:2]
    span = panels // LANES
    (copy,) = fetch(((list_hbm, list_ref),), sems)
    beta = state_ref[nrhs:, :1]
    far0 = state_ref[:nrhs, :]
    terms, stats = message_parts(got, panels)
    summed = total(stats)
    h00 = stat_column(summed, 1, nrhs, rank)
    away = shifted(stats, 2) - shifted(summed, 1)
    rest = total(shifted(stats, 3) + stats * away * away)
    h10 = jnp.sqrt(stat_column(rest, 0, nrhs, rank))
    mine = lax.axis_index("strip")
    basis0 = own0_ref[mine, :, :panels] / beta
    basis1 = (own_ref[mine, :, :panels] - h00 * basis0) / h10
    for inside, strip, other, place in window_places(strips):
        field = (got[other][strip, :, :panels] - h00 * (got0[other][strip, :, :panels] / beta)) / h10
        put_blocks(jnp.where(inside, field, 0.0), place * span, window)
    far = (far_sum_of(terms, nrhs, rank) - h00 * far0) / h10
    copy.wait()
    near = near_field(window, tiles_ref, list_ref, sums)
    image = image_of(basis1, far, self_ref, rows_ref, near)
    columns = [jnp.sum(a * image, axis=1, keepdims=True) for a in (basis0, basis1, image)]
    sent_ref[:, 0, :] = jnp.broadcast_to(stats_row(columns, rank), (CORES * strips, LANES))
    basis_ref[...] = jnp.concatenate([basis0, basis1], axis=0)
    coeff_ref[...] = jnp.concatenate([jnp.broadcast_to(v, (nrhs, LANES)) for v in (beta, h00, h10)], axis=0)


def finish_kernel(rank, got_ref, basis_ref, coeff_ref, out_ref):
    nrhs = out_ref.shape[0]
    row = total(got_ref[:, 0, :])
    h01, h11, gram11 = (stat_column(row, k, nrhs, rank) for k in range(3))
    beta, h00, h10 = (coeff_ref[k * nrhs : (k + 1) * nrhs, :1] for k in range(3))
    gram00 = h00 * h00 + h10 * h10
    gram01 = h00 * h01 + h10 * h11
    lower00 = jnp.sqrt(gram00)
    lower10 = gram01 / lower00
    lower11 = jnp.sqrt(gram11 - lower10 * lower10)
    middle0 = beta * h00 / lower00
    middle1 = (beta * h01 - lower10 * middle0) / lower11
    y1 = middle1 / lower11
    y0 = (middle0 - lower10 * y1) / lower00
    out_ref[...] = y0 * basis_ref[:nrhs, :] + y1 * basis_ref[nrhs:, :]


def call(kernel, args, outs, scratch=(), held=()):
    args = [pltpu.with_memory_space_constraint(a, pltpu.HBM) if i in held else a for i, a in enumerate(args)]
    return pl.pallas_call(
        kernel,
        out_shape=[
            in_vmem_like(out) if hasattr(out, "dtype") else jax.ShapeDtypeStruct(out, F32) for out in outs
        ],
        in_specs=[pl.BlockSpec(memory_space=pl.ANY if i in held else pltpu.VMEM) for i in range(len(args))],
        out_specs=[pl.BlockSpec(memory_space=pltpu.VMEM)] * len(outs),
        scratch_shapes=list(scratch),
        compiler_params=pltpu.CompilerParams(vmem_limit_bytes=24 * 2**20),
    )(*args)


def in_vmem_like(array):
    return pltpu.VMEM(array.shape, array.dtype)


def in_vmem(arrays):
    return [pltpu.with_memory_space_constraint(a, pltpu.VMEM) for a in arrays]


def exchanged(sent):
    got = lax.all_to_all(sent, "strip", 0, 0, tiled=True)
    return got, lax.ppermute(got, "clus", [(0, 1), (1, 0)])


def body(loads, self_term, near_tiles, near_list, far_rows, far_cols, coupling, ranks):
    nrhs, panels = loads.shape
    rank = far_cols.shape[0]
    tile = near_tiles.shape[1]
    rows = panels // tile
    strips = coupling.shape[0] // CORES
    couple = coupling.reshape(CORES * strips * rank, rank)
    near_list = near_list.T
    ranks = ranks.reshape(1, CORES * strips)
    self_term = self_term.reshape(1, panels)
    indices = [pltpu.SMEM(near_list.shape, jnp.int32), pltpu.SMEM(ranks.shape, jnp.int32)]
    scratch = [pltpu.VMEM((3 * CORES * rows, 2 * nrhs, tile), F32)]
    scratch += [pltpu.VMEM((rows, 2 * nrhs, tile), F32)] * 4
    message = (strips, nrhs, panels + LANES)

    sent, far_cols, couple, done = call(
        start_kernel,
        (loads, far_cols, couple, ranks),
        [message, far_cols, couple, (8, LANES)],
        [pltpu.VMEM(loads.shape, F32), indices[1], pltpu.SemaphoreType.DMA((4,))],
        held=range(4),
    )
    near_tiles, far_rows, self_term = call(
        fetch_kernel,
        (done, near_tiles, far_rows, self_term),
        [near_tiles, far_rows, self_term],
        [pltpu.SemaphoreType.DMA((PIECES + 2,))],
        held=range(1, 4),
    )
    far_cols, couple, near_tiles, far_rows, self_term = in_vmem((far_cols, couple, near_tiles, far_rows, self_term))
    got0 = exchanged(sent)
    sent, state = call(
        step0_kernel,
        (*got0, far_cols, couple, far_rows, self_term, near_tiles, near_list, ranks),
        [message, (2 * nrhs, LANES)],
        indices + [pltpu.SemaphoreType.DMA((2,))] + scratch,
        held=(7, 8),
    )
    got1 = exchanged(sent)
    sent, basis, coeff = call(
        step1_kernel,
        (*got0, *got1, state, far_rows, self_term, near_tiles, near_list),
        [(CORES * strips, 1, LANES), (2 * nrhs, panels), (3 * nrhs, LANES)],
        indices[:1] + [pltpu.SemaphoreType.DMA((1,))] + scratch,
        held=(8,),
    )
    got = lax.all_to_all(sent, GROUP, 0, 0, tiled=True)
    return call(functools.partial(finish_kernel, rank), (got, basis, coeff), [loads.shape])[0]


def solution(mesh):
    every = ("case",) + GROUP
    in_specs = (
        P(None, every),
        P(every),
        P(every, None, None),
        P(every, None),
        P(None, every),
        P(None, every),
        P(None, GROUP, None, None),
        P(None, GROUP),
    )
    return jax.shard_map(body, mesh=mesh, in_specs=in_specs, out_specs=P(None, every), check_vma=False)
```

```python
import functools

import jax
import jax.numpy as jnp
from jax import lax
from jax.experimental import pallas as pl
from jax.experimental.pallas import tpu as pltpu
from jax.sharding import PartitionSpec as P

GROUP = ("strip", "clus")
CORES = 2
LANES = 128
CHUNK = 16
PIECES = 4
F32 = jnp.float32
BF16 = jnp.bfloat16


def lanes_of(shape):
    return lax.broadcasted_iota(jnp.int32, shape, 1)


def rows_of(shape):
    return lax.broadcasted_iota(jnp.int32, shape, 0)


def total(rows):
    return jnp.sum(rows, axis=0, keepdims=True)


def stats_row(columns, rank):
    shape = (columns[0].shape[0], LANES)
    first = lanes_of(shape) - rank * rows_of(shape)
    spread = sum(jnp.where(first == k, column, 0.0) for k, column in enumerate(columns))
    return total(spread)


def stat_column(row, k, nrhs, rank):
    shape = (nrhs, LANES)
    first = lanes_of(shape) - rank * rows_of(shape)
    return jnp.sum(jnp.where(first == k, row, 0.0), axis=1, keepdims=True)


def shifted(value, k):
    return pltpu.roll(value, LANES - k, 1)


def far_sum_of(row, nrhs, rank):
    shape = (nrhs, LANES)
    first = lanes_of(shape) - rank * rows_of(shape)
    own = jnp.where((first >= 0) & (first < rank), row, 0.0)
    return sum((pltpu.roll(own, k * rank, 1) for k in range(1, LANES // rank)), own)


def halves(value):
    high = value.astype(BF16)
    return high, (value - high.astype(F32)).astype(BF16)


def product(left, right_high, right_low, side=0):
    rows = left.shape[0]
    high, low = halves(left)
    dims = (((1,), (side,)), ((), ()))
    both = lax.dot_general(jnp.concatenate([high, low], axis=0), right_high, dims, preferred_element_type=F32)
    return both[:rows] + (both[rows:] + lax.dot_general(high, right_low, dims, preferred_element_type=F32))


def fetch(pairs, sems):
    copies = [pltpu.make_async_copy(a, b, sems.at[i]) for i, (a, b) in enumerate(pairs)]
    for copy in copies:
        copy.start()
    return copies


def put_message(field, columns, cols, couple, masks_ref, sent_ref):
    (nrhs, panels), rank = field.shape, cols[0].shape[0]
    strips = sent_ref.shape[0]
    half = CHUNK // 2
    for i in range(strips):
        sent_ref[i, :, :panels] = field
    proj = product(field, cols[0][...], cols[1][...], 1)
    wide = jnp.concatenate([proj] * CHUNK, axis=1)
    row = stats_row(columns, rank)
    blank = jnp.zeros((nrhs - 3, LANES), F32)
    for start in range(0, strips, half):
        mask = masks_ref[pl.ds(CORES * start, CHUNK), :]
        spread = jnp.concatenate([mask * wide[r : r + 1] for r in range(nrhs)], axis=0)
        here = pl.ds(CORES * start * rank, CHUNK * rank)
        terms = product(spread, couple[0][here, :], couple[1][here, :])
        terms = jnp.concatenate([terms[r * CHUNK : (r + 1) * CHUNK] for r in range(nrhs)], axis=1)
        for i in range(half):
            tail = [terms[i : i + 1], terms[half + i : half + i + 1], row, blank]
            sent_ref[start + i, :, panels:] = jnp.concatenate(tail, axis=0)


def message_parts(got, panels):
    terms = sum(jnp.sum(ref[:, :, panels:], axis=0) for ref in got)
    terms = jnp.where(lax.axis_index("clus") == 0, terms[0:1], terms[1:2])
    return terms, jnp.concatenate([ref[:, 2, panels:] for ref in got], axis=0)


def window_parts(got, panels):
    strips = got[0].shape[0]
    for step in range(3):
        owner = lax.axis_index("strip") + (step - 1)
        inside = (owner >= 0) & (owner < strips)
        owner = jnp.clip(owner, 0, strips - 1)
        yield inside, jnp.concatenate([ref[owner, :, :panels] for ref in got], axis=0)


def put_blocks(part, first, window):
    part = part.astype(BF16).astype(F32)
    for c in range(part.shape[1] // LANES):
        window[first + c] = part[:, c * LANES : (c + 1) * LANES]


def near_field(window, tiles, list_ref, sums, nrhs):
    for held in sums:
        held[...] = jnp.zeros_like(held)
    n = 0
    for tiles_ref in tiles:
        for i in range(tiles_ref.shape[0]):
            held = sums[n % len(sums)]
            source = window[list_ref[1, n]].astype(BF16)
            held[list_ref[0, n]] += jnp.dot(source, tiles_ref[i], preferred_element_type=F32)
            n += 1
    whole = sum((held[...] for held in sums[1:]), sums[0][...])
    rows = whole.shape[0] // CORES
    return jnp.concatenate([whole[b, :nrhs] + whole[rows + b, nrhs:] for b in range(rows)], axis=1)


def start_kernel(
    loads_hbm, cols_hbm, couple_hbm, ranks_hbm, sent_ref, cols_high, cols_low, couple_high, couple_low, masks_ref,
    done_ref, loads_ref, cols_ref, couple_ref, ranks_ref, sems,
):
    rank = cols_ref.shape[0]
    pairs = ((ranks_hbm, ranks_ref), (loads_hbm, loads_ref), (cols_hbm, cols_ref), (couple_hbm, couple_ref))
    copies = fetch(pairs, sems)
    done_ref[...] = jnp.zeros_like(done_ref)
    copies[0].wait()
    shape = (CHUNK, CHUNK * rank)
    owner = lax.div(lanes_of(shape), rank)
    inner = lax.rem(lanes_of(shape), rank)
    half = CHUNK // 2
    number = rows_of(shape)
    number = jnp.where(number < half, CORES * number, CORES * (number - half) + 1)
    for start in range(0, masks_ref.shape[0], CHUNK):
        limit = jnp.zeros((1, CHUNK * rank), jnp.int32)
        for i in range(CHUNK):
            limit = jnp.where(owner[:1] == i, ranks_ref[0, start + i], limit)
        masks_ref[pl.ds(start, CHUNK), :] = jnp.where((owner == number) & (inner < limit), 1.0, 0.0)
    copies[1].wait()
    loads = loads_ref[...]
    square = jnp.sum(loads * loads, axis=1, keepdims=True)
    copies[2].wait()
    cols_high[...], cols_low[...] = halves(cols_ref[...])
    copies[3].wait()
    couple_high[...], couple_low[...] = halves(couple_ref[...])
    put_message(loads, [square], (cols_high, cols_low), (couple_high, couple_low), masks_ref, sent_ref)


def copy_tiles(tiles_hbm, first, tiles_ref, sems):
    every = tiles_ref.shape[0] // PIECES
    pairs = [(pl.ds(first + i * every, every), pl.ds(i * every, every)) for i in range(PIECES)]
    return fetch([(tiles_hbm.at[a], tiles_ref.at[b]) for a, b in pairs], sems)


def fetch0_kernel(done_ref, tiles_hbm, rows_hbm, self_hbm, list_hbm, tiles_ref, rows_high, rows_low, self_ref, list_ref,
                  rows_ref, raw_ref, sems, other_sems):
    del done_ref
    pairs = ((list_hbm, raw_ref), (rows_hbm, rows_ref), (self_hbm, self_ref))
    copies = fetch(pairs, other_sems)
    pieces = copy_tiles(tiles_hbm, 0, tiles_ref, sems)
    copies[0].wait()
    rows = self_ref.shape[1] // tiles_ref.shape[1]
    target, source = raw_ref[0:1, :], raw_ref[1:2, :]
    group, block = lax.div(source, rows), lax.rem(source, rows)
    strip, core = lax.div(group, CORES), lax.rem(group, CORES)
    apart = jnp.where(core == lax.axis_index("clus"), 0, 1)
    list_ref[...] = jnp.concatenate([apart * rows + target, strip * rows + block], axis=0)
    copies[1].wait()
    rows_high[...], rows_low[...] = halves(rows_ref[...])
    copies[2].wait()
    for piece in pieces:
        piece.wait()


def fetch1_kernel(done_ref, tiles_hbm, tiles_ref, sems):
    del done_ref
    for piece in copy_tiles(tiles_hbm, tiles_ref.shape[0], tiles_ref, sems):
        piece.wait()


def image_of(field, far, self_ref, far_rows, near):
    rank = far_rows[0].shape[0]
    return self_ref[...] * field + near + product(far[:, :rank], far_rows[0][...], far_rows[1][...])


def step0_kernel(
    own_ref, other_ref, cols_high, cols_low, couple_high, couple_low, masks_ref, rows_high, rows_low, self_ref,
    tiles0_ref, tiles1_ref, list_vmem, sent_ref, state_ref, list_ref, sems, window, *sums,
):
    rank, panels = rows_high.shape
    nrhs = own_ref.shape[1]
    span = panels // LANES
    (copy,) = fetch(((list_vmem, list_ref),), sems)
    got = (own_ref, other_ref)
    terms, stats = message_parts(got, panels)
    beta = jnp.sqrt(stat_column(total(stats), 0, nrhs, rank))
    scale = 1.0 / beta
    both = jnp.concatenate([scale, scale], axis=0)
    for step, (inside, part) in enumerate(window_parts(got, panels)):
        put_blocks(jnp.where(inside, part * both, 0.0), step * span, window)
    basis = own_ref[lax.axis_index("strip"), :, :panels] * scale
    far = far_sum_of(terms, nrhs, rank) * scale
    copy.wait()
    near = near_field(window, (tiles0_ref, tiles1_ref), list_ref, sums, nrhs)
    image = image_of(basis, far, self_ref, (rows_high, rows_low), near)
    state_ref[...] = jnp.concatenate([far, jnp.broadcast_to(beta, far.shape)], axis=0)
    norm = jnp.sum(basis * basis, axis=1, keepdims=True)
    dot = jnp.sum(basis * image, axis=1, keepdims=True)
    share = jnp.where(norm > 0, dot / jnp.where(norm > 0, norm, 1.0), 0.0)
    rest = image - share * basis
    rest = jnp.sum(rest * rest, axis=1, keepdims=True)
    columns = [norm, dot, share, rest]
    put_message(image, columns, (cols_high, cols_low), (couple_high, couple_low), masks_ref, sent_ref)


def step1_kernel(
    own0_ref, other0_ref, own_ref, other_ref, state_ref, rows_high, rows_low, self_ref, tiles0_ref, tiles1_ref,
    list_vmem, sent_ref, basis_ref, coeff_ref, list_ref, sems, window, *sums,
):
    rank, panels = rows_high.shape
    nrhs = own_ref.shape[1]
    span = panels // LANES
    (copy,) = fetch(((list_vmem, list_ref),), sems)
    got0, got = (own0_ref, other0_ref), (own_ref, other_ref)
    beta = state_ref[nrhs:, :1]
    far0 = state_ref[:nrhs, :]
    terms, stats = message_parts(got, panels)
    summed = total(stats)
    h00 = stat_column(summed, 1, nrhs, rank)
    away = shifted(stats, 2) - shifted(summed, 1)
    rest = total(shifted(stats, 3) + stats * away * away)
    h10 = jnp.sqrt(stat_column(rest, 0, nrhs, rank))
    scale0, scale = 1.0 / beta, 1.0 / h10
    both0, both, both_h00 = (jnp.concatenate([a, a], axis=0) for a in (scale0, scale, h00))
    parts = zip(window_parts(got0, panels), window_parts(got, panels))
    for step, ((inside, part0), (_, part)) in enumerate(parts):
        part = (part - both_h00 * (part0 * both0)) * both
        put_blocks(jnp.where(inside, part, 0.0), step * span, window)
    mine = lax.axis_index("strip")
    basis0 = own0_ref[mine, :, :panels] * scale0
    basis1 = (own_ref[mine, :, :panels] - h00 * basis0) * scale
    far = (far_sum_of(terms, nrhs, rank) - h00 * far0) * scale
    copy.wait()
    near = near_field(window, (tiles0_ref, tiles1_ref), list_ref, sums, nrhs)
    image = image_of(basis1, far, self_ref, (rows_high, rows_low), near)
    columns = [jnp.sum(a * image, axis=1, keepdims=True) for a in (basis0, basis1, image)]
    sent_ref[:, 0, :] = jnp.broadcast_to(stats_row(columns, rank), (sent_ref.shape[0], LANES))
    basis_ref[...] = jnp.concatenate([basis0, basis1], axis=0)
    coeff_ref[...] = jnp.concatenate([jnp.broadcast_to(v, (nrhs, LANES)) for v in (beta, h00, h10)], axis=0)


def finish_kernel(rank, got_ref, basis_ref, coeff_ref, out_ref):
    nrhs = out_ref.shape[0]
    row = total(got_ref[:, 0, :])
    h01, h11, gram11 = (stat_column(row, k, nrhs, rank) for k in range(3))
    beta, h00, h10 = (coeff_ref[k * nrhs : (k + 1) * nrhs, :1] for k in range(3))
    gram00 = h00 * h00 + h10 * h10
    gram01 = h00 * h01 + h10 * h11
    lower00 = jnp.sqrt(gram00)
    lower10 = gram01 / lower00
    lower11 = jnp.sqrt(gram11 - lower10 * lower10)
    middle0 = beta * h00 / lower00
    middle1 = (beta * h01 - lower10 * middle0) / lower11
    y1 = middle1 / lower11
    y0 = (middle0 - lower10 * y1) / lower00
    out_ref[...] = y0 * basis_ref[:nrhs, :] + y1 * basis_ref[nrhs:, :]


def in_vmem_like(array):
    return pltpu.VMEM(array.shape, array.dtype)


def in_vmem(arrays):
    return [pltpu.with_memory_space_constraint(a, pltpu.VMEM) for a in arrays]


def call(kernel, args, outs, scratch=(), held=(), flops=0):
    args = [pltpu.with_memory_space_constraint(a, pltpu.HBM) if i in held else a for i, a in enumerate(args)]
    moved = sum(a.size * a.dtype.itemsize for a in args)
    return pl.pallas_call(
        kernel,
        out_shape=[
            jax.ShapeDtypeStruct(out, F32) if isinstance(out, tuple) else in_vmem_like(out) for out in outs
        ],
        in_specs=[pl.BlockSpec(memory_space=pl.ANY if i in held else pltpu.VMEM) for i in range(len(args))],
        out_specs=[pl.BlockSpec(memory_space=pltpu.VMEM)] * len(outs),
        scratch_shapes=list(scratch),
        compiler_params=pltpu.CompilerParams(vmem_limit_bytes=24 * 2**20),
        cost_estimate=pl.CostEstimate(flops=flops, bytes_accessed=moved, transcendentals=0),
    )(*args)


def exchanged(sent):
    got = lax.all_to_all(sent, "strip", 0, 0, tiled=True)
    return got, lax.ppermute(got, "clus", [(0, 1), (1, 0)])


def body(loads, self_term, near_tiles, near_list, far_rows, far_cols, coupling, ranks):
    nrhs, panels = loads.shape
    rank = far_cols.shape[0]
    blocks, tile = near_tiles.shape[:2]
    rows = panels // tile
    strips = coupling.shape[0] // CORES
    couple = coupling.reshape(CORES * strips * rank, rank)
    near_list = near_list.T
    ranks = ranks.reshape(1, CORES * strips)
    self_term = self_term.reshape(1, panels)
    message = (strips, nrhs, panels + LANES)
    index = pltpu.SMEM(near_list.shape, jnp.int32)
    scratch = [index, pltpu.SemaphoreType.DMA((1,)), pltpu.VMEM((3 * rows, CORES * nrhs, tile), F32)]
    scratch += [pltpu.VMEM((CORES * rows, CORES * nrhs, tile), F32)] * 4

    def twice(array):
        return [jax.ShapeDtypeStruct(array.shape, BF16)] * 2

    sent, *source_side, done = call(
        start_kernel,
        (loads, far_cols, couple, ranks),
        [message, *twice(far_cols), *twice(couple), jax.ShapeDtypeStruct((CORES * strips, CHUNK * rank), F32), (8, LANES)],
        [
            pltpu.VMEM(loads.shape, F32), pltpu.VMEM(far_cols.shape, F32), pltpu.VMEM(couple.shape, F32),
            pltpu.SMEM(ranks.shape, jnp.int32), pltpu.SemaphoreType.DMA((4,)),
        ],
        held=range(4),
    )
    part = jax.ShapeDtypeStruct((blocks // 2, tile, tile), BF16)
    tiles0, *target_side, near_list = call(
        fetch0_kernel,
        (done, near_tiles, far_rows, self_term, near_list),
        [part, *twice(far_rows), self_term, near_list],
        [
            pltpu.VMEM(far_rows.shape, F32), pltpu.VMEM(near_list.shape, jnp.int32),
            pltpu.SemaphoreType.DMA((PIECES,)), pltpu.SemaphoreType.DMA((3,)),
        ],
        held=range(1, 5),
    )
    (tiles1,) = call(
        fetch1_kernel, (done, near_tiles), [part], [pltpu.SemaphoreType.DMA((PIECES,))], held=(1,)
    )
    source_side, target_side = in_vmem(source_side), in_vmem([*target_side, tiles0, tiles1, near_list])
    got0 = exchanged(sent)
    sent, state = call(
        step0_kernel, (*got0, *source_side, *target_side), [message, (CORES * nrhs, LANES)], scratch
    )
    got1 = exchanged(sent)
    sent, basis, coeff = call(
        step1_kernel,
        (*got0, *got1, state, *target_side),
        [(CORES * strips, 1, LANES), (2 * nrhs, panels), (3 * nrhs, LANES)],
        scratch,
    )
    got = lax.all_to_all(sent, GROUP, 0, 0, tiled=True)
    return call(functools.partial(finish_kernel, rank), (got, basis, coeff), [loads.shape])[0]


def solution(mesh):
    every = ("case",) + GROUP
    in_specs = (
        P(None, every),
        P(every),
        P(every, None, None),
        P(every, None),
        P(None, every),
        P(None, every),
        P(None, GROUP, None, None),
        P(None, GROUP),
    )
    return jax.shard_map(body, mesh=mesh, in_specs=in_specs, out_specs=P(None, every), check_vma=False)
```

```python
import functools

import jax
import jax.numpy as jnp
from jax import lax
from jax.experimental import pallas as pl
from jax.experimental.pallas import tpu as pltpu
from jax.sharding import PartitionSpec as P

GROUP = ("strip", "clus")
CORES = 2
LANES = 128
CHUNK = 16
PIECES = 4
F32 = jnp.float32
BF16 = jnp.bfloat16

STEP = 7
TOP = 32767.0
ONE = float(2**30)


def lanes_of(shape):
    return lax.broadcasted_iota(jnp.int32, shape, 1)


def rows_of(shape):
    return lax.broadcasted_iota(jnp.int32, shape, 0)


def total(rows):
    return jnp.sum(rows, axis=0, keepdims=True)


def stats_row(columns, nrhs, rank):
    shape = (nrhs, LANES)
    first = lanes_of(shape) - rank * rows_of(shape)
    spread = sum(jnp.where(first == k, column, 0.0) for k, column in enumerate(columns))
    return total(spread)


def stat_column(row, k, nrhs, rank):
    shape = (nrhs, LANES)
    first = lanes_of(shape) - rank * rows_of(shape)
    return jnp.sum(jnp.where(first == k, row, 0.0), axis=1, keepdims=True)


def shifted(value, k):
    return pltpu.roll(value, LANES - k, 1)


def far_sum_of(row, nrhs, rank):
    shape = (nrhs, LANES)
    first = lanes_of(shape) - rank * rows_of(shape)
    own = jnp.where((first >= 0) & (first < rank), row, 0.0)
    return sum((pltpu.roll(own, k * rank, 1) for k in range(1, LANES // rank)), own)


def halves(value):
    high = value.astype(BF16)
    return high, (value - high.astype(F32)).astype(BF16)


def product(left, right_high, right_low, side=0):
    rows = left.shape[0]
    high, low = halves(left)
    dims = (((1,), (side,)), ((), ()))
    both = lax.dot_general(jnp.concatenate([high, low], axis=0), right_high, dims, preferred_element_type=F32)
    return both[:rows] + (both[rows:] + lax.dot_general(high, right_low, dims, preferred_element_type=F32))


def coded(value):
    exponent = jnp.ceil(jnp.log2(jnp.maximum(jnp.abs(value), 1e-30)))
    return (value * jnp.exp2(-exponent) * ONE).astype(jnp.int32), exponent.astype(jnp.int32)


def decoded(mantissa, exponent):
    return mantissa.astype(F32) * (1.0 / ONE) * jnp.exp2(exponent.astype(F32))


def packed(field):
    top = jnp.max(jnp.abs(field), axis=1, keepdims=True)
    step = jnp.maximum(top, 1e-30) * (1.0 / TOP)
    codes = jnp.floor(field * (1.0 / step) + 0.5).astype(jnp.int32)
    width = field.shape[1] // 2
    return (codes[:, :width] << 16) | (codes[:, width:] & 0xFFFF), step


def unpacked(words):
    return jnp.concatenate([words >> 16, (words << 16) >> 16], axis=1).astype(F32)


def fetch(pairs, sems):
    copies = [pltpu.make_async_copy(a, b, sems.at[i]) for i, (a, b) in enumerate(pairs)]
    for copy in copies:
        copy.start()
    return copies


def put_message(field, columns, cols, couple, masks_ref, sent_ref):
    nrhs, rank = field.shape[0], cols[0].shape[0]
    words, step = packed(field)
    width = words.shape[1]
    for i in range(sent_ref.shape[0]):
        sent_ref[i, :, :width] = words
    columns = columns + [0.0] * (STEP - len(columns)) + [step]
    stats = coded(stats_row(columns, nrhs, rank))
    proj = product(field, cols[0][...], cols[1][...], 1)
    wide = jnp.concatenate([proj] * CHUNK, axis=1)
    for start in range(0, sent_ref.shape[0], CHUNK):
        mask = masks_ref[pl.ds(start, CHUNK), :]
        spread = jnp.concatenate([mask * wide[r : r + 1] for r in range(nrhs)], axis=0)
        here = pl.ds(start * rank, CHUNK * rank)
        terms = product(spread, couple[0][here, :], couple[1][here, :])
        terms = coded(jnp.concatenate([terms[r * CHUNK : (r + 1) * CHUNK] for r in range(nrhs)], axis=1))
        for i in range(CHUNK):
            tail = [term[i : i + 1] for term in terms] + list(stats)
            sent_ref[start + i, :, width:] = jnp.concatenate(tail, axis=0)


def message_parts(got_ref):
    width = got_ref.shape[2] - LANES
    terms, stats = (decoded(got_ref[:, k, width:], got_ref[:, k + 1, width:]) for k in (0, 2))
    return total(terms), stats


def window_parts(got_ref, rank):
    nrhs, width = got_ref.shape[1], got_ref.shape[2] - LANES
    strips = got_ref.shape[0] // CORES
    shape = (CORES * nrhs, LANES)
    for step in range(3):
        owner = lax.axis_index("strip") + (step - 1)
        inside = (owner >= 0) & (owner < strips)
        owner = CORES * jnp.clip(owner, 0, strips - 1)
        words = jnp.concatenate([got_ref[owner + core, :, :width] for core in range(CORES)], axis=0)
        tails = [got_ref[owner + core, :, width:] for core in range(CORES)]
        rows = [decoded(tail[2:3], tail[3:4]) for tail in tails]
        rows = jnp.where(rows_of(shape) < nrhs, rows[0], rows[1])
        wanted = lanes_of(shape) == rank * lax.rem(rows_of(shape), nrhs) + STEP
        yield inside, unpacked(words), jnp.sum(jnp.where(wanted, rows, 0.0), axis=1, keepdims=True)


def put_blocks(part, first, window):
    part = part.astype(BF16).astype(F32)
    for c in range(part.shape[1] // LANES):
        window[first + c] = part[:, c * LANES : (c + 1) * LANES]


def near_field(window, tiles, list_ref, sums, nrhs):
    for held in sums:
        held[...] = jnp.zeros_like(held)
    n = 0
    for tiles_ref in tiles:
        for i in range(tiles_ref.shape[0]):
            held = sums[n % len(sums)]
            source = window[list_ref[1, n]].astype(BF16)
            held[list_ref[0, n]] += jnp.dot(source, tiles_ref[i], preferred_element_type=F32)
            n += 1
    whole = sum((held[...] for held in sums[1:]), sums[0][...])
    rows = whole.shape[0] // CORES
    return jnp.concatenate([whole[b, :nrhs] + whole[rows + b, nrhs:] for b in range(rows)], axis=1)


def start_kernel(
    loads_hbm, cols_hbm, couple_hbm, ranks_hbm, sent_ref, cols_high, cols_low, couple_high, couple_low, masks_ref,
    loads_ref, done_ref, cols_ref, couple_ref, ranks_ref, sems,
):
    rank = cols_ref.shape[0]
    pairs = ((ranks_hbm, ranks_ref), (loads_hbm, loads_ref), (cols_hbm, cols_ref), (couple_hbm, couple_ref))
    copies = fetch(pairs, sems)
    done_ref[...] = jnp.zeros_like(done_ref)
    copies[0].wait()
    shape = (CHUNK, CHUNK * rank)
    owner = lax.div(lanes_of(shape), rank)
    inner = lax.rem(lanes_of(shape), rank)
    for start in range(0, masks_ref.shape[0], CHUNK):
        limit = jnp.zeros((1, CHUNK * rank), jnp.int32)
        for i in range(CHUNK):
            limit = jnp.where(owner[:1] == i, ranks_ref[0, start + i], limit)
        masks_ref[pl.ds(start, CHUNK), :] = jnp.where((owner == rows_of(shape)) & (inner < limit), 1.0, 0.0)
    copies[1].wait()
    loads = loads_ref[...]
    square = jnp.sum(loads * loads, axis=1, keepdims=True)
    copies[2].wait()
    cols_high[...], cols_low[...] = halves(cols_ref[...])
    copies[3].wait()
    couple_high[...], couple_low[...] = halves(couple_ref[...])
    put_message(loads, [square], (cols_high, cols_low), (couple_high, couple_low), masks_ref, sent_ref)


def copy_tiles(tiles_hbm, first, tiles_ref, sems):
    every = tiles_ref.shape[0] // PIECES
    pairs = [(pl.ds(first + i * every, every), pl.ds(i * every, every)) for i in range(PIECES)]
    return fetch([(tiles_hbm.at[a], tiles_ref.at[b]) for a, b in pairs], sems)


def fetch0_kernel(done_ref, tiles_hbm, rows_hbm, self_hbm, list_hbm, tiles_ref, rows_high, rows_low, self_ref, list_ref,
                  rows_ref, raw_ref, sems, other_sems):
    del done_ref
    pairs = ((list_hbm, raw_ref), (rows_hbm, rows_ref), (self_hbm, self_ref))
    copies = fetch(pairs, other_sems)
    pieces = copy_tiles(tiles_hbm, 0, tiles_ref, sems)
    copies[0].wait()
    rows = self_ref.shape[1] // tiles_ref.shape[1]
    target, source = raw_ref[0:1, :], raw_ref[1:2, :]
    group, block = lax.div(source, rows), lax.rem(source, rows)
    strip, core = lax.div(group, CORES), lax.rem(group, CORES)
    list_ref[...] = jnp.concatenate([core * rows + target, strip * rows + block], axis=0)
    copies[1].wait()
    rows_high[...], rows_low[...] = halves(rows_ref[...])
    copies[2].wait()
    for piece in pieces:
        piece.wait()


def fetch1_kernel(done_ref, tiles_hbm, tiles_ref, sems):
    del done_ref
    for piece in copy_tiles(tiles_hbm, tiles_ref.shape[0], tiles_ref, sems):
        piece.wait()


def image_of(field, far, self_ref, far_rows, near):
    rank = far_rows[0].shape[0]
    return self_ref[...] * field + near + product(far[:, :rank], far_rows[0][...], far_rows[1][...])


def step0_kernel(
    got_ref, loads_ref, cols_high, cols_low, couple_high, couple_low, masks_ref, rows_high, rows_low, self_ref,
    tiles0_ref, tiles1_ref, list_vmem, sent_ref, image_ref, window0_ref, state_ref, list_ref, sems, window, *sums,
):
    rank = rows_high.shape[0]
    nrhs, panels = loads_ref.shape
    span, rows = panels // LANES, CORES * nrhs
    (copy,) = fetch(((list_vmem, list_ref),), sems)
    terms, stats = message_parts(got_ref)
    beta = jnp.sqrt(stat_column(total(stats), 0, nrhs, rank))
    scale = 1.0 / beta
    both = jnp.concatenate([scale] * CORES, axis=0)
    for step, (inside, part, unit) in enumerate(window_parts(got_ref, rank)):
        part = jnp.where(inside, part * (unit * both), 0.0)
        window0_ref[step * rows : (step + 1) * rows, :] = part
        put_blocks(part, step * span, window)
    basis = loads_ref[...] * scale
    far = far_sum_of(terms, nrhs, rank) * scale
    copy.wait()
    near = near_field(window, (tiles0_ref, tiles1_ref), list_ref, sums, nrhs)
    image = image_of(basis, far, self_ref, (rows_high, rows_low), near)
    image_ref[...] = image
    state_ref[...] = jnp.concatenate([far, jnp.broadcast_to(beta, far.shape)], axis=0)
    norm = jnp.sum(basis * basis, axis=1, keepdims=True)
    dot = jnp.sum(basis * image, axis=1, keepdims=True)
    share = jnp.where(norm > 0, dot / jnp.where(norm > 0, norm, 1.0), 0.0)
    rest = image - share * basis
    rest = jnp.sum(rest * rest, axis=1, keepdims=True)
    columns = [norm, dot, share, rest]
    put_message(image, columns, (cols_high, cols_low), (couple_high, couple_low), masks_ref, sent_ref)


def step1_kernel(
    got_ref, loads_ref, image_ref, window0_ref, state_ref, rows_high, rows_low, self_ref, tiles0_ref, tiles1_ref,
    list_vmem, sent_ref, basis_ref, coeff_ref, list_ref, sems, window, *sums,
):
    rank = rows_high.shape[0]
    nrhs, panels = loads_ref.shape
    span, rows = panels // LANES, CORES * nrhs
    (copy,) = fetch(((list_vmem, list_ref),), sems)
    beta = state_ref[nrhs:, :1]
    far0 = state_ref[:nrhs, :]
    terms, stats = message_parts(got_ref)
    summed = total(stats)
    h00 = stat_column(summed, 1, nrhs, rank)
    away = shifted(stats, 2) - shifted(summed, 1)
    rest = total(shifted(stats, 3) + stats * away * away)
    h10 = jnp.sqrt(stat_column(rest, 0, nrhs, rank))
    scale = 1.0 / h10
    both, both_h00 = (jnp.concatenate([a] * CORES, axis=0) for a in (scale, h00))
    for step, (inside, part, unit) in enumerate(window_parts(got_ref, rank)):
        part = (part * unit - both_h00 * window0_ref[step * rows : (step + 1) * rows, :]) * both
        put_blocks(jnp.where(inside, part, 0.0), step * span, window)
    basis0 = loads_ref[...] * (1.0 / beta)
    basis1 = (image_ref[...] - h00 * basis0) * scale
    far = (far_sum_of(terms, nrhs, rank) - h00 * far0) * scale
    copy.wait()
    near = near_field(window, (tiles0_ref, tiles1_ref), list_ref, sums, nrhs)
    image = image_of(basis1, far, self_ref, (rows_high, rows_low), near)
    columns = [jnp.sum(a * image, axis=1, keepdims=True) for a in (basis0, basis1, image)]
    sent_ref[:, 0, :] = jnp.broadcast_to(stats_row(columns, nrhs, rank), (sent_ref.shape[0], LANES))
    basis_ref[...] = jnp.concatenate([basis0, basis1], axis=0)
    coeff_ref[...] = jnp.concatenate([jnp.broadcast_to(v, (nrhs, LANES)) for v in (beta, h00, h10)], axis=0)


def finish_kernel(rank, got_ref, basis_ref, coeff_ref, out_ref):
    nrhs = out_ref.shape[0]
    row = total(got_ref[:, 0, :])
    h01, h11, gram11 = (stat_column(row, k, nrhs, rank) for k in range(3))
    beta, h00, h10 = (coeff_ref[k * nrhs : (k + 1) * nrhs, :1] for k in range(3))
    gram00 = h00 * h00 + h10 * h10
    gram01 = h00 * h01 + h10 * h11
    lower00 = jnp.sqrt(gram00)
    lower10 = gram01 / lower00
    lower11 = jnp.sqrt(gram11 - lower10 * lower10)
    middle0 = beta * h00 / lower00
    middle1 = (beta * h01 - lower10 * middle0) / lower11
    y1 = middle1 / lower11
    y0 = (middle0 - lower10 * y1) / lower00
    out_ref[...] = y0 * basis_ref[:nrhs, :] + y1 * basis_ref[nrhs:, :]


class Plain(jax.ShapeDtypeStruct):
    pass


def in_vmem_like(array):
    return pltpu.VMEM(array.shape, array.dtype)


def in_vmem(arrays):
    return [pltpu.with_memory_space_constraint(a, pltpu.VMEM) for a in arrays]


def call(kernel, args, outs, scratch=(), held=(), flops=0):
    args = [pltpu.with_memory_space_constraint(a, pltpu.HBM) if i in held else a for i, a in enumerate(args)]
    moved = sum(a.size * a.dtype.itemsize for a in args)
    return pl.pallas_call(
        kernel,
        out_shape=[
            jax.ShapeDtypeStruct(out, F32) if isinstance(out, tuple) else out if isinstance(out, Plain) else in_vmem_like(out)
            for out in outs
        ],
        in_specs=[pl.BlockSpec(memory_space=pl.ANY if i in held else pltpu.VMEM) for i in range(len(args))],
        out_specs=[pl.BlockSpec(memory_space=pltpu.VMEM)] * len(outs),
        scratch_shapes=list(scratch),
        compiler_params=pltpu.CompilerParams(vmem_limit_bytes=24 * 2**20),
        cost_estimate=pl.CostEstimate(flops=flops, bytes_accessed=moved, transcendentals=0),
    )(*args)


def exchanged(sent):
    return lax.all_to_all(sent, GROUP, 0, 0, tiled=True)


def body(loads, self_term, near_tiles, near_list, far_rows, far_cols, coupling, ranks):
    nrhs, panels = loads.shape
    rank = far_cols.shape[0]
    blocks, tile = near_tiles.shape[:2]
    rows = panels // tile
    strips = coupling.shape[0] // CORES
    couple = coupling.reshape(CORES * strips * rank, rank)
    near_list = near_list.T
    ranks = ranks.reshape(1, CORES * strips)
    self_term = self_term.reshape(1, panels)
    groups = CORES * strips
    message = Plain((groups, nrhs, panels // 2 + LANES), jnp.int32)
    index = pltpu.SMEM(near_list.shape, jnp.int32)
    scratch = [index, pltpu.SemaphoreType.DMA((1,)), pltpu.VMEM((3 * rows, CORES * nrhs, tile), F32)]
    scratch += [pltpu.VMEM((CORES * rows, CORES * nrhs, tile), F32)] * 4

    def twice(array):
        return [jax.ShapeDtypeStruct(array.shape, BF16)] * 2

    sent, *source_side, loads, done = call(
        start_kernel,
        (loads, far_cols, couple, ranks),
        [message, *twice(far_cols), *twice(couple), jax.ShapeDtypeStruct((groups, CHUNK * rank), F32), loads, (8, LANES)],
        [
            pltpu.VMEM(far_cols.shape, F32), pltpu.VMEM(couple.shape, F32),
            pltpu.SMEM(ranks.shape, jnp.int32), pltpu.SemaphoreType.DMA((4,)),
        ],
        held=range(4),
    )
    part = jax.ShapeDtypeStruct((blocks // 2, tile, tile), BF16)
    tiles0, *target_side, near_list = call(
        fetch0_kernel,
        (done, near_tiles, far_rows, self_term, near_list),
        [part, *twice(far_rows), self_term, near_list],
        [
            pltpu.VMEM(far_rows.shape, F32), pltpu.VMEM(near_list.shape, jnp.int32),
            pltpu.SemaphoreType.DMA((PIECES,)), pltpu.SemaphoreType.DMA((3,)),
        ],
        held=range(1, 5),
    )
    (tiles1,) = call(
        fetch1_kernel, (done, near_tiles), [part], [pltpu.SemaphoreType.DMA((PIECES,))], held=(1,)
    )
    source_side, target_side = in_vmem([loads, *source_side]), in_vmem([*target_side, tiles0, tiles1, near_list])
    loads = source_side[0]
    sent, image, window0, state = call(
        step0_kernel,
        (exchanged(sent), *source_side, *target_side),
        [message, loads.shape, (3 * CORES * nrhs, panels), (CORES * nrhs, LANES)],
        scratch,
    )
    sent, basis, coeff = call(
        step1_kernel,
        (exchanged(sent), loads, image, window0, state, *target_side),
        [(groups, 1, LANES), (2 * nrhs, panels), (3 * nrhs, LANES)],
        scratch,
    )
    return call(functools.partial(finish_kernel, rank), (exchanged(sent), basis, coeff), [loads.shape])[0]


def solution(mesh):
    every = ("case",) + GROUP
    in_specs = (
        P(None, every),
        P(every),
        P(every, None, None),
        P(every, None),
        P(None, every),
        P(None, every),
        P(None, GROUP, None, None),
        P(None, GROUP),
    )
    return jax.shard_map(body, mesh=mesh, in_specs=in_specs, out_specs=P(None, every), check_vma=False)
```

```python
import functools

import jax
import jax.numpy as jnp
from jax import lax
from jax.experimental import pallas as pl
from jax.experimental.pallas import tpu as pltpu
from jax.sharding import PartitionSpec as P

GROUP = ("strip", "clus")
CORES = 2
LANES = 128
CHUNK = 16
PIECES = 4
F32 = jnp.float32
BF16 = jnp.bfloat16

STEP = 8
COLS_TOP = 0.1875
COUPLE_TOP = 0.375
TOP = 32767.0
ONE = float(2**30)


def lanes_of(shape):
    return lax.broadcasted_iota(jnp.int32, shape, 1)


def rows_of(shape):
    return lax.broadcasted_iota(jnp.int32, shape, 0)


def total(rows):
    return jnp.sum(rows, axis=0, keepdims=True)


def stats_row(columns, rank, step=None):
    shape = (columns[0].shape[0], LANES)
    first = lanes_of(shape) - rank * rows_of(shape)
    spread = sum(jnp.where(first == k, column, 0.0) for k, column in enumerate(columns))
    if step is not None:
        spread = jnp.where((first >= STEP) & (first < rank), step, spread)
    return total(spread)


def steps_of(stats, rank):
    inner = lax.rem(lanes_of(stats.shape), rank)
    return jnp.where(inner < STEP, shifted(stats, STEP), stats)


def term_unit(panels, rank):
    return panels * rank * COLS_TOP * COUPLE_TOP * TOP / ONE


def stat_column(row, k, nrhs, rank):
    shape = (nrhs, LANES)
    first = lanes_of(shape) - rank * rows_of(shape)
    return jnp.sum(jnp.where(first == k, row, 0.0), axis=1, keepdims=True)


def shifted(value, k):
    return pltpu.roll(value, LANES - k, 1)


def far_sum_of(row, nrhs, rank):
    shape = (nrhs, LANES)
    first = lanes_of(shape) - rank * rows_of(shape)
    own = jnp.where((first >= 0) & (first < rank), row, 0.0)
    return sum((pltpu.roll(own, k * rank, 1) for k in range(1, LANES // rank)), own)


def halves(value):
    high = value.astype(BF16)
    return high, (value - high.astype(F32)).astype(BF16)


def product(left, right_high, right_low, side=0):
    rows = left.shape[0]
    high, low = halves(left)
    dims = (((1,), (side,)), ((), ()))
    both = lax.dot_general(jnp.concatenate([high, low], axis=0), right_high, dims, preferred_element_type=F32)
    return both[:rows] + (both[rows:] + lax.dot_general(high, right_low, dims, preferred_element_type=F32))


def coded(value):
    exponent = jnp.ceil(jnp.log2(jnp.maximum(jnp.abs(value), 1e-30)))
    return (value * jnp.exp2(-exponent) * ONE).astype(jnp.int32), exponent.astype(jnp.int32)


def decoded(mantissa, exponent):
    return mantissa.astype(F32) * (1.0 / ONE) * jnp.exp2(exponent.astype(F32))


def packed(field):
    top = jnp.max(jnp.abs(field), axis=1, keepdims=True)
    step = jnp.maximum(top, 1e-30) * (1.0 / TOP)
    codes = jnp.floor(field * (1.0 / step) + 0.5).astype(jnp.int32)
    width = field.shape[1] // 2
    return (codes[:, :width] << 16) | (codes[:, width:] & 0xFFFF), step


def unpacked(words):
    return jnp.concatenate([words >> 16, (words << 16) >> 16], axis=1).astype(F32)


def fetch(pairs, sems):
    copies = [pltpu.make_async_copy(a, b, sems.at[i]) for i, (a, b) in enumerate(pairs)]
    for copy in copies:
        copy.start()
    return copies


def put_message(field, columns, cols, couple, masks_ref, sent_ref):
    nrhs, rank = field.shape[0], cols[0].shape[0]
    unit = term_unit(field.shape[1], rank)
    proj = product(field, cols[0][...], cols[1][...], 1)
    wide = jnp.concatenate([proj] * CHUNK, axis=1)
    words, step = packed(field)
    width = words.shape[1]
    row = stats_row(columns, rank, step)
    finer = 1.0 / (steps_of(row, rank) * unit)
    for i in range(sent_ref.shape[0]):
        sent_ref[i, :, :width] = words
    stats = [jnp.broadcast_to(a, (CHUNK, LANES)) for a in coded(row)]
    for start in range(0, sent_ref.shape[0], CHUNK):
        mask = masks_ref[pl.ds(start, CHUNK), :]
        spread = jnp.concatenate([mask * wide[r : r + 1] for r in range(nrhs)], axis=0)
        here = pl.ds(start * rank, CHUNK * rank)
        terms = product(spread, couple[0][here, :], couple[1][here, :])
        terms = jnp.concatenate([terms[r * CHUNK : (r + 1) * CHUNK] for r in range(nrhs)], axis=1)
        here = pl.ds(start, CHUNK)
        for k, value in enumerate([(terms * finer).astype(jnp.int32)] + stats + [stats[0]] * (nrhs - 3)):
            sent_ref[here, k, width:] = value


def message_parts(got_ref, rank):
    width = got_ref.shape[2] - LANES
    stats = decoded(got_ref[:, 1, width:], got_ref[:, 2, width:])
    terms = got_ref[:, 0, width:].astype(F32) * (steps_of(stats, rank) * term_unit(2 * width, rank))
    return total(terms), stats


def window_parts(got_ref, rank):
    nrhs, width = got_ref.shape[1], got_ref.shape[2] - LANES
    strips = got_ref.shape[0] // CORES
    shape = (CORES * nrhs, LANES)
    for step in range(3):
        owner = lax.axis_index("strip") + (step - 1)
        inside = (owner >= 0) & (owner < strips)
        owner = CORES * jnp.clip(owner, 0, strips - 1)
        words = jnp.concatenate([got_ref[owner + core, :, :width] for core in range(CORES)], axis=0)
        tails = [got_ref[owner + core, :, width:] for core in range(CORES)]
        rows = [decoded(tail[1:2], tail[2:3]) for tail in tails]
        rows = jnp.where(rows_of(shape) < nrhs, rows[0], rows[1])
        wanted = lanes_of(shape) == rank * lax.rem(rows_of(shape), nrhs) + STEP
        yield inside, unpacked(words), jnp.sum(jnp.where(wanted, rows, 0.0), axis=1, keepdims=True)


def put_blocks(part, first, window):
    part = part.astype(BF16).astype(F32)
    for c in range(part.shape[1] // LANES):
        window[first + c] = part[:, c * LANES : (c + 1) * LANES]


def near_field(window, tiles, list_ref, sums, nrhs):
    for held in sums:
        held[...] = jnp.zeros_like(held)
    n = 0
    for tiles_ref in tiles:
        for first in range(0, tiles_ref.shape[0], 4):
            sources = [window[list_ref[1, n + i]] for i in range(4)]
            blank = jnp.zeros_like(sources[0])
            upper = [sources[0], blank, sources[2], blank]
            lower = [blank, sources[1], blank, sources[3]]
            left = jnp.concatenate([jnp.concatenate(a, axis=0).astype(BF16) for a in (upper, lower)], axis=1)
            four = [tiles_ref[first + i] for i in range(4)]
            right = [jnp.concatenate([four[i], four[i + 2]], axis=1) for i in range(2)]
            both = jnp.dot(left, jnp.concatenate(right, axis=0), preferred_element_type=F32)
            for i, held in enumerate(sums):
                side = i // 2 * LANES
                rows = i * window.shape[1]
                held[list_ref[0, n + i]] += both[rows : rows + window.shape[1], side : side + LANES]
            n += 4
    whole = sum((held[...] for held in sums[1:]), sums[0][...])
    rows = whole.shape[0] // CORES
    return jnp.concatenate([whole[b, :nrhs] + whole[rows + b, nrhs:] for b in range(rows)], axis=1)


def start_kernel(
    loads_hbm, cols_hbm, couple_hbm, ranks_hbm, sent_ref, cols_high, cols_low, couple_high, couple_low, masks_ref,
    loads_ref, done_ref, cols_ref, couple_ref, ranks_ref, sems,
):
    rank = cols_ref.shape[0]
    pairs = ((loads_hbm, loads_ref), (cols_hbm, cols_ref), (couple_hbm, couple_ref), (ranks_hbm, ranks_ref))
    copies = fetch(pairs, sems)
    done_ref[...] = jnp.zeros_like(done_ref)
    copies[0].wait()
    loads = loads_ref[...]
    square = jnp.sum(loads * loads, axis=1, keepdims=True)
    copies[1].wait()
    cols_high[...], cols_low[...] = halves(cols_ref[...])
    copies[2].wait()
    couple_high[...], couple_low[...] = halves(couple_ref[...])
    copies[3].wait()
    shape = (CHUNK, CHUNK * rank)
    owner = lax.div(lanes_of(shape), rank)
    inner = lax.rem(lanes_of(shape), rank)
    for start in range(0, masks_ref.shape[0], CHUNK):
        limit = jnp.zeros((1, CHUNK * rank), jnp.int32)
        for i in range(CHUNK):
            limit = jnp.where(owner[:1] == i, ranks_ref[0, start + i], limit)
        masks_ref[pl.ds(start, CHUNK), :] = jnp.where((owner == rows_of(shape)) & (inner < limit), 1.0, 0.0)
    put_message(loads, [square], (cols_high, cols_low), (couple_high, couple_low), masks_ref, sent_ref)


def copy_tiles(tiles_hbm, first, tiles_ref, sems):
    every = tiles_ref.shape[0] // PIECES
    pairs = [(pl.ds(first + i * every, every), pl.ds(i * every, every)) for i in range(PIECES)]
    return fetch([(tiles_hbm.at[a], tiles_ref.at[b]) for a, b in pairs], sems)


def fetch0_kernel(done_ref, tiles_hbm, rows_hbm, self_hbm, list_hbm, tiles_ref, rows_high, rows_low, self_ref, list_ref,
                  rows_ref, raw_ref, sems, other_sems):
    del done_ref
    pairs = ((list_hbm, raw_ref), (rows_hbm, rows_ref), (self_hbm, self_ref))
    copies = fetch(pairs, other_sems)
    pieces = copy_tiles(tiles_hbm, 0, tiles_ref, sems)
    copies[0].wait()
    rows = self_ref.shape[1] // tiles_ref.shape[1]
    target, source = raw_ref[0:1, :], raw_ref[1:2, :]
    group, block = lax.div(source, rows), lax.rem(source, rows)
    strip, core = lax.div(group, CORES), lax.rem(group, CORES)
    list_ref[...] = jnp.concatenate([core * rows + target, strip * rows + block], axis=0)
    copies[1].wait()
    rows_high[...], rows_low[...] = halves(rows_ref[...])
    copies[2].wait()
    for piece in pieces:
        piece.wait()


def fetch1_kernel(done_ref, tiles_hbm, tiles_ref, sems):
    del done_ref
    for piece in copy_tiles(tiles_hbm, tiles_ref.shape[0], tiles_ref, sems):
        piece.wait()


def image_of(field, far, self_ref, far_rows, near):
    rank = far_rows[0].shape[0]
    return self_ref[...] * field + near + product(far[:, :rank], far_rows[0][...], far_rows[1][...])


def step0_kernel(
    got_ref, loads_ref, cols_high, cols_low, couple_high, couple_low, masks_ref, rows_high, rows_low, self_ref,
    tiles0_ref, tiles1_ref, list_vmem, sent_ref, image_ref, window0_ref, state_ref, list_ref, sems, window, *sums,
):
    rank = rows_high.shape[0]
    nrhs, panels = loads_ref.shape
    span, rows = panels // LANES, CORES * nrhs
    (copy,) = fetch(((list_vmem, list_ref),), sems)
    terms, stats = message_parts(got_ref, rank)
    beta = jnp.sqrt(stat_column(total(stats), 0, nrhs, rank))
    scale = 1.0 / beta
    both = jnp.concatenate([scale] * CORES, axis=0)
    for step, (inside, part, unit) in enumerate(window_parts(got_ref, rank)):
        part = jnp.where(inside, part * (unit * both), 0.0)
        window0_ref[step * rows : (step + 1) * rows, :] = part
        put_blocks(part, step * span, window)
    basis = loads_ref[...] * scale
    far = far_sum_of(terms, nrhs, rank) * scale
    copy.wait()
    near = near_field(window, (tiles0_ref, tiles1_ref), list_ref, sums, nrhs)
    image = image_of(basis, far, self_ref, (rows_high, rows_low), near)
    image_ref[...] = image
    state_ref[...] = jnp.concatenate([far, jnp.broadcast_to(beta, far.shape)], axis=0)
    norm = jnp.sum(basis * basis, axis=1, keepdims=True)
    dot = jnp.sum(basis * image, axis=1, keepdims=True)
    share = jnp.where(norm > 0, dot / jnp.where(norm > 0, norm, 1.0), 0.0)
    rest = image - share * basis
    rest = jnp.sum(rest * rest, axis=1, keepdims=True)
    columns = [norm, dot, share, rest]
    put_message(image, columns, (cols_high, cols_low), (couple_high, couple_low), masks_ref, sent_ref)


def step1_kernel(
    got_ref, loads_ref, image_ref, window0_ref, state_ref, rows_high, rows_low, self_ref, tiles0_ref, tiles1_ref,
    list_vmem, sent_ref, basis_ref, coeff_ref, list_ref, sems, window, *sums,
):
    rank = rows_high.shape[0]
    nrhs, panels = loads_ref.shape
    span, rows = panels // LANES, CORES * nrhs
    (copy,) = fetch(((list_vmem, list_ref),), sems)
    beta = state_ref[nrhs:, :1]
    far0 = state_ref[:nrhs, :]
    terms, stats = message_parts(got_ref, rank)
    summed = total(stats)
    h00 = stat_column(summed, 1, nrhs, rank)
    away = shifted(stats, 2) - shifted(summed, 1)
    rest = total(shifted(stats, 3) + stats * away * away)
    h10 = jnp.sqrt(stat_column(rest, 0, nrhs, rank))
    scale = 1.0 / h10
    both, both_h00 = (jnp.concatenate([a] * CORES, axis=0) for a in (scale, h00))
    for step, (inside, part, unit) in enumerate(window_parts(got_ref, rank)):
        part = (part * unit - both_h00 * window0_ref[step * rows : (step + 1) * rows, :]) * both
        put_blocks(jnp.where(inside, part, 0.0), step * span, window)
    basis0 = loads_ref[...] * (1.0 / beta)
    basis1 = (image_ref[...] - h00 * basis0) * scale
    far = (far_sum_of(terms, nrhs, rank) - h00 * far0) * scale
    copy.wait()
    near = near_field(window, (tiles0_ref, tiles1_ref), list_ref, sums, nrhs)
    image = image_of(basis1, far, self_ref, (rows_high, rows_low), near)
    columns = [jnp.sum(a * image, axis=1, keepdims=True) for a in (basis0, basis1, image)]
    sent_ref[:, 0, :] = jnp.broadcast_to(stats_row(columns, rank), (sent_ref.shape[0], LANES))
    basis_ref[...] = jnp.concatenate([basis0, basis1], axis=0)
    coeff_ref[...] = jnp.concatenate([jnp.broadcast_to(v, (nrhs, LANES)) for v in (beta, h00, h10)], axis=0)


def finish_kernel(rank, got_ref, basis_ref, coeff_ref, out_ref):
    nrhs = out_ref.shape[0]
    row = total(got_ref[:, 0, :])
    h01, h11, gram11 = (stat_column(row, k, nrhs, rank) for k in range(3))
    beta, h00, h10 = (coeff_ref[k * nrhs : (k + 1) * nrhs, :1] for k in range(3))
    gram00 = h00 * h00 + h10 * h10
    gram01 = h00 * h01 + h10 * h11
    lower00 = jnp.sqrt(gram00)
    lower10 = gram01 / lower00
    lower11 = jnp.sqrt(gram11 - lower10 * lower10)
    middle0 = beta * h00 / lower00
    middle1 = (beta * h01 - lower10 * middle0) / lower11
    y1 = middle1 / lower11
    y0 = (middle0 - lower10 * y1) / lower00
    out_ref[...] = y0 * basis_ref[:nrhs, :] + y1 * basis_ref[nrhs:, :]


class Plain(jax.ShapeDtypeStruct):
    pass


def in_vmem_like(array):
    return pltpu.VMEM(array.shape, array.dtype)


def in_vmem(arrays):
    return [pltpu.with_memory_space_constraint(a, pltpu.VMEM) for a in arrays]


def call(kernel, args, outs, scratch=(), held=(), flops=0):
    args = [pltpu.with_memory_space_constraint(a, pltpu.HBM) if i in held else a for i, a in enumerate(args)]
    moved = sum(a.size * a.dtype.itemsize for a in args)
    return pl.pallas_call(
        kernel,
        out_shape=[
            jax.ShapeDtypeStruct(out, F32) if isinstance(out, tuple) else out if isinstance(out, Plain) else in_vmem_like(out)
            for out in outs
        ],
        in_specs=[pl.BlockSpec(memory_space=pl.ANY if i in held else pltpu.VMEM) for i in range(len(args))],
        out_specs=[pl.BlockSpec(memory_space=pltpu.VMEM)] * len(outs),
        scratch_shapes=list(scratch),
        compiler_params=pltpu.CompilerParams(vmem_limit_bytes=24 * 2**20),
        cost_estimate=pl.CostEstimate(flops=flops, bytes_accessed=moved, transcendentals=0),
    )(*args)


def exchanged(sent):
    return lax.all_to_all(sent, GROUP, 0, 0, tiled=True)


def body(loads, self_term, near_tiles, near_list, far_rows, far_cols, coupling, ranks):
    nrhs, panels = loads.shape
    rank = far_cols.shape[0]
    blocks, tile = near_tiles.shape[:2]
    rows = panels // tile
    strips = coupling.shape[0] // CORES
    couple = coupling.reshape(CORES * strips * rank, rank)
    near_list = near_list.T
    ranks = ranks.reshape(1, CORES * strips)
    self_term = self_term.reshape(1, panels)
    groups = CORES * strips
    message = Plain((groups, nrhs, panels // 2 + LANES), jnp.int32)
    index = pltpu.SMEM(near_list.shape, jnp.int32)
    scratch = [index, pltpu.SemaphoreType.DMA((1,)), pltpu.VMEM((3 * rows, CORES * nrhs, tile), F32)]
    scratch += [pltpu.VMEM((CORES * rows, CORES * nrhs, tile), F32)] * 4

    def twice(array):
        return [jax.ShapeDtypeStruct(array.shape, BF16)] * 2

    sent, *source_side, loads, done = call(
        start_kernel,
        (loads, far_cols, couple, ranks),
        [message, *twice(far_cols), *twice(couple), jax.ShapeDtypeStruct((groups, CHUNK * rank), F32), loads, (8, LANES)],
        [
            pltpu.VMEM(far_cols.shape, F32), pltpu.VMEM(couple.shape, F32),
            pltpu.SMEM(ranks.shape, jnp.int32), pltpu.SemaphoreType.DMA((4,)),
        ],
        held=range(4),
    )
    part = jax.ShapeDtypeStruct((blocks // 2, tile, tile), BF16)
    tiles0, *target_side, near_list = call(
        fetch0_kernel,
        (done, near_tiles, far_rows, self_term, near_list),
        [part, *twice(far_rows), self_term, near_list],
        [
            pltpu.VMEM(far_rows.shape, F32), pltpu.VMEM(near_list.shape, jnp.int32),
            pltpu.SemaphoreType.DMA((PIECES,)), pltpu.SemaphoreType.DMA((3,)),
        ],
        held=range(1, 5),
    )
    (tiles1,) = call(
        fetch1_kernel, (done, near_tiles), [part], [pltpu.SemaphoreType.DMA((PIECES,))], held=(1,)
    )
    source_side, target_side = in_vmem([loads, *source_side]), in_vmem([*target_side, tiles0, tiles1, near_list])
    loads = source_side[0]
    sent, image, window0, state = call(
        step0_kernel,
        (exchanged(sent), *source_side, *target_side),
        [message, loads.shape, (3 * CORES * nrhs, panels), (CORES * nrhs, LANES)],
        scratch,
    )
    sent, basis, coeff = call(
        step1_kernel,
        (exchanged(sent), loads, image, window0, state, *target_side),
        [(groups, 1, LANES), (2 * nrhs, panels), (3 * nrhs, LANES)],
        scratch,
    )
    return call(functools.partial(finish_kernel, rank), (exchanged(sent), basis, coeff), [loads.shape])[0]


def solution(mesh):
    every = ("case",) + GROUP
    in_specs = (
        P(None, every),
        P(every),
        P(every, None, None),
        P(every, None),
        P(None, every),
        P(None, every),
        P(None, GROUP, None, None),
        P(None, GROUP),
    )
    return jax.shard_map(body, mesh=mesh, in_specs=in_specs, out_specs=P(None, every), check_vma=False)
```

```python
import functools

import jax
import jax.numpy as jnp
from jax import lax
from jax.experimental import pallas as pl
from jax.experimental.pallas import tpu as pltpu
from jax.sharding import PartitionSpec as P

GROUP = ("strip", "clus")
CORES = 2
LANES = 128
CHUNK = 16
PIECES = 4
F32 = jnp.float32
BF16 = jnp.bfloat16

STEP = 8
COLS_TOP = 0.1875
COUPLE_TOP = 0.375
TOP = 32767.0
ONE = float(2**30)


def lanes_of(shape):
    return lax.broadcasted_iota(jnp.int32, shape, 1)


def rows_of(shape):
    return lax.broadcasted_iota(jnp.int32, shape, 0)


def total(rows):
    return jnp.sum(rows, axis=0, keepdims=True)


def stats_row(columns, rank, step=None):
    shape = (columns[0].shape[0], LANES)
    first = lanes_of(shape) - rank * rows_of(shape)
    spread = sum(jnp.where(first == k, column, 0.0) for k, column in enumerate(columns))
    if step is not None:
        spread = jnp.where((first >= STEP) & (first < rank), step, spread)
    return total(spread)


def steps_of(stats, rank):
    inner = lax.rem(lanes_of(stats.shape), rank)
    return jnp.where(inner < STEP, shifted(stats, STEP), stats)


def term_unit(panels, rank):
    return panels * rank * COLS_TOP * COUPLE_TOP * TOP / ONE


def stat_column(row, k, nrhs, rank):
    shape = (nrhs, LANES)
    first = lanes_of(shape) - rank * rows_of(shape)
    return jnp.sum(jnp.where(first == k, row, 0.0), axis=1, keepdims=True)


def shifted(value, k):
    return pltpu.roll(value, LANES - k, 1)


def far_sum_of(row, nrhs, rank):
    shape = (nrhs, LANES)
    first = lanes_of(shape) - rank * rows_of(shape)
    own = jnp.where((first >= 0) & (first < rank), row, 0.0)
    return sum((pltpu.roll(own, k * rank, 1) for k in range(1, LANES // rank)), own)


def halves(value):
    high = value.astype(BF16)
    return high, (value - high.astype(F32)).astype(BF16)


def product(left, right_high, right_low, side=0):
    rows = left.shape[0]
    high, low = halves(left)
    dims = (((1,), (side,)), ((), ()))
    both = lax.dot_general(jnp.concatenate([high, low], axis=0), right_high, dims, preferred_element_type=F32)
    return both[:rows] + (both[rows:] + lax.dot_general(high, right_low, dims, preferred_element_type=F32))


def coded(value):
    exponent = jnp.ceil(jnp.log2(jnp.maximum(jnp.abs(value), 1e-30)))
    return (value * jnp.exp2(-exponent) * ONE).astype(jnp.int32), exponent.astype(jnp.int32)


def decoded(mantissa, exponent):
    return mantissa.astype(F32) * (1.0 / ONE) * jnp.exp2(exponent.astype(F32))


def packed(field):
    top = jnp.max(jnp.abs(field), axis=1, keepdims=True)
    step = jnp.maximum(top, 1e-30) * (1.0 / TOP)
    codes = jnp.floor(field * (1.0 / step) + 0.5).astype(jnp.int32)
    width = field.shape[1] // 2
    return (codes[:, :width] << 16) | (codes[:, width:] & 0xFFFF), step


def unpacked(words):
    return jnp.concatenate([words >> 16, (words << 16) >> 16], axis=1).astype(F32)


def fetch(pairs, sems):
    copies = [pltpu.make_async_copy(a, b, sems.at[i]) for i, (a, b) in enumerate(pairs)]
    for copy in copies:
        copy.start()
    return copies


def put_message(field, columns, cols, couple, masks_ref, sent_ref):
    nrhs, rank = field.shape[0], cols[0].shape[0]
    unit = term_unit(field.shape[1], rank)
    proj = product(field, cols[0][...], cols[1][...], 1)
    wide = jnp.concatenate([proj] * CHUNK, axis=1)
    words, step = packed(field)
    width = words.shape[1]
    row = stats_row(columns, rank, step)
    finer = 1.0 / (steps_of(row, rank) * unit)
    for i in range(sent_ref.shape[0]):
        sent_ref[i, :, :width] = words
    stats = [jnp.broadcast_to(a, (CHUNK, LANES)) for a in coded(row)]
    for start in range(0, sent_ref.shape[0], CHUNK):
        mask = masks_ref[pl.ds(start, CHUNK), :]
        spread = jnp.concatenate([mask * wide[r : r + 1] for r in range(nrhs)], axis=0)
        here = pl.ds(start * rank, CHUNK * rank)
        terms = product(spread, couple[0][here, :], couple[1][here, :])
        terms = jnp.concatenate([terms[r * CHUNK : (r + 1) * CHUNK] for r in range(nrhs)], axis=1)
        here = pl.ds(start, CHUNK)
        for k, value in enumerate([(terms * finer).astype(jnp.int32)] + stats + [stats[0]] * (nrhs - 3)):
            sent_ref[here, k, width:] = value


def message_parts(got_ref, rank):
    width = got_ref.shape[2] - LANES
    stats = decoded(got_ref[:, 1, width:], got_ref[:, 2, width:])
    terms = got_ref[:, 0, width:].astype(F32) * (steps_of(stats, rank) * term_unit(2 * width, rank))
    return total(terms), stats


def window_parts(got_ref, rank):
    nrhs, width = got_ref.shape[1], got_ref.shape[2] - LANES
    strips = got_ref.shape[0] // CORES
    shape = (CORES * nrhs, LANES)
    for step in range(3):
        owner = lax.axis_index("strip") + (step - 1)
        inside = (owner >= 0) & (owner < strips)
        owner = CORES * jnp.clip(owner, 0, strips - 1)
        words = jnp.concatenate([got_ref[owner + core, :, :width] for core in range(CORES)], axis=0)
        tails = [got_ref[owner + core, :, width:] for core in range(CORES)]
        rows = [decoded(tail[1:2], tail[2:3]) for tail in tails]
        rows = jnp.where(rows_of(shape) < nrhs, rows[0], rows[1])
        wanted = lanes_of(shape) == rank * lax.rem(rows_of(shape), nrhs) + STEP
        yield inside, unpacked(words), jnp.sum(jnp.where(wanted, rows, 0.0), axis=1, keepdims=True)


def put_blocks(part, first, window):
    part = part.astype(BF16).astype(F32)
    for c in range(part.shape[1] // LANES):
        window[first + c] = part[:, c * LANES : (c + 1) * LANES]


def near_field(window, tiles, list_ref, sums, nrhs):
    for held in sums:
        held[...] = jnp.zeros_like(held)
    n = 0
    for tiles_ref in tiles:
        for first in range(0, tiles_ref.shape[0], 4):
            sources = [window[list_ref[1, n + i]] for i in range(4)]
            blank = jnp.zeros_like(sources[0])
            upper = [sources[0], blank, sources[2], blank]
            lower = [blank, sources[1], blank, sources[3]]
            left = jnp.concatenate([jnp.concatenate(a, axis=0).astype(BF16) for a in (upper, lower)], axis=1)
            four = [tiles_ref[first + i] for i in range(4)]
            right = [jnp.concatenate([four[i], four[i + 2]], axis=1) for i in range(2)]
            both = jnp.dot(left, jnp.concatenate(right, axis=0), preferred_element_type=F32)
            for i, held in enumerate(sums):
                side = i // 2 * LANES
                rows = i * window.shape[1]
                held[list_ref[0, n + i]] += both[rows : rows + window.shape[1], side : side + LANES]
            n += 4
    whole = sum((held[...] for held in sums[1:]), sums[0][...])
    rows = whole.shape[0] // CORES
    return jnp.concatenate([whole[b, :nrhs] + whole[rows + b, nrhs:] for b in range(rows)], axis=1)


def start_kernel(
    loads_hbm, cols_hbm, couple_hbm, ranks_hbm, sent_ref, cols_high, cols_low, couple_high, couple_low, masks_ref,
    loads_ref, done_ref, cols_ref, couple_ref, ranks_ref, sems,
):
    rank = cols_ref.shape[0]
    pairs = ((loads_hbm, loads_ref), (cols_hbm, cols_ref), (couple_hbm, couple_ref), (ranks_hbm, ranks_ref))
    copies = fetch(pairs, sems)
    done_ref[...] = jnp.zeros_like(done_ref)
    copies[0].wait()
    loads = loads_ref[...]
    square = jnp.sum(loads * loads, axis=1, keepdims=True)
    copies[1].wait()
    cols_high[...], cols_low[...] = halves(cols_ref[...])
    copies[2].wait()
    couple_high[...], couple_low[...] = halves(couple_ref[...])
    copies[3].wait()
    shape = (CHUNK, CHUNK * rank)
    owner = lax.div(lanes_of(shape), rank)
    inner = lax.rem(lanes_of(shape), rank)
    for start in range(0, masks_ref.shape[0], CHUNK):
        limit = jnp.zeros((1, CHUNK * rank), jnp.int32)
        for i in range(CHUNK):
            limit = jnp.where(owner[:1] == i, ranks_ref[0, start + i], limit)
        masks_ref[pl.ds(start, CHUNK), :] = jnp.where((owner == rows_of(shape)) & (inner < limit), 1.0, 0.0)
    put_message(loads, [square], (cols_high, cols_low), (couple_high, couple_low), masks_ref, sent_ref)


def copy_tiles(tiles_hbm, first, tiles_ref, sems):
    every = tiles_ref.shape[0] // PIECES
    pairs = [(pl.ds(first + i * every, every), pl.ds(i * every, every)) for i in range(PIECES)]
    return fetch([(tiles_hbm.at[a], tiles_ref.at[b]) for a, b in pairs], sems)


def fetch0_kernel(done_ref, tiles_hbm, rows_hbm, self_hbm, list_hbm, tiles_ref, rows_high, rows_low, self_ref, list_ref,
                  rows_ref, raw_ref, sems, other_sems):
    del done_ref
    pairs = ((list_hbm, raw_ref), (rows_hbm, rows_ref), (self_hbm, self_ref))
    copies = fetch(pairs, other_sems)
    pieces = copy_tiles(tiles_hbm, 0, tiles_ref, sems)
    copies[0].wait()
    rows = self_ref.shape[1] // tiles_ref.shape[1]
    target, source = raw_ref[0:1, :], raw_ref[1:2, :]
    group, block = lax.div(source, rows), lax.rem(source, rows)
    strip, core = lax.div(group, CORES), lax.rem(group, CORES)
    list_ref[...] = jnp.concatenate([core * rows + target, strip * rows + block], axis=0)
    copies[1].wait()
    rows_high[...], rows_low[...] = halves(rows_ref[...])
    copies[2].wait()
    for piece in pieces:
        piece.wait()


def fetch1_kernel(done_ref, tiles_hbm, tiles_ref, sems):
    del done_ref
    for piece in copy_tiles(tiles_hbm, tiles_ref.shape[0], tiles_ref, sems):
        piece.wait()


def image_of(field, far, self_ref, far_rows, near):
    rank = far_rows[0].shape[0]
    return self_ref[...] * field + near + product(far[:, :rank], far_rows[0][...], far_rows[1][...])


def step0_kernel(
    got_ref, loads_ref, cols_high, cols_low, couple_high, couple_low, masks_ref, rows_high, rows_low, self_ref,
    tiles0_ref, tiles1_ref, list_vmem, sent_ref, image_ref, window0_ref, state_ref, list_ref, sems, window, *sums,
):
    rank = rows_high.shape[0]
    nrhs, panels = loads_ref.shape
    span, rows = panels // LANES, CORES * nrhs
    (copy,) = fetch(((list_vmem, list_ref),), sems)
    terms, stats = message_parts(got_ref, rank)
    beta = jnp.sqrt(stat_column(total(stats), 0, nrhs, rank))
    scale = 1.0 / beta
    both = jnp.concatenate([scale] * CORES, axis=0)
    for step, (inside, part, unit) in enumerate(window_parts(got_ref, rank)):
        part = jnp.where(inside, part * (unit * both), 0.0)
        window0_ref[step * rows : (step + 1) * rows, :] = part
        put_blocks(part, step * span, window)
    basis = loads_ref[...] * scale
    far = far_sum_of(terms, nrhs, rank) * scale
    copy.wait()
    near = near_field(window, (tiles0_ref, tiles1_ref), list_ref, sums, nrhs)
    image = image_of(basis, far, self_ref, (rows_high, rows_low), near)
    image_ref[...] = image
    state_ref[...] = jnp.concatenate([far, jnp.broadcast_to(beta, far.shape)], axis=0)
    norm = jnp.sum(basis * basis, axis=1, keepdims=True)
    dot = jnp.sum(basis * image, axis=1, keepdims=True)
    share = jnp.where(norm > 0, dot / jnp.where(norm > 0, norm, 1.0), 0.0)
    rest = image - share * basis
    rest = jnp.sum(rest * rest, axis=1, keepdims=True)
    columns = [norm, dot, share, rest]
    put_message(image, columns, (cols_high, cols_low), (couple_high, couple_low), masks_ref, sent_ref)


def step1_kernel(
    got_ref, loads_ref, image_ref, window0_ref, state_ref, rows_high, rows_low, self_ref, tiles0_ref, tiles1_ref,
    list_vmem, sent_ref, basis_ref, coeff_ref, list_ref, sems, window, *sums,
):
    rank = rows_high.shape[0]
    nrhs, panels = loads_ref.shape
    span, rows = panels // LANES, CORES * nrhs
    (copy,) = fetch(((list_vmem, list_ref),), sems)
    beta = state_ref[nrhs:, :1]
    far0 = state_ref[:nrhs, :]
    terms, stats = message_parts(got_ref, rank)
    summed = total(stats)
    h00 = stat_column(summed, 1, nrhs, rank)
    away = shifted(stats, 2) - shifted(summed, 1)
    rest = total(shifted(stats, 3) + stats * away * away)
    h10 = jnp.sqrt(stat_column(rest, 0, nrhs, rank))
    scale = 1.0 / h10
    both, both_h00 = (jnp.concatenate([a] * CORES, axis=0) for a in (scale, h00))
    for step, (inside, part, unit) in enumerate(window_parts(got_ref, rank)):
        part = (part * unit - both_h00 * window0_ref[step * rows : (step + 1) * rows, :]) * both
        put_blocks(jnp.where(inside, part, 0.0), step * span, window)
    basis0 = loads_ref[...] * (1.0 / beta)
    basis1 = (image_ref[...] - h00 * basis0) * scale
    far = (far_sum_of(terms, nrhs, rank) - h00 * far0) * scale
    copy.wait()
    near = near_field(window, (tiles0_ref, tiles1_ref), list_ref, sums, nrhs)
    image = image_of(basis1, far, self_ref, (rows_high, rows_low), near)
    columns = [jnp.sum(a * image, axis=1, keepdims=True) for a in (basis0, basis1, image)]
    sent_ref[:, 0, :] = jnp.broadcast_to(stats_row(columns, rank), (sent_ref.shape[0], LANES))
    basis_ref[...] = jnp.concatenate([basis0, basis1], axis=0)
    coeff_ref[...] = jnp.concatenate([jnp.broadcast_to(v, (nrhs, LANES)) for v in (beta, h00, h10)], axis=0)


def finish_kernel(rank, got_ref, basis_ref, coeff_ref, out_ref):
    nrhs = out_ref.shape[0]
    row = total(got_ref[:, 0, :])
    h01, h11, gram11 = (stat_column(row, k, nrhs, rank) for k in range(3))
    beta, h00, h10 = (coeff_ref[k * nrhs : (k + 1) * nrhs, :1] for k in range(3))
    gram00 = h00 * h00 + h10 * h10
    gram01 = h00 * h01 + h10 * h11
    lower00 = jnp.sqrt(gram00)
    lower10 = gram01 / lower00
    lower11 = jnp.sqrt(gram11 - lower10 * lower10)
    middle0 = beta * h00 / lower00
    middle1 = (beta * h01 - lower10 * middle0) / lower11
    y1 = middle1 / lower11
    y0 = (middle0 - lower10 * y1) / lower00
    out_ref[...] = y0 * basis_ref[:nrhs, :] + y1 * basis_ref[nrhs:, :]


class Plain(jax.ShapeDtypeStruct):
    pass


def in_vmem_like(array):
    return pltpu.VMEM(array.shape, array.dtype)


def in_vmem(arrays):
    return [pltpu.with_memory_space_constraint(a, pltpu.VMEM) for a in arrays]


def call(kernel, args, outs, scratch=(), held=(), flops=0):
    args = [pltpu.with_memory_space_constraint(a, pltpu.HBM) if i in held else a for i, a in enumerate(args)]
    moved = sum(a.size * a.dtype.itemsize for a in args)
    return pl.pallas_call(
        kernel,
        out_shape=[
            jax.ShapeDtypeStruct(out, F32) if isinstance(out, tuple) else out if isinstance(out, Plain) else in_vmem_like(out)
            for out in outs
        ],
        in_specs=[pl.BlockSpec(memory_space=pl.ANY if i in held else pltpu.VMEM) for i in range(len(args))],
        out_specs=[pl.BlockSpec(memory_space=pltpu.VMEM)] * len(outs),
        scratch_shapes=list(scratch),
        compiler_params=pltpu.CompilerParams(vmem_limit_bytes=24 * 2**20),
        cost_estimate=pl.CostEstimate(flops=flops, bytes_accessed=moved, transcendentals=0),
    )(*args)


def exchanged(sent):
    return lax.all_to_all(sent, GROUP, 0, 0, tiled=True)


def body(loads, self_term, near_tiles, near_list, far_rows, far_cols, coupling, ranks):
    nrhs, panels = loads.shape
    rank = far_cols.shape[0]
    blocks, tile = near_tiles.shape[:2]
    rows = panels // tile
    strips = coupling.shape[0] // CORES
    couple = coupling.reshape(CORES * strips * rank, rank)
    near_list = near_list.T
    ranks = ranks.reshape(1, CORES * strips)
    self_term = self_term.reshape(1, panels)
    groups = CORES * strips
    message = jax.ShapeDtypeStruct((groups, nrhs, panels // 2 + LANES), jnp.int32)
    index = pltpu.SMEM(near_list.shape, jnp.int32)
    scratch = [index, pltpu.SemaphoreType.DMA((1,)), pltpu.VMEM((3 * rows, CORES * nrhs, tile), F32)]
    scratch += [pltpu.VMEM((CORES * rows, CORES * nrhs, tile), F32)] * 4

    def twice(array):
        return [jax.ShapeDtypeStruct(array.shape, BF16)] * 2

    sent, *source_side, loads, done = call(
        start_kernel,
        (loads, far_cols, couple, ranks),
        [message, *twice(far_cols), *twice(couple), jax.ShapeDtypeStruct((groups, CHUNK * rank), F32), loads, (8, LANES)],
        [
            pltpu.VMEM(far_cols.shape, F32), pltpu.VMEM(couple.shape, F32),
            pltpu.SMEM(ranks.shape, jnp.int32), pltpu.SemaphoreType.DMA((4,)),
        ],
        held=range(4),
    )
    part = jax.ShapeDtypeStruct((blocks // 2, tile, tile), BF16)
    tiles0, *target_side, near_list = call(
        fetch0_kernel,
        (done, near_tiles, far_rows, self_term, near_list),
        [part, *twice(far_rows), self_term, near_list],
        [
            pltpu.VMEM(far_rows.shape, F32), pltpu.VMEM(near_list.shape, jnp.int32),
            pltpu.SemaphoreType.DMA((PIECES,)), pltpu.SemaphoreType.DMA((3,)),
        ],
        held=range(1, 5),
    )
    (tiles1,) = call(
        fetch1_kernel, (done, near_tiles), [part], [pltpu.SemaphoreType.DMA((PIECES,))], held=(1,)
    )
    source_side, target_side = in_vmem([loads, *source_side]), in_vmem([*target_side, tiles0, tiles1, near_list])
    loads = source_side[0]
    sent, image, window0, state = call(
        step0_kernel,
        (exchanged(sent), *source_side, *target_side),
        [message, loads.shape, (3 * CORES * nrhs, panels), (CORES * nrhs, LANES)],
        scratch,
    )
    sent, basis, coeff = call(
        step1_kernel,
        (exchanged(sent), loads, image, window0, state, *target_side),
        [(groups, 1, LANES), (2 * nrhs, panels), (3 * nrhs, LANES)],
        scratch,
    )
    return call(functools.partial(finish_kernel, rank), (exchanged(sent), basis, coeff), [loads.shape])[0]


def solution(mesh):
    every = ("case",) + GROUP
    in_specs = (
        P(None, every),
        P(every),
        P(every, None, None),
        P(every, None),
        P(None, every),
        P(None, every),
        P(None, GROUP, None, None),
        P(None, GROUP),
    )
    return jax.shard_map(body, mesh=mesh, in_specs=in_specs, out_specs=P(None, every), check_vma=False)
```

```python
import functools

import jax
import jax.numpy as jnp
from jax import lax
from jax.experimental import pallas as pl
from jax.experimental.pallas import tpu as pltpu
from jax.sharding import PartitionSpec as P

GROUP = ("strip", "clus")
CORES = 2
LANES = 128
CHUNK = 16
PIECES = 4
F32 = jnp.float32
BF16 = jnp.bfloat16

STEP = 8
COLS_TOP = 0.1875
COUPLE_TOP = 0.375
TOP = 32767.0
ONE = float(2**30)


def lanes_of(shape):
    return lax.broadcasted_iota(jnp.int32, shape, 1)


def rows_of(shape):
    return lax.broadcasted_iota(jnp.int32, shape, 0)


def total(rows):
    return jnp.sum(rows, axis=0, keepdims=True)


def stats_row(columns, rank, step=None):
    shape = (columns[0].shape[0], LANES)
    first = lanes_of(shape) - rank * rows_of(shape)
    spread = sum(jnp.where(first == k, column, 0.0) for k, column in enumerate(columns))
    if step is not None:
        spread = jnp.where((first >= STEP) & (first < rank), step, spread)
    return total(spread)


def steps_of(stats, rank):
    inner = lax.rem(lanes_of(stats.shape), rank)
    return jnp.where(inner < STEP, shifted(stats, STEP), stats)


def term_unit(panels, rank):
    return panels * rank * COLS_TOP * COUPLE_TOP * TOP / ONE


def stat_column(row, k, nrhs, rank):
    shape = (nrhs, LANES)
    first = lanes_of(shape) - rank * rows_of(shape)
    return jnp.sum(jnp.where(first == k, row, 0.0), axis=1, keepdims=True)


def shifted(value, k):
    return pltpu.roll(value, LANES - k, 1)


def far_sum_of(row, nrhs, rank):
    shape = (nrhs, LANES)
    first = lanes_of(shape) - rank * rows_of(shape)
    own = jnp.where((first >= 0) & (first < rank), row, 0.0)
    return sum((pltpu.roll(own, k * rank, 1) for k in range(1, LANES // rank)), own)


def halves(value):
    high = value.astype(BF16)
    return high, (value - high.astype(F32)).astype(BF16)


def product(left, right_high, right_low, side=0):
    rows = left.shape[0]
    high, low = halves(left)
    dims = (((1,), (side,)), ((), ()))
    both = lax.dot_general(jnp.concatenate([high, low], axis=0), right_high, dims, preferred_element_type=F32)
    return both[:rows] + (both[rows:] + lax.dot_general(high, right_low, dims, preferred_element_type=F32))


def coded(value):
    exponent = jnp.ceil(jnp.log2(jnp.maximum(jnp.abs(value), 1e-30)))
    return (value * jnp.exp2(-exponent) * ONE).astype(jnp.int32), exponent.astype(jnp.int32)


def decoded(mantissa, exponent):
    return mantissa.astype(F32) * (1.0 / ONE) * jnp.exp2(exponent.astype(F32))


def packed(field):
    top = jnp.max(jnp.abs(field), axis=1, keepdims=True)
    step = jnp.maximum(top, 1e-30) * (1.0 / TOP)
    codes = jnp.floor(field * (1.0 / step) + 0.5).astype(jnp.int32)
    width = field.shape[1] // 2
    return (codes[:, :width] << 16) | (codes[:, width:] & 0xFFFF), step


def unpacked(words):
    return jnp.concatenate([words >> 16, (words << 16) >> 16], axis=1).astype(F32)


def fetch(pairs, sems):
    copies = [pltpu.make_async_copy(a, b, sems.at[i]) for i, (a, b) in enumerate(pairs)]
    for copy in copies:
        copy.start()
    return copies


def put_message(field, columns, cols, couple, masks_ref, sent_ref, field_is_put=lambda: None):
    nrhs, rank = field.shape[0], cols[0].shape[0]
    unit = term_unit(field.shape[1], rank)
    words, step = packed(field)
    width = words.shape[1]
    for i in range(sent_ref.shape[0]):
        sent_ref[i, :, :width] = words
    field_is_put()
    proj = product(field, cols[0][...], cols[1][...], 1)
    wide = jnp.concatenate([proj] * CHUNK, axis=1)
    row = stats_row(columns, rank, step)
    finer = 1.0 / (steps_of(row, rank) * unit)
    stats = [jnp.broadcast_to(a, (CHUNK, LANES)) for a in coded(row)]
    for start in range(0, sent_ref.shape[0], CHUNK):
        mask = masks_ref[pl.ds(start, CHUNK), :]
        spread = jnp.concatenate([mask * wide[r : r + 1] for r in range(nrhs)], axis=0)
        here = pl.ds(start * rank, CHUNK * rank)
        terms = product(spread, couple[0][here, :], couple[1][here, :])
        terms = jnp.concatenate([terms[r * CHUNK : (r + 1) * CHUNK] for r in range(nrhs)], axis=1)
        here = pl.ds(start, CHUNK)
        for k, value in enumerate([(terms * finer).astype(jnp.int32)] + stats + [stats[0]] * (nrhs - 3)):
            sent_ref[here, k, width:] = value


def message_parts(got_ref, rank):
    width = got_ref.shape[2] - LANES
    stats = decoded(got_ref[:, 1, width:], got_ref[:, 2, width:])
    terms = got_ref[:, 0, width:].astype(F32) * (steps_of(stats, rank) * term_unit(2 * width, rank))
    return total(terms), stats


def window_parts(got_ref, rank):
    nrhs, width = got_ref.shape[1], got_ref.shape[2] - LANES
    strips = got_ref.shape[0] // CORES
    shape = (CORES * nrhs, LANES)
    for step in range(3):
        owner = lax.axis_index("strip") + (step - 1)
        inside = (owner >= 0) & (owner < strips)
        owner = CORES * jnp.clip(owner, 0, strips - 1)
        words = jnp.concatenate([got_ref[owner + core, :, :width] for core in range(CORES)], axis=0)
        tails = [got_ref[owner + core, :, width:] for core in range(CORES)]
        rows = [decoded(tail[1:2], tail[2:3]) for tail in tails]
        rows = jnp.where(rows_of(shape) < nrhs, rows[0], rows[1])
        wanted = lanes_of(shape) == rank * lax.rem(rows_of(shape), nrhs) + STEP
        yield inside, unpacked(words), jnp.sum(jnp.where(wanted, rows, 0.0), axis=1, keepdims=True)


def put_blocks(part, first, window):
    part = part.astype(BF16).astype(F32)
    for c in range(part.shape[1] // LANES):
        window[first + c] = part[:, c * LANES : (c + 1) * LANES]


def near_field(window, tiles, list_ref, sums, nrhs):
    for held in sums:
        held[...] = jnp.zeros_like(held)
    n = 0
    for tiles_ref in tiles:
        for first in range(0, tiles_ref.shape[0], 4):
            sources = [window[list_ref[1, n + i]] for i in range(4)]
            blank = jnp.zeros_like(sources[0])
            upper = [sources[0], blank, sources[2], blank]
            lower = [blank, sources[1], blank, sources[3]]
            left = jnp.concatenate([jnp.concatenate(a, axis=0).astype(BF16) for a in (upper, lower)], axis=1)
            four = [tiles_ref[first + i] for i in range(4)]
            right = [jnp.concatenate([four[i], four[i + 2]], axis=1) for i in range(2)]
            both = jnp.dot(left, jnp.concatenate(right, axis=0), preferred_element_type=F32)
            for i, held in enumerate(sums):
                side = i // 2 * LANES
                rows = i * window.shape[1]
                held[list_ref[0, n + i]] += both[rows : rows + window.shape[1], side : side + LANES]
            n += 4
    whole = sum((held[...] for held in sums[1:]), sums[0][...])
    rows = whole.shape[0] // CORES
    return jnp.concatenate([whole[b, :nrhs] + whole[rows + b, nrhs:] for b in range(rows)], axis=1)


def start_kernel(
    loads_hbm, cols_hbm, couple_hbm, ranks_hbm, sent_any, cols_high, cols_low, couple_high, couple_low, masks_ref,
    loads_ref, done_ref, cols_ref, couple_ref, ranks_ref, sent_ref, sems, sent_sems,
):
    rank, panels = cols_ref.shape
    pairs = ((loads_hbm, loads_ref), (cols_hbm, cols_ref), (couple_hbm, couple_ref), (ranks_hbm, ranks_ref))
    copies = fetch(pairs, sems)
    done_ref[...] = jnp.zeros_like(done_ref)
    copies[0].wait()
    loads = loads_ref[...]
    square = jnp.sum(loads * loads, axis=1, keepdims=True)
    width = panels // 2
    sides = [pl.ds(0, width), pl.ds(width, LANES)]
    out = [
        pltpu.make_async_copy(sent_ref.at[:, :, side], sent_any.at[:, :, side], sent_sems.at[i])
        for i, side in enumerate(sides)
    ]

    def field_is_put():
        out[0].start()
        copies[1].wait()
        cols_high[...], cols_low[...] = halves(cols_ref[...])
        copies[2].wait()
        couple_high[...], couple_low[...] = halves(couple_ref[...])
        copies[3].wait()
        shape = (CHUNK, CHUNK * rank)
        owner = lax.div(lanes_of(shape), rank)
        inner = lax.rem(lanes_of(shape), rank)
        for start in range(0, masks_ref.shape[0], CHUNK):
            limit = jnp.zeros((1, CHUNK * rank), jnp.int32)
            for i in range(CHUNK):
                limit = jnp.where(owner[:1] == i, ranks_ref[0, start + i], limit)
            masks_ref[pl.ds(start, CHUNK), :] = jnp.where((owner == rows_of(shape)) & (inner < limit), 1.0, 0.0)

    cols, couple = (cols_high, cols_low), (couple_high, couple_low)
    put_message(loads, [square], cols, couple, masks_ref, sent_ref, field_is_put)
    out[1].start()
    for copy in out:
        copy.wait()


def copy_tiles(tiles_hbm, first, tiles_ref, sems):
    every = tiles_ref.shape[0] // PIECES
    pairs = [(pl.ds(first + i * every, every), pl.ds(i * every, every)) for i in range(PIECES)]
    return fetch([(tiles_hbm.at[a], tiles_ref.at[b]) for a, b in pairs], sems)


def fetch0_kernel(done_ref, tiles_hbm, rows_hbm, self_hbm, list_hbm, tiles_ref, rows_high, rows_low, self_ref, list_ref,
                  rows_ref, raw_ref, sems, other_sems):
    del done_ref
    pairs = ((list_hbm, raw_ref), (rows_hbm, rows_ref), (self_hbm, self_ref))
    copies = fetch(pairs, other_sems)
    pieces = copy_tiles(tiles_hbm, 0, tiles_ref, sems)
    copies[0].wait()
    rows = self_ref.shape[1] // tiles_ref.shape[1]
    target, source = raw_ref[0:1, :], raw_ref[1:2, :]
    group, block = lax.div(source, rows), lax.rem(source, rows)
    strip, core = lax.div(group, CORES), lax.rem(group, CORES)
    list_ref[...] = jnp.concatenate([core * rows + target, strip * rows + block], axis=0)
    copies[1].wait()
    rows_high[...], rows_low[...] = halves(rows_ref[...])
    copies[2].wait()
    for piece in pieces:
        piece.wait()


def fetch1_kernel(done_ref, tiles_hbm, tiles_ref, sems):
    del done_ref
    for piece in copy_tiles(tiles_hbm, tiles_ref.shape[0], tiles_ref, sems):
        piece.wait()


def image_of(field, far, self_ref, far_rows, near):
    rank = far_rows[0].shape[0]
    return self_ref[...] * field + near + product(far[:, :rank], far_rows[0][...], far_rows[1][...])


def step0_kernel(
    got_ref, loads_ref, cols_high, cols_low, couple_high, couple_low, masks_ref, rows_high, rows_low, self_ref,
    tiles0_ref, tiles1_ref, list_vmem, sent_ref, image_ref, window0_ref, state_ref, list_ref, sems, window, *sums,
):
    rank = rows_high.shape[0]
    nrhs, panels = loads_ref.shape
    span, rows = panels // LANES, CORES * nrhs
    (copy,) = fetch(((list_vmem, list_ref),), sems)
    terms, stats = message_parts(got_ref, rank)
    beta = jnp.sqrt(stat_column(total(stats), 0, nrhs, rank))
    scale = 1.0 / beta
    both = jnp.concatenate([scale] * CORES, axis=0)
    for step, (inside, part, unit) in enumerate(window_parts(got_ref, rank)):
        part = jnp.where(inside, part * (unit * both), 0.0)
        window0_ref[step * rows : (step + 1) * rows, :] = part
        put_blocks(part, step * span, window)
    basis = loads_ref[...] * scale
    far = far_sum_of(terms, nrhs, rank) * scale
    copy.wait()
    near = near_field(window, (tiles0_ref, tiles1_ref), list_ref, sums, nrhs)
    image = image_of(basis, far, self_ref, (rows_high, rows_low), near)
    image_ref[...] = image
    state_ref[...] = jnp.concatenate([far, jnp.broadcast_to(beta, far.shape)], axis=0)
    norm = jnp.sum(basis * basis, axis=1, keepdims=True)
    dot = jnp.sum(basis * image, axis=1, keepdims=True)
    share = jnp.where(norm > 0, dot / jnp.where(norm > 0, norm, 1.0), 0.0)
    rest = image - share * basis
    rest = jnp.sum(rest * rest, axis=1, keepdims=True)
    columns = [norm, dot, share, rest]
    put_message(image, columns, (cols_high, cols_low), (couple_high, couple_low), masks_ref, sent_ref)


def step1_kernel(
    got_ref, loads_ref, image_ref, window0_ref, state_ref, rows_high, rows_low, self_ref, tiles0_ref, tiles1_ref,
    list_vmem, sent_ref, basis_ref, coeff_ref, list_ref, sems, window, *sums,
):
    rank = rows_high.shape[0]
    nrhs, panels = loads_ref.shape
    span, rows = panels // LANES, CORES * nrhs
    (copy,) = fetch(((list_vmem, list_ref),), sems)
    beta = state_ref[nrhs:, :1]
    far0 = state_ref[:nrhs, :]
    terms, stats = message_parts(got_ref, rank)
    summed = total(stats)
    h00 = stat_column(summed, 1, nrhs, rank)
    away = shifted(stats, 2) - shifted(summed, 1)
    rest = total(shifted(stats, 3) + stats * away * away)
    h10 = jnp.sqrt(stat_column(rest, 0, nrhs, rank))
    scale = 1.0 / h10
    both, both_h00 = (jnp.concatenate([a] * CORES, axis=0) for a in (scale, h00))
    for step, (inside, part, unit) in enumerate(window_parts(got_ref, rank)):
        part = (part * unit - both_h00 * window0_ref[step * rows : (step + 1) * rows, :]) * both
        put_blocks(jnp.where(inside, part, 0.0), step * span, window)
    basis0 = loads_ref[...] * (1.0 / beta)
    basis1 = (image_ref[...] - h00 * basis0) * scale
    far = (far_sum_of(terms, nrhs, rank) - h00 * far0) * scale
    copy.wait()
    near = near_field(window, (tiles0_ref, tiles1_ref), list_ref, sums, nrhs)
    image = image_of(basis1, far, self_ref, (rows_high, rows_low), near)
    columns = [jnp.sum(a * image, axis=1, keepdims=True) for a in (basis0, basis1, image)]
    sent_ref[:, 0, :] = jnp.broadcast_to(stats_row(columns, rank), (sent_ref.shape[0], LANES))
    basis_ref[...] = jnp.concatenate([basis0, basis1], axis=0)
    coeff_ref[...] = jnp.concatenate([jnp.broadcast_to(v, (nrhs, LANES)) for v in (beta, h00, h10)], axis=0)


def finish_kernel(rank, got_ref, basis_ref, coeff_ref, out_ref):
    nrhs = out_ref.shape[0]
    row = total(got_ref[:, 0, :])
    h01, h11, gram11 = (stat_column(row, k, nrhs, rank) for k in range(3))
    beta, h00, h10 = (coeff_ref[k * nrhs : (k + 1) * nrhs, :1] for k in range(3))
    gram00 = h00 * h00 + h10 * h10
    gram01 = h00 * h01 + h10 * h11
    lower00 = jnp.sqrt(gram00)
    lower10 = gram01 / lower00
    lower11 = jnp.sqrt(gram11 - lower10 * lower10)
    middle0 = beta * h00 / lower00
    middle1 = (beta * h01 - lower10 * middle0) / lower11
    y1 = middle1 / lower11
    y0 = (middle0 - lower10 * y1) / lower00
    out_ref[...] = y0 * basis_ref[:nrhs, :] + y1 * basis_ref[nrhs:, :]


class Plain(jax.ShapeDtypeStruct):
    pass


def in_vmem_like(array):
    return pltpu.VMEM(array.shape, array.dtype)


def in_vmem(arrays):
    return [pltpu.with_memory_space_constraint(a, pltpu.VMEM) for a in arrays]


def call(kernel, args, outs, scratch=(), held=(), placed=()):
    args = [pltpu.with_memory_space_constraint(a, pltpu.HBM) if i in held else a for i, a in enumerate(args)]
    moved = sum(a.size * a.dtype.itemsize for a in args)
    return pl.pallas_call(
        kernel,
        out_shape=[
            jax.ShapeDtypeStruct(out, F32) if isinstance(out, tuple) else out if isinstance(out, Plain) else in_vmem_like(out)
            for out in outs
        ],
        in_specs=[pl.BlockSpec(memory_space=pl.ANY if i in held else pltpu.VMEM) for i in range(len(args))],
        out_specs=[pl.BlockSpec(memory_space=pl.ANY if i in placed else pltpu.VMEM) for i in range(len(outs))],
        scratch_shapes=list(scratch),
        compiler_params=pltpu.CompilerParams(vmem_limit_bytes=24 * 2**20),
        cost_estimate=pl.CostEstimate(flops=0, bytes_accessed=moved, transcendentals=0),
    )(*args)


def exchanged(sent):
    return lax.all_to_all(sent, GROUP, 0, 0, tiled=True)


def body(loads, self_term, near_tiles, near_list, far_rows, far_cols, coupling, ranks):
    nrhs, panels = loads.shape
    rank = far_cols.shape[0]
    blocks, tile = near_tiles.shape[:2]
    rows = panels // tile
    strips = coupling.shape[0] // CORES
    couple = coupling.reshape(CORES * strips * rank, rank)
    near_list = near_list.T
    ranks = ranks.reshape(1, CORES * strips)
    self_term = self_term.reshape(1, panels)
    groups = CORES * strips
    message = Plain((groups, nrhs, panels // 2 + LANES), jnp.int32)
    index = pltpu.SMEM(near_list.shape, jnp.int32)
    scratch = [index, pltpu.SemaphoreType.DMA((1,)), pltpu.VMEM((3 * rows, CORES * nrhs, tile), F32)]
    scratch += [pltpu.VMEM((CORES * rows, CORES * nrhs, tile), F32)] * 4

    def twice(array):
        return [jax.ShapeDtypeStruct(array.shape, BF16)] * 2

    sent, *source_side, loads, done = call(
        start_kernel,
        (loads, far_cols, couple, ranks),
        [message, *twice(far_cols), *twice(couple), jax.ShapeDtypeStruct((groups, CHUNK * rank), F32), loads, (8, LANES)],
        [
            pltpu.VMEM(far_cols.shape, F32), pltpu.VMEM(couple.shape, F32), pltpu.SMEM(ranks.shape, jnp.int32),
            pltpu.VMEM(message.shape, jnp.int32), pltpu.SemaphoreType.DMA((4,)), pltpu.SemaphoreType.DMA((2,)),
        ],
        held=range(4),
        placed=(0,),
    )
    part = jax.ShapeDtypeStruct((blocks // 2, tile, tile), BF16)
    tiles0, *target_side, near_list = call(
        fetch0_kernel,
        (done, near_tiles, far_rows, self_term, near_list),
        [part, *twice(far_rows), self_term, near_list],
        [
            pltpu.VMEM(far_rows.shape, F32), pltpu.VMEM(near_list.shape, jnp.int32),
            pltpu.SemaphoreType.DMA((PIECES,)), pltpu.SemaphoreType.DMA((3,)),
        ],
        held=range(1, 5),
    )
    (tiles1,) = call(
        fetch1_kernel, (done, near_tiles), [part], [pltpu.SemaphoreType.DMA((PIECES,))], held=(1,)
    )
    source_side, target_side = in_vmem([loads, *source_side]), in_vmem([*target_side, tiles0, tiles1, near_list])
    loads = source_side[0]
    sent, image, window0, state = call(
        step0_kernel,
        (exchanged(sent), *source_side, *target_side),
        [message, loads.shape, (3 * CORES * nrhs, panels), (CORES * nrhs, LANES)],
        scratch,
    )
    sent, basis, coeff = call(
        step1_kernel,
        (exchanged(sent), loads, image, window0, state, *target_side),
        [(groups, 1, LANES), (2 * nrhs, panels), (3 * nrhs, LANES)],
        scratch,
    )
    return call(functools.partial(finish_kernel, rank), (exchanged(sent), basis, coeff), [loads.shape])[0]


def solution(mesh):
    every = ("case",) + GROUP
    in_specs = (
        P(None, every),
        P(every),
        P(every, None, None),
        P(every, None),
        P(None, every),
        P(None, every),
        P(None, GROUP, None, None),
        P(None, GROUP),
    )
    return jax.shard_map(body, mesh=mesh, in_specs=in_specs, out_specs=P(None, every), check_vma=False)
```

```python
import functools

import jax
import jax.numpy as jnp
from jax import lax
from jax.experimental import pallas as pl
from jax.experimental.pallas import tpu as pltpu
from jax.sharding import PartitionSpec as P

GROUP = ("strip", "clus")
CORES = 2
LANES = 128
CHUNK = 16
PIECES = 10
F32 = jnp.float32
BF16 = jnp.bfloat16

STEP = 8
COLS_TOP = 0.1875
COUPLE_TOP = 0.375
TOP = 32767.0
ONE = float(2**30)


def lanes_of(shape):
    return lax.broadcasted_iota(jnp.int32, shape, 1)


def rows_of(shape):
    return lax.broadcasted_iota(jnp.int32, shape, 0)


def total(rows):
    return jnp.sum(rows, axis=0, keepdims=True)


def stats_row(columns, rank, step=None):
    shape = (columns[0].shape[0], LANES)
    first = lanes_of(shape) - rank * rows_of(shape)
    spread = sum(jnp.where(first == k, column, 0.0) for k, column in enumerate(columns))
    if step is not None:
        spread = jnp.where((first >= STEP) & (first < rank), step, spread)
    return total(spread)


def steps_of(stats, rank):
    inner = lax.rem(lanes_of(stats.shape), rank)
    return jnp.where(inner < STEP, shifted(stats, STEP), stats)


def term_unit(panels, rank):
    return panels * rank * COLS_TOP * COUPLE_TOP * TOP / ONE


def stat_column(row, k, nrhs, rank):
    shape = (nrhs, LANES)
    first = lanes_of(shape) - rank * rows_of(shape)
    return jnp.sum(jnp.where(first == k, row, 0.0), axis=1, keepdims=True)


def shifted(value, k):
    return pltpu.roll(value, LANES - k, 1)


def far_sum_of(row, nrhs, rank):
    shape = (nrhs, LANES)
    first = lanes_of(shape) - rank * rows_of(shape)
    own = jnp.where((first >= 0) & (first < rank), row, 0.0)
    return sum((pltpu.roll(own, k * rank, 1) for k in range(1, LANES // rank)), own)


def halves(value):
    high = value.astype(BF16)
    return high, (value - high.astype(F32)).astype(BF16)


def product(left, right_high, right_low, side=0):
    rows = left.shape[0]
    high, low = halves(left)
    dims = (((1,), (side,)), ((), ()))
    both = lax.dot_general(jnp.concatenate([high, low], axis=0), right_high, dims, preferred_element_type=F32)
    return both[:rows] + (both[rows:] + lax.dot_general(high, right_low, dims, preferred_element_type=F32))


def coded(value):
    exponent = jnp.ceil(jnp.log2(jnp.maximum(jnp.abs(value), 1e-30)))
    return (value * jnp.exp2(-exponent) * ONE).astype(jnp.int32), exponent.astype(jnp.int32)


def decoded(mantissa, exponent):
    return mantissa.astype(F32) * (1.0 / ONE) * jnp.exp2(exponent.astype(F32))


def packed(field):
    top = jnp.max(jnp.abs(field), axis=1, keepdims=True)
    step = jnp.maximum(top, 1e-30) * (1.0 / TOP)
    codes = jnp.floor(field * (1.0 / step) + 0.5).astype(jnp.int32)
    width = field.shape[1] // 2
    return (codes[:, :width] << 16) | (codes[:, width:] & 0xFFFF), step


def unpacked(words):
    return jnp.concatenate([words >> 16, (words << 16) >> 16], axis=1).astype(F32)


def fetch(pairs, sems):
    copies = [pltpu.make_async_copy(a, b, sems.at[i]) for i, (a, b) in enumerate(pairs)]
    for copy in copies:
        copy.start()
    return copies


def put_message(field, columns, cols, couple, masks_ref, sent_ref):
    nrhs, rank = field.shape[0], cols[0].shape[0]
    unit = term_unit(field.shape[1], rank)
    proj = product(field, cols[0][...], cols[1][...], 1)
    wide = jnp.concatenate([proj] * CHUNK, axis=1)
    words, step = packed(field)
    width = words.shape[1]
    row = stats_row(columns, rank, step)
    finer = 1.0 / (steps_of(row, rank) * unit)
    for i in range(sent_ref.shape[0]):
        sent_ref[i, :, :width] = words
    stats = [jnp.broadcast_to(a, (CHUNK, LANES)) for a in coded(row)]
    for start in range(0, sent_ref.shape[0], CHUNK):
        mask = masks_ref[pl.ds(start, CHUNK), :]
        spread = jnp.concatenate([mask * wide[r : r + 1] for r in range(nrhs)], axis=0)
        here = pl.ds(start * rank, CHUNK * rank)
        terms = product(spread, couple[0][here, :], couple[1][here, :])
        terms = jnp.concatenate([terms[r * CHUNK : (r + 1) * CHUNK] for r in range(nrhs)], axis=1)
        here = pl.ds(start, CHUNK)
        for k, value in enumerate([(terms * finer).astype(jnp.int32)] + stats + [stats[0]] * (nrhs - 3)):
            sent_ref[here, k, width:] = value


def message_parts(got_ref, rank):
    width = got_ref.shape[2] - LANES
    stats = decoded(got_ref[:, 1, width:], got_ref[:, 2, width:])
    terms = got_ref[:, 0, width:].astype(F32) * (steps_of(stats, rank) * term_unit(2 * width, rank))
    return total(terms), stats


def window_parts(got_ref, rank):
    nrhs, width = got_ref.shape[1], got_ref.shape[2] - LANES
    strips = got_ref.shape[0] // CORES
    shape = (CORES * nrhs, LANES)
    for step in range(3):
        owner = lax.axis_index("strip") + (step - 1)
        inside = (owner >= 0) & (owner < strips)
        owner = CORES * jnp.clip(owner, 0, strips - 1)
        words = jnp.concatenate([got_ref[owner + core, :, :width] for core in range(CORES)], axis=0)
        tails = [got_ref[owner + core, :, width:] for core in range(CORES)]
        rows = [decoded(tail[1:2], tail[2:3]) for tail in tails]
        rows = jnp.where(rows_of(shape) < nrhs, rows[0], rows[1])
        wanted = lanes_of(shape) == rank * lax.rem(rows_of(shape), nrhs) + STEP
        yield inside, unpacked(words), jnp.sum(jnp.where(wanted, rows, 0.0), axis=1, keepdims=True)


def put_blocks(part, first, window):
    part = part.astype(BF16).astype(F32)
    for c in range(part.shape[1] // LANES):
        window[first + c] = part[:, c * LANES : (c + 1) * LANES]


def near_field(window, tiles, list_ref, sums, nrhs):
    for held in sums:
        held[...] = jnp.zeros_like(held)
    n = 0
    for tiles_ref in tiles:
        for first in range(0, tiles_ref.shape[0], 4):
            sources = [window[list_ref[1, n + i]] for i in range(4)]
            blank = jnp.zeros_like(sources[0])
            upper = [sources[0], blank, sources[2], blank]
            lower = [blank, sources[1], blank, sources[3]]
            left = jnp.concatenate([jnp.concatenate(a, axis=0).astype(BF16) for a in (upper, lower)], axis=1)
            four = [tiles_ref[first + i] for i in range(4)]
            right = [jnp.concatenate([four[i], four[i + 2]], axis=1) for i in range(2)]
            both = jnp.dot(left, jnp.concatenate(right, axis=0), preferred_element_type=F32)
            for i, held in enumerate(sums):
                side = i // 2 * LANES
                rows = i * window.shape[1]
                held[list_ref[0, n + i]] += both[rows : rows + window.shape[1], side : side + LANES]
            n += 4
    whole = sum((held[...] for held in sums[1:]), sums[0][...])
    rows = whole.shape[0] // CORES
    return jnp.concatenate([whole[b, :nrhs] + whole[rows + b, nrhs:] for b in range(rows)], axis=1)


def start_kernel(
    loads_hbm, cols_hbm, couple_hbm, ranks_hbm, list_hbm, rows_hbm, self_hbm, tiles_hbm, sent_ref, cols_high, cols_low, couple_high,
    couple_low, masks_ref, rows_high, rows_low, list_ref, loads_ref, self_ref, tiles_ref, cols_ref, couple_ref, ranks_ref, raw_ref,
    rows_ref, sems,
):
    rank, panels = cols_ref.shape
    pairs = (
        (loads_hbm, loads_ref), (cols_hbm, cols_ref), (couple_hbm, couple_ref), (ranks_hbm, ranks_ref),
        (list_hbm, raw_ref), (rows_hbm, rows_ref), (self_hbm, self_ref),
    )
    every = tiles_ref.shape[0] // PIECES
    pieces = [pl.ds(i * every, every) for i in range(PIECES)]
    copies = fetch(pairs + tuple((tiles_hbm.at[p], tiles_ref.at[p]) for p in pieces), sems)
    copies[0].wait()
    loads = loads_ref[...]
    square = jnp.sum(loads * loads, axis=1, keepdims=True)
    copies[1].wait()
    cols_high[...], cols_low[...] = halves(cols_ref[...])
    copies[2].wait()
    couple_high[...], couple_low[...] = halves(couple_ref[...])
    copies[3].wait()
    shape = (CHUNK, CHUNK * rank)
    owner = lax.div(lanes_of(shape), rank)
    inner = lax.rem(lanes_of(shape), rank)
    for start in range(0, masks_ref.shape[0], CHUNK):
        limit = jnp.zeros((1, CHUNK * rank), jnp.int32)
        for i in range(CHUNK):
            limit = jnp.where(owner[:1] == i, ranks_ref[0, start + i], limit)
        masks_ref[pl.ds(start, CHUNK), :] = jnp.where((owner == rows_of(shape)) & (inner < limit), 1.0, 0.0)
    copies[4].wait()
    count = panels // LANES
    target, source = raw_ref[0:1, :], raw_ref[1:2, :]
    group, block = lax.div(source, count), lax.rem(source, count)
    strip, core = lax.div(group, CORES), lax.rem(group, CORES)
    list_ref[...] = jnp.concatenate([core * count + target, strip * count + block], axis=0)
    copies[5].wait()
    rows_high[...], rows_low[...] = halves(rows_ref[...])
    put_message(loads, [square], (cols_high, cols_low), (couple_high, couple_low), masks_ref, sent_ref)
    for copy in copies[6:]:
        copy.wait()


def image_of(field, far, self_ref, far_rows, near):
    rank = far_rows[0].shape[0]
    return self_ref[...] * field + near + product(far[:, :rank], far_rows[0][...], far_rows[1][...])


def step0_kernel(
    got_ref, loads_ref, cols_high, cols_low, couple_high, couple_low, masks_ref, rows_high, rows_low, self_ref,
    tiles_ref, list_vmem, sent_ref, image_ref, window0_ref, state_ref, list_ref, sems, window, *sums,
):
    rank = rows_high.shape[0]
    nrhs, panels = loads_ref.shape
    span, rows = panels // LANES, CORES * nrhs
    (copy,) = fetch(((list_vmem, list_ref),), sems)
    terms, stats = message_parts(got_ref, rank)
    beta = jnp.sqrt(stat_column(total(stats), 0, nrhs, rank))
    scale = 1.0 / beta
    both = jnp.concatenate([scale] * CORES, axis=0)
    for step, (inside, part, unit) in enumerate(window_parts(got_ref, rank)):
        part = jnp.where(inside, part * (unit * both), 0.0)
        window0_ref[step * rows : (step + 1) * rows, :] = part
        put_blocks(part, step * span, window)
    basis = loads_ref[...] * scale
    far = far_sum_of(terms, nrhs, rank) * scale
    copy.wait()
    near = near_field(window, (tiles_ref,), list_ref, sums, nrhs)
    image = image_of(basis, far, self_ref, (rows_high, rows_low), near)
    image_ref[...] = image
    state_ref[...] = jnp.concatenate([far, jnp.broadcast_to(beta, far.shape)], axis=0)
    norm = jnp.sum(basis * basis, axis=1, keepdims=True)
    dot = jnp.sum(basis * image, axis=1, keepdims=True)
    share = jnp.where(norm > 0, dot / jnp.where(norm > 0, norm, 1.0), 0.0)
    rest = image - share * basis
    rest = jnp.sum(rest * rest, axis=1, keepdims=True)
    columns = [norm, dot, share, rest]
    put_message(image, columns, (cols_high, cols_low), (couple_high, couple_low), masks_ref, sent_ref)


def step1_kernel(
    got_ref, loads_ref, image_ref, window0_ref, state_ref, rows_high, rows_low, self_ref, tiles_ref,
    list_vmem, sent_ref, basis_ref, coeff_ref, list_ref, sems, window, *sums,
):
    rank = rows_high.shape[0]
    nrhs, panels = loads_ref.shape
    span, rows = panels // LANES, CORES * nrhs
    (copy,) = fetch(((list_vmem, list_ref),), sems)
    beta = state_ref[nrhs:, :1]
    far0 = state_ref[:nrhs, :]
    terms, stats = message_parts(got_ref, rank)
    summed = total(stats)
    h00 = stat_column(summed, 1, nrhs, rank)
    away = shifted(stats, 2) - shifted(summed, 1)
    rest = total(shifted(stats, 3) + stats * away * away)
    h10 = jnp.sqrt(stat_column(rest, 0, nrhs, rank))
    scale = 1.0 / h10
    both, both_h00 = (jnp.concatenate([a] * CORES, axis=0) for a in (scale, h00))
    for step, (inside, part, unit) in enumerate(window_parts(got_ref, rank)):
        part = (part * unit - both_h00 * window0_ref[step * rows : (step + 1) * rows, :]) * both
        put_blocks(jnp.where(inside, part, 0.0), step * span, window)
    basis0 = loads_ref[...] * (1.0 / beta)
    basis1 = (image_ref[...] - h00 * basis0) * scale
    far = (far_sum_of(terms, nrhs, rank) - h00 * far0) * scale
    copy.wait()
    near = near_field(window, (tiles_ref,), list_ref, sums, nrhs)
    image = image_of(basis1, far, self_ref, (rows_high, rows_low), near)
    columns = [jnp.sum(a * image, axis=1, keepdims=True) for a in (basis0, basis1, image)]
    sent_ref[:, 0, :] = jnp.broadcast_to(stats_row(columns, rank), (sent_ref.shape[0], LANES))
    basis_ref[...] = jnp.concatenate([basis0, basis1], axis=0)
    coeff_ref[...] = jnp.concatenate([jnp.broadcast_to(v, (nrhs, LANES)) for v in (beta, h00, h10)], axis=0)


def finish_kernel(rank, got_ref, basis_ref, coeff_ref, out_ref):
    nrhs = out_ref.shape[0]
    row = total(got_ref[:, 0, :])
    h01, h11, gram11 = (stat_column(row, k, nrhs, rank) for k in range(3))
    beta, h00, h10 = (coeff_ref[k * nrhs : (k + 1) * nrhs, :1] for k in range(3))
    gram00 = h00 * h00 + h10 * h10
    gram01 = h00 * h01 + h10 * h11
    lower00 = jnp.sqrt(gram00)
    lower10 = gram01 / lower00
    lower11 = jnp.sqrt(gram11 - lower10 * lower10)
    middle0 = beta * h00 / lower00
    middle1 = (beta * h01 - lower10 * middle0) / lower11
    y1 = middle1 / lower11
    y0 = (middle0 - lower10 * y1) / lower00
    out_ref[...] = y0 * basis_ref[:nrhs, :] + y1 * basis_ref[nrhs:, :]


class Plain(jax.ShapeDtypeStruct):
    pass


def in_vmem_like(array):
    return pltpu.VMEM(array.shape, array.dtype)


def in_vmem(arrays):
    return [pltpu.with_memory_space_constraint(a, pltpu.VMEM) for a in arrays]


def call(kernel, args, outs, scratch=(), held=()):
    args = [pltpu.with_memory_space_constraint(a, pltpu.HBM) if i in held else a for i, a in enumerate(args)]
    moved = sum(a.size * a.dtype.itemsize for a in args)
    return pl.pallas_call(
        kernel,
        out_shape=[
            jax.ShapeDtypeStruct(out, F32) if isinstance(out, tuple) else out if isinstance(out, Plain) else in_vmem_like(out)
            for out in outs
        ],
        in_specs=[pl.BlockSpec(memory_space=pl.ANY if i in held else pltpu.VMEM) for i in range(len(args))],
        out_specs=[pl.BlockSpec(memory_space=pltpu.VMEM)] * len(outs),
        scratch_shapes=list(scratch),
        compiler_params=pltpu.CompilerParams(vmem_limit_bytes=24 * 2**20),
        cost_estimate=pl.CostEstimate(flops=0, bytes_accessed=moved, transcendentals=0),
    )(*args)


def exchanged(sent):
    return lax.all_to_all(sent, GROUP, 0, 0, tiled=True)


def body(loads, self_term, near_tiles, near_list, far_rows, far_cols, coupling, ranks):
    nrhs, panels = loads.shape
    rank = far_cols.shape[0]
    blocks, tile = near_tiles.shape[:2]
    rows = panels // tile
    strips = coupling.shape[0] // CORES
    couple = coupling.reshape(CORES * strips * rank, rank)
    near_list = near_list.T
    ranks = ranks.reshape(1, CORES * strips)
    self_term = self_term.reshape(1, panels)
    groups = CORES * strips
    message = Plain((groups, nrhs, panels // 2 + LANES), jnp.int32)
    index = pltpu.SMEM(near_list.shape, jnp.int32)
    scratch = [index, pltpu.SemaphoreType.DMA((1,)), pltpu.VMEM((3 * rows, CORES * nrhs, tile), F32)]
    scratch += [pltpu.VMEM((CORES * rows, CORES * nrhs, tile), F32)] * 4

    def twice(array):
        return [jax.ShapeDtypeStruct(array.shape, BF16)] * 2

    sent, *held, near_list, loads, self_term, near_tiles = call(
        start_kernel,
        (loads, far_cols, couple, ranks, near_list, far_rows, self_term, near_tiles),
        [
            message, *twice(far_cols), *twice(couple), jax.ShapeDtypeStruct((groups, CHUNK * rank), F32),
            *twice(far_rows), near_list, loads, self_term, near_tiles,
        ],
        [
            pltpu.VMEM(far_cols.shape, F32), pltpu.VMEM(couple.shape, F32), pltpu.SMEM(ranks.shape, jnp.int32),
            pltpu.VMEM(near_list.shape, jnp.int32), pltpu.VMEM(far_rows.shape, F32), pltpu.SemaphoreType.DMA((7 + PIECES,)),
        ],
        held=range(8),
    )
    loads, *held, self_term, near_tiles, near_list = in_vmem([loads, *held, self_term, near_tiles, near_list])
    source_side, target_side = [loads, *held[:5]], [*held[5:], self_term, near_tiles, near_list]
    sent, image, window0, state = call(
        step0_kernel,
        (exchanged(sent), *source_side, *target_side),
        [message, loads.shape, (3 * CORES * nrhs, panels), (CORES * nrhs, LANES)],
        scratch,
    )
    sent, basis, coeff = call(
        step1_kernel,
        (exchanged(sent), loads, image, window0, state, *target_side),
        [(groups, 1, LANES), (2 * nrhs, panels), (3 * nrhs, LANES)],
        scratch,
    )
    got = lax.all_to_all(sent, GROUP[::-1], 0, 0, tiled=True)
    return call(functools.partial(finish_kernel, rank), (got, basis, coeff), [loads.shape])[0]


def solution(mesh):
    every = ("case",) + GROUP
    in_specs = (
        P(None, every),
        P(every),
        P(every, None, None),
        P(every, None),
        P(None, every),
        P(None, every),
        P(None, GROUP, None, None),
        P(None, GROUP),
    )
    return jax.shard_map(body, mesh=mesh, in_specs=in_specs, out_specs=P(None, every), check_vma=False)
```

```python
import functools

import jax
import jax.numpy as jnp
from jax import lax
from jax.experimental import pallas as pl
from jax.experimental.pallas import tpu as pltpu
from jax.sharding import PartitionSpec as P

GROUP = ("strip", "clus")
CORES = 2
LANES = 128
CHUNK = 16
PIECE = 4
F32 = jnp.float32
BF16 = jnp.bfloat16

STEP = 8
COLS_TOP = 0.1875
COUPLE_TOP = 0.375
TOP = 32767.0
ONE = float(2**30)


def lanes_of(shape):
    return lax.broadcasted_iota(jnp.int32, shape, 1)


def rows_of(shape):
    return lax.broadcasted_iota(jnp.int32, shape, 0)


def total(rows):
    return jnp.sum(rows, axis=0, keepdims=True)


def stats_row(columns, rank, step=None):
    shape = (columns[0].shape[0], LANES)
    first = lanes_of(shape) - rank * rows_of(shape)
    spread = sum(jnp.where(first == k, column, 0.0) for k, column in enumerate(columns))
    if step is not None:
        spread = jnp.where((first >= STEP) & (first < rank), step, spread)
    return total(spread)


def steps_of(stats, rank):
    inner = lax.rem(lanes_of(stats.shape), rank)
    return jnp.where(inner < STEP, shifted(stats, STEP), stats)


def term_unit(panels, rank):
    return panels * rank * COLS_TOP * COUPLE_TOP * TOP / ONE


def stat_column(row, k, nrhs, rank):
    shape = (nrhs, LANES)
    first = lanes_of(shape) - rank * rows_of(shape)
    return jnp.sum(jnp.where(first == k, row, 0.0), axis=1, keepdims=True)


def shifted(value, k):
    return pltpu.roll(value, LANES - k, 1)


def far_sum_of(row, nrhs, rank):
    shape = (nrhs, LANES)
    first = lanes_of(shape) - rank * rows_of(shape)
    own = jnp.where((first >= 0) & (first < rank), row, 0.0)
    return sum((pltpu.roll(own, k * rank, 1) for k in range(1, LANES // rank)), own)


def halves(value):
    high = value.astype(BF16)
    return high, (value - high.astype(F32)).astype(BF16)


def product(left, right_high, right_low, side=0):
    rows = left.shape[0]
    high, low = halves(left)
    dims = (((1,), (side,)), ((), ()))
    both = lax.dot_general(jnp.concatenate([high, low], axis=0), right_high, dims, preferred_element_type=F32)
    return both[:rows] + (both[rows:] + lax.dot_general(high, right_low, dims, preferred_element_type=F32))


def coded(value):
    exponent = jnp.ceil(jnp.log2(jnp.maximum(jnp.abs(value), 1e-30)))
    return (value * jnp.exp2(-exponent) * ONE).astype(jnp.int32), exponent.astype(jnp.int32)


def decoded(mantissa, exponent):
    return mantissa.astype(F32) * (1.0 / ONE) * jnp.exp2(exponent.astype(F32))


def packed(field):
    top = jnp.max(jnp.abs(field), axis=1, keepdims=True)
    step = jnp.maximum(top, 1e-30) * (1.0 / TOP)
    codes = jnp.floor(field * (1.0 / step) + 0.5).astype(jnp.int32)
    width = field.shape[1] // 2
    return (codes[:, :width] << 16) | (codes[:, width:] & 0xFFFF), step


def unpacked(words):
    return jnp.concatenate([words >> 16, (words << 16) >> 16], axis=1).astype(F32)


def fetch(pairs, sems):
    copies = [pltpu.make_async_copy(a, b, sems.at[i]) for i, (a, b) in enumerate(pairs)]
    for copy in copies:
        copy.start()
    return copies


def put_message(field, columns, cols, couple, masks_ref, sent_ref):
    nrhs, rank = field.shape[0], cols[0].shape[0]
    unit = term_unit(field.shape[1], rank)
    proj = product(field, cols[0][...], cols[1][...], 1)
    wide = jnp.concatenate([proj] * CHUNK, axis=1)
    words, step = packed(field)
    width = words.shape[1]
    row = stats_row(columns, rank, step)
    finer = 1.0 / (steps_of(row, rank) * unit)
    for i in range(sent_ref.shape[0]):
        sent_ref[i, :, :width] = words
    stats = [jnp.broadcast_to(a, (CHUNK, LANES)) for a in coded(row)]
    for start in range(0, sent_ref.shape[0], CHUNK):
        mask = masks_ref[pl.ds(start, CHUNK), :]
        spread = jnp.concatenate([mask * wide[r : r + 1] for r in range(nrhs)], axis=0)
        here = pl.ds(start * rank, CHUNK * rank)
        terms = product(spread, couple[0][here, :], couple[1][here, :])
        terms = jnp.concatenate([terms[r * CHUNK : (r + 1) * CHUNK] for r in range(nrhs)], axis=1)
        here = pl.ds(start, CHUNK)
        for k, value in enumerate([(terms * finer).astype(jnp.int32)] + stats + [stats[0]] * (nrhs - 3)):
            sent_ref[here, k, width:] = value


def message_parts(got_ref, rank):
    width = got_ref.shape[2] - LANES
    stats = decoded(got_ref[:, 1, width:], got_ref[:, 2, width:])
    terms = got_ref[:, 0, width:].astype(F32) * (steps_of(stats, rank) * term_unit(2 * width, rank))
    return total(terms), stats


def window_parts(got_ref, rank):
    nrhs, width = got_ref.shape[1], got_ref.shape[2] - LANES
    strips = got_ref.shape[0] // CORES
    shape = (CORES * nrhs, LANES)
    for step in range(3):
        owner = lax.axis_index("strip") + (step - 1)
        inside = (owner >= 0) & (owner < strips)
        owner = CORES * jnp.clip(owner, 0, strips - 1)
        words = jnp.concatenate([got_ref[owner + core, :, :width] for core in range(CORES)], axis=0)
        tails = [got_ref[owner + core, :, width:] for core in range(CORES)]
        rows = [decoded(tail[1:2], tail[2:3]) for tail in tails]
        rows = jnp.where(rows_of(shape) < nrhs, rows[0], rows[1])
        wanted = lanes_of(shape) == rank * lax.rem(rows_of(shape), nrhs) + STEP
        yield inside, unpacked(words), jnp.sum(jnp.where(wanted, rows, 0.0), axis=1, keepdims=True)


def put_blocks(part, first, window):
    part = part.astype(BF16).astype(F32)
    for c in range(part.shape[1] // LANES):
        window[first + c] = part[:, c * LANES : (c + 1) * LANES]


def near_field(window, tiles, list_ref, sums, nrhs, copies=()):
    for held in sums:
        held[...] = jnp.zeros_like(held)
    n = 0
    for tiles_ref in tiles:
        for first in range(0, tiles_ref.shape[0], 4):
            if copies and tiles_ref is tiles[1]:
                copies[first // PIECE].wait()
            sources = [window[list_ref[1, n + i]] for i in range(4)]
            blank = jnp.zeros_like(sources[0])
            upper = [sources[0], blank, sources[2], blank]
            lower = [blank, sources[1], blank, sources[3]]
            left = jnp.concatenate([jnp.concatenate(a, axis=0).astype(BF16) for a in (upper, lower)], axis=1)
            four = [tiles_ref[first + i] for i in range(4)]
            right = [jnp.concatenate([four[i], four[i + 2]], axis=1) for i in range(2)]
            both = jnp.dot(left, jnp.concatenate(right, axis=0), preferred_element_type=F32)
            for i, held in enumerate(sums):
                side = i // 2 * LANES
                rows = i * window.shape[1]
                held[list_ref[0, n + i]] += both[rows : rows + window.shape[1], side : side + LANES]
            n += 4
    whole = sum((held[...] for held in sums[1:]), sums[0][...])
    rows = whole.shape[0] // CORES
    return jnp.concatenate([whole[b, :nrhs] + whole[rows + b, nrhs:] for b in range(rows)], axis=1)


def tile_pieces(tiles_hbm, first, tiles_ref):
    starts = range(0, tiles_ref.shape[0], PIECE)
    return tuple((tiles_hbm.at[pl.ds(first + i, PIECE)], tiles_ref.at[pl.ds(i, PIECE)]) for i in starts)


def start_kernel(
    loads_hbm, cols_hbm, couple_hbm, ranks_hbm, list_hbm, rows_hbm, self_hbm, tiles_hbm, sent_ref, cols_high, cols_low, couple_high,
    couple_low, masks_ref, rows_high, rows_low, list_ref, loads_ref, self_ref, tiles_ref, cols_ref, couple_ref, ranks_ref, raw_ref,
    rows_ref, sems,
):
    rank, panels = cols_ref.shape
    pairs = (
        (loads_hbm, loads_ref), (cols_hbm, cols_ref), (couple_hbm, couple_ref), (ranks_hbm, ranks_ref),
        (list_hbm, raw_ref), (rows_hbm, rows_ref), (self_hbm, self_ref),
    )
    copies = fetch(pairs + tile_pieces(tiles_hbm, 0, tiles_ref), sems)
    copies[0].wait()
    loads = loads_ref[...]
    square = jnp.sum(loads * loads, axis=1, keepdims=True)
    copies[1].wait()
    cols_high[...], cols_low[...] = halves(cols_ref[...])
    copies[2].wait()
    couple_high[...], couple_low[...] = halves(couple_ref[...])
    copies[3].wait()
    shape = (CHUNK, CHUNK * rank)
    owner = lax.div(lanes_of(shape), rank)
    inner = lax.rem(lanes_of(shape), rank)
    for start in range(0, masks_ref.shape[0], CHUNK):
        limit = jnp.zeros((1, CHUNK * rank), jnp.int32)
        for i in range(CHUNK):
            limit = jnp.where(owner[:1] == i, ranks_ref[0, start + i], limit)
        masks_ref[pl.ds(start, CHUNK), :] = jnp.where((owner == rows_of(shape)) & (inner < limit), 1.0, 0.0)
    copies[4].wait()
    count = panels // LANES
    target, source = raw_ref[0:1, :], raw_ref[1:2, :]
    group, block = lax.div(source, count), lax.rem(source, count)
    strip, core = lax.div(group, CORES), lax.rem(group, CORES)
    list_ref[...] = jnp.concatenate([core * count + target, strip * count + block], axis=0)
    copies[5].wait()
    rows_high[...], rows_low[...] = halves(rows_ref[...])
    put_message(loads, [square], (cols_high, cols_low), (couple_high, couple_low), masks_ref, sent_ref)
    for copy in copies[6:]:
        copy.wait()


def image_of(field, far, self_ref, far_rows, near):
    rank = far_rows[0].shape[0]
    return self_ref[...] * field + near + product(far[:, :rank], far_rows[0][...], far_rows[1][...])


def step0_kernel(
    got_ref, loads_ref, cols_high, cols_low, couple_high, couple_low, masks_ref, rows_high, rows_low, self_ref,
    tiles0_ref, list_vmem, tiles_hbm, sent_ref, image_ref, window0_ref, state_ref, tiles1_ref, list_ref, sems, tile_sems,
    window, *sums,
):
    rank = rows_high.shape[0]
    nrhs, panels = loads_ref.shape
    span, rows = panels // LANES, CORES * nrhs
    (copy,) = fetch(((list_vmem, list_ref),), sems)
    copies = fetch(tile_pieces(tiles_hbm, tiles0_ref.shape[0], tiles1_ref), tile_sems)
    terms, stats = message_parts(got_ref, rank)
    beta = jnp.sqrt(stat_column(total(stats), 0, nrhs, rank))
    scale = 1.0 / beta
    both = jnp.concatenate([scale] * CORES, axis=0)
    for step, (inside, part, unit) in enumerate(window_parts(got_ref, rank)):
        part = jnp.where(inside, part * (unit * both), 0.0)
        window0_ref[step * rows : (step + 1) * rows, :] = part
        put_blocks(part, step * span, window)
    basis = loads_ref[...] * scale
    far = far_sum_of(terms, nrhs, rank) * scale
    copy.wait()
    near = near_field(window, (tiles0_ref, tiles1_ref), list_ref, sums, nrhs, copies)
    image = image_of(basis, far, self_ref, (rows_high, rows_low), near)
    image_ref[...] = image
    state_ref[...] = jnp.concatenate([far, jnp.broadcast_to(beta, far.shape)], axis=0)
    norm = jnp.sum(basis * basis, axis=1, keepdims=True)
    dot = jnp.sum(basis * image, axis=1, keepdims=True)
    share = jnp.where(norm > 0, dot / jnp.where(norm > 0, norm, 1.0), 0.0)
    rest = image - share * basis
    rest = jnp.sum(rest * rest, axis=1, keepdims=True)
    columns = [norm, dot, share, rest]
    put_message(image, columns, (cols_high, cols_low), (couple_high, couple_low), masks_ref, sent_ref)


def step1_kernel(
    got_ref, loads_ref, image_ref, window0_ref, state_ref, rows_high, rows_low, self_ref, tiles0_ref,
    list_vmem, tiles1_ref, sent_ref, basis_ref, coeff_ref, list_ref, sems, window, *sums,
):
    rank = rows_high.shape[0]
    nrhs, panels = loads_ref.shape
    span, rows = panels // LANES, CORES * nrhs
    (copy,) = fetch(((list_vmem, list_ref),), sems)
    beta = state_ref[nrhs:, :1]
    far0 = state_ref[:nrhs, :]
    terms, stats = message_parts(got_ref, rank)
    summed = total(stats)
    h00 = stat_column(summed, 1, nrhs, rank)
    away = shifted(stats, 2) - shifted(summed, 1)
    rest = total(shifted(stats, 3) + stats * away * away)
    h10 = jnp.sqrt(stat_column(rest, 0, nrhs, rank))
    scale = 1.0 / h10
    both, both_h00 = (jnp.concatenate([a] * CORES, axis=0) for a in (scale, h00))
    for step, (inside, part, unit) in enumerate(window_parts(got_ref, rank)):
        part = (part * unit - both_h00 * window0_ref[step * rows : (step + 1) * rows, :]) * both
        put_blocks(jnp.where(inside, part, 0.0), step * span, window)
    basis0 = loads_ref[...] * (1.0 / beta)
    basis1 = (image_ref[...] - h00 * basis0) * scale
    far = (far_sum_of(terms, nrhs, rank) - h00 * far0) * scale
    copy.wait()
    near = near_field(window, (tiles0_ref, tiles1_ref), list_ref, sums, nrhs)
    image = image_of(basis1, far, self_ref, (rows_high, rows_low), near)
    columns = [jnp.sum(a * image, axis=1, keepdims=True) for a in (basis0, basis1, image)]
    sent_ref[:, 0, :] = jnp.broadcast_to(stats_row(columns, rank), (sent_ref.shape[0], LANES))
    basis_ref[...] = jnp.concatenate([basis0, basis1], axis=0)
    coeff_ref[...] = jnp.concatenate([jnp.broadcast_to(v, (nrhs, LANES)) for v in (beta, h00, h10)], axis=0)


def finish_kernel(rank, got_ref, basis_ref, coeff_ref, out_ref):
    nrhs = out_ref.shape[0]
    row = total(got_ref[:, 0, :])
    h01, h11, gram11 = (stat_column(row, k, nrhs, rank) for k in range(3))
    beta, h00, h10 = (coeff_ref[k * nrhs : (k + 1) * nrhs, :1] for k in range(3))
    gram00 = h00 * h00 + h10 * h10
    gram01 = h00 * h01 + h10 * h11
    lower00 = jnp.sqrt(gram00)
    lower10 = gram01 / lower00
    lower11 = jnp.sqrt(gram11 - lower10 * lower10)
    middle0 = beta * h00 / lower00
    middle1 = (beta * h01 - lower10 * middle0) / lower11
    y1 = middle1 / lower11
    y0 = (middle0 - lower10 * y1) / lower00
    out_ref[...] = y0 * basis_ref[:nrhs, :] + y1 * basis_ref[nrhs:, :]


class Plain(jax.ShapeDtypeStruct):
    pass


def in_vmem_like(array):
    return pltpu.VMEM(array.shape, array.dtype)


def in_vmem(arrays):
    return [pltpu.with_memory_space_constraint(a, pltpu.VMEM) for a in arrays]


def call(kernel, args, outs, scratch=(), held=()):
    args = [pltpu.with_memory_space_constraint(a, pltpu.HBM) if i in held else a for i, a in enumerate(args)]
    moved = sum(a.size * a.dtype.itemsize for a in args)
    return pl.pallas_call(
        kernel,
        out_shape=[
            jax.ShapeDtypeStruct(out, F32) if isinstance(out, tuple) else out if isinstance(out, Plain) else in_vmem_like(out)
            for out in outs
        ],
        in_specs=[pl.BlockSpec(memory_space=pl.ANY if i in held else pltpu.VMEM) for i in range(len(args))],
        out_specs=[pl.BlockSpec(memory_space=pltpu.VMEM)] * len(outs),
        scratch_shapes=list(scratch),
        compiler_params=pltpu.CompilerParams(vmem_limit_bytes=24 * 2**20),
        cost_estimate=pl.CostEstimate(flops=0, bytes_accessed=moved, transcendentals=0),
    )(*args)


def exchanged(sent):
    return lax.all_to_all(sent, GROUP, 0, 0, tiled=True)


def body(loads, self_term, near_tiles, near_list, far_rows, far_cols, coupling, ranks):
    nrhs, panels = loads.shape
    rank = far_cols.shape[0]
    blocks, tile = near_tiles.shape[:2]
    rows = panels // tile
    strips = coupling.shape[0] // CORES
    couple = coupling.reshape(CORES * strips * rank, rank)
    near_list = near_list.T
    ranks = ranks.reshape(1, CORES * strips)
    self_term = self_term.reshape(1, panels)
    groups = CORES * strips
    message = Plain((groups, nrhs, panels // 2 + LANES), jnp.int32)
    index = pltpu.SMEM(near_list.shape, jnp.int32)
    index = [index, pltpu.SemaphoreType.DMA((1,))]
    scratch = [pltpu.VMEM((3 * rows, CORES * nrhs, tile), F32)]
    early = PIECE * (blocks * 3 // (5 * PIECE))
    tiles0, tiles1 = (jax.ShapeDtypeStruct((count, tile, tile), BF16) for count in (early, blocks - early))
    scratch += [pltpu.VMEM((CORES * rows, CORES * nrhs, tile), F32)] * 4

    def twice(array):
        return [jax.ShapeDtypeStruct(array.shape, BF16)] * 2

    sent, *held, near_list, loads, self_term, tiles0 = call(
        start_kernel,
        (loads, far_cols, couple, ranks, near_list, far_rows, self_term, near_tiles),
        [
            message, *twice(far_cols), *twice(couple), jax.ShapeDtypeStruct((groups, CHUNK * rank), F32),
            *twice(far_rows), near_list, loads, self_term, tiles0,
        ],
        [
            pltpu.VMEM(far_cols.shape, F32), pltpu.VMEM(couple.shape, F32), pltpu.SMEM(ranks.shape, jnp.int32),
            pltpu.VMEM(near_list.shape, jnp.int32), pltpu.VMEM(far_rows.shape, F32), pltpu.SemaphoreType.DMA((7 + early // PIECE,)),
        ],
        held=range(8),
    )
    loads, *held, self_term, tiles0, near_list = in_vmem([loads, *held, self_term, tiles0, near_list])
    source_side, target_side = [loads, *held[:5]], [*held[5:], self_term, tiles0, near_list]
    sent, image, window0, state, tiles1 = call(
        step0_kernel,
        (exchanged(sent), *source_side, *target_side, near_tiles),
        [message, loads.shape, (3 * CORES * nrhs, panels), (CORES * nrhs, LANES), tiles1],
        index + [pltpu.SemaphoreType.DMA((tiles1.shape[0] // PIECE,))] + scratch,
        held=(1 + len(source_side) + len(target_side),),
    )
    sent, basis, coeff = call(
        step1_kernel,
        (exchanged(sent), loads, image, window0, state, *target_side, *in_vmem([tiles1])),
        [(groups, 1, LANES), (2 * nrhs, panels), (3 * nrhs, LANES)],
        index + scratch,
    )
    return call(functools.partial(finish_kernel, rank), (exchanged(sent), basis, coeff), [loads.shape])[0]


def solution(mesh):
    every = ("case",) + GROUP
    in_specs = (
        P(None, every),
        P(every),
        P(every, None, None),
        P(every, None),
        P(None, every),
        P(None, every),
        P(None, GROUP, None, None),
        P(None, GROUP),
    )
    return jax.shard_map(body, mesh=mesh, in_specs=in_specs, out_specs=P(None, every), check_vma=False)
```

```python
import functools

import jax
import jax.numpy as jnp
from jax import lax
from jax.experimental import pallas as pl
from jax.experimental.pallas import tpu as pltpu
from jax.sharding import PartitionSpec as P

GROUP = ("strip", "clus")
CORES = 2
LANES = 128
CHUNK = 16
PIECES = 10
F32 = jnp.float32
BF16 = jnp.bfloat16

STEP = 8
COLS_TOP = 0.1875
COUPLE_TOP = 0.375
TOP = 32767.0
ONE = float(2**30)


def lanes_of(shape):
    return lax.broadcasted_iota(jnp.int32, shape, 1)


def rows_of(shape):
    return lax.broadcasted_iota(jnp.int32, shape, 0)


def total(rows):
    return jnp.sum(rows, axis=0, keepdims=True)


def stats_row(columns, rank, step=None):
    shape = (columns[0].shape[0], LANES)
    first = lanes_of(shape) - rank * rows_of(shape)
    spread = sum(jnp.where(first == k, column, 0.0) for k, column in enumerate(columns))
    if step is not None:
        spread = jnp.where((first >= STEP) & (first < rank), step, spread)
    return total(spread)


def steps_of(stats, rank):
    inner = lax.rem(lanes_of(stats.shape), rank)
    return jnp.where(inner < STEP, shifted(stats, STEP), stats)


def term_unit(panels, rank):
    return panels * rank * COLS_TOP * COUPLE_TOP * TOP / ONE


def stat_column(row, k, nrhs, rank):
    shape = (nrhs, LANES)
    first = lanes_of(shape) - rank * rows_of(shape)
    return jnp.sum(jnp.where(first == k, row, 0.0), axis=1, keepdims=True)


def shifted(value, k):
    return pltpu.roll(value, LANES - k, 1)


def far_sum_of(row, nrhs, rank):
    shape = (nrhs, LANES)
    first = lanes_of(shape) - rank * rows_of(shape)
    own = jnp.where((first >= 0) & (first < rank), row, 0.0)
    return sum((pltpu.roll(own, k * rank, 1) for k in range(1, LANES // rank)), own)


def halves(value):
    high = value.astype(BF16)
    return high, (value - high.astype(F32)).astype(BF16)


def product(left, right_high, right_low, side=0):
    rows = left.shape[0]
    high, low = halves(left)
    dims = (((1,), (side,)), ((), ()))
    both = lax.dot_general(jnp.concatenate([high, low], axis=0), right_high, dims, preferred_element_type=F32)
    return both[:rows] + (both[rows:] + lax.dot_general(high, right_low, dims, preferred_element_type=F32))


def coded(value):
    exponent = jnp.ceil(jnp.log2(jnp.maximum(jnp.abs(value), 1e-30)))
    return (value * jnp.exp2(-exponent) * ONE).astype(jnp.int32), exponent.astype(jnp.int32)


def decoded(mantissa, exponent):
    return mantissa.astype(F32) * (1.0 / ONE) * jnp.exp2(exponent.astype(F32))


def packed(field):
    top = jnp.max(jnp.abs(field), axis=1, keepdims=True)
    step = jnp.maximum(top, 1e-30) * (1.0 / TOP)
    codes = jnp.floor(field * (1.0 / step) + 0.5).astype(jnp.int32)
    width = field.shape[1] // 2
    return (codes[:, :width] << 16) | (codes[:, width:] & 0xFFFF), step


def unpacked(words):
    return jnp.concatenate([words >> 16, (words << 16) >> 16], axis=1).astype(F32)


def fetch(pairs, sems):
    copies = [pltpu.make_async_copy(a, b, sems.at[i]) for i, (a, b) in enumerate(pairs)]
    for copy in copies:
        copy.start()
    return copies


def put_message(field, columns, cols, couple, masks_ref, sent_ref):
    nrhs, rank = field.shape[0], cols[0].shape[0]
    unit = term_unit(field.shape[1], rank)
    proj = product(field, cols[0][...], cols[1][...], 1)
    wide = jnp.concatenate([proj] * CHUNK, axis=1)
    words, step = packed(field)
    width = words.shape[1]
    row = stats_row(columns, rank, step)
    finer = 1.0 / (steps_of(row, rank) * unit)
    for i in range(sent_ref.shape[0]):
        sent_ref[i, :, :width] = words
    stats = [jnp.broadcast_to(a, (CHUNK, LANES)) for a in coded(row)]
    for start in range(0, sent_ref.shape[0], CHUNK):
        mask = masks_ref[pl.ds(start, CHUNK), :]
        spread = jnp.concatenate([mask * wide[r : r + 1] for r in range(nrhs)], axis=0)
        here = pl.ds(start * rank, CHUNK * rank)
        terms = product(spread, couple[0][here, :], couple[1][here, :])
        terms = jnp.concatenate([terms[r * CHUNK : (r + 1) * CHUNK] for r in range(nrhs)], axis=1)
        here = pl.ds(start, CHUNK)
        for k, value in enumerate([(terms * finer).astype(jnp.int32)] + stats + [stats[0]] * (nrhs - 3)):
            sent_ref[here, k, width:] = value


def message_parts(got_ref, rank):
    width = got_ref.shape[2] - LANES
    stats = decoded(got_ref[:, 1, width:], got_ref[:, 2, width:])
    terms = got_ref[:, 0, width:].astype(F32) * (steps_of(stats, rank) * term_unit(2 * width, rank))
    return total(terms), stats


def window_parts(got_ref, rank):
    nrhs, width = got_ref.shape[1], got_ref.shape[2] - LANES
    strips = got_ref.shape[0] // CORES
    shape = (CORES * nrhs, LANES)
    for step in range(3):
        owner = lax.axis_index("strip") + (step - 1)
        inside = (owner >= 0) & (owner < strips)
        owner = CORES * jnp.clip(owner, 0, strips - 1)
        words = jnp.concatenate([got_ref[owner + core, :, :width] for core in range(CORES)], axis=0)
        tails = [got_ref[owner + core, :, width:] for core in range(CORES)]
        rows = [decoded(tail[1:2], tail[2:3]) for tail in tails]
        rows = jnp.where(rows_of(shape) < nrhs, rows[0], rows[1])
        wanted = lanes_of(shape) == rank * lax.rem(rows_of(shape), nrhs) + STEP
        yield inside, unpacked(words), jnp.sum(jnp.where(wanted, rows, 0.0), axis=1, keepdims=True)


def put_blocks(part, first, window):
    part = part.astype(BF16).astype(F32)
    for c in range(part.shape[1] // LANES):
        window[first + c] = part[:, c * LANES : (c + 1) * LANES]


def near_field(window, tiles, list_ref, sums, nrhs):
    for held in sums:
        held[...] = jnp.zeros_like(held)
    n = 0
    for tiles_ref in tiles:
        for first in range(0, tiles_ref.shape[0], 2):
            left = jnp.concatenate([window[list_ref[1, n + i]] for i in range(2)], axis=0).astype(BF16)
            right = jnp.concatenate([tiles_ref[first + i] for i in range(2)], axis=1)
            both = jnp.dot(left, right, preferred_element_type=F32)
            rows = window.shape[1]
            for i in range(2):
                held = sums[(n + i) % len(sums)]
                held[list_ref[0, n + i]] += both[i * rows : (i + 1) * rows, i * LANES : (i + 1) * LANES]
            n += 2
    whole = sum((held[...] for held in sums[1:]), sums[0][...])
    rows = whole.shape[0] // CORES
    return jnp.concatenate([whole[b, :nrhs] + whole[rows + b, nrhs:] for b in range(rows)], axis=1)


def start_kernel(
    loads_hbm, cols_hbm, couple_hbm, ranks_hbm, list_hbm, rows_hbm, self_hbm, tiles_hbm, sent_ref, cols_high, cols_low, couple_high,
    couple_low, masks_ref, rows_high, rows_low, list_ref, loads_ref, self_ref, tiles_ref, cols_ref, couple_ref, ranks_ref, raw_ref,
    rows_ref, sems,
):
    rank, panels = cols_ref.shape
    pairs = (
        (loads_hbm, loads_ref), (cols_hbm, cols_ref), (couple_hbm, couple_ref), (ranks_hbm, ranks_ref),
        (list_hbm, raw_ref), (rows_hbm, rows_ref), (self_hbm, self_ref),
    )
    every = tiles_ref.shape[0] // PIECES
    pieces = [pl.ds(i * every, every) for i in range(PIECES)]
    copies = fetch(pairs + tuple((tiles_hbm.at[p], tiles_ref.at[p]) for p in pieces), sems)
    copies[0].wait()
    loads = loads_ref[...]
    square = jnp.sum(loads * loads, axis=1, keepdims=True)
    copies[1].wait()
    cols_high[...], cols_low[...] = halves(cols_ref[...])
    copies[2].wait()
    couple_high[...], couple_low[...] = halves(couple_ref[...])
    copies[3].wait()
    shape = (CHUNK, CHUNK * rank)
    owner = lax.div(lanes_of(shape), rank)
    inner = lax.rem(lanes_of(shape), rank)
    for start in range(0, masks_ref.shape[0], CHUNK):
        limit = jnp.zeros((1, CHUNK * rank), jnp.int32)
        for i in range(CHUNK):
            limit = jnp.where(owner[:1] == i, ranks_ref[0, start + i], limit)
        masks_ref[pl.ds(start, CHUNK), :] = jnp.where((owner == rows_of(shape)) & (inner < limit), 1.0, 0.0)
    copies[4].wait()
    count = panels // LANES
    target, source = raw_ref[0:1, :], raw_ref[1:2, :]
    group, block = lax.div(source, count), lax.rem(source, count)
    strip, core = lax.div(group, CORES), lax.rem(group, CORES)
    list_ref[...] = jnp.concatenate([core * count + target, strip * count + block], axis=0)
    copies[5].wait()
    rows_high[...], rows_low[...] = halves(rows_ref[...])
    put_message(loads, [square], (cols_high, cols_low), (couple_high, couple_low), masks_ref, sent_ref)
    for copy in copies[6:]:
        copy.wait()


def image_of(field, far, self_ref, far_rows, near):
    rank = far_rows[0].shape[0]
    return self_ref[...] * field + near + product(far[:, :rank], far_rows[0][...], far_rows[1][...])


def step0_kernel(
    got_ref, loads_ref, cols_high, cols_low, couple_high, couple_low, masks_ref, rows_high, rows_low, self_ref,
    tiles_ref, list_vmem, sent_ref, image_ref, window0_ref, state_ref, list_ref, sems, window, *sums,
):
    rank = rows_high.shape[0]
    nrhs, panels = loads_ref.shape
    span, rows = panels // LANES, CORES * nrhs
    (copy,) = fetch(((list_vmem, list_ref),), sems)
    terms, stats = message_parts(got_ref, rank)
    beta = jnp.sqrt(stat_column(total(stats), 0, nrhs, rank))
    scale = 1.0 / beta
    both = jnp.concatenate([scale] * CORES, axis=0)
    for step, (inside, part, unit) in enumerate(window_parts(got_ref, rank)):
        part = jnp.where(inside, part * (unit * both), 0.0)
        window0_ref[step * rows : (step + 1) * rows, :] = part
        put_blocks(part, step * span, window)
    basis = loads_ref[...] * scale
    far = far_sum_of(terms, nrhs, rank) * scale
    copy.wait()
    near = near_field(window, (tiles_ref,), list_ref, sums, nrhs)
    image = image_of(basis, far, self_ref, (rows_high, rows_low), near)
    image_ref[...] = image
    state_ref[...] = jnp.concatenate([far, jnp.broadcast_to(beta, far.shape)], axis=0)
    norm = jnp.sum(basis * basis, axis=1, keepdims=True)
    dot = jnp.sum(basis * image, axis=1, keepdims=True)
    share = jnp.where(norm > 0, dot / jnp.where(norm > 0, norm, 1.0), 0.0)
    rest = image - share * basis
    rest = jnp.sum(rest * rest, axis=1, keepdims=True)
    columns = [norm, dot, share, rest]
    put_message(image, columns, (cols_high, cols_low), (couple_high, couple_low), masks_ref, sent_ref)


def step1_kernel(
    got_ref, loads_ref, image_ref, window0_ref, state_ref, rows_high, rows_low, self_ref, tiles_ref,
    list_vmem, sent_ref, basis_ref, coeff_ref, list_ref, sems, window, *sums,
):
    rank = rows_high.shape[0]
    nrhs, panels = loads_ref.shape
    span, rows = panels // LANES, CORES * nrhs
    (copy,) = fetch(((list_vmem, list_ref),), sems)
    beta = state_ref[nrhs:, :1]
    far0 = state_ref[:nrhs, :]
    terms, stats = message_parts(got_ref, rank)
    summed = total(stats)
    h00 = stat_column(summed, 1, nrhs, rank)
    away = shifted(stats, 2) - shifted(summed, 1)
    rest = total(shifted(stats, 3) + stats * away * away)
    h10 = jnp.sqrt(stat_column(rest, 0, nrhs, rank))
    scale = 1.0 / h10
    both, both_h00 = (jnp.concatenate([a] * CORES, axis=0) for a in (scale, h00))
    for step, (inside, part, unit) in enumerate(window_parts(got_ref, rank)):
        part = (part * unit - both_h00 * window0_ref[step * rows : (step + 1) * rows, :]) * both
        put_blocks(jnp.where(inside, part, 0.0), step * span, window)
    basis0 = loads_ref[...] * (1.0 / beta)
    basis1 = (image_ref[...] - h00 * basis0) * scale
    far = (far_sum_of(terms, nrhs, rank) - h00 * far0) * scale
    copy.wait()
    near = near_field(window, (tiles_ref,), list_ref, sums, nrhs)
    image = image_of(basis1, far, self_ref, (rows_high, rows_low), near)
    columns = [jnp.sum(a * image, axis=1, keepdims=True) for a in (basis0, basis1, image)]
    sent_ref[...] = jnp.broadcast_to(stats_row(columns, rank)[None], sent_ref.shape)
    basis_ref[...] = jnp.concatenate([basis0, basis1], axis=0)
    coeff_ref[...] = jnp.concatenate([jnp.broadcast_to(v, (nrhs, LANES)) for v in (beta, h00, h10)], axis=0)


def finish_kernel(rank, got_ref, basis_ref, coeff_ref, out_ref):
    nrhs = out_ref.shape[0]
    row = total(got_ref[:, 0, :])
    h01, h11, gram11 = (stat_column(row, k, nrhs, rank) for k in range(3))
    beta, h00, h10 = (coeff_ref[k * nrhs : (k + 1) * nrhs, :1] for k in range(3))
    gram00 = h00 * h00 + h10 * h10
    gram01 = h00 * h01 + h10 * h11
    lower00 = jnp.sqrt(gram00)
    lower10 = gram01 / lower00
    lower11 = jnp.sqrt(gram11 - lower10 * lower10)
    middle0 = beta * h00 / lower00
    middle1 = (beta * h01 - lower10 * middle0) / lower11
    y1 = middle1 / lower11
    y0 = (middle0 - lower10 * y1) / lower00
    out_ref[...] = y0 * basis_ref[:nrhs, :] + y1 * basis_ref[nrhs:, :]


class Plain(jax.ShapeDtypeStruct):
    pass


def in_vmem_like(array):
    return pltpu.VMEM(array.shape, array.dtype)


def in_vmem(arrays):
    return [pltpu.with_memory_space_constraint(a, pltpu.VMEM) for a in arrays]


def call(kernel, args, outs, scratch=(), held=()):
    args = [pltpu.with_memory_space_constraint(a, pltpu.HBM) if i in held else a for i, a in enumerate(args)]
    moved = sum(a.size * a.dtype.itemsize for a in args)
    return pl.pallas_call(
        kernel,
        out_shape=[
            jax.ShapeDtypeStruct(out, F32) if isinstance(out, tuple) else out if isinstance(out, Plain) else in_vmem_like(out)
            for out in outs
        ],
        in_specs=[pl.BlockSpec(memory_space=pl.ANY if i in held else pltpu.VMEM) for i in range(len(args))],
        out_specs=[pl.BlockSpec(memory_space=pltpu.VMEM)] * len(outs),
        scratch_shapes=list(scratch),
        compiler_params=pltpu.CompilerParams(vmem_limit_bytes=24 * 2**20),
        cost_estimate=pl.CostEstimate(flops=0, bytes_accessed=moved, transcendentals=0),
    )(*args)


def exchanged(sent):
    return lax.all_to_all(sent, GROUP, 0, 0, tiled=True)


def body(loads, self_term, near_tiles, near_list, far_rows, far_cols, coupling, ranks):
    nrhs, panels = loads.shape
    rank = far_cols.shape[0]
    blocks, tile = near_tiles.shape[:2]
    rows = panels // tile
    strips = coupling.shape[0] // CORES
    couple = coupling.reshape(CORES * strips * rank, rank)
    near_list = near_list.T
    ranks = ranks.reshape(1, CORES * strips)
    self_term = self_term.reshape(1, panels)
    groups = CORES * strips
    message = Plain((groups, nrhs, panels // 2 + LANES), jnp.int32)
    index = pltpu.SMEM(near_list.shape, jnp.int32)
    scratch = [index, pltpu.SemaphoreType.DMA((1,)), pltpu.VMEM((3 * rows, CORES * nrhs, tile), F32)]
    scratch += [pltpu.VMEM((CORES * rows, CORES * nrhs, tile), F32)] * 4

    def twice(array):
        return [jax.ShapeDtypeStruct(array.shape, BF16)] * 2

    sent, *held, near_list, loads, self_term, near_tiles = call(
        start_kernel,
        (loads, far_cols, couple, ranks, near_list, far_rows, self_term, near_tiles),
        [
            message, *twice(far_cols), *twice(couple), jax.ShapeDtypeStruct((groups, CHUNK * rank), F32),
            *twice(far_rows), near_list, loads, self_term, near_tiles,
        ],
        [
            pltpu.VMEM(far_cols.shape, F32), pltpu.VMEM(couple.shape, F32), pltpu.SMEM(ranks.shape, jnp.int32),
            pltpu.VMEM(near_list.shape, jnp.int32), pltpu.VMEM(far_rows.shape, F32), pltpu.SemaphoreType.DMA((7 + PIECES,)),
        ],
        held=range(8),
    )
    loads, *held, self_term, near_tiles, near_list = in_vmem([loads, *held, self_term, near_tiles, near_list])
    source_side, target_side = [loads, *held[:5]], [*held[5:], self_term, near_tiles, near_list]
    sent, image, window0, state = call(
        step0_kernel,
        (exchanged(sent), *source_side, *target_side),
        [message, loads.shape, (3 * CORES * nrhs, panels), (CORES * nrhs, LANES)],
        scratch,
    )
    sent, basis, coeff = call(
        step1_kernel,
        (exchanged(sent), loads, image, window0, state, *target_side),
        [(groups, 8, LANES), (2 * nrhs, panels), (3 * nrhs, LANES)],
        scratch,
    )
    return call(functools.partial(finish_kernel, rank), (exchanged(sent), basis, coeff), [loads.shape])[0]


def solution(mesh):
    every = ("case",) + GROUP
    in_specs = (
        P(None, every),
        P(every),
        P(every, None, None),
        P(every, None),
        P(None, every),
        P(None, every),
        P(None, GROUP, None, None),
        P(None, GROUP),
    )
    return jax.shard_map(body, mesh=mesh, in_specs=in_specs, out_specs=P(None, every), check_vma=False)
```

```python
import functools

import jax
import jax.numpy as jnp
from jax import lax
from jax.experimental import pallas as pl
from jax.experimental.pallas import tpu as pltpu
from jax.sharding import PartitionSpec as P

GROUP = ("strip", "clus")
CORES = 2
LANES = 128
CHUNK = 16
PIECES = 10
F32 = jnp.float32
BF16 = jnp.bfloat16

STEP = 8
COLS_TOP = 0.1875
COUPLE_TOP = 0.375
TOP = 32767.0
ONE = float(2**30)


def lanes_of(shape):
    return lax.broadcasted_iota(jnp.int32, shape, 1)


def rows_of(shape):
    return lax.broadcasted_iota(jnp.int32, shape, 0)


def total(rows):
    return jnp.sum(rows, axis=0, keepdims=True)


def stats_row(columns, rank, step=None):
    shape = (columns[0].shape[0], LANES)
    first = lanes_of(shape) - rank * rows_of(shape)
    spread = sum(jnp.where(first == k, column, 0.0) for k, column in enumerate(columns))
    if step is not None:
        spread = jnp.where((first >= STEP) & (first < rank), step, spread)
    return total(spread)


def steps_of(stats, rank):
    inner = lax.rem(lanes_of(stats.shape), rank)
    return jnp.where(inner < STEP, shifted(stats, STEP), stats)


def term_unit(panels, rank):
    return panels * rank * COLS_TOP * COUPLE_TOP * TOP / ONE


def stat_column(row, k, nrhs, rank):
    shape = (nrhs, LANES)
    first = lanes_of(shape) - rank * rows_of(shape)
    return jnp.sum(jnp.where(first == k, row, 0.0), axis=1, keepdims=True)


def shifted(value, k):
    return pltpu.roll(value, LANES - k, 1)


def far_sum_of(row, nrhs, rank):
    shape = (nrhs, LANES)
    first = lanes_of(shape) - rank * rows_of(shape)
    own = jnp.where((first >= 0) & (first < rank), row, 0.0)
    return sum((pltpu.roll(own, k * rank, 1) for k in range(1, LANES // rank)), own)


def halves(value):
    high = value.astype(BF16)
    return high, (value - high.astype(F32)).astype(BF16)


def product(left, right_high, right_low, side=0):
    rows = left.shape[0]
    high, low = halves(left)
    dims = (((1,), (side,)), ((), ()))
    both = lax.dot_general(jnp.concatenate([high, low], axis=0), right_high, dims, preferred_element_type=F32)
    return both[:rows] + (both[rows:] + lax.dot_general(high, right_low, dims, preferred_element_type=F32))


def coded(value):
    exponent = jnp.ceil(jnp.log2(jnp.maximum(jnp.abs(value), 1e-30)))
    return (value * jnp.exp2(-exponent) * ONE).astype(jnp.int32), exponent.astype(jnp.int32)


def decoded(mantissa, exponent):
    return mantissa.astype(F32) * (1.0 / ONE) * jnp.exp2(exponent.astype(F32))


def packed(field):
    top = jnp.max(jnp.abs(field), axis=1, keepdims=True)
    step = jnp.maximum(top, 1e-30) * (1.0 / TOP)
    codes = jnp.floor(field * (1.0 / step) + 0.5).astype(jnp.int32)
    width = field.shape[1] // 2
    return (codes[:, :width] << 16) | (codes[:, width:] & 0xFFFF), step


def unpacked(words):
    return jnp.concatenate([words >> 16, (words << 16) >> 16], axis=1).astype(F32)


def fetch(pairs, sems):
    copies = [pltpu.make_async_copy(a, b, sems.at[i]) for i, (a, b) in enumerate(pairs)]
    for copy in copies:
        copy.start()
    return copies


def put_message(field, columns, cols, couple, masks_ref, sent_ref):
    nrhs, rank = field.shape[0], cols[0].shape[0]
    unit = term_unit(field.shape[1], rank)
    proj = product(field, cols[0][...], cols[1][...], 1)
    wide = jnp.concatenate([proj] * CHUNK, axis=1)
    words, step = packed(field)
    width = words.shape[1]
    row = stats_row(columns, rank, step)
    finer = 1.0 / (steps_of(row, rank) * unit)
    for i in range(sent_ref.shape[0]):
        sent_ref[i, :, :width] = words
    stats = [jnp.broadcast_to(a, (CHUNK, LANES)) for a in coded(row)]
    for start in range(0, sent_ref.shape[0], CHUNK):
        mask = masks_ref[pl.ds(start, CHUNK), :]
        spread = jnp.concatenate([mask * wide[r : r + 1] for r in range(nrhs)], axis=0)
        here = pl.ds(start * rank, CHUNK * rank)
        terms = product(spread, couple[0][here, :], couple[1][here, :])
        terms = jnp.concatenate([terms[r * CHUNK : (r + 1) * CHUNK] for r in range(nrhs)], axis=1)
        here = pl.ds(start, CHUNK)
        for k, value in enumerate([(terms * finer).astype(jnp.int32)] + stats + [stats[0]] * (nrhs - 3)):
            sent_ref[here, k, width:] = value


def message_parts(got_ref, rank):
    width = got_ref.shape[2] - LANES
    stats = decoded(got_ref[:, 1, width:], got_ref[:, 2, width:])
    terms = got_ref[:, 0, width:].astype(F32) * (steps_of(stats, rank) * term_unit(2 * width, rank))
    return total(terms), stats


def window_parts(got_ref, rank):
    nrhs, width = got_ref.shape[1], got_ref.shape[2] - LANES
    strips = got_ref.shape[0] // CORES
    shape = (CORES * nrhs, LANES)
    for step in range(3):
        owner = lax.axis_index("strip") + (step - 1)
        inside = (owner >= 0) & (owner < strips)
        owner = CORES * jnp.clip(owner, 0, strips - 1)
        words = jnp.concatenate([got_ref[owner + core, :, :width] for core in range(CORES)], axis=0)
        tails = [got_ref[owner + core, :, width:] for core in range(CORES)]
        rows = [decoded(tail[1:2], tail[2:3]) for tail in tails]
        rows = jnp.where(rows_of(shape) < nrhs, rows[0], rows[1])
        wanted = lanes_of(shape) == rank * lax.rem(rows_of(shape), nrhs) + STEP
        yield inside, unpacked(words), jnp.sum(jnp.where(wanted, rows, 0.0), axis=1, keepdims=True)


def put_blocks(part, first, window):
    part = part.astype(BF16).astype(F32)
    for c in range(part.shape[1] // LANES):
        window[first + c] = part[:, c * LANES : (c + 1) * LANES]


def near_field(window, tiles, list_ref, sums, nrhs):
    for held in sums:
        held[...] = jnp.zeros_like(held)
    n = 0
    for tiles_ref in tiles:
        for first in range(0, tiles_ref.shape[0], 2):
            left = jnp.concatenate([window[list_ref[1, n + i]] for i in range(2)], axis=0).astype(BF16)
            right = jnp.concatenate([tiles_ref[first + i] for i in range(2)], axis=1)
            both = jnp.dot(left, right, preferred_element_type=F32)
            rows = window.shape[1]
            for i in range(2):
                held = sums[(n + i) % len(sums)]
                held[list_ref[0, n + i]] += both[i * rows : (i + 1) * rows, i * LANES : (i + 1) * LANES]
            n += 2
    whole = sum((held[...] for held in sums[1:]), sums[0][...])
    rows = whole.shape[0] // CORES
    return jnp.concatenate([whole[b, :nrhs] + whole[rows + b, nrhs:] for b in range(rows)], axis=1)


def start_kernel(
    loads_hbm, cols_hbm, couple_hbm, ranks_hbm, list_hbm, rows_hbm, self_hbm, tiles_hbm, sent_ref, cols_high, cols_low, couple_high,
    couple_low, masks_ref, rows_high, rows_low, list_ref, loads_ref, self_ref, tiles_ref, cols_ref, couple_ref, ranks_ref, raw_ref,
    rows_ref, sems,
):
    rank, panels = cols_ref.shape
    pairs = (
        (loads_hbm, loads_ref), (cols_hbm, cols_ref), (couple_hbm, couple_ref), (ranks_hbm, ranks_ref),
        (list_hbm, raw_ref), (rows_hbm, rows_ref), (self_hbm, self_ref),
    )
    every = tiles_ref.shape[0] // PIECES
    pieces = [pl.ds(i * every, every) for i in range(PIECES)]
    copies = fetch(pairs + tuple((tiles_hbm.at[p], tiles_ref.at[p]) for p in pieces), sems)
    copies[0].wait()
    loads = loads_ref[...]
    square = jnp.sum(loads * loads, axis=1, keepdims=True)
    copies[1].wait()
    cols_high[...], cols_low[...] = halves(cols_ref[...])
    copies[2].wait()
    couple_high[...], couple_low[...] = halves(couple_ref[...])
    copies[3].wait()
    shape = (CHUNK, CHUNK * rank)
    owner = lax.div(lanes_of(shape), rank)
    inner = lax.rem(lanes_of(shape), rank)
    for start in range(0, masks_ref.shape[0], CHUNK):
        limit = jnp.zeros((1, CHUNK * rank), jnp.int32)
        for i in range(CHUNK):
            limit = jnp.where(owner[:1] == i, ranks_ref[0, start + i], limit)
        masks_ref[pl.ds(start, CHUNK), :] = jnp.where((owner == rows_of(shape)) & (inner < limit), 1.0, 0.0)
    copies[4].wait()
    count = panels // LANES
    target, source = raw_ref[0:1, :], raw_ref[1:2, :]
    group, block = lax.div(source, count), lax.rem(source, count)
    strip, core = lax.div(group, CORES), lax.rem(group, CORES)
    list_ref[...] = jnp.concatenate([core * count + target, strip * count + block], axis=0)
    copies[5].wait()
    rows_high[...], rows_low[...] = halves(rows_ref[...])
    put_message(loads, [square], (cols_high, cols_low), (couple_high, couple_low), masks_ref, sent_ref)
    for copy in copies[6:]:
        copy.wait()


def image_of(field, far, self_ref, far_rows, near):
    rank = far_rows[0].shape[0]
    return self_ref[...] * field + near + product(far[:, :rank], far_rows[0][...], far_rows[1][...])


def step0_kernel(
    got_ref, loads_ref, cols_high, cols_low, couple_high, couple_low, masks_ref, rows_high, rows_low, self_ref,
    tiles_ref, list_vmem, sent_ref, image_ref, window0_ref, state_ref, list_ref, sems, window, *sums,
):
    rank = rows_high.shape[0]
    nrhs, panels = loads_ref.shape
    span, rows = panels // LANES, CORES * nrhs
    (copy,) = fetch(((list_vmem, list_ref),), sems)
    terms, stats = message_parts(got_ref, rank)
    beta = jnp.sqrt(stat_column(total(stats), 0, nrhs, rank))
    scale = 1.0 / beta
    both = jnp.concatenate([scale] * CORES, axis=0)
    for step, (inside, part, unit) in enumerate(window_parts(got_ref, rank)):
        part = jnp.where(inside, part * (unit * both), 0.0)
        window0_ref[step * rows : (step + 1) * rows, :] = part
        put_blocks(part, step * span, window)
    basis = loads_ref[...] * scale
    far = far_sum_of(terms, nrhs, rank) * scale
    copy.wait()
    near = near_field(window, (tiles_ref,), list_ref, sums, nrhs)
    image = image_of(basis, far, self_ref, (rows_high, rows_low), near)
    image_ref[...] = image
    state_ref[...] = jnp.concatenate([far, jnp.broadcast_to(beta, far.shape)], axis=0)
    norm = jnp.sum(basis * basis, axis=1, keepdims=True)
    dot = jnp.sum(basis * image, axis=1, keepdims=True)
    share = jnp.where(norm > 0, dot / jnp.where(norm > 0, norm, 1.0), 0.0)
    rest = image - share * basis
    rest = jnp.sum(rest * rest, axis=1, keepdims=True)
    columns = [norm, dot, share, rest]
    put_message(image, columns, (cols_high, cols_low), (couple_high, couple_low), masks_ref, sent_ref)


def step1_kernel(
    got_ref, loads_ref, image_ref, window0_ref, state_ref, rows_high, rows_low, self_ref, tiles_ref,
    list_vmem, sent_ref, basis_ref, coeff_ref, list_ref, sems, window, *sums,
):
    rank = rows_high.shape[0]
    nrhs, panels = loads_ref.shape
    span, rows = panels // LANES, CORES * nrhs
    (copy,) = fetch(((list_vmem, list_ref),), sems)
    beta = state_ref[nrhs:, :1]
    far0 = state_ref[:nrhs, :]
    terms, stats = message_parts(got_ref, rank)
    summed = total(stats)
    h00 = stat_column(summed, 1, nrhs, rank)
    away = shifted(stats, 2) - shifted(summed, 1)
    rest = total(shifted(stats, 3) + stats * away * away)
    h10 = jnp.sqrt(stat_column(rest, 0, nrhs, rank))
    scale = 1.0 / h10
    both, both_h00 = (jnp.concatenate([a] * CORES, axis=0) for a in (scale, h00))
    for step, (inside, part, unit) in enumerate(window_parts(got_ref, rank)):
        part = (part * unit - both_h00 * window0_ref[step * rows : (step + 1) * rows, :]) * both
        put_blocks(jnp.where(inside, part, 0.0), step * span, window)
    basis0 = loads_ref[...] * (1.0 / beta)
    basis1 = (image_ref[...] - h00 * basis0) * scale
    far = (far_sum_of(terms, nrhs, rank) - h00 * far0) * scale
    copy.wait()
    near = near_field(window, (tiles_ref,), list_ref, sums, nrhs)
    image = image_of(basis1, far, self_ref, (rows_high, rows_low), near)
    columns = [jnp.sum(a * image, axis=1, keepdims=True) for a in (basis0, basis1, image)]
    sent_ref[:, 0, :] = jnp.broadcast_to(stats_row(columns, rank), (sent_ref.shape[0], LANES))
    basis_ref[...] = jnp.concatenate([basis0, basis1], axis=0)
    coeff_ref[...] = jnp.concatenate([jnp.broadcast_to(v, (nrhs, LANES)) for v in (beta, h00, h10)], axis=0)


def finish_kernel(rank, got_ref, basis_ref, coeff_ref, out_ref):
    nrhs = out_ref.shape[0]
    row = total(got_ref[:, 0, :])
    h01, h11, gram11 = (stat_column(row, k, nrhs, rank) for k in range(3))
    beta, h00, h10 = (coeff_ref[k * nrhs : (k + 1) * nrhs, :1] for k in range(3))
    gram00 = h00 * h00 + h10 * h10
    gram01 = h00 * h01 + h10 * h11
    lower00 = jnp.sqrt(gram00)
    lower10 = gram01 / lower00
    lower11 = jnp.sqrt(gram11 - lower10 * lower10)
    middle0 = beta * h00 / lower00
    middle1 = (beta * h01 - lower10 * middle0) / lower11
    y1 = middle1 / lower11
    y0 = (middle0 - lower10 * y1) / lower00
    out_ref[...] = y0 * basis_ref[:nrhs, :] + y1 * basis_ref[nrhs:, :]


class Plain(jax.ShapeDtypeStruct):
    pass


def in_vmem_like(array):
    return pltpu.VMEM(array.shape, array.dtype)


def in_vmem(arrays):
    return [pltpu.with_memory_space_constraint(a, pltpu.VMEM) for a in arrays]


def call(kernel, args, outs, scratch=(), held=()):
    args = [pltpu.with_memory_space_constraint(a, pltpu.HBM) if i in held else a for i, a in enumerate(args)]
    moved = sum(a.size * a.dtype.itemsize for a in args)
    return pl.pallas_call(
        kernel,
        out_shape=[
            jax.ShapeDtypeStruct(out, F32) if isinstance(out, tuple) else out if isinstance(out, Plain) else in_vmem_like(out)
            for out in outs
        ],
        in_specs=[pl.BlockSpec(memory_space=pl.ANY if i in held else pltpu.VMEM) for i in range(len(args))],
        out_specs=[pl.BlockSpec(memory_space=pltpu.VMEM)] * len(outs),
        scratch_shapes=list(scratch),
        compiler_params=pltpu.CompilerParams(vmem_limit_bytes=24 * 2**20),
        cost_estimate=pl.CostEstimate(flops=0, bytes_accessed=moved, transcendentals=0),
    )(*args)


def exchanged(sent):
    return lax.all_to_all(sent, GROUP, 0, 0, tiled=True)


def body(loads, self_term, near_tiles, near_list, far_rows, far_cols, coupling, ranks):
    nrhs, panels = loads.shape
    rank = far_cols.shape[0]
    blocks, tile = near_tiles.shape[:2]
    rows = panels // tile
    strips = coupling.shape[0] // CORES
    couple = coupling.reshape(CORES * strips * rank, rank)
    near_list = near_list.T
    ranks = ranks.reshape(1, CORES * strips)
    self_term = self_term.reshape(1, panels)
    groups = CORES * strips
    message = Plain((groups, nrhs, panels // 2 + LANES), jnp.int32)
    index = pltpu.SMEM(near_list.shape, jnp.int32)
    scratch = [index, pltpu.SemaphoreType.DMA((1,)), pltpu.VMEM((3 * rows, CORES * nrhs, tile), F32)]
    scratch += [pltpu.VMEM((CORES * rows, CORES * nrhs, tile), F32)] * 4

    def twice(array):
        return [jax.ShapeDtypeStruct(array.shape, BF16)] * 2

    sent, *held, near_list, loads, self_term, near_tiles = call(
        start_kernel,
        (loads, far_cols, couple, ranks, near_list, far_rows, self_term, near_tiles),
        [
            message, *twice(far_cols), *twice(couple), jax.ShapeDtypeStruct((groups, CHUNK * rank), F32),
            *twice(far_rows), near_list, loads, self_term, near_tiles,
        ],
        [
            pltpu.VMEM(far_cols.shape, F32), pltpu.VMEM(couple.shape, F32), pltpu.SMEM(ranks.shape, jnp.int32),
            pltpu.VMEM(near_list.shape, jnp.int32), pltpu.VMEM(far_rows.shape, F32), pltpu.SemaphoreType.DMA((7 + PIECES,)),
        ],
        held=range(8),
    )
    loads, *held, self_term, near_tiles, near_list = in_vmem([loads, *held, self_term, near_tiles, near_list])
    source_side, target_side = [loads, *held[:5]], [*held[5:], self_term, near_tiles, near_list]
    sent, image, window0, state = call(
        step0_kernel,
        (exchanged(sent), *source_side, *target_side),
        [message, loads.shape, (3 * CORES * nrhs, panels), (CORES * nrhs, LANES)],
        scratch,
    )
    sent, basis, coeff = call(
        step1_kernel,
        (exchanged(sent), loads, image, window0, state, *target_side),
        [(groups, 1, LANES), (2 * nrhs, panels), (3 * nrhs, LANES)],
        scratch,
    )
    return call(functools.partial(finish_kernel, rank), (exchanged(sent), basis, coeff), [loads.shape])[0]


def solution(mesh):
    every = ("case",) + GROUP
    in_specs = (
        P(None, every),
        P(every),
        P(every, None, None),
        P(every, None),
        P(None, every),
        P(None, every),
        P(None, GROUP, None, None),
        P(None, GROUP),
    )
    return jax.shard_map(body, mesh=mesh, in_specs=in_specs, out_specs=P(None, every), check_vma=False)
```

```python
import functools

import jax
import jax.numpy as jnp
from jax import lax
from jax.experimental import pallas as pl
from jax.experimental.pallas import tpu as pltpu
from jax.sharding import PartitionSpec as P

GROUP = ("strip", "clus")
CORES = 2
LANES = 128
CHUNK = 16
PIECES = 5
F32 = jnp.float32
BF16 = jnp.bfloat16

STEP = 8
COLS_TOP = 0.1875
COUPLE_TOP = 0.375
TOP = 32767.0
ONE = float(2**30)


def lanes_of(shape):
    return lax.broadcasted_iota(jnp.int32, shape, 1)


def rows_of(shape):
    return lax.broadcasted_iota(jnp.int32, shape, 0)


def total(rows):
    return jnp.sum(rows, axis=0, keepdims=True)


def stats_row(columns, rank, step=None):
    shape = (columns[0].shape[0], LANES)
    first = lanes_of(shape) - rank * rows_of(shape)
    spread = sum(jnp.where(first == k, column, 0.0) for k, column in enumerate(columns))
    if step is not None:
        spread = jnp.where((first >= STEP) & (first < rank), step, spread)
    return total(spread)


def steps_of(stats, rank):
    inner = lax.rem(lanes_of(stats.shape), rank)
    return jnp.where(inner < STEP, shifted(stats, STEP), stats)


def term_unit(panels, rank):
    return panels * rank * COLS_TOP * COUPLE_TOP * TOP / ONE


def stat_column(row, k, nrhs, rank):
    shape = (nrhs, LANES)
    first = lanes_of(shape) - rank * rows_of(shape)
    return jnp.sum(jnp.where(first == k, row, 0.0), axis=1, keepdims=True)


def shifted(value, k):
    return pltpu.roll(value, LANES - k, 1)


def far_sum_of(row, nrhs, rank):
    shape = (nrhs, LANES)
    first = lanes_of(shape) - rank * rows_of(shape)
    own = jnp.where((first >= 0) & (first < rank), row, 0.0)
    return sum((pltpu.roll(own, k * rank, 1) for k in range(1, LANES // rank)), own)


def halves(value):
    high = value.astype(BF16)
    return high, (value - high.astype(F32)).astype(BF16)


def product(left, right_high, right_low, side=0):
    rows = left.shape[0]
    high, low = halves(left)
    dims = (((1,), (side,)), ((), ()))
    both = lax.dot_general(jnp.concatenate([high, low], axis=0), right_high, dims, preferred_element_type=F32)
    return both[:rows] + (both[rows:] + lax.dot_general(high, right_low, dims, preferred_element_type=F32))


def coded(value):
    exponent = jnp.ceil(jnp.log2(jnp.maximum(jnp.abs(value), 1e-30)))
    return (value * jnp.exp2(-exponent) * ONE).astype(jnp.int32), exponent.astype(jnp.int32)


def decoded(mantissa, exponent):
    return mantissa.astype(F32) * (1.0 / ONE) * jnp.exp2(exponent.astype(F32))


def packed(field):
    top = jnp.max(jnp.abs(field), axis=1, keepdims=True)
    step = jnp.maximum(top, 1e-30) * (1.0 / TOP)
    codes = jnp.floor(field * (1.0 / step) + 0.5).astype(jnp.int32)
    width = field.shape[1] // 2
    return (codes[:, :width] << 16) | (codes[:, width:] & 0xFFFF), step


def unpacked(words):
    return jnp.concatenate([words >> 16, (words << 16) >> 16], axis=1).astype(F32)


def fetch(pairs, sems):
    copies = [pltpu.make_async_copy(a, b, sems.at[i]) for i, (a, b) in enumerate(pairs)]
    for copy in copies:
        copy.start()
    return copies


def put_message(field, columns, cols, couple, masks_ref, sent_ref):
    nrhs, rank = field.shape[0], cols[0].shape[0]
    unit = term_unit(field.shape[1], rank)
    proj = product(field, cols[0][...], cols[1][...], 1)
    wide = jnp.concatenate([proj] * CHUNK, axis=1)
    words, step = packed(field)
    width = words.shape[1]
    row = stats_row(columns, rank, step)
    finer = 1.0 / (steps_of(row, rank) * unit)
    for i in range(sent_ref.shape[0]):
        sent_ref[i, :, :width] = words
    stats = [jnp.broadcast_to(a, (CHUNK, LANES)) for a in coded(row)]
    for start in range(0, sent_ref.shape[0], CHUNK):
        mask = masks_ref[pl.ds(start, CHUNK), :]
        spread = jnp.concatenate([mask * wide[r : r + 1] for r in range(nrhs)], axis=0)
        here = pl.ds(start * rank, CHUNK * rank)
        terms = product(spread, couple[0][here, :], couple[1][here, :])
        terms = jnp.concatenate([terms[r * CHUNK : (r + 1) * CHUNK] for r in range(nrhs)], axis=1)
        here = pl.ds(start, CHUNK)
        for k, value in enumerate([(terms * finer).astype(jnp.int32)] + stats + [stats[0]] * (nrhs - 3)):
            sent_ref[here, k, width:] = value


def message_parts(got_ref, rank):
    width = got_ref.shape[2] - LANES
    stats = decoded(got_ref[:, 1, width:], got_ref[:, 2, width:])
    terms = got_ref[:, 0, width:].astype(F32) * (steps_of(stats, rank) * term_unit(2 * width, rank))
    return total(terms), stats


def window_parts(got_ref, rank):
    nrhs, width = got_ref.shape[1], got_ref.shape[2] - LANES
    strips = got_ref.shape[0] // CORES
    shape = (CORES * nrhs, LANES)
    for step in range(3):
        owner = lax.axis_index("strip") + (step - 1)
        inside = (owner >= 0) & (owner < strips)
        owner = CORES * jnp.clip(owner, 0, strips - 1)
        words = jnp.concatenate([got_ref[owner + core, :, :width] for core in range(CORES)], axis=0)
        tails = [got_ref[owner + core, :, width:] for core in range(CORES)]
        rows = [decoded(tail[1:2], tail[2:3]) for tail in tails]
        rows = jnp.where(rows_of(shape) < nrhs, rows[0], rows[1])
        wanted = lanes_of(shape) == rank * lax.rem(rows_of(shape), nrhs) + STEP
        yield inside, unpacked(words), jnp.sum(jnp.where(wanted, rows, 0.0), axis=1, keepdims=True)


def put_blocks(part, first, window):
    part = part.astype(BF16).astype(F32)
    for c in range(part.shape[1] // LANES):
        window[first + c] = part[:, c * LANES : (c + 1) * LANES]


def near_field(window, tiles, list_ref, sums, nrhs):
    for held in sums:
        held[...] = jnp.zeros_like(held)
    n = 0
    for tiles_ref in tiles:
        for first in range(0, tiles_ref.shape[0], 2):
            left = jnp.concatenate([window[list_ref[1, n + i]] for i in range(2)], axis=0).astype(BF16)
            right = jnp.concatenate([tiles_ref[first + i] for i in range(2)], axis=1)
            both = jnp.dot(left, right, preferred_element_type=F32)
            rows = window.shape[1]
            for i in range(2):
                held = sums[(n + i) % len(sums)]
                held[list_ref[0, n + i]] += both[i * rows : (i + 1) * rows, i * LANES : (i + 1) * LANES]
            n += 2
    whole = sum((held[...] for held in sums[1:]), sums[0][...])
    rows = whole.shape[0] // CORES
    return jnp.concatenate([whole[b, :nrhs] + whole[rows + b, nrhs:] for b in range(rows)], axis=1)


def start_kernel(
    loads_hbm, cols_hbm, couple_hbm, ranks_hbm, list_hbm, rows_hbm, self_hbm, tiles_hbm, sent_ref, cols_high, cols_low, couple_high,
    couple_low, masks_ref, rows_high, rows_low, list_ref, loads_ref, self_ref, tiles_ref, cols_ref, couple_ref, ranks_ref, raw_ref,
    rows_ref, sems,
):
    rank, panels = cols_ref.shape
    pairs = (
        (loads_hbm, loads_ref), (cols_hbm, cols_ref), (couple_hbm, couple_ref), (ranks_hbm, ranks_ref),
        (list_hbm, raw_ref), (rows_hbm, rows_ref), (self_hbm, self_ref),
    )
    every = tiles_ref.shape[0] // PIECES
    pieces = [pl.ds(i * every, every) for i in range(PIECES)]
    copies = fetch(pairs + tuple((tiles_hbm.at[p], tiles_ref.at[p]) for p in pieces), sems)
    for copy in copies[: len(pairs)]:
        copy.wait()
    loads = loads_ref[...]
    square = jnp.sum(loads * loads, axis=1, keepdims=True)
    cols_high[...], cols_low[...] = halves(cols_ref[...])
    couple_high[...], couple_low[...] = halves(couple_ref[...])
    shape = (CHUNK, CHUNK * rank)
    owner = lax.div(lanes_of(shape), rank)
    inner = lax.rem(lanes_of(shape), rank)
    for start in range(0, masks_ref.shape[0], CHUNK):
        limit = jnp.zeros((1, CHUNK * rank), jnp.int32)
        for i in range(CHUNK):
            limit = jnp.where(owner[:1] == i, ranks_ref[0, start + i], limit)
        masks_ref[pl.ds(start, CHUNK), :] = jnp.where((owner == rows_of(shape)) & (inner < limit), 1.0, 0.0)
    put_message(loads, [square], (cols_high, cols_low), (couple_high, couple_low), masks_ref, sent_ref)
    count = panels // LANES
    target, source = raw_ref[0:1, :], raw_ref[1:2, :]
    group, block = lax.div(source, count), lax.rem(source, count)
    strip, core = lax.div(group, CORES), lax.rem(group, CORES)
    list_ref[...] = jnp.concatenate([core * count + target, strip * count + block], axis=0)
    rows_high[...], rows_low[...] = halves(rows_ref[...])
    for copy in copies[len(pairs) :]:
        copy.wait()


def far_field(far, far_rows):
    return product(far[:, : far_rows[0].shape[0]], far_rows[0][...], far_rows[1][...])


def step0_kernel(
    got_ref, loads_ref, cols_high, cols_low, couple_high, couple_low, masks_ref, rows_high, rows_low, self_ref,
    tiles_ref, list_vmem, sent_ref, image_ref, window0_ref, state_ref, list_ref, sems, window, *sums,
):
    rank = rows_high.shape[0]
    nrhs, panels = loads_ref.shape
    span, rows = panels // LANES, CORES * nrhs
    (copy,) = fetch(((list_vmem, list_ref),), sems)
    terms, stats = message_parts(got_ref, rank)
    beta = jnp.sqrt(stat_column(total(stats), 0, nrhs, rank))
    scale = 1.0 / beta
    both = jnp.concatenate([scale] * CORES, axis=0)
    for step, (inside, part, unit) in enumerate(window_parts(got_ref, rank)):
        part = jnp.where(inside, part * (unit * both), 0.0)
        window0_ref[step * rows : (step + 1) * rows, :] = part
        put_blocks(part, step * span, window)
    basis = loads_ref[...] * scale
    far = far_sum_of(terms, nrhs, rank) * scale
    image = self_ref[...] * basis + far_field(far, (rows_high, rows_low))
    norm = jnp.sum(basis * basis, axis=1, keepdims=True)
    copy.wait()
    image = image + near_field(window, (tiles_ref,), list_ref, sums, nrhs)
    image_ref[...] = image
    state_ref[...] = jnp.concatenate([far, jnp.broadcast_to(beta, far.shape)], axis=0)
    dot = jnp.sum(basis * image, axis=1, keepdims=True)
    share = jnp.where(norm > 0, dot / jnp.where(norm > 0, norm, 1.0), 0.0)
    rest = image - share * basis
    rest = jnp.sum(rest * rest, axis=1, keepdims=True)
    columns = [norm, dot, share, rest]
    put_message(image, columns, (cols_high, cols_low), (couple_high, couple_low), masks_ref, sent_ref)


def step1_kernel(
    got_ref, loads_ref, image_ref, window0_ref, state_ref, rows_high, rows_low, self_ref, tiles_ref,
    list_vmem, sent_ref, basis_ref, coeff_ref, list_ref, sems, window, *sums,
):
    rank = rows_high.shape[0]
    nrhs, panels = loads_ref.shape
    span, rows = panels // LANES, CORES * nrhs
    (copy,) = fetch(((list_vmem, list_ref),), sems)
    beta = state_ref[nrhs:, :1]
    far0 = state_ref[:nrhs, :]
    terms, stats = message_parts(got_ref, rank)
    summed = total(stats)
    h00 = stat_column(summed, 1, nrhs, rank)
    away = shifted(stats, 2) - shifted(summed, 1)
    rest = total(shifted(stats, 3) + stats * away * away)
    h10 = jnp.sqrt(stat_column(rest, 0, nrhs, rank))
    scale = 1.0 / h10
    both, both_h00 = (jnp.concatenate([a] * CORES, axis=0) for a in (scale, h00))
    for step, (inside, part, unit) in enumerate(window_parts(got_ref, rank)):
        part = (part * unit - both_h00 * window0_ref[step * rows : (step + 1) * rows, :]) * both
        put_blocks(jnp.where(inside, part, 0.0), step * span, window)
    basis0 = loads_ref[...] * (1.0 / beta)
    basis1 = (image_ref[...] - h00 * basis0) * scale
    far = (far_sum_of(terms, nrhs, rank) - h00 * far0) * scale
    image = self_ref[...] * basis1 + far_field(far, (rows_high, rows_low))
    copy.wait()
    image = image + near_field(window, (tiles_ref,), list_ref, sums, nrhs)
    columns = [jnp.sum(a * image, axis=1, keepdims=True) for a in (basis0, basis1, image)]
    sent_ref[:, 0, :] = jnp.broadcast_to(stats_row(columns, rank), (sent_ref.shape[0], LANES))
    basis_ref[...] = jnp.concatenate([basis0, basis1], axis=0)
    coeff_ref[...] = jnp.concatenate([jnp.broadcast_to(v, (nrhs, LANES)) for v in (beta, h00, h10)], axis=0)


def finish_kernel(rank, got_ref, basis_ref, coeff_ref, out_ref):
    nrhs = out_ref.shape[0]
    row = total(got_ref[:, 0, :])
    h01, h11, gram11 = (stat_column(row, k, nrhs, rank) for k in range(3))
    beta, h00, h10 = (coeff_ref[k * nrhs : (k + 1) * nrhs, :1] for k in range(3))
    gram00 = h00 * h00 + h10 * h10
    gram01 = h00 * h01 + h10 * h11
    lower00 = jnp.sqrt(gram00)
    lower10 = gram01 / lower00
    lower11 = jnp.sqrt(gram11 - lower10 * lower10)
    middle0 = beta * h00 / lower00
    middle1 = (beta * h01 - lower10 * middle0) / lower11
    y1 = middle1 / lower11
    y0 = (middle0 - lower10 * y1) / lower00
    out_ref[...] = y0 * basis_ref[:nrhs, :] + y1 * basis_ref[nrhs:, :]


class Plain(jax.ShapeDtypeStruct):
    pass


def in_vmem_like(array):
    return pltpu.VMEM(array.shape, array.dtype)


def in_vmem(arrays):
    return [pltpu.with_memory_space_constraint(a, pltpu.VMEM) for a in arrays]


def call(kernel, args, outs, scratch=(), held=()):
    args = [pltpu.with_memory_space_constraint(a, pltpu.HBM) if i in held else a for i, a in enumerate(args)]
    moved = sum(a.size * a.dtype.itemsize for a in args)
    return pl.pallas_call(
        kernel,
        out_shape=[
            jax.ShapeDtypeStruct(out, F32) if isinstance(out, tuple) else out if isinstance(out, Plain) else in_vmem_like(out)
            for out in outs
        ],
        in_specs=[pl.BlockSpec(memory_space=pl.ANY if i in held else pltpu.VMEM) for i in range(len(args))],
        out_specs=[pl.BlockSpec(memory_space=pltpu.VMEM)] * len(outs),
        scratch_shapes=list(scratch),
        compiler_params=pltpu.CompilerParams(vmem_limit_bytes=24 * 2**20),
        cost_estimate=pl.CostEstimate(flops=0, bytes_accessed=moved, transcendentals=0),
    )(*args)


def exchanged(sent):
    return lax.all_to_all(sent, GROUP, 0, 0, tiled=True)


def body(loads, self_term, near_tiles, near_list, far_rows, far_cols, coupling, ranks):
    nrhs, panels = loads.shape
    rank = far_cols.shape[0]
    blocks, tile = near_tiles.shape[:2]
    rows = panels // tile
    strips = coupling.shape[0] // CORES
    couple = coupling.reshape(CORES * strips * rank, rank)
    near_list = near_list.T
    ranks = ranks.reshape(1, CORES * strips)
    self_term = self_term.reshape(1, panels)
    groups = CORES * strips
    message = Plain((groups, nrhs, panels // 2 + LANES), jnp.int32)
    index = pltpu.SMEM(near_list.shape, jnp.int32)
    scratch = [index, pltpu.SemaphoreType.DMA((1,)), pltpu.VMEM((3 * rows, CORES * nrhs, tile), F32)]
    scratch += [pltpu.VMEM((CORES * rows, CORES * nrhs, tile), F32)] * 4

    def twice(array):
        return [jax.ShapeDtypeStruct(array.shape, BF16)] * 2

    sent, *held, near_list, loads, self_term, near_tiles = call(
        start_kernel,
        (loads, far_cols, couple, ranks, near_list, far_rows, self_term, near_tiles),
        [
            message, *twice(far_cols), *twice(couple), jax.ShapeDtypeStruct((groups, CHUNK * rank), F32),
            *twice(far_rows), near_list, loads, self_term, near_tiles,
        ],
        [
            pltpu.VMEM(far_cols.shape, F32), pltpu.VMEM(couple.shape, F32), pltpu.SMEM(ranks.shape, jnp.int32),
            pltpu.VMEM(near_list.shape, jnp.int32), pltpu.VMEM(far_rows.shape, F32), pltpu.SemaphoreType.DMA((7 + PIECES,)),
        ],
        held=range(8),
    )
    loads, *held, self_term, near_tiles, near_list = in_vmem([loads, *held, self_term, near_tiles, near_list])
    source_side, target_side = [loads, *held[:5]], [*held[5:], self_term, near_tiles, near_list]
    sent, image, window0, state = call(
        step0_kernel,
        (exchanged(sent), *source_side, *target_side),
        [message, loads.shape, (3 * CORES * nrhs, panels), (CORES * nrhs, LANES)],
        scratch,
    )
    sent, basis, coeff = call(
        step1_kernel,
        (exchanged(sent), loads, image, window0, state, *target_side),
        [(groups, 1, LANES), (2 * nrhs, panels), (3 * nrhs, LANES)],
        scratch,
    )
    return call(functools.partial(finish_kernel, rank), (exchanged(sent), basis, coeff), [loads.shape])[0]


def solution(mesh):
    every = ("case",) + GROUP
    in_specs = (
        P(None, every),
        P(every),
        P(every, None, None),
        P(every, None),
        P(None, every),
        P(None, every),
        P(None, GROUP, None, None),
        P(None, GROUP),
    )
    return jax.shard_map(body, mesh=mesh, in_specs=in_specs, out_specs=P(None, every), check_vma=False)
```

```python
import functools

import jax
import jax.numpy as jnp
from jax import lax
from jax.experimental import pallas as pl
from jax.experimental.pallas import tpu as pltpu
from jax.sharding import PartitionSpec as P

GROUP = ("strip", "clus")
CORES = 2
LANES = 128
CHUNK = 16
PIECES = 10
F32 = jnp.float32
BF16 = jnp.bfloat16

STEP = 8
COLS_TOP = 0.1875
COUPLE_TOP = 0.375
TOP = 32767.0
ONE = float(2**30)


def lanes_of(shape):
    return lax.broadcasted_iota(jnp.int32, shape, 1)


def rows_of(shape):
    return lax.broadcasted_iota(jnp.int32, shape, 0)


def total(rows):
    return jnp.sum(rows, axis=0, keepdims=True)


def stats_row(columns, rank, step=None):
    shape = (columns[0].shape[0], LANES)
    first = lanes_of(shape) - rank * rows_of(shape)
    spread = sum(jnp.where(first == k, column, 0.0) for k, column in enumerate(columns))
    if step is not None:
        spread = jnp.where((first >= STEP) & (first < rank), step, spread)
    return total(spread)


def steps_of(stats, rank):
    inner = lax.rem(lanes_of(stats.shape), rank)
    return jnp.where(inner < STEP, shifted(stats, STEP), stats)


def term_unit(panels, rank):
    return panels * rank * COLS_TOP * COUPLE_TOP * TOP / ONE


def stat_column(row, k, nrhs, rank):
    shape = (nrhs, LANES)
    first = lanes_of(shape) - rank * rows_of(shape)
    return jnp.sum(jnp.where(first == k, row, 0.0), axis=1, keepdims=True)


def shifted(value, k):
    return pltpu.roll(value, LANES - k, 1)


def far_sum_of(row, nrhs, rank):
    shape = (nrhs, LANES)
    first = lanes_of(shape) - rank * rows_of(shape)
    own = jnp.where((first >= 0) & (first < rank), row, 0.0)
    return sum((pltpu.roll(own, k * rank, 1) for k in range(1, LANES // rank)), own)


def halves(value):
    high = value.astype(BF16)
    return high, (value - high.astype(F32)).astype(BF16)


def product(left, right_high, right_low, side=0):
    rows = left.shape[0]
    high, low = halves(left)
    dims = (((1,), (side,)), ((), ()))
    both = lax.dot_general(jnp.concatenate([high, low], axis=0), right_high, dims, preferred_element_type=F32)
    return both[:rows] + (both[rows:] + lax.dot_general(high, right_low, dims, preferred_element_type=F32))


def coded(value):
    exponent = jnp.ceil(jnp.log2(jnp.maximum(jnp.abs(value), 1e-30)))
    return (value * jnp.exp2(-exponent) * ONE).astype(jnp.int32), exponent.astype(jnp.int32)


def decoded(mantissa, exponent):
    return mantissa.astype(F32) * (1.0 / ONE) * jnp.exp2(exponent.astype(F32))


def packed(field):
    top = jnp.max(jnp.abs(field), axis=1, keepdims=True)
    step = jnp.maximum(top, 1e-30) * (1.0 / TOP)
    codes = jnp.floor(field * (1.0 / step) + 0.5).astype(jnp.int32)
    width = field.shape[1] // 2
    return (codes[:, :width] << 16) | (codes[:, width:] & 0xFFFF), step


def unpacked(words):
    return jnp.concatenate([words >> 16, (words << 16) >> 16], axis=1).astype(F32)


def fetch(pairs, sems):
    copies = [pltpu.make_async_copy(a, b, sems.at[i]) for i, (a, b) in enumerate(pairs)]
    for copy in copies:
        copy.start()
    return copies


def put_message(field, columns, cols, couple, masks_ref, sent_ref):
    nrhs, rank = field.shape[0], cols[0].shape[0]
    unit = term_unit(field.shape[1], rank)
    proj = product(field, cols[0][...], cols[1][...], 1)
    wide = jnp.concatenate([proj] * CHUNK, axis=1)
    words, step = packed(field)
    width = words.shape[1]
    row = stats_row(columns, rank, step)
    finer = 1.0 / (steps_of(row, rank) * unit)
    for i in range(sent_ref.shape[0]):
        sent_ref[i, :, :width] = words
    stats = [jnp.broadcast_to(a, (CHUNK, LANES)) for a in coded(row)]
    for start in range(0, sent_ref.shape[0], CHUNK):
        mask = masks_ref[pl.ds(start, CHUNK), :]
        spread = jnp.concatenate([mask * wide[r : r + 1] for r in range(nrhs)], axis=0)
        here = pl.ds(start * rank, CHUNK * rank)
        terms = product(spread, couple[0][here, :], couple[1][here, :])
        terms = jnp.concatenate([terms[r * CHUNK : (r + 1) * CHUNK] for r in range(nrhs)], axis=1)
        here = pl.ds(start, CHUNK)
        for k, value in enumerate([(terms * finer).astype(jnp.int32)] + stats + [stats[0]] * (nrhs - 3)):
            sent_ref[here, k, width:] = value


def message_parts(got_ref, rank):
    width = got_ref.shape[2] - LANES
    stats = decoded(got_ref[:, 1, width:], got_ref[:, 2, width:])
    terms = got_ref[:, 0, width:].astype(F32) * (steps_of(stats, rank) * term_unit(2 * width, rank))
    return total(terms), stats


def window_parts(got_ref, rank):
    nrhs, width = got_ref.shape[1], got_ref.shape[2] - LANES
    strips = got_ref.shape[0] // CORES
    shape = (CORES * nrhs, LANES)
    for step in range(3):
        owner = lax.axis_index("strip") + (step - 1)
        inside = (owner >= 0) & (owner < strips)
        owner = CORES * jnp.clip(owner, 0, strips - 1)
        words = jnp.concatenate([got_ref[owner + core, :, :width] for core in range(CORES)], axis=0)
        tails = [got_ref[owner + core, :, width:] for core in range(CORES)]
        rows = [decoded(tail[1:2], tail[2:3]) for tail in tails]
        rows = jnp.where(rows_of(shape) < nrhs, rows[0], rows[1])
        wanted = lanes_of(shape) == rank * lax.rem(rows_of(shape), nrhs) + STEP
        yield inside, unpacked(words), jnp.sum(jnp.where(wanted, rows, 0.0), axis=1, keepdims=True)


def put_blocks(part, first, window):
    part = part.astype(BF16).astype(F32)
    for c in range(part.shape[1] // LANES):
        window[first + c] = part[:, c * LANES : (c + 1) * LANES]


def near_field(window, tiles, list_ref, sums, nrhs):
    for held in sums:
        held[...] = jnp.zeros_like(held)
    n = 0
    for tiles_ref in tiles:
        for first in range(0, tiles_ref.shape[0], 2):
            left = jnp.concatenate([window[list_ref[1, n + i]] for i in range(2)], axis=0).astype(BF16)
            right = jnp.concatenate([tiles_ref[first + i] for i in range(2)], axis=1)
            both = jnp.dot(left, right, preferred_element_type=F32)
            rows = window.shape[1]
            for i in range(2):
                held = sums[(n + i) % len(sums)]
                held[list_ref[0, n + i]] += both[i * rows : (i + 1) * rows, i * LANES : (i + 1) * LANES]
            n += 2
    whole = sum((held[...] for held in sums[1:]), sums[0][...])
    rows = whole.shape[0] // CORES
    return jnp.concatenate([whole[b, :nrhs] + whole[rows + b, nrhs:] for b in range(rows)], axis=1)


def start_kernel(
    loads_hbm, cols_hbm, couple_hbm, ranks_hbm, list_hbm, rows_hbm, self_hbm, tiles_hbm, sent_ref, cols_high, cols_low, couple_high,
    couple_low, masks_ref, rows_high, rows_low, list_ref, loads_ref, self_ref, tiles_ref, cols_ref, couple_ref, ranks_ref, raw_ref,
    rows_ref, sems,
):
    rank, panels = cols_ref.shape
    pairs = (
        (loads_hbm, loads_ref), (cols_hbm, cols_ref), (couple_hbm, couple_ref), (ranks_hbm, ranks_ref),
        (list_hbm, raw_ref), (rows_hbm, rows_ref), (self_hbm, self_ref),
    )
    every = tiles_ref.shape[0] // PIECES
    pieces = [pl.ds(i * every, every) for i in range(PIECES)]
    copies = fetch(pairs + tuple((tiles_hbm.at[p], tiles_ref.at[p]) for p in pieces), sems)
    copies[0].wait()
    loads = loads_ref[...]
    square = jnp.sum(loads * loads, axis=1, keepdims=True)
    copies[1].wait()
    cols_high[...], cols_low[...] = halves(cols_ref[...])
    copies[2].wait()
    couple_high[...], couple_low[...] = halves(couple_ref[...])
    copies[3].wait()
    shape = (CHUNK, CHUNK * rank)
    owner = lax.div(lanes_of(shape), rank)
    inner = lax.rem(lanes_of(shape), rank)
    for start in range(0, masks_ref.shape[0], CHUNK):
        limit = jnp.zeros((1, CHUNK * rank), jnp.int32)
        for i in range(CHUNK):
            limit = jnp.where(owner[:1] == i, ranks_ref[0, start + i], limit)
        masks_ref[pl.ds(start, CHUNK), :] = jnp.where((owner == rows_of(shape)) & (inner < limit), 1.0, 0.0)
    copies[4].wait()
    count = panels // LANES
    target, source = raw_ref[0:1, :], raw_ref[1:2, :]
    group, block = lax.div(source, count), lax.rem(source, count)
    strip, core = lax.div(group, CORES), lax.rem(group, CORES)
    list_ref[...] = jnp.concatenate([core * count + target, strip * count + block], axis=0)
    copies[5].wait()
    rows_high[...], rows_low[...] = halves(rows_ref[...])
    put_message(loads, [square], (cols_high, cols_low), (couple_high, couple_low), masks_ref, sent_ref)
    for copy in copies[6:]:
        copy.wait()


def image_of(field, far, self_ref, far_rows, near):
    rank = far_rows[0].shape[0]
    return self_ref[...] * field + near + product(far[:, :rank], far_rows[0][...], far_rows[1][...])


def step0_kernel(
    got_ref, loads_ref, cols_high, cols_low, couple_high, couple_low, masks_ref, rows_high, rows_low, self_ref,
    tiles_ref, list_vmem, sent_ref, image_ref, window0_ref, state_ref, list_ref, sems, window, *sums,
):
    rank = rows_high.shape[0]
    nrhs, panels = loads_ref.shape
    span, rows = panels // LANES, CORES * nrhs
    (copy,) = fetch(((list_vmem, list_ref),), sems)
    terms, stats = message_parts(got_ref, rank)
    beta = jnp.sqrt(stat_column(total(stats), 0, nrhs, rank))
    scale = 1.0 / beta
    copy.wait()
    both = jnp.concatenate([scale] * CORES, axis=0)
    for step, (inside, part, unit) in enumerate(window_parts(got_ref, rank)):
        part = jnp.where(inside, part * (unit * both), 0.0)
        window0_ref[step * rows : (step + 1) * rows, :] = part
        put_blocks(part, step * span, window)
    basis = loads_ref[...] * scale
    far = far_sum_of(terms, nrhs, rank) * scale
    near = near_field(window, (tiles_ref,), list_ref, sums, nrhs)
    image = image_of(basis, far, self_ref, (rows_high, rows_low), near)
    image_ref[...] = image
    state_ref[...] = jnp.concatenate([far, jnp.broadcast_to(beta, far.shape)], axis=0)
    norm = jnp.sum(basis * basis, axis=1, keepdims=True)
    dot = jnp.sum(basis * image, axis=1, keepdims=True)
    share = jnp.where(norm > 0, dot / jnp.where(norm > 0, norm, 1.0), 0.0)
    rest = image - share * basis
    rest = jnp.sum(rest * rest, axis=1, keepdims=True)
    columns = [norm, dot, share, rest]
    put_message(image, columns, (cols_high, cols_low), (couple_high, couple_low), masks_ref, sent_ref)


def step1_kernel(
    got_ref, loads_ref, image_ref, window0_ref, state_ref, rows_high, rows_low, self_ref, tiles_ref,
    list_vmem, sent_ref, basis_ref, coeff_ref, list_ref, sems, window, *sums,
):
    rank = rows_high.shape[0]
    nrhs, panels = loads_ref.shape
    span, rows = panels // LANES, CORES * nrhs
    (copy,) = fetch(((list_vmem, list_ref),), sems)
    beta = state_ref[nrhs:, :1]
    far0 = state_ref[:nrhs, :]
    terms, stats = message_parts(got_ref, rank)
    summed = total(stats)
    h00 = stat_column(summed, 1, nrhs, rank)
    away = shifted(stats, 2) - shifted(summed, 1)
    rest = total(shifted(stats, 3) + stats * away * away)
    h10 = jnp.sqrt(stat_column(rest, 0, nrhs, rank))
    scale = 1.0 / h10
    copy.wait()
    both, both_h00 = (jnp.concatenate([a] * CORES, axis=0) for a in (scale, h00))
    for step, (inside, part, unit) in enumerate(window_parts(got_ref, rank)):
        part = (part * unit - both_h00 * window0_ref[step * rows : (step + 1) * rows, :]) * both
        put_blocks(jnp.where(inside, part, 0.0), step * span, window)
    basis0 = loads_ref[...] * (1.0 / beta)
    basis1 = (image_ref[...] - h00 * basis0) * scale
    far = (far_sum_of(terms, nrhs, rank) - h00 * far0) * scale
    near = near_field(window, (tiles_ref,), list_ref, sums, nrhs)
    image = image_of(basis1, far, self_ref, (rows_high, rows_low), near)
    columns = [jnp.sum(a * image, axis=1, keepdims=True) for a in (basis0, basis1, image)]
    sent_ref[:, 0, :] = jnp.broadcast_to(stats_row(columns, rank), (sent_ref.shape[0], LANES))
    basis_ref[...] = jnp.concatenate([basis0, basis1], axis=0)
    coeff_ref[...] = jnp.concatenate([jnp.broadcast_to(v, (nrhs, LANES)) for v in (beta, h00, h10)], axis=0)


def finish_kernel(rank, got_ref, basis_ref, coeff_ref, out_ref):
    nrhs = out_ref.shape[0]
    row = total(got_ref[:, 0, :])
    h01, h11, gram11 = (stat_column(row, k, nrhs, rank) for k in range(3))
    beta, h00, h10 = (coeff_ref[k * nrhs : (k + 1) * nrhs, :1] for k in range(3))
    gram00 = h00 * h00 + h10 * h10
    gram01 = h00 * h01 + h10 * h11
    lower00 = jnp.sqrt(gram00)
    lower10 = gram01 / lower00
    lower11 = jnp.sqrt(gram11 - lower10 * lower10)
    middle0 = beta * h00 / lower00
    middle1 = (beta * h01 - lower10 * middle0) / lower11
    y1 = middle1 / lower11
    y0 = (middle0 - lower10 * y1) / lower00
    out_ref[...] = y0 * basis_ref[:nrhs, :] + y1 * basis_ref[nrhs:, :]


class Plain(jax.ShapeDtypeStruct):
    pass


def in_vmem_like(array):
    return pltpu.VMEM(array.shape, array.dtype)


def in_vmem(arrays):
    return [pltpu.with_memory_space_constraint(a, pltpu.VMEM) for a in arrays]


def call(kernel, args, outs, scratch=(), held=()):
    args = [pltpu.with_memory_space_constraint(a, pltpu.HBM) if i in held else a for i, a in enumerate(args)]
    moved = sum(a.size * a.dtype.itemsize for a in args)
    return pl.pallas_call(
        kernel,
        out_shape=[
            jax.ShapeDtypeStruct(out, F32) if isinstance(out, tuple) else out if isinstance(out, Plain) else in_vmem_like(out)
            for out in outs
        ],
        in_specs=[pl.BlockSpec(memory_space=pl.ANY if i in held else pltpu.VMEM) for i in range(len(args))],
        out_specs=[pl.BlockSpec(memory_space=pltpu.VMEM)] * len(outs),
        scratch_shapes=list(scratch),
        compiler_params=pltpu.CompilerParams(vmem_limit_bytes=24 * 2**20),
        cost_estimate=pl.CostEstimate(flops=0, bytes_accessed=moved, transcendentals=0),
    )(*args)


def exchanged(sent):
    return lax.all_to_all(sent, GROUP, 0, 0, tiled=True)


def body(loads, self_term, near_tiles, near_list, far_rows, far_cols, coupling, ranks):
    nrhs, panels = loads.shape
    rank = far_cols.shape[0]
    blocks, tile = near_tiles.shape[:2]
    rows = panels // tile
    strips = coupling.shape[0] // CORES
    couple = coupling.reshape(CORES * strips * rank, rank)
    near_list = near_list.T
    ranks = ranks.reshape(1, CORES * strips)
    self_term = self_term.reshape(1, panels)
    groups = CORES * strips
    message = Plain((groups, nrhs, panels // 2 + LANES), jnp.int32)
    index = pltpu.SMEM(near_list.shape, jnp.int32)
    scratch = [index, pltpu.SemaphoreType.DMA((1,)), pltpu.VMEM((3 * rows, CORES * nrhs, tile), F32)]
    scratch += [pltpu.VMEM((CORES * rows, CORES * nrhs, tile), F32)] * 4

    def twice(array):
        return [jax.ShapeDtypeStruct(array.shape, BF16)] * 2

    sent, *held, near_list, loads, self_term, near_tiles = call(
        start_kernel,
        (loads, far_cols, couple, ranks, near_list, far_rows, self_term, near_tiles),
        [
            message, *twice(far_cols), *twice(couple), jax.ShapeDtypeStruct((groups, CHUNK * rank), F32),
            *twice(far_rows), near_list, loads, self_term, near_tiles,
        ],
        [
            pltpu.VMEM(far_cols.shape, F32), pltpu.VMEM(couple.shape, F32), pltpu.SMEM(ranks.shape, jnp.int32),
            pltpu.VMEM(near_list.shape, jnp.int32), pltpu.VMEM(far_rows.shape, F32), pltpu.SemaphoreType.DMA((7 + PIECES,)),
        ],
        held=range(8),
    )
    loads, *held, self_term, near_tiles, near_list = in_vmem([loads, *held, self_term, near_tiles, near_list])
    source_side, target_side = [loads, *held[:5]], [*held[5:], self_term, near_tiles, near_list]
    sent, image, window0, state = call(
        step0_kernel,
        (exchanged(sent), *source_side, *target_side),
        [message, loads.shape, (3 * CORES * nrhs, panels), (CORES * nrhs, LANES)],
        scratch,
    )
    sent, basis, coeff = call(
        step1_kernel,
        (exchanged(sent), loads, image, window0, state, *target_side),
        [(groups, 1, LANES), (2 * nrhs, panels), (3 * nrhs, LANES)],
        scratch,
    )
    return call(functools.partial(finish_kernel, rank), (exchanged(sent), basis, coeff), [loads.shape])[0]


def solution(mesh):
    every = ("case",) + GROUP
    in_specs = (
        P(None, every),
        P(every),
        P(every, None, None),
        P(every, None),
        P(None, every),
        P(None, every),
        P(None, GROUP, None, None),
        P(None, GROUP),
    )
    return jax.shard_map(body, mesh=mesh, in_specs=in_specs, out_specs=P(None, every), check_vma=False)
```

```python
import functools

import jax
import jax.numpy as jnp
from jax import lax
from jax.experimental import pallas as pl
from jax.experimental.pallas import tpu as pltpu
from jax.sharding import PartitionSpec as P

GROUP = ("strip", "clus")
CORES = 2
LANES = 128
CHUNK = 16
PIECES = 10
F32 = jnp.float32
BF16 = jnp.bfloat16

STEP = 8
COLS_TOP = 0.1875
COUPLE_TOP = 0.375
TOP = 32767.0
ONE = float(2**30)


def lanes_of(shape):
    return lax.broadcasted_iota(jnp.int32, shape, 1)


def rows_of(shape):
    return lax.broadcasted_iota(jnp.int32, shape, 0)


def total(rows):
    return jnp.sum(rows, axis=0, keepdims=True)


def stats_row(columns, rank, step=None):
    shape = (columns[0].shape[0], LANES)
    first = lanes_of(shape) - rank * rows_of(shape)
    spread = sum(jnp.where(first == k, column, 0.0) for k, column in enumerate(columns))
    if step is not None:
        spread = jnp.where((first >= STEP) & (first < rank), step, spread)
    return total(spread)


def steps_of(stats, rank):
    inner = lax.rem(lanes_of(stats.shape), rank)
    return jnp.where(inner < STEP, shifted(stats, STEP), stats)


def term_unit(panels, rank):
    return panels * rank * COLS_TOP * COUPLE_TOP * TOP / ONE


def stat_column(row, k, nrhs, rank):
    shape = (nrhs, LANES)
    first = lanes_of(shape) - rank * rows_of(shape)
    return jnp.sum(jnp.where(first == k, row, 0.0), axis=1, keepdims=True)


def shifted(value, k):
    return pltpu.roll(value, LANES - k, 1)


def far_sum_of(row, nrhs, rank):
    shape = (nrhs, LANES)
    first = lanes_of(shape) - rank * rows_of(shape)
    own = jnp.where((first >= 0) & (first < rank), row, 0.0)
    return sum((pltpu.roll(own, k * rank, 1) for k in range(1, LANES // rank)), own)


def halves(value):
    high = value.astype(BF16)
    return high, (value - high.astype(F32)).astype(BF16)


def product(left, right_high, right_low, side=0):
    rows = left.shape[0]
    high, low = halves(left)
    dims = (((1,), (side,)), ((), ()))
    both = lax.dot_general(jnp.concatenate([high, low], axis=0), right_high, dims, preferred_element_type=F32)
    return both[:rows] + (both[rows:] + lax.dot_general(high, right_low, dims, preferred_element_type=F32))


def coded(value):
    exponent = jnp.ceil(jnp.log2(jnp.maximum(jnp.abs(value), 1e-30)))
    return (value * jnp.exp2(-exponent) * ONE).astype(jnp.int32), exponent.astype(jnp.int32)


def decoded(mantissa, exponent):
    return mantissa.astype(F32) * (1.0 / ONE) * jnp.exp2(exponent.astype(F32))


def packed(field):
    top = jnp.max(jnp.abs(field), axis=1, keepdims=True)
    step = jnp.maximum(top, 1e-30) * (1.0 / TOP)
    codes = jnp.floor(field * (1.0 / step) + 0.5).astype(jnp.int32)
    width = field.shape[1] // 2
    return (codes[:, :width] << 16) | (codes[:, width:] & 0xFFFF), step


def unpacked(words):
    return jnp.concatenate([words >> 16, (words << 16) >> 16], axis=1).astype(F32)


def fetch(pairs, sems):
    copies = [pltpu.make_async_copy(a, b, sems.at[i]) for i, (a, b) in enumerate(pairs)]
    for copy in copies:
        copy.start()
    return copies


def put_message(field, columns, cols, couple, masks_ref, sent_ref):
    nrhs, rank = field.shape[0], cols[0].shape[0]
    unit = term_unit(field.shape[1], rank)
    proj = product(field, cols[0][...], cols[1][...], 1)
    wide = jnp.concatenate([proj] * CHUNK, axis=1)
    words, step = packed(field)
    width = words.shape[1]
    row = stats_row(columns, rank, step)
    finer = 1.0 / (steps_of(row, rank) * unit)
    for i in range(sent_ref.shape[0]):
        sent_ref[i, :, :width] = words
    stats = [jnp.broadcast_to(a, (CHUNK, LANES)) for a in coded(row)]
    for start in range(0, sent_ref.shape[0], CHUNK):
        mask = masks_ref[pl.ds(start, CHUNK), :]
        spread = jnp.concatenate([mask * wide[r : r + 1] for r in range(nrhs)], axis=0)
        here = pl.ds(start * rank, CHUNK * rank)
        terms = product(spread, couple[0][here, :], couple[1][here, :])
        terms = jnp.concatenate([terms[r * CHUNK : (r + 1) * CHUNK] for r in range(nrhs)], axis=1)
        here = pl.ds(start, CHUNK)
        for k, value in enumerate([(terms * finer).astype(jnp.int32)] + stats + [stats[0]] * (nrhs - 3)):
            sent_ref[here, k, width:] = value


def message_parts(got_ref, rank):
    width = got_ref.shape[2] - LANES
    stats = decoded(got_ref[:, 1, width:], got_ref[:, 2, width:])
    terms = got_ref[:, 0, width:].astype(F32) * (steps_of(stats, rank) * term_unit(2 * width, rank))
    return total(terms), stats


def window_parts(got_ref, rank):
    nrhs, width = got_ref.shape[1], got_ref.shape[2] - LANES
    strips = got_ref.shape[0] // CORES
    shape = (CORES * nrhs, LANES)
    for step in range(3):
        owner = lax.axis_index("strip") + (step - 1)
        inside = (owner >= 0) & (owner < strips)
        owner = CORES * jnp.clip(owner, 0, strips - 1)
        words = jnp.concatenate([got_ref[owner + core, :, :width] for core in range(CORES)], axis=0)
        tails = [got_ref[owner + core, :, width:] for core in range(CORES)]
        rows = [decoded(tail[1:2], tail[2:3]) for tail in tails]
        rows = jnp.where(rows_of(shape) < nrhs, rows[0], rows[1])
        wanted = lanes_of(shape) == rank * lax.rem(rows_of(shape), nrhs) + STEP
        yield inside, unpacked(words), jnp.sum(jnp.where(wanted, rows, 0.0), axis=1, keepdims=True)


def put_blocks(part, first, window):
    part = part.astype(BF16).astype(F32)
    for c in range(part.shape[1] // LANES):
        window[first + c] = part[:, c * LANES : (c + 1) * LANES]


def near_field(window, tiles, list_ref, sums, nrhs):
    n = 0
    for tiles_ref in tiles:
        for first in range(0, tiles_ref.shape[0], 2):
            left = jnp.concatenate([window[list_ref[1, n + i]] for i in range(2)], axis=0).astype(BF16)
            right = jnp.concatenate([tiles_ref[first + i] for i in range(2)], axis=1)
            both = jnp.dot(left, right, preferred_element_type=F32)
            rows = window.shape[1]
            for i in range(2):
                held = sums[(n + i) % len(sums)]
                held[list_ref[0, n + i]] += both[i * rows : (i + 1) * rows, i * LANES : (i + 1) * LANES]
            n += 2
    whole = sum((held[...] for held in sums[1:]), sums[0][...])
    rows = whole.shape[0] // CORES
    return jnp.concatenate([whole[b, :nrhs] + whole[rows + b, nrhs:] for b in range(rows)], axis=1)


def start_kernel(
    loads_hbm, cols_hbm, couple_hbm, ranks_hbm, list_hbm, rows_hbm, self_hbm, tiles_hbm, sent_ref, cols_high, cols_low, couple_high,
    couple_low, masks_ref, rows_high, rows_low, list_ref, loads_ref, self_ref, tiles_ref, cols_ref, couple_ref, ranks_ref, raw_ref,
    rows_ref, sems,
):
    rank, panels = cols_ref.shape
    pairs = (
        (loads_hbm, loads_ref), (cols_hbm, cols_ref), (couple_hbm, couple_ref), (ranks_hbm, ranks_ref),
        (list_hbm, raw_ref), (rows_hbm, rows_ref), (self_hbm, self_ref),
    )
    every = tiles_ref.shape[0] // PIECES
    pieces = [pl.ds(i * every, every) for i in range(PIECES)]
    copies = fetch(pairs + tuple((tiles_hbm.at[p], tiles_ref.at[p]) for p in pieces), sems)
    copies[0].wait()
    loads = loads_ref[...]
    square = jnp.sum(loads * loads, axis=1, keepdims=True)
    copies[1].wait()
    cols_high[...], cols_low[...] = halves(cols_ref[...])
    copies[2].wait()
    couple_high[...], couple_low[...] = halves(couple_ref[...])
    copies[3].wait()
    shape = (CHUNK, CHUNK * rank)
    owner = lax.div(lanes_of(shape), rank)
    inner = lax.rem(lanes_of(shape), rank)
    for start in range(0, masks_ref.shape[0], CHUNK):
        limit = jnp.zeros((1, CHUNK * rank), jnp.int32)
        for i in range(CHUNK):
            limit = jnp.where(owner[:1] == i, ranks_ref[0, start + i], limit)
        masks_ref[pl.ds(start, CHUNK), :] = jnp.where((owner == rows_of(shape)) & (inner < limit), 1.0, 0.0)
    copies[4].wait()
    count = panels // LANES
    target, source = raw_ref[0:1, :], raw_ref[1:2, :]
    group, block = lax.div(source, count), lax.rem(source, count)
    strip, core = lax.div(group, CORES), lax.rem(group, CORES)
    list_ref[...] = jnp.concatenate([core * count + target, strip * count + block], axis=0)
    copies[5].wait()
    rows_high[...], rows_low[...] = halves(rows_ref[...])
    put_message(loads, [square], (cols_high, cols_low), (couple_high, couple_low), masks_ref, sent_ref)
    for copy in copies[6:]:
        copy.wait()


def image_of(field, far, self_ref, far_rows, near):
    rank = far_rows[0].shape[0]
    return self_ref[...] * field + near + product(far[:, :rank], far_rows[0][...], far_rows[1][...])


def step0_kernel(
    got_ref, loads_ref, cols_high, cols_low, couple_high, couple_low, masks_ref, rows_high, rows_low, self_ref,
    tiles_ref, list_vmem, sent_ref, image_ref, window0_ref, state_ref, list_ref, sems, window, *sums,
):
    rank = rows_high.shape[0]
    nrhs, panels = loads_ref.shape
    span, rows = panels // LANES, CORES * nrhs
    (copy,) = fetch(((list_vmem, list_ref),), sems)
    for held in sums:
        held[...] = jnp.zeros_like(held)
    terms, stats = message_parts(got_ref, rank)
    beta = jnp.sqrt(stat_column(total(stats), 0, nrhs, rank))
    scale = 1.0 / beta
    both = jnp.concatenate([scale] * CORES, axis=0)
    for step, (inside, part, unit) in enumerate(window_parts(got_ref, rank)):
        part = jnp.where(inside, part * (unit * both), 0.0)
        window0_ref[step * rows : (step + 1) * rows, :] = part
        put_blocks(part, step * span, window)
    basis = loads_ref[...] * scale
    far = far_sum_of(terms, nrhs, rank) * scale
    norm = jnp.sum(basis * basis, axis=1, keepdims=True)
    copy.wait()
    near = near_field(window, (tiles_ref,), list_ref, sums, nrhs)
    image = image_of(basis, far, self_ref, (rows_high, rows_low), near)
    image_ref[...] = image
    state_ref[...] = jnp.concatenate([far, jnp.broadcast_to(beta, far.shape)], axis=0)
    dot = jnp.sum(basis * image, axis=1, keepdims=True)
    share = jnp.where(norm > 0, dot / jnp.where(norm > 0, norm, 1.0), 0.0)
    rest = image - share * basis
    rest = jnp.sum(rest * rest, axis=1, keepdims=True)
    columns = [norm, dot, share, rest]
    put_message(image, columns, (cols_high, cols_low), (couple_high, couple_low), masks_ref, sent_ref)


def step1_kernel(
    got_ref, loads_ref, image_ref, window0_ref, state_ref, rows_high, rows_low, self_ref, tiles_ref,
    list_vmem, sent_ref, basis_ref, coeff_ref, list_ref, sems, window, *sums,
):
    rank = rows_high.shape[0]
    nrhs, panels = loads_ref.shape
    span, rows = panels // LANES, CORES * nrhs
    (copy,) = fetch(((list_vmem, list_ref),), sems)
    beta = state_ref[nrhs:, :1]
    far0 = state_ref[:nrhs, :]
    for held in sums:
        held[...] = jnp.zeros_like(held)
    terms, stats = message_parts(got_ref, rank)
    summed = total(stats)
    h00 = stat_column(summed, 1, nrhs, rank)
    away = shifted(stats, 2) - shifted(summed, 1)
    rest = total(shifted(stats, 3) + stats * away * away)
    h10 = jnp.sqrt(stat_column(rest, 0, nrhs, rank))
    scale = 1.0 / h10
    both, both_h00 = (jnp.concatenate([a] * CORES, axis=0) for a in (scale, h00))
    for step, (inside, part, unit) in enumerate(window_parts(got_ref, rank)):
        part = (part * unit - both_h00 * window0_ref[step * rows : (step + 1) * rows, :]) * both
        put_blocks(jnp.where(inside, part, 0.0), step * span, window)
    basis0 = loads_ref[...] * (1.0 / beta)
    basis1 = (image_ref[...] - h00 * basis0) * scale
    far = (far_sum_of(terms, nrhs, rank) - h00 * far0) * scale
    copy.wait()
    near = near_field(window, (tiles_ref,), list_ref, sums, nrhs)
    image = image_of(basis1, far, self_ref, (rows_high, rows_low), near)
    columns = [jnp.sum(a * image, axis=1, keepdims=True) for a in (basis0, basis1, image)]
    sent_ref[:, 0, :] = jnp.broadcast_to(stats_row(columns, rank), (sent_ref.shape[0], LANES))
    basis_ref[...] = jnp.concatenate([basis0, basis1], axis=0)
    coeff_ref[...] = jnp.concatenate([jnp.broadcast_to(v, (nrhs, LANES)) for v in (beta, h00, h10)], axis=0)


def finish_kernel(rank, got_ref, basis_ref, coeff_ref, out_ref):
    nrhs = out_ref.shape[0]
    row = total(got_ref[:, 0, :])
    h01, h11, gram11 = (stat_column(row, k, nrhs, rank) for k in range(3))
    beta, h00, h10 = (coeff_ref[k * nrhs : (k + 1) * nrhs, :1] for k in range(3))
    gram00 = h00 * h00 + h10 * h10
    gram01 = h00 * h01 + h10 * h11
    lower00 = jnp.sqrt(gram00)
    lower10 = gram01 / lower00
    lower11 = jnp.sqrt(gram11 - lower10 * lower10)
    middle0 = beta * h00 / lower00
    middle1 = (beta * h01 - lower10 * middle0) / lower11
    y1 = middle1 / lower11
    y0 = (middle0 - lower10 * y1) / lower00
    out_ref[...] = y0 * basis_ref[:nrhs, :] + y1 * basis_ref[nrhs:, :]


class Plain(jax.ShapeDtypeStruct):
    pass


def in_vmem_like(array):
    return pltpu.VMEM(array.shape, array.dtype)


def in_vmem(arrays):
    return [pltpu.with_memory_space_constraint(a, pltpu.VMEM) for a in arrays]


def call(kernel, args, outs, scratch=(), held=()):
    args = [pltpu.with_memory_space_constraint(a, pltpu.HBM) if i in held else a for i, a in enumerate(args)]
    moved = sum(a.size * a.dtype.itemsize for a in args)
    return pl.pallas_call(
        kernel,
        out_shape=[
            jax.ShapeDtypeStruct(out, F32) if isinstance(out, tuple) else out if isinstance(out, Plain) else in_vmem_like(out)
            for out in outs
        ],
        in_specs=[pl.BlockSpec(memory_space=pl.ANY if i in held else pltpu.VMEM) for i in range(len(args))],
        out_specs=[pl.BlockSpec(memory_space=pltpu.VMEM)] * len(outs),
        scratch_shapes=list(scratch),
        compiler_params=pltpu.CompilerParams(vmem_limit_bytes=24 * 2**20),
        cost_estimate=pl.CostEstimate(flops=0, bytes_accessed=moved, transcendentals=0),
    )(*args)


def exchanged(sent):
    return lax.all_to_all(sent, GROUP, 0, 0, tiled=True)


def body(loads, self_term, near_tiles, near_list, far_rows, far_cols, coupling, ranks):
    nrhs, panels = loads.shape
    rank = far_cols.shape[0]
    blocks, tile = near_tiles.shape[:2]
    rows = panels // tile
    strips = coupling.shape[0] // CORES
    couple = coupling.reshape(CORES * strips * rank, rank)
    near_list = near_list.T
    ranks = ranks.reshape(1, CORES * strips)
    self_term = self_term.reshape(1, panels)
    groups = CORES * strips
    message = Plain((groups, nrhs, panels // 2 + LANES), jnp.int32)
    index = pltpu.SMEM(near_list.shape, jnp.int32)
    scratch = [index, pltpu.SemaphoreType.DMA((1,)), pltpu.VMEM((3 * rows, CORES * nrhs, tile), F32)]
    scratch += [pltpu.VMEM((CORES * rows, CORES * nrhs, tile), F32)] * 4

    def twice(array):
        return [jax.ShapeDtypeStruct(array.shape, BF16)] * 2

    sent, *held, near_list, loads, self_term, near_tiles = call(
        start_kernel,
        (loads, far_cols, couple, ranks, near_list, far_rows, self_term, near_tiles),
        [
            message, *twice(far_cols), *twice(couple), jax.ShapeDtypeStruct((groups, CHUNK * rank), F32),
            *twice(far_rows), near_list, loads, self_term, near_tiles,
        ],
        [
            pltpu.VMEM(far_cols.shape, F32), pltpu.VMEM(couple.shape, F32), pltpu.SMEM(ranks.shape, jnp.int32),
            pltpu.VMEM(near_list.shape, jnp.int32), pltpu.VMEM(far_rows.shape, F32), pltpu.SemaphoreType.DMA((7 + PIECES,)),
        ],
        held=range(8),
    )
    loads, *held, self_term, near_tiles, near_list = in_vmem([loads, *held, self_term, near_tiles, near_list])
    source_side, target_side = [loads, *held[:5]], [*held[5:], self_term, near_tiles, near_list]
    sent, image, window0, state = call(
        step0_kernel,
        (exchanged(sent), *source_side, *target_side),
        [message, loads.shape, (3 * CORES * nrhs, panels), (CORES * nrhs, LANES)],
        scratch,
    )
    sent, basis, coeff = call(
        step1_kernel,
        (exchanged(sent), loads, image, window0, state, *target_side),
        [(groups, 1, LANES), (2 * nrhs, panels), (3 * nrhs, LANES)],
        scratch,
    )
    return call(functools.partial(finish_kernel, rank), (exchanged(sent), basis, coeff), [loads.shape])[0]


def solution(mesh):
    every = ("case",) + GROUP
    in_specs = (
        P(None, every),
        P(every),
        P(every, None, None),
        P(every, None),
        P(None, every),
        P(None, every),
        P(None, GROUP, None, None),
        P(None, GROUP),
    )
    return jax.shard_map(body, mesh=mesh, in_specs=in_specs, out_specs=P(None, every), check_vma=False)
```

```python
import functools

import jax
import jax.numpy as jnp
from jax import lax
from jax.experimental import pallas as pl
from jax.experimental.pallas import tpu as pltpu
from jax.sharding import PartitionSpec as P

GROUP = ("strip", "clus")
CORES = 2
LANES = 128
CHUNK = 16
PIECES = 10
F32 = jnp.float32
BF16 = jnp.bfloat16

STEP = 8
COLS_TOP = 0.1875
COUPLE_TOP = 0.375
TOP = 32767.0
ONE = float(2**30)


def lanes_of(shape):
    return lax.broadcasted_iota(jnp.int32, shape, 1)


def rows_of(shape):
    return lax.broadcasted_iota(jnp.int32, shape, 0)


def total(rows):
    return jnp.sum(rows, axis=0, keepdims=True)


def stats_row(columns, rank, step=None):
    shape = (columns[0].shape[0], LANES)
    first = lanes_of(shape) - rank * rows_of(shape)
    spread = sum(jnp.where(first == k, column, 0.0) for k, column in enumerate(columns))
    if step is not None:
        spread = jnp.where((first >= STEP) & (first < rank), step, spread)
    return total(spread)


def steps_of(stats, rank):
    inner = lax.rem(lanes_of(stats.shape), rank)
    return jnp.where(inner < STEP, shifted(stats, STEP), stats)


def term_unit(panels, rank):
    return panels * rank * COLS_TOP * COUPLE_TOP * TOP / ONE


def stat_column(row, k, nrhs, rank):
    shape = (nrhs, LANES)
    first = lanes_of(shape) - rank * rows_of(shape)
    return jnp.sum(jnp.where(first == k, row, 0.0), axis=1, keepdims=True)


def shifted(value, k):
    return pltpu.roll(value, LANES - k, 1)


def far_sum_of(row, nrhs, rank):
    shape = (nrhs, LANES)
    first = lanes_of(shape) - rank * rows_of(shape)
    own = jnp.where((first >= 0) & (first < rank), row, 0.0)
    return sum((pltpu.roll(own, k * rank, 1) for k in range(1, LANES // rank)), own)


def halves(value):
    high = value.astype(BF16)
    return high, (value - high.astype(F32)).astype(BF16)


def product(left, right_high, right_low, side=0):
    rows = left.shape[0]
    high, low = halves(left)
    dims = (((1,), (side,)), ((), ()))
    both = lax.dot_general(jnp.concatenate([high, low], axis=0), right_high, dims, preferred_element_type=F32)
    return both[:rows] + (both[rows:] + lax.dot_general(high, right_low, dims, preferred_element_type=F32))


def coded(value):
    exponent = jnp.ceil(jnp.log2(jnp.maximum(jnp.abs(value), 1e-30)))
    return (value * jnp.exp2(-exponent) * ONE).astype(jnp.int32), exponent.astype(jnp.int32)


def decoded(mantissa, exponent):
    return mantissa.astype(F32) * (1.0 / ONE) * jnp.exp2(exponent.astype(F32))


def packed(field):
    top = jnp.max(jnp.abs(field), axis=1, keepdims=True)
    step = jnp.maximum(top, 1e-30) * (1.0 / TOP)
    codes = jnp.floor(field * (1.0 / step) + 0.5).astype(jnp.int32)
    width = field.shape[1] // 2
    return (codes[:, :width] << 16) | (codes[:, width:] & 0xFFFF), step


def unpacked(words):
    return jnp.concatenate([words >> 16, (words << 16) >> 16], axis=1).astype(F32)


def fetch(pairs, sems):
    copies = [pltpu.make_async_copy(a, b, sems.at[i]) for i, (a, b) in enumerate(pairs)]
    for copy in copies:
        copy.start()
    return copies


def put_message(field, columns, cols, couple, masks_ref, sent_ref):
    nrhs, rank = field.shape[0], cols[0].shape[0]
    unit = term_unit(field.shape[1], rank)
    proj = product(field, cols[0][...], cols[1][...], 1)
    wide = jnp.concatenate([proj] * CHUNK, axis=1)
    words, step = packed(field)
    width = words.shape[1]
    row = stats_row(columns, rank, step)
    finer = 1.0 / (steps_of(row, rank) * unit)
    for i in range(sent_ref.shape[0]):
        sent_ref[i, :, :width] = words
    half = CHUNK // CORES
    stats = [jnp.broadcast_to(a, (half, LANES)) for a in coded(row)]
    for start in range(0, sent_ref.shape[0], half):
        mask = masks_ref[pl.ds(CORES * start, CHUNK), :]
        spread = jnp.concatenate([mask * wide[r : r + 1] for r in range(nrhs)], axis=0)
        here = pl.ds(CORES * start * rank, CHUNK * rank)
        terms = product(spread, couple[0][here, :], couple[1][here, :])
        terms = jnp.concatenate([terms[r * CHUNK : (r + 1) * CHUNK] for r in range(nrhs)], axis=1)
        terms = (terms * finer).astype(jnp.int32)
        here = pl.ds(start, half)
        for k, value in enumerate([terms[:half], terms[half:]] + stats):
            sent_ref[here, k, width:] = value


def message_parts(got, rank):
    width = got[0].shape[2] - LANES
    first, second, mantissa, exponent = (jnp.concatenate([ref[:, k, width:] for ref in got], axis=0) for k in range(4))
    stats = decoded(mantissa, exponent)
    terms = jnp.where(lax.axis_index("clus") == 0, first, second).astype(F32)
    return total(terms * (steps_of(stats, rank) * term_unit(2 * width, rank))), stats


def window_parts(got, rank):
    strips, nrhs, width = got[0].shape
    width -= LANES
    shape = (CORES * nrhs, LANES)
    for step in range(3):
        owner = lax.axis_index("strip") + (step - 1)
        inside = (owner >= 0) & (owner < strips)
        owner = jnp.clip(owner, 0, strips - 1)
        words = jnp.concatenate([ref[owner, :, :width] for ref in got], axis=0)
        tails = [ref[owner, :, width:] for ref in got]
        rows = [decoded(tail[2:3], tail[3:4]) for tail in tails]
        rows = jnp.where(rows_of(shape) < nrhs, rows[0], rows[1])
        wanted = lanes_of(shape) == rank * lax.rem(rows_of(shape), nrhs) + STEP
        yield inside, unpacked(words), jnp.sum(jnp.where(wanted, rows, 0.0), axis=1, keepdims=True)


def put_blocks(part, first, window):
    part = part.astype(BF16).astype(F32)
    for c in range(part.shape[1] // LANES):
        window[first + c] = part[:, c * LANES : (c + 1) * LANES]


def near_field(window, tiles, list_ref, sums, nrhs):
    n = 0
    for tiles_ref in tiles:
        for first in range(0, tiles_ref.shape[0], 2):
            left = jnp.concatenate([window[list_ref[1, n + i]] for i in range(2)], axis=0).astype(BF16)
            right = jnp.concatenate([tiles_ref[first + i] for i in range(2)], axis=1)
            both = jnp.dot(left, right, preferred_element_type=F32)
            rows = window.shape[1]
            for i in range(2):
                held = sums[(n + i) % len(sums)]
                held[list_ref[0, n + i]] += both[i * rows : (i + 1) * rows, i * LANES : (i + 1) * LANES]
            n += 2
    whole = sum((held[...] for held in sums[1:]), sums[0][...])
    rows = whole.shape[0] // CORES
    return jnp.concatenate([whole[b, :nrhs] + whole[rows + b, nrhs:] for b in range(rows)], axis=1)


def start_kernel(
    loads_hbm, cols_hbm, couple_hbm, ranks_hbm, list_hbm, rows_hbm, self_hbm, tiles_hbm, sent_ref, cols_high, cols_low, couple_high,
    couple_low, masks_ref, rows_high, rows_low, list_ref, loads_ref, self_ref, tiles_ref, cols_ref, couple_ref, ranks_ref, raw_ref,
    rows_ref, sems,
):
    rank, panels = cols_ref.shape
    pairs = (
        (loads_hbm, loads_ref), (cols_hbm, cols_ref), (couple_hbm, couple_ref), (ranks_hbm, ranks_ref),
        (list_hbm, raw_ref), (rows_hbm, rows_ref), (self_hbm, self_ref),
    )
    every = tiles_ref.shape[0] // PIECES
    pieces = [pl.ds(i * every, every) for i in range(PIECES)]
    copies = fetch(pairs + tuple((tiles_hbm.at[p], tiles_ref.at[p]) for p in pieces), sems)
    copies[0].wait()
    loads = loads_ref[...]
    square = jnp.sum(loads * loads, axis=1, keepdims=True)
    copies[1].wait()
    cols_high[...], cols_low[...] = halves(cols_ref[...])
    copies[2].wait()
    couple_high[...], couple_low[...] = halves(couple_ref[...])
    copies[3].wait()
    shape = (CHUNK, CHUNK * rank)
    owner = lax.div(lanes_of(shape), rank)
    inner = lax.rem(lanes_of(shape), rank)
    half = CHUNK // CORES
    number = CORES * lax.rem(rows_of(shape), half) + lax.div(rows_of(shape), half)
    for start in range(0, masks_ref.shape[0], CHUNK):
        limit = jnp.zeros((1, CHUNK * rank), jnp.int32)
        for i in range(CHUNK):
            limit = jnp.where(owner[:1] == i, ranks_ref[0, start + i], limit)
        masks_ref[pl.ds(start, CHUNK), :] = jnp.where((owner == number) & (inner < limit), 1.0, 0.0)
    copies[4].wait()
    count = panels // LANES
    target, source = raw_ref[0:1, :], raw_ref[1:2, :]
    group, block = lax.div(source, count), lax.rem(source, count)
    strip, core = lax.div(group, CORES), lax.rem(group, CORES)
    apart = jnp.where(core == lax.axis_index("clus"), 0, 1)
    list_ref[...] = jnp.concatenate([apart * count + target, strip * count + block], axis=0)
    copies[5].wait()
    rows_high[...], rows_low[...] = halves(rows_ref[...])
    put_message(loads, [square], (cols_high, cols_low), (couple_high, couple_low), masks_ref, sent_ref)
    for copy in copies[6:]:
        copy.wait()


def image_of(field, far, self_ref, far_rows, near):
    rank = far_rows[0].shape[0]
    return self_ref[...] * field + near + product(far[:, :rank], far_rows[0][...], far_rows[1][...])


def step0_kernel(
    own_ref, other_ref, loads_ref, cols_high, cols_low, couple_high, couple_low, masks_ref, rows_high, rows_low, self_ref,
    tiles_ref, list_vmem, sent_ref, image_ref, window0_ref, state_ref, list_ref, sems, window, *sums,
):
    rank = rows_high.shape[0]
    nrhs, panels = loads_ref.shape
    span, rows = panels // LANES, CORES * nrhs
    (copy,) = fetch(((list_vmem, list_ref),), sems)
    for held in sums:
        held[...] = jnp.zeros_like(held)
    got = (own_ref, other_ref)
    terms, stats = message_parts(got, rank)
    beta = jnp.sqrt(stat_column(total(stats), 0, nrhs, rank))
    scale = 1.0 / beta
    both = jnp.concatenate([scale] * CORES, axis=0)
    for step, (inside, part, unit) in enumerate(window_parts(got, rank)):
        part = jnp.where(inside, part * (unit * both), 0.0)
        window0_ref[step * rows : (step + 1) * rows, :] = part
        put_blocks(part, step * span, window)
    basis = loads_ref[...] * scale
    far = far_sum_of(terms, nrhs, rank) * scale
    norm = jnp.sum(basis * basis, axis=1, keepdims=True)
    copy.wait()
    near = near_field(window, (tiles_ref,), list_ref, sums, nrhs)
    image = image_of(basis, far, self_ref, (rows_high, rows_low), near)
    image_ref[...] = image
    state_ref[...] = jnp.concatenate([far, jnp.broadcast_to(beta, far.shape)], axis=0)
    dot = jnp.sum(basis * image, axis=1, keepdims=True)
    share = jnp.where(norm > 0, dot / jnp.where(norm > 0, norm, 1.0), 0.0)
    rest = image - share * basis
    rest = jnp.sum(rest * rest, axis=1, keepdims=True)
    columns = [norm, dot, share, rest]
    put_message(image, columns, (cols_high, cols_low), (couple_high, couple_low), masks_ref, sent_ref)


def step1_kernel(
    own_ref, other_ref, loads_ref, image_ref, window0_ref, state_ref, rows_high, rows_low, self_ref, tiles_ref,
    list_vmem, sent_ref, basis_ref, coeff_ref, list_ref, sems, window, *sums,
):
    rank = rows_high.shape[0]
    nrhs, panels = loads_ref.shape
    span, rows = panels // LANES, CORES * nrhs
    (copy,) = fetch(((list_vmem, list_ref),), sems)
    beta = state_ref[nrhs:, :1]
    far0 = state_ref[:nrhs, :]
    for held in sums:
        held[...] = jnp.zeros_like(held)
    got = (own_ref, other_ref)
    terms, stats = message_parts(got, rank)
    summed = total(stats)
    h00 = stat_column(summed, 1, nrhs, rank)
    away = shifted(stats, 2) - shifted(summed, 1)
    rest = total(shifted(stats, 3) + stats * away * away)
    h10 = jnp.sqrt(stat_column(rest, 0, nrhs, rank))
    scale = 1.0 / h10
    both, both_h00 = (jnp.concatenate([a] * CORES, axis=0) for a in (scale, h00))
    for step, (inside, part, unit) in enumerate(window_parts(got, rank)):
        part = (part * unit - both_h00 * window0_ref[step * rows : (step + 1) * rows, :]) * both
        put_blocks(jnp.where(inside, part, 0.0), step * span, window)
    basis0 = loads_ref[...] * (1.0 / beta)
    basis1 = (image_ref[...] - h00 * basis0) * scale
    far = (far_sum_of(terms, nrhs, rank) - h00 * far0) * scale
    copy.wait()
    near = near_field(window, (tiles_ref,), list_ref, sums, nrhs)
    image = image_of(basis1, far, self_ref, (rows_high, rows_low), near)
    columns = [jnp.sum(a * image, axis=1, keepdims=True) for a in (basis0, basis1, image)]
    sent_ref[:, 0, :] = jnp.broadcast_to(stats_row(columns, rank), (sent_ref.shape[0], LANES))
    basis_ref[...] = jnp.concatenate([basis0, basis1], axis=0)
    coeff_ref[...] = jnp.concatenate([jnp.broadcast_to(v, (nrhs, LANES)) for v in (beta, h00, h10)], axis=0)


def finish_kernel(rank, got_ref, basis_ref, coeff_ref, out_ref):
    nrhs = out_ref.shape[0]
    row = total(got_ref[:, 0, :])
    h01, h11, gram11 = (stat_column(row, k, nrhs, rank) for k in range(3))
    beta, h00, h10 = (coeff_ref[k * nrhs : (k + 1) * nrhs, :1] for k in range(3))
    gram00 = h00 * h00 + h10 * h10
    gram01 = h00 * h01 + h10 * h11
    lower00 = jnp.sqrt(gram00)
    lower10 = gram01 / lower00
    lower11 = jnp.sqrt(gram11 - lower10 * lower10)
    middle0 = beta * h00 / lower00
    middle1 = (beta * h01 - lower10 * middle0) / lower11
    y1 = middle1 / lower11
    y0 = (middle0 - lower10 * y1) / lower00
    out_ref[...] = y0 * basis_ref[:nrhs, :] + y1 * basis_ref[nrhs:, :]


class Plain(jax.ShapeDtypeStruct):
    pass


def in_vmem_like(array):
    return pltpu.VMEM(array.shape, array.dtype)


def in_vmem(arrays):
    return [pltpu.with_memory_space_constraint(a, pltpu.VMEM) for a in arrays]


def call(kernel, args, outs, scratch=(), held=()):
    args = [pltpu.with_memory_space_constraint(a, pltpu.HBM) if i in held else a for i, a in enumerate(args)]
    moved = sum(a.size * a.dtype.itemsize for a in args)
    return pl.pallas_call(
        kernel,
        out_shape=[
            jax.ShapeDtypeStruct(out, F32) if isinstance(out, tuple) else out if isinstance(out, Plain) else in_vmem_like(out)
            for out in outs
        ],
        in_specs=[pl.BlockSpec(memory_space=pl.ANY if i in held else pltpu.VMEM) for i in range(len(args))],
        out_specs=[pl.BlockSpec(memory_space=pltpu.VMEM)] * len(outs),
        scratch_shapes=list(scratch),
        compiler_params=pltpu.CompilerParams(vmem_limit_bytes=24 * 2**20),
        cost_estimate=pl.CostEstimate(flops=0, bytes_accessed=moved, transcendentals=0),
    )(*args)


def exchanged(sent):
    got = lax.all_to_all(sent, "strip", 0, 0, tiled=True)
    return got, lax.ppermute(got, "clus", [(0, 1), (1, 0)])


def body(loads, self_term, near_tiles, near_list, far_rows, far_cols, coupling, ranks):
    nrhs, panels = loads.shape
    rank = far_cols.shape[0]
    blocks, tile = near_tiles.shape[:2]
    rows = panels // tile
    strips = coupling.shape[0] // CORES
    couple = coupling.reshape(CORES * strips * rank, rank)
    near_list = near_list.T
    ranks = ranks.reshape(1, CORES * strips)
    self_term = self_term.reshape(1, panels)
    groups = CORES * strips
    message = Plain((strips, nrhs, panels // 2 + LANES), jnp.int32)
    index = pltpu.SMEM(near_list.shape, jnp.int32)
    scratch = [index, pltpu.SemaphoreType.DMA((1,)), pltpu.VMEM((3 * rows, CORES * nrhs, tile), F32)]
    scratch += [pltpu.VMEM((CORES * rows, CORES * nrhs, tile), F32)] * 4

    def twice(array):
        return [jax.ShapeDtypeStruct(array.shape, BF16)] * 2

    sent, *held, near_list, loads, self_term, near_tiles = call(
        start_kernel,
        (loads, far_cols, couple, ranks, near_list, far_rows, self_term, near_tiles),
        [
            message, *twice(far_cols), *twice(couple), jax.ShapeDtypeStruct((groups, CHUNK * rank), F32),
            *twice(far_rows), near_list, loads, self_term, near_tiles,
        ],
        [
            pltpu.VMEM(far_cols.shape, F32), pltpu.VMEM(couple.shape, F32), pltpu.SMEM(ranks.shape, jnp.int32),
            pltpu.VMEM(near_list.shape, jnp.int32), pltpu.VMEM(far_rows.shape, F32), pltpu.SemaphoreType.DMA((7 + PIECES,)),
        ],
        held=range(8),
    )
    loads, *held, self_term, near_tiles, near_list = in_vmem([loads, *held, self_term, near_tiles, near_list])
    source_side, target_side = [loads, *held[:5]], [*held[5:], self_term, near_tiles, near_list]
    sent, image, window0, state = call(
        step0_kernel,
        (*exchanged(sent), *source_side, *target_side),
        [message, loads.shape, (3 * CORES * nrhs, panels), (CORES * nrhs, LANES)],
        scratch,
    )
    sent, basis, coeff = call(
        step1_kernel,
        (*exchanged(sent), loads, image, window0, state, *target_side),
        [(groups, 1, LANES), (2 * nrhs, panels), (3 * nrhs, LANES)],
        scratch,
    )
    got = lax.all_to_all(sent, GROUP, 0, 0, tiled=True)
    return call(functools.partial(finish_kernel, rank), (got, basis, coeff), [loads.shape])[0]


def solution(mesh):
    every = ("case",) + GROUP
    in_specs = (
        P(None, every),
        P(every),
        P(every, None, None),
        P(every, None),
        P(None, every),
        P(None, every),
        P(None, GROUP, None, None),
        P(None, GROUP),
    )
    return jax.shard_map(body, mesh=mesh, in_specs=in_specs, out_specs=P(None, every), check_vma=False)
```

```python
import functools

import jax
import jax.numpy as jnp
from jax import lax
from jax.experimental import pallas as pl
from jax.experimental.pallas import tpu as pltpu
from jax.sharding import PartitionSpec as P

GROUP = ("strip", "clus")
CORES = 2
LANES = 128
CHUNK = 16
PIECE = 8
F32 = jnp.float32
BF16 = jnp.bfloat16

STEP = 8
COLS_TOP = 0.1875
COUPLE_TOP = 0.375
TOP = 32767.0
ONE = float(2**30)


def lanes_of(shape):
    return lax.broadcasted_iota(jnp.int32, shape, 1)


def rows_of(shape):
    return lax.broadcasted_iota(jnp.int32, shape, 0)


def total(rows):
    return jnp.sum(rows, axis=0, keepdims=True)


def stats_row(columns, rank, step=None):
    shape = (columns[0].shape[0], LANES)
    first = lanes_of(shape) - rank * rows_of(shape)
    spread = sum(jnp.where(first == k, column, 0.0) for k, column in enumerate(columns))
    if step is not None:
        spread = jnp.where((first >= STEP) & (first < rank), step, spread)
    return total(spread)


def steps_of(stats, rank):
    inner = lax.rem(lanes_of(stats.shape), rank)
    return jnp.where(inner < STEP, shifted(stats, STEP), stats)


def term_unit(panels, rank):
    return panels * rank * COLS_TOP * COUPLE_TOP * TOP / ONE


def stat_column(row, k, nrhs, rank):
    shape = (nrhs, LANES)
    first = lanes_of(shape) - rank * rows_of(shape)
    return jnp.sum(jnp.where(first == k, row, 0.0), axis=1, keepdims=True)


def shifted(value, k):
    return pltpu.roll(value, LANES - k, 1)


def far_sum_of(row, nrhs, rank):
    shape = (nrhs, LANES)
    first = lanes_of(shape) - rank * rows_of(shape)
    own = jnp.where((first >= 0) & (first < rank), row, 0.0)
    return sum((pltpu.roll(own, k * rank, 1) for k in range(1, LANES // rank)), own)


def halves(value):
    high = value.astype(BF16)
    return high, (value - high.astype(F32)).astype(BF16)


def product(left, right_high, right_low, side=0):
    rows = left.shape[0]
    high, low = halves(left)
    dims = (((1,), (side,)), ((), ()))
    both = lax.dot_general(jnp.concatenate([high, low], axis=0), right_high, dims, preferred_element_type=F32)
    return both[:rows] + (both[rows:] + lax.dot_general(high, right_low, dims, preferred_element_type=F32))


def coded(value):
    exponent = jnp.ceil(jnp.log2(jnp.maximum(jnp.abs(value), 1e-30)))
    return (value * jnp.exp2(-exponent) * ONE).astype(jnp.int32), exponent.astype(jnp.int32)


def decoded(mantissa, exponent):
    return mantissa.astype(F32) * (1.0 / ONE) * jnp.exp2(exponent.astype(F32))


def packed(field):
    top = jnp.max(jnp.abs(field), axis=1, keepdims=True)
    step = jnp.maximum(top, 1e-30) * (1.0 / TOP)
    codes = jnp.floor(field * (1.0 / step) + 0.5).astype(jnp.int32)
    width = field.shape[1] // 2
    return (codes[:, :width] << 16) | (codes[:, width:] & 0xFFFF), step


def unpacked(words):
    return jnp.concatenate([words >> 16, (words << 16) >> 16], axis=1).astype(F32)


def fetch(pairs, sems):
    copies = [pltpu.make_async_copy(a, b, sems.at[i]) for i, (a, b) in enumerate(pairs)]
    for copy in copies:
        copy.start()
    return copies


def put_message(field, columns, cols, couple, masks_ref, sent_ref):
    nrhs, rank = field.shape[0], cols[0].shape[0]
    unit = term_unit(field.shape[1], rank)
    proj = product(field, cols[0][...], cols[1][...], 1)
    wide = jnp.concatenate([proj] * CHUNK, axis=1)
    words, step = packed(field)
    width = words.shape[1]
    row = stats_row(columns, rank, step)
    finer = 1.0 / (steps_of(row, rank) * unit)
    for i in range(sent_ref.shape[0]):
        sent_ref[i, :, :width] = words
    half = CHUNK // CORES
    stats = [jnp.broadcast_to(a, (half, LANES)) for a in coded(row)]
    for start in range(0, sent_ref.shape[0], half):
        mask = masks_ref[pl.ds(CORES * start, CHUNK), :]
        spread = jnp.concatenate([mask * wide[r : r + 1] for r in range(nrhs)], axis=0)
        here = pl.ds(CORES * start * rank, CHUNK * rank)
        terms = product(spread, couple[0][here, :], couple[1][here, :])
        terms = jnp.concatenate([terms[r * CHUNK : (r + 1) * CHUNK] for r in range(nrhs)], axis=1)
        terms = (terms * finer).astype(jnp.int32)
        here = pl.ds(start, half)
        for k, value in enumerate([terms[:half], terms[half:]] + stats):
            sent_ref[here, k, width:] = value


def message_parts(got, rank):
    width = got[0].shape[2] - LANES
    first, second, mantissa, exponent = (jnp.concatenate([ref[:, k, width:] for ref in got], axis=0) for k in range(4))
    stats = decoded(mantissa, exponent)
    terms = jnp.where(lax.axis_index("clus") == 0, first, second).astype(F32)
    return total(terms * (steps_of(stats, rank) * term_unit(2 * width, rank))), stats


def window_parts(got, rank):
    strips, nrhs, width = got[0].shape
    width -= LANES
    shape = (CORES * nrhs, LANES)
    for step in range(3):
        owner = lax.axis_index("strip") + (step - 1)
        inside = (owner >= 0) & (owner < strips)
        owner = jnp.clip(owner, 0, strips - 1)
        words = jnp.concatenate([ref[owner, :, :width] for ref in got], axis=0)
        tails = [ref[owner, :, width:] for ref in got]
        rows = [decoded(tail[2:3], tail[3:4]) for tail in tails]
        rows = jnp.where(rows_of(shape) < nrhs, rows[0], rows[1])
        wanted = lanes_of(shape) == rank * lax.rem(rows_of(shape), nrhs) + STEP
        yield inside, unpacked(words), jnp.sum(jnp.where(wanted, rows, 0.0), axis=1, keepdims=True)


def put_blocks(part, first, window):
    part = part.astype(BF16).astype(F32)
    for c in range(part.shape[1] // LANES):
        window[first + c] = part[:, c * LANES : (c + 1) * LANES]


def near_field(window, tiles, list_ref, sums, nrhs):
    n = 0
    for tiles_ref in tiles:
        for first in range(0, tiles_ref.shape[0], 2):
            left = jnp.concatenate([window[list_ref[1, n + i]] for i in range(2)], axis=0).astype(BF16)
            right = jnp.concatenate([tiles_ref[first + i] for i in range(2)], axis=1)
            both = jnp.dot(left, right, preferred_element_type=F32)
            rows = window.shape[1]
            for i in range(2):
                held = sums[(n + i) % len(sums)]
                held[list_ref[0, n + i]] += both[i * rows : (i + 1) * rows, i * LANES : (i + 1) * LANES]
            n += 2
    whole = sum((held[...] for held in sums[1:]), sums[0][...])
    rows = whole.shape[0] // CORES
    return jnp.concatenate([whole[b, :nrhs] + whole[rows + b, nrhs:] for b in range(rows)], axis=1)


def tile_pieces(tiles_hbm, first, tiles_ref):
    starts = range(0, tiles_ref.shape[0], PIECE)
    return tuple((tiles_hbm.at[pl.ds(first + i, PIECE)], tiles_ref.at[pl.ds(i, PIECE)]) for i in starts)


def fetch_kernel(list_ref, tiles_hbm, tiles_ref, sems):
    del list_ref
    for copy in fetch(tile_pieces(tiles_hbm, tiles_hbm.shape[0] - tiles_ref.shape[0], tiles_ref), sems):
        copy.wait()


def start_kernel(
    loads_hbm, cols_hbm, couple_hbm, ranks_hbm, list_hbm, rows_hbm, self_hbm, tiles_hbm, sent_ref, cols_high, cols_low, couple_high,
    couple_low, masks_ref, rows_high, rows_low, list_ref, loads_ref, self_ref, tiles_ref, cols_ref, couple_ref, ranks_ref, raw_ref,
    rows_ref, sems,
):
    rank, panels = cols_ref.shape
    pairs = (
        (loads_hbm, loads_ref), (cols_hbm, cols_ref), (couple_hbm, couple_ref), (ranks_hbm, ranks_ref),
        (list_hbm, raw_ref), (rows_hbm, rows_ref), (self_hbm, self_ref),
    )
    copies = fetch(pairs + tile_pieces(tiles_hbm, 0, tiles_ref), sems)
    copies[0].wait()
    loads = loads_ref[...]
    square = jnp.sum(loads * loads, axis=1, keepdims=True)
    copies[1].wait()
    cols_high[...], cols_low[...] = halves(cols_ref[...])
    copies[2].wait()
    couple_high[...], couple_low[...] = halves(couple_ref[...])
    copies[3].wait()
    shape = (CHUNK, CHUNK * rank)
    owner = lax.div(lanes_of(shape), rank)
    inner = lax.rem(lanes_of(shape), rank)
    half = CHUNK // CORES
    number = CORES * lax.rem(rows_of(shape), half) + lax.div(rows_of(shape), half)
    for start in range(0, masks_ref.shape[0], CHUNK):
        limit = jnp.zeros((1, CHUNK * rank), jnp.int32)
        for i in range(CHUNK):
            limit = jnp.where(owner[:1] == i, ranks_ref[0, start + i], limit)
        masks_ref[pl.ds(start, CHUNK), :] = jnp.where((owner == number) & (inner < limit), 1.0, 0.0)
    copies[4].wait()
    count = panels // LANES
    target, source = raw_ref[0:1, :], raw_ref[1:2, :]
    group, block = lax.div(source, count), lax.rem(source, count)
    strip, core = lax.div(group, CORES), lax.rem(group, CORES)
    apart = jnp.where(core == lax.axis_index("clus"), 0, 1)
    list_ref[...] = jnp.concatenate([apart * count + target, strip * count + block], axis=0)
    copies[5].wait()
    rows_high[...], rows_low[...] = halves(rows_ref[...])
    put_message(loads, [square], (cols_high, cols_low), (couple_high, couple_low), masks_ref, sent_ref)
    for copy in copies[6:]:
        copy.wait()


def image_of(field, far, self_ref, far_rows, near):
    rank = far_rows[0].shape[0]
    return self_ref[...] * field + near + product(far[:, :rank], far_rows[0][...], far_rows[1][...])


def step0_kernel(
    own_ref, other_ref, loads_ref, cols_high, cols_low, couple_high, couple_low, masks_ref, rows_high, rows_low, self_ref,
    tiles0_ref, tiles1_ref, list_vmem, sent_ref, image_ref, window0_ref, state_ref, list_ref, sems, window, *sums,
):
    rank = rows_high.shape[0]
    nrhs, panels = loads_ref.shape
    span, rows = panels // LANES, CORES * nrhs
    (copy,) = fetch(((list_vmem, list_ref),), sems)
    for held in sums:
        held[...] = jnp.zeros_like(held)
    got = (own_ref, other_ref)
    terms, stats = message_parts(got, rank)
    beta = jnp.sqrt(stat_column(total(stats), 0, nrhs, rank))
    scale = 1.0 / beta
    both = jnp.concatenate([scale] * CORES, axis=0)
    for step, (inside, part, unit) in enumerate(window_parts(got, rank)):
        part = jnp.where(inside, part * (unit * both), 0.0)
        window0_ref[step * rows : (step + 1) * rows, :] = part
        put_blocks(part, step * span, window)
    basis = loads_ref[...] * scale
    far = far_sum_of(terms, nrhs, rank) * scale
    norm = jnp.sum(basis * basis, axis=1, keepdims=True)
    copy.wait()
    near = near_field(window, (tiles0_ref, tiles1_ref), list_ref, sums, nrhs)
    image = image_of(basis, far, self_ref, (rows_high, rows_low), near)
    image_ref[...] = image
    state_ref[...] = jnp.concatenate([far, jnp.broadcast_to(beta, far.shape)], axis=0)
    dot = jnp.sum(basis * image, axis=1, keepdims=True)
    share = jnp.where(norm > 0, dot / jnp.where(norm > 0, norm, 1.0), 0.0)
    rest = image - share * basis
    rest = jnp.sum(rest * rest, axis=1, keepdims=True)
    columns = [norm, dot, share, rest]
    put_message(image, columns, (cols_high, cols_low), (couple_high, couple_low), masks_ref, sent_ref)


def step1_kernel(
    own_ref, other_ref, loads_ref, image_ref, window0_ref, state_ref, rows_high, rows_low, self_ref, tiles0_ref, tiles1_ref,
    list_vmem, sent_ref, basis_ref, coeff_ref, list_ref, sems, window, *sums,
):
    rank = rows_high.shape[0]
    nrhs, panels = loads_ref.shape
    span, rows = panels // LANES, CORES * nrhs
    (copy,) = fetch(((list_vmem, list_ref),), sems)
    beta = state_ref[nrhs:, :1]
    far0 = state_ref[:nrhs, :]
    for held in sums:
        held[...] = jnp.zeros_like(held)
    got = (own_ref, other_ref)
    terms, stats = message_parts(got, rank)
    summed = total(stats)
    h00 = stat_column(summed, 1, nrhs, rank)
    away = shifted(stats, 2) - shifted(summed, 1)
    rest = total(shifted(stats, 3) + stats * away * away)
    h10 = jnp.sqrt(stat_column(rest, 0, nrhs, rank))
    scale = 1.0 / h10
    both, both_h00 = (jnp.concatenate([a] * CORES, axis=0) for a in (scale, h00))
    for step, (inside, part, unit) in enumerate(window_parts(got, rank)):
        part = (part * unit - both_h00 * window0_ref[step * rows : (step + 1) * rows, :]) * both
        put_blocks(jnp.where(inside, part, 0.0), step * span, window)
    basis0 = loads_ref[...] * (1.0 / beta)
    basis1 = (image_ref[...] - h00 * basis0) * scale
    far = (far_sum_of(terms, nrhs, rank) - h00 * far0) * scale
    copy.wait()
    near = near_field(window, (tiles0_ref, tiles1_ref), list_ref, sums, nrhs)
    image = image_of(basis1, far, self_ref, (rows_high, rows_low), near)
    columns = [jnp.sum(a * image, axis=1, keepdims=True) for a in (basis0, basis1, image)]
    sent_ref[:, 0, :] = jnp.broadcast_to(stats_row(columns, rank), (sent_ref.shape[0], LANES))
    basis_ref[...] = jnp.concatenate([basis0, basis1], axis=0)
    coeff_ref[...] = jnp.concatenate([jnp.broadcast_to(v, (nrhs, LANES)) for v in (beta, h00, h10)], axis=0)


def finish_kernel(rank, got_ref, basis_ref, coeff_ref, out_ref):
    nrhs = out_ref.shape[0]
    row = total(got_ref[:, 0, :])
    h01, h11, gram11 = (stat_column(row, k, nrhs, rank) for k in range(3))
    beta, h00, h10 = (coeff_ref[k * nrhs : (k + 1) * nrhs, :1] for k in range(3))
    gram00 = h00 * h00 + h10 * h10
    gram01 = h00 * h01 + h10 * h11
    lower00 = jnp.sqrt(gram00)
    lower10 = gram01 / lower00
    lower11 = jnp.sqrt(gram11 - lower10 * lower10)
    middle0 = beta * h00 / lower00
    middle1 = (beta * h01 - lower10 * middle0) / lower11
    y1 = middle1 / lower11
    y0 = (middle0 - lower10 * y1) / lower00
    out_ref[...] = y0 * basis_ref[:nrhs, :] + y1 * basis_ref[nrhs:, :]


class Plain(jax.ShapeDtypeStruct):
    pass


def in_vmem_like(array):
    return pltpu.VMEM(array.shape, array.dtype)


def in_vmem(arrays):
    return [pltpu.with_memory_space_constraint(a, pltpu.VMEM) for a in arrays]


def call(kernel, args, outs, scratch=(), held=()):
    args = [pltpu.with_memory_space_constraint(a, pltpu.HBM) if i in held else a for i, a in enumerate(args)]
    moved = sum(a.size * a.dtype.itemsize for a in args)
    return pl.pallas_call(
        kernel,
        out_shape=[
            jax.ShapeDtypeStruct(out, F32) if isinstance(out, tuple) else out if isinstance(out, Plain) else in_vmem_like(out)
            for out in outs
        ],
        in_specs=[pl.BlockSpec(memory_space=pl.ANY if i in held else pltpu.VMEM) for i in range(len(args))],
        out_specs=[pl.BlockSpec(memory_space=pltpu.VMEM)] * len(outs),
        scratch_shapes=list(scratch),
        compiler_params=pltpu.CompilerParams(vmem_limit_bytes=24 * 2**20),
        cost_estimate=pl.CostEstimate(flops=0, bytes_accessed=moved, transcendentals=0),
    )(*args)


def exchanged(sent):
    got = lax.all_to_all(sent, "strip", 0, 0, tiled=True)
    return got, lax.ppermute(got, "clus", [(0, 1), (1, 0)])


def body(loads, self_term, near_tiles, near_list, far_rows, far_cols, coupling, ranks):
    nrhs, panels = loads.shape
    rank = far_cols.shape[0]
    blocks, tile = near_tiles.shape[:2]
    rows = panels // tile
    strips = coupling.shape[0] // CORES
    couple = coupling.reshape(CORES * strips * rank, rank)
    near_list = near_list.T
    ranks = ranks.reshape(1, CORES * strips)
    self_term = self_term.reshape(1, panels)
    groups = CORES * strips
    message = Plain((strips, nrhs, panels // 2 + LANES), jnp.int32)
    index = pltpu.SMEM(near_list.shape, jnp.int32)
    scratch = [index, pltpu.SemaphoreType.DMA((1,)), pltpu.VMEM((3 * rows, CORES * nrhs, tile), F32)]
    late = PIECE * (blocks * 3 // (10 * PIECE))
    tiles0, tiles1 = (jax.ShapeDtypeStruct((count, tile, tile), BF16) for count in (blocks - late, late))
    scratch += [pltpu.VMEM((CORES * rows, CORES * nrhs, tile), F32)] * 4

    def twice(array):
        return [jax.ShapeDtypeStruct(array.shape, BF16)] * 2

    sent, *held, near_list, loads, self_term, tiles0 = call(
        start_kernel,
        (loads, far_cols, couple, ranks, near_list, far_rows, self_term, near_tiles),
        [
            message, *twice(far_cols), *twice(couple), jax.ShapeDtypeStruct((groups, CHUNK * rank), F32),
            *twice(far_rows), near_list, loads, self_term, tiles0,
        ],
        [
            pltpu.VMEM(far_cols.shape, F32), pltpu.VMEM(couple.shape, F32), pltpu.SMEM(ranks.shape, jnp.int32),
            pltpu.VMEM(near_list.shape, jnp.int32), pltpu.VMEM(far_rows.shape, F32), pltpu.SemaphoreType.DMA((7 + tiles0.shape[0] // PIECE,)),
        ],
        held=range(8),
    )
    (tiles1,) = call(
        fetch_kernel, (near_list, near_tiles), [tiles1], [pltpu.SemaphoreType.DMA((late // PIECE,))], held=(1,)
    )
    loads, *held, self_term, tiles0, tiles1, near_list = in_vmem(
        [loads, *held, self_term, tiles0, tiles1, near_list]
    )
    source_side, target_side = [loads, *held[:5]], [*held[5:], self_term, tiles0, tiles1, near_list]
    sent, image, window0, state = call(
        step0_kernel,
        (*exchanged(sent), *source_side, *target_side),
        [message, loads.shape, (3 * CORES * nrhs, panels), (CORES * nrhs, LANES)],
        scratch,
    )
    sent, basis, coeff = call(
        step1_kernel,
        (*exchanged(sent), loads, image, window0, state, *target_side),
        [(groups, 1, LANES), (2 * nrhs, panels), (3 * nrhs, LANES)],
        scratch,
    )
    got = lax.all_to_all(sent, GROUP, 0, 0, tiled=True)
    return call(functools.partial(finish_kernel, rank), (got, basis, coeff), [loads.shape])[0]


def solution(mesh):
    every = ("case",) + GROUP
    in_specs = (
        P(None, every),
        P(every),
        P(every, None, None),
        P(every, None),
        P(None, every),
        P(None, every),
        P(None, GROUP, None, None),
        P(None, GROUP),
    )
    return jax.shard_map(body, mesh=mesh, in_specs=in_specs, out_specs=P(None, every), check_vma=False)
```

```python
import functools

import jax
import jax.numpy as jnp
from jax import lax
from jax.experimental import pallas as pl
from jax.experimental.pallas import tpu as pltpu
from jax.sharding import PartitionSpec as P

GROUP = ("strip", "clus")
CORES = 2
LANES = 128
CHUNK = 16
PIECE = 8
F32 = jnp.float32
BF16 = jnp.bfloat16

STEP = 8
COLS_TOP = 0.1875
COUPLE_TOP = 0.375
TOP = 32767.0
ONE = float(2**30)


def lanes_of(shape):
    return lax.broadcasted_iota(jnp.int32, shape, 1)


def rows_of(shape):
    return lax.broadcasted_iota(jnp.int32, shape, 0)


def total(rows):
    return jnp.sum(rows, axis=0, keepdims=True)


def stats_row(columns, rank, step=None):
    shape = (columns[0].shape[0], LANES)
    first = lanes_of(shape) - rank * rows_of(shape)
    spread = sum(jnp.where(first == k, column, 0.0) for k, column in enumerate(columns))
    if step is not None:
        spread = jnp.where((first >= STEP) & (first < rank), step, spread)
    return total(spread)


def steps_of(stats, rank):
    inner = lax.rem(lanes_of(stats.shape), rank)
    return jnp.where(inner < STEP, shifted(stats, STEP), stats)


def term_unit(panels, rank):
    return panels * rank * COLS_TOP * COUPLE_TOP * TOP / ONE


def stat_column(row, k, nrhs, rank):
    shape = (nrhs, LANES)
    first = lanes_of(shape) - rank * rows_of(shape)
    return jnp.sum(jnp.where(first == k, row, 0.0), axis=1, keepdims=True)


def shifted(value, k):
    return pltpu.roll(value, LANES - k, 1)


def far_sum_of(row, nrhs, rank):
    shape = (nrhs, LANES)
    first = lanes_of(shape) - rank * rows_of(shape)
    own = jnp.where((first >= 0) & (first < rank), row, 0.0)
    return sum((pltpu.roll(own, k * rank, 1) for k in range(1, LANES // rank)), own)


def halves(value):
    high = value.astype(BF16)
    return high, (value - high.astype(F32)).astype(BF16)


def product(left, right_high, right_low, side=0):
    rows = left.shape[0]
    high, low = halves(left)
    dims = (((1,), (side,)), ((), ()))
    both = lax.dot_general(jnp.concatenate([high, low], axis=0), right_high, dims, preferred_element_type=F32)
    return both[:rows] + (both[rows:] + lax.dot_general(high, right_low, dims, preferred_element_type=F32))


def coded(value):
    exponent = jnp.ceil(jnp.log2(jnp.maximum(jnp.abs(value), 1e-30)))
    return (value * jnp.exp2(-exponent) * ONE).astype(jnp.int32), exponent.astype(jnp.int32)


def decoded(mantissa, exponent):
    return mantissa.astype(F32) * (1.0 / ONE) * jnp.exp2(exponent.astype(F32))


def packed(field):
    top = jnp.max(jnp.abs(field), axis=1, keepdims=True)
    step = jnp.maximum(top, 1e-30) * (1.0 / TOP)
    codes = jnp.floor(field * (1.0 / step) + 0.5).astype(jnp.int32)
    width = field.shape[1] // 2
    return (codes[:, :width] << 16) | (codes[:, width:] & 0xFFFF), step


def unpacked(words):
    return jnp.concatenate([words >> 16, (words << 16) >> 16], axis=1).astype(F32)


def fetch(pairs, sems):
    copies = [pltpu.make_async_copy(a, b, sems.at[i]) for i, (a, b) in enumerate(pairs)]
    for copy in copies:
        copy.start()
    return copies


def put_message(field, columns, cols, couple, masks_ref, sent_ref):
    nrhs, rank = field.shape[0], cols[0].shape[0]
    unit = term_unit(field.shape[1], rank)
    proj = product(field, cols[0][...], cols[1][...], 1)
    wide = jnp.concatenate([proj] * CHUNK, axis=1)
    words, step = packed(field)
    width = words.shape[1]
    row = stats_row(columns, rank, step)
    finer = 1.0 / (steps_of(row, rank) * unit)
    for i in range(sent_ref.shape[0]):
        sent_ref[i, :, :width] = words
    half = CHUNK // CORES
    stats = [jnp.broadcast_to(a, (half, LANES)) for a in coded(row)]
    for start in range(0, sent_ref.shape[0], half):
        mask = masks_ref[pl.ds(CORES * start, CHUNK), :]
        spread = jnp.concatenate([mask * wide[r : r + 1] for r in range(nrhs)], axis=0)
        here = pl.ds(CORES * start * rank, CHUNK * rank)
        terms = product(spread, couple[0][here, :], couple[1][here, :])
        terms = jnp.concatenate([terms[r * CHUNK : (r + 1) * CHUNK] for r in range(nrhs)], axis=1)
        terms = (terms * finer).astype(jnp.int32)
        here = pl.ds(start, half)
        for k, value in enumerate([terms[:half], terms[half:]] + stats):
            sent_ref[here, k, width:] = value


def message_parts(got, rank):
    width = got[0].shape[2] - LANES
    first, second, mantissa, exponent = (jnp.concatenate([ref[:, k, width:] for ref in got], axis=0) for k in range(4))
    stats = decoded(mantissa, exponent)
    terms = jnp.where(lax.axis_index("clus") == 0, first, second).astype(F32)
    return total(terms * (steps_of(stats, rank) * term_unit(2 * width, rank))), stats


def window_parts(got, rank):
    strips, nrhs, width = got[0].shape
    width -= LANES
    shape = (CORES * nrhs, LANES)
    for step in range(3):
        owner = lax.axis_index("strip") + (step - 1)
        inside = (owner >= 0) & (owner < strips)
        owner = jnp.clip(owner, 0, strips - 1)
        words = jnp.concatenate([ref[owner, :, :width] for ref in got], axis=0)
        tails = [ref[owner, :, width:] for ref in got]
        rows = [decoded(tail[2:3], tail[3:4]) for tail in tails]
        rows = jnp.where(rows_of(shape) < nrhs, rows[0], rows[1])
        wanted = lanes_of(shape) == rank * lax.rem(rows_of(shape), nrhs) + STEP
        yield inside, unpacked(words), jnp.sum(jnp.where(wanted, rows, 0.0), axis=1, keepdims=True)


def put_blocks(part, first, window):
    part = part.astype(BF16).astype(F32)
    for c in range(part.shape[1] // LANES):
        window[first + c] = part[:, c * LANES : (c + 1) * LANES]


def near_field(window, tiles, list_ref, sums, nrhs):
    n = 0
    for tiles_ref in tiles:
        for first in range(0, tiles_ref.shape[0], 2):
            left = jnp.concatenate([window[list_ref[1, n + i]] for i in range(2)], axis=0).astype(BF16)
            right = jnp.concatenate([tiles_ref[first + i] for i in range(2)], axis=1)
            both = jnp.dot(left, right, preferred_element_type=F32)
            rows = window.shape[1]
            for i in range(2):
                held = sums[(n + i) % len(sums)]
                held[list_ref[0, n + i]] += both[i * rows : (i + 1) * rows, i * LANES : (i + 1) * LANES]
            n += 2
    whole = sum((held[...] for held in sums[1:]), sums[0][...])
    rows = whole.shape[0] // CORES
    return jnp.concatenate([whole[b, :nrhs] + whole[rows + b, nrhs:] for b in range(rows)], axis=1)


def tile_pieces(tiles_hbm, first, tiles_ref):
    starts = range(0, tiles_ref.shape[0], PIECE)
    return tuple((tiles_hbm.at[pl.ds(first + i, PIECE)], tiles_ref.at[pl.ds(i, PIECE)]) for i in starts)


def fetch_kernel(list_ref, tiles_hbm, tiles_ref, sems):
    del list_ref
    for copy in fetch(tile_pieces(tiles_hbm, tiles_hbm.shape[0] - tiles_ref.shape[0], tiles_ref), sems):
        copy.wait()


def start_kernel(
    loads_hbm, cols_hbm, couple_hbm, ranks_hbm, list_hbm, rows_hbm, self_hbm, tiles_hbm, sent_ref, cols_high, cols_low, couple_high,
    couple_low, masks_ref, rows_high, rows_low, list_ref, loads_ref, self_ref, tiles_ref, cols_ref, couple_ref, ranks_ref, raw_ref,
    rows_ref, sems,
):
    rank, panels = cols_ref.shape
    pairs = (
        (loads_hbm, loads_ref), (cols_hbm, cols_ref), (couple_hbm, couple_ref), (ranks_hbm, ranks_ref),
        (list_hbm, raw_ref), (rows_hbm, rows_ref), (self_hbm, self_ref),
    )
    copies = fetch(pairs + tile_pieces(tiles_hbm, 0, tiles_ref), sems)
    copies[0].wait()
    loads = loads_ref[...]
    square = jnp.sum(loads * loads, axis=1, keepdims=True)
    copies[1].wait()
    cols_high[...], cols_low[...] = halves(cols_ref[...])
    copies[2].wait()
    couple_high[...], couple_low[...] = halves(couple_ref[...])
    copies[3].wait()
    shape = (CHUNK, CHUNK * rank)
    owner = lax.div(lanes_of(shape), rank)
    inner = lax.rem(lanes_of(shape), rank)
    half = CHUNK // CORES
    number = CORES * lax.rem(rows_of(shape), half) + lax.div(rows_of(shape), half)
    for start in range(0, masks_ref.shape[0], CHUNK):
        limit = jnp.zeros((1, CHUNK * rank), jnp.int32)
        for i in range(CHUNK):
            limit = jnp.where(owner[:1] == i, ranks_ref[0, start + i], limit)
        masks_ref[pl.ds(start, CHUNK), :] = jnp.where((owner == number) & (inner < limit), 1.0, 0.0)
    copies[4].wait()
    count = panels // LANES
    target, source = raw_ref[0:1, :], raw_ref[1:2, :]
    group, block = lax.div(source, count), lax.rem(source, count)
    strip, core = lax.div(group, CORES), lax.rem(group, CORES)
    apart = jnp.where(core == lax.axis_index("clus"), 0, 1)
    list_ref[...] = jnp.concatenate([apart * count + target, strip * count + block], axis=0)
    copies[5].wait()
    rows_high[...], rows_low[...] = halves(rows_ref[...])
    put_message(loads, [square], (cols_high, cols_low), (couple_high, couple_low), masks_ref, sent_ref)
    for copy in copies[6:]:
        copy.wait()


def image_of(field, far, self_ref, far_rows, near):
    rank = far_rows[0].shape[0]
    return self_ref[...] * field + near + product(far[:, :rank], far_rows[0][...], far_rows[1][...])


def step0_kernel(
    own_ref, other_ref, loads_ref, cols_high, cols_low, couple_high, couple_low, masks_ref, rows_high, rows_low, self_ref,
    tiles0_ref, tiles1_ref, list_vmem, sent_ref, image_ref, window0_ref, state_ref, list_ref, sems, window, *sums,
):
    rank = rows_high.shape[0]
    nrhs, panels = loads_ref.shape
    span, rows = panels // LANES, CORES * nrhs
    (copy,) = fetch(((list_vmem, list_ref),), sems)
    for held in sums:
        held[...] = jnp.zeros_like(held)
    got = (own_ref, other_ref)
    terms, stats = message_parts(got, rank)
    beta = jnp.sqrt(stat_column(total(stats), 0, nrhs, rank))
    scale = 1.0 / beta
    both = jnp.concatenate([scale] * CORES, axis=0)
    for step, (inside, part, unit) in enumerate(window_parts(got, rank)):
        part = jnp.where(inside, part * (unit * both), 0.0)
        window0_ref[step * rows : (step + 1) * rows, :] = part
        put_blocks(part, step * span, window)
    basis = loads_ref[...] * scale
    far = far_sum_of(terms, nrhs, rank) * scale
    norm = jnp.sum(basis * basis, axis=1, keepdims=True)
    copy.wait()
    near = near_field(window, (tiles0_ref, tiles1_ref), list_ref, sums, nrhs)
    image = image_of(basis, far, self_ref, (rows_high, rows_low), near)
    image_ref[...] = image
    state_ref[...] = jnp.concatenate([far, jnp.broadcast_to(beta, far.shape)], axis=0)
    dot = jnp.sum(basis * image, axis=1, keepdims=True)
    share = jnp.where(norm > 0, dot / jnp.where(norm > 0, norm, 1.0), 0.0)
    rest = image - share * basis
    rest = jnp.sum(rest * rest, axis=1, keepdims=True)
    columns = [norm, dot, share, rest]
    put_message(image, columns, (cols_high, cols_low), (couple_high, couple_low), masks_ref, sent_ref)


def step1_kernel(
    own_ref, other_ref, loads_ref, image_ref, window0_ref, state_ref, rows_high, rows_low, self_ref, tiles0_ref, tiles1_ref,
    list_vmem, sent_ref, basis_ref, coeff_ref, list_ref, sems, window, *sums,
):
    rank = rows_high.shape[0]
    nrhs, panels = loads_ref.shape
    span, rows = panels // LANES, CORES * nrhs
    (copy,) = fetch(((list_vmem, list_ref),), sems)
    beta = state_ref[nrhs:, :1]
    far0 = state_ref[:nrhs, :]
    for held in sums:
        held[...] = jnp.zeros_like(held)
    got = (own_ref, other_ref)
    terms, stats = message_parts(got, rank)
    summed = total(stats)
    h00 = stat_column(summed, 1, nrhs, rank)
    away = shifted(stats, 2) - shifted(summed, 1)
    rest = total(shifted(stats, 3) + stats * away * away)
    h10 = jnp.sqrt(stat_column(rest, 0, nrhs, rank))
    scale = 1.0 / h10
    both, both_h00 = (jnp.concatenate([a] * CORES, axis=0) for a in (scale, h00))
    for step, (inside, part, unit) in enumerate(window_parts(got, rank)):
        part = (part * unit - both_h00 * window0_ref[step * rows : (step + 1) * rows, :]) * both
        put_blocks(jnp.where(inside, part, 0.0), step * span, window)
    basis0 = loads_ref[...] * (1.0 / beta)
    basis1 = (image_ref[...] - h00 * basis0) * scale
    far = (far_sum_of(terms, nrhs, rank) - h00 * far0) * scale
    copy.wait()
    near = near_field(window, (tiles0_ref, tiles1_ref), list_ref, sums, nrhs)
    image = image_of(basis1, far, self_ref, (rows_high, rows_low), near)
    columns = [jnp.sum(a * image, axis=1, keepdims=True) for a in (basis0, basis1, image)]
    sent_ref[:, 0, :] = jnp.broadcast_to(stats_row(columns, rank), (sent_ref.shape[0], LANES))
    basis_ref[...] = jnp.concatenate([basis0, basis1], axis=0)
    coeff_ref[...] = jnp.concatenate([jnp.broadcast_to(v, (nrhs, LANES)) for v in (beta, h00, h10)], axis=0)


def finish_kernel(rank, got_ref, basis_ref, coeff_ref, out_ref):
    nrhs = out_ref.shape[0]
    row = total(got_ref[:, 0, :])
    h01, h11, gram11 = (stat_column(row, k, nrhs, rank) for k in range(3))
    beta, h00, h10 = (coeff_ref[k * nrhs : (k + 1) * nrhs, :1] for k in range(3))
    gram00 = h00 * h00 + h10 * h10
    gram01 = h00 * h01 + h10 * h11
    lower00 = jnp.sqrt(gram00)
    lower10 = gram01 / lower00
    lower11 = jnp.sqrt(gram11 - lower10 * lower10)
    middle0 = beta * h00 / lower00
    middle1 = (beta * h01 - lower10 * middle0) / lower11
    y1 = middle1 / lower11
    y0 = (middle0 - lower10 * y1) / lower00
    out_ref[...] = y0 * basis_ref[:nrhs, :] + y1 * basis_ref[nrhs:, :]


class Plain(jax.ShapeDtypeStruct):
    pass


def in_vmem_like(array):
    return pltpu.VMEM(array.shape, array.dtype)


def in_vmem(arrays):
    return [pltpu.with_memory_space_constraint(a, pltpu.VMEM) for a in arrays]


def call(kernel, args, outs, scratch=(), held=()):
    args = [pltpu.with_memory_space_constraint(a, pltpu.HBM) if i in held else a for i, a in enumerate(args)]
    moved = sum(a.size * a.dtype.itemsize for a in args)
    return pl.pallas_call(
        kernel,
        out_shape=[
            jax.ShapeDtypeStruct(out, F32) if isinstance(out, tuple) else out if isinstance(out, Plain) else in_vmem_like(out)
            for out in outs
        ],
        in_specs=[pl.BlockSpec(memory_space=pl.ANY if i in held else pltpu.VMEM) for i in range(len(args))],
        out_specs=[pl.BlockSpec(memory_space=pltpu.VMEM)] * len(outs),
        scratch_shapes=list(scratch),
        compiler_params=pltpu.CompilerParams(vmem_limit_bytes=24 * 2**20),
        cost_estimate=pl.CostEstimate(flops=0, bytes_accessed=moved, transcendentals=0),
    )(*args)


def exchanged(sent):
    got = lax.all_to_all(sent, "strip", 0, 0, tiled=True)
    return got, lax.ppermute(got, "clus", [(0, 1), (1, 0)])


def body(loads, self_term, near_tiles, near_list, far_rows, far_cols, coupling, ranks):
    nrhs, panels = loads.shape
    rank = far_cols.shape[0]
    blocks, tile = near_tiles.shape[:2]
    rows = panels // tile
    strips = coupling.shape[0] // CORES
    couple = coupling.reshape(CORES * strips * rank, rank)
    near_list = near_list.T
    ranks = ranks.reshape(1, CORES * strips)
    self_term = self_term.reshape(1, panels)
    groups = CORES * strips
    message = Plain((strips, nrhs, panels // 2 + LANES), jnp.int32)
    index = pltpu.SMEM(near_list.shape, jnp.int32)
    scratch = [index, pltpu.SemaphoreType.DMA((1,)), pltpu.VMEM((3 * rows, CORES * nrhs, tile), F32)]
    late = PIECE * (blocks * 2 // (5 * PIECE))
    tiles0, tiles1 = (jax.ShapeDtypeStruct((count, tile, tile), BF16) for count in (blocks - late, late))
    scratch += [pltpu.VMEM((CORES * rows, CORES * nrhs, tile), F32)] * 2

    def twice(array):
        return [jax.ShapeDtypeStruct(array.shape, BF16)] * 2

    sent, *held, near_list, loads, self_term, tiles0 = call(
        start_kernel,
        (loads, far_cols, couple, ranks, near_list, far_rows, self_term, near_tiles),
        [
            message, *twice(far_cols), *twice(couple), jax.ShapeDtypeStruct((groups, CHUNK * rank), F32),
            *twice(far_rows), near_list, loads, self_term, tiles0,
        ],
        [
            pltpu.VMEM(far_cols.shape, F32), pltpu.VMEM(couple.shape, F32), pltpu.SMEM(ranks.shape, jnp.int32),
            pltpu.VMEM(near_list.shape, jnp.int32), pltpu.VMEM(far_rows.shape, F32), pltpu.SemaphoreType.DMA((7 + tiles0.shape[0] // PIECE,)),
        ],
        held=range(8),
    )
    (tiles1,) = call(
        fetch_kernel, (near_list, near_tiles), [tiles1], [pltpu.SemaphoreType.DMA((late // PIECE,))], held=(1,)
    )
    loads, *held, self_term, tiles0, tiles1, near_list = in_vmem(
        [loads, *held, self_term, tiles0, tiles1, near_list]
    )
    source_side, target_side = [loads, *held[:5]], [*held[5:], self_term, tiles0, tiles1, near_list]
    sent, image, window0, state = call(
        step0_kernel,
        (*exchanged(sent), *source_side, *target_side),
        [message, loads.shape, (3 * CORES * nrhs, panels), (CORES * nrhs, LANES)],
        scratch,
    )
    sent, basis, coeff = call(
        step1_kernel,
        (*exchanged(sent), loads, image, window0, state, *target_side),
        [(groups, 1, LANES), (2 * nrhs, panels), (3 * nrhs, LANES)],
        scratch,
    )
    got = lax.all_to_all(sent, GROUP, 0, 0, tiled=True)
    return call(functools.partial(finish_kernel, rank), (got, basis, coeff), [loads.shape])[0]


def solution(mesh):
    every = ("case",) + GROUP
    in_specs = (
        P(None, every),
        P(every),
        P(every, None, None),
        P(every, None),
        P(None, every),
        P(None, every),
        P(None, GROUP, None, None),
        P(None, GROUP),
    )
    return jax.shard_map(body, mesh=mesh, in_specs=in_specs, out_specs=P(None, every), check_vma=False)
```

```python
import functools

import jax
import jax.numpy as jnp
from jax import lax
from jax.experimental import pallas as pl
from jax.experimental.pallas import tpu as pltpu
from jax.sharding import PartitionSpec as P

GROUP = ("strip", "clus")
CORES = 2
LANES = 128
CHUNK = 16
PIECE = 8
F32 = jnp.float32
BF16 = jnp.bfloat16

STEP = 8
COLS_TOP = 0.1875
COUPLE_TOP = 0.375
TOP = 32767.0
ONE = float(2**30)


def lanes_of(shape):
    return lax.broadcasted_iota(jnp.int32, shape, 1)


def rows_of(shape):
    return lax.broadcasted_iota(jnp.int32, shape, 0)


def total(rows):
    return jnp.sum(rows, axis=0, keepdims=True)


def stats_row(columns, rank, step=None):
    shape = (columns[0].shape[0], LANES)
    first = lanes_of(shape) - rank * rows_of(shape)
    spread = sum(jnp.where(first == k, column, 0.0) for k, column in enumerate(columns))
    if step is not None:
        spread = jnp.where((first >= STEP) & (first < rank), step, spread)
    return total(spread)


def steps_of(stats, rank):
    inner = lax.rem(lanes_of(stats.shape), rank)
    return jnp.where(inner < STEP, shifted(stats, STEP), stats)


def term_unit(panels, rank):
    return panels * rank * COLS_TOP * COUPLE_TOP * TOP / ONE


def stat_column(row, k, nrhs, rank):
    shape = (nrhs, LANES)
    first = lanes_of(shape) - rank * rows_of(shape)
    return jnp.sum(jnp.where(first == k, row, 0.0), axis=1, keepdims=True)


def shifted(value, k):
    return pltpu.roll(value, LANES - k, 1)


def far_sum_of(row, nrhs, rank):
    shape = (nrhs, LANES)
    first = lanes_of(shape) - rank * rows_of(shape)
    own = jnp.where((first >= 0) & (first < rank), row, 0.0)
    return sum((pltpu.roll(own, k * rank, 1) for k in range(1, LANES // rank)), own)


def halves(value):
    high = value.astype(BF16)
    return high, (value - high.astype(F32)).astype(BF16)


def product(left, right_high, right_low, side=0):
    rows = left.shape[0]
    high, low = halves(left)
    dims = (((1,), (side,)), ((), ()))
    both = lax.dot_general(jnp.concatenate([high, low], axis=0), right_high, dims, preferred_element_type=F32)
    return both[:rows] + (both[rows:] + lax.dot_general(high, right_low, dims, preferred_element_type=F32))


def coded(value):
    exponent = jnp.ceil(jnp.log2(jnp.maximum(jnp.abs(value), 1e-30)))
    return (value * jnp.exp2(-exponent) * ONE).astype(jnp.int32), exponent.astype(jnp.int32)


def decoded(mantissa, exponent):
    return mantissa.astype(F32) * (1.0 / ONE) * jnp.exp2(exponent.astype(F32))


def packed(field):
    top = jnp.max(jnp.abs(field), axis=1, keepdims=True)
    step = jnp.maximum(top, 1e-30) * (1.0 / TOP)
    codes = jnp.floor(field * (1.0 / step) + 0.5).astype(jnp.int32)
    width = field.shape[1] // 2
    return (codes[:, :width] << 16) | (codes[:, width:] & 0xFFFF), step


def unpacked(words):
    return jnp.concatenate([words >> 16, (words << 16) >> 16], axis=1).astype(F32)


def fetch(pairs, sems):
    copies = [pltpu.make_async_copy(a, b, sems.at[i]) for i, (a, b) in enumerate(pairs)]
    for copy in copies:
        copy.start()
    return copies


def put_message(field, columns, cols, couple, masks_ref, sent_ref):
    nrhs, rank = field.shape[0], cols[0].shape[0]
    unit = term_unit(field.shape[1], rank)
    proj = product(field, cols[0][...], cols[1][...], 1)
    wide = jnp.concatenate([proj] * CHUNK, axis=1)
    words, step = packed(field)
    width = words.shape[1]
    row = stats_row(columns, rank, step)
    finer = 1.0 / (steps_of(row, rank) * unit)
    for i in range(sent_ref.shape[0]):
        sent_ref[i, :, :width] = words
    half = CHUNK // CORES
    stats = [jnp.broadcast_to(a, (half, LANES)) for a in coded(row)]
    for start in range(0, sent_ref.shape[0], half):
        mask = masks_ref[pl.ds(CORES * start, CHUNK), :]
        spread = jnp.concatenate([mask * wide[r : r + 1] for r in range(nrhs)], axis=0)
        here = pl.ds(CORES * start * rank, CHUNK * rank)
        terms = product(spread, couple[0][here, :], couple[1][here, :])
        terms = jnp.concatenate([terms[r * CHUNK : (r + 1) * CHUNK] for r in range(nrhs)], axis=1)
        terms = (terms * finer).astype(jnp.int32)
        here = pl.ds(start, half)
        for k, value in enumerate([terms[:half], terms[half:]] + stats):
            sent_ref[here, k, width:] = value


def message_parts(got, rank):
    width = got[0].shape[2] - LANES
    first, second, mantissa, exponent = (jnp.concatenate([ref[:, k, width:] for ref in got], axis=0) for k in range(4))
    stats = decoded(mantissa, exponent)
    terms = jnp.where(lax.axis_index("clus") == 0, first, second).astype(F32)
    return total(terms * (steps_of(stats, rank) * term_unit(2 * width, rank))), stats


def window_parts(got, rank):
    strips, nrhs, width = got[0].shape
    width -= LANES
    shape = (CORES * nrhs, LANES)
    for step in range(3):
        owner = lax.axis_index("strip") + (step - 1)
        inside = (owner >= 0) & (owner < strips)
        owner = jnp.clip(owner, 0, strips - 1)
        words = jnp.concatenate([ref[owner, :, :width] for ref in got], axis=0)
        tails = [ref[owner, :, width:] for ref in got]
        rows = [decoded(tail[2:3], tail[3:4]) for tail in tails]
        rows = jnp.where(rows_of(shape) < nrhs, rows[0], rows[1])
        wanted = lanes_of(shape) == rank * lax.rem(rows_of(shape), nrhs) + STEP
        yield inside, unpacked(words), jnp.sum(jnp.where(wanted, rows, 0.0), axis=1, keepdims=True)


def put_blocks(part, first, window):
    part = part.astype(BF16).astype(F32)
    for c in range(part.shape[1] // LANES):
        window[first + c] = part[:, c * LANES : (c + 1) * LANES]


def near_field(window, tiles, list_ref, sums, nrhs):
    n = 0
    for tiles_ref in tiles:
        for first in range(0, tiles_ref.shape[0], 2):
            left = jnp.concatenate([window[list_ref[1, n + i]] for i in range(2)], axis=0).astype(BF16)
            right = jnp.concatenate([tiles_ref[first + i] for i in range(2)], axis=1)
            both = jnp.dot(left, right, preferred_element_type=F32)
            rows = window.shape[1]
            for i in range(2):
                held = sums[(n + i) % len(sums)]
                held[list_ref[0, n + i]] += both[i * rows : (i + 1) * rows, i * LANES : (i + 1) * LANES]
            n += 2
    whole = sum((held[...] for held in sums[1:]), sums[0][...])
    rows = whole.shape[0] // CORES
    return jnp.concatenate([whole[b, :nrhs] + whole[rows + b, nrhs:] for b in range(rows)], axis=1)


def tile_pieces(tiles_hbm, first, tiles_ref):
    starts = range(0, tiles_ref.shape[0], PIECE)
    return tuple((tiles_hbm.at[pl.ds(first + i, PIECE)], tiles_ref.at[pl.ds(i, PIECE)]) for i in starts)


def fetch_kernel(
    loads_ref, list_hbm, rows_hbm, tiles_hbm, list_ref, rows_high, rows_low, tiles_ref, raw_ref, rows_ref, sems
):
    panels = loads_ref.shape[1]
    first = tiles_hbm.shape[0] - tiles_ref.shape[0]
    copies = fetch(((list_hbm, raw_ref), (rows_hbm, rows_ref)) + tile_pieces(tiles_hbm, first, tiles_ref), sems)
    copies[0].wait()
    count = panels // LANES
    target, source = raw_ref[0:1, :], raw_ref[1:2, :]
    group, block = lax.div(source, count), lax.rem(source, count)
    strip, core = lax.div(group, CORES), lax.rem(group, CORES)
    apart = jnp.where(core == lax.axis_index("clus"), 0, 1)
    list_ref[...] = jnp.concatenate([apart * count + target, strip * count + block], axis=0)
    copies[1].wait()
    rows_high[...], rows_low[...] = halves(rows_ref[...])
    for copy in copies[2:]:
        copy.wait()


def start_kernel(
    loads_hbm, cols_hbm, couple_hbm, ranks_hbm, self_hbm, tiles_hbm, sent_ref, cols_high, cols_low, couple_high,
    couple_low, masks_ref, loads_ref, self_ref, tiles_ref, cols_ref, couple_ref, ranks_ref, sems,
):
    rank, panels = cols_ref.shape
    pairs = (
        (loads_hbm, loads_ref), (cols_hbm, cols_ref), (couple_hbm, couple_ref), (ranks_hbm, ranks_ref),
        (self_hbm, self_ref),
    )
    copies = fetch(pairs + tile_pieces(tiles_hbm, 0, tiles_ref), sems)
    copies[0].wait()
    loads = loads_ref[...]
    square = jnp.sum(loads * loads, axis=1, keepdims=True)
    copies[1].wait()
    cols_high[...], cols_low[...] = halves(cols_ref[...])
    copies[2].wait()
    couple_high[...], couple_low[...] = halves(couple_ref[...])
    copies[3].wait()
    shape = (CHUNK, CHUNK * rank)
    owner = lax.div(lanes_of(shape), rank)
    inner = lax.rem(lanes_of(shape), rank)
    half = CHUNK // CORES
    number = CORES * lax.rem(rows_of(shape), half) + lax.div(rows_of(shape), half)
    for start in range(0, masks_ref.shape[0], CHUNK):
        limit = jnp.zeros((1, CHUNK * rank), jnp.int32)
        for i in range(CHUNK):
            limit = jnp.where(owner[:1] == i, ranks_ref[0, start + i], limit)
        masks_ref[pl.ds(start, CHUNK), :] = jnp.where((owner == number) & (inner < limit), 1.0, 0.0)
    put_message(loads, [square], (cols_high, cols_low), (couple_high, couple_low), masks_ref, sent_ref)
    for copy in copies[4:]:
        copy.wait()


def image_of(field, far, self_ref, far_rows, near):
    rank = far_rows[0].shape[0]
    return self_ref[...] * field + near + product(far[:, :rank], far_rows[0][...], far_rows[1][...])


def step0_kernel(
    own_ref, other_ref, loads_ref, cols_high, cols_low, couple_high, couple_low, masks_ref, rows_high, rows_low, self_ref,
    tiles0_ref, tiles1_ref, list_vmem, sent_ref, image_ref, window0_ref, state_ref, list_ref, sems, window, *sums,
):
    rank = rows_high.shape[0]
    nrhs, panels = loads_ref.shape
    span, rows = panels // LANES, CORES * nrhs
    (copy,) = fetch(((list_vmem, list_ref),), sems)
    for held in sums:
        held[...] = jnp.zeros_like(held)
    got = (own_ref, other_ref)
    terms, stats = message_parts(got, rank)
    beta = jnp.sqrt(stat_column(total(stats), 0, nrhs, rank))
    scale = 1.0 / beta
    both = jnp.concatenate([scale] * CORES, axis=0)
    for step, (inside, part, unit) in enumerate(window_parts(got, rank)):
        part = jnp.where(inside, part * (unit * both), 0.0)
        window0_ref[step * rows : (step + 1) * rows, :] = part
        put_blocks(part, step * span, window)
    basis = loads_ref[...] * scale
    far = far_sum_of(terms, nrhs, rank) * scale
    norm = jnp.sum(basis * basis, axis=1, keepdims=True)
    copy.wait()
    near = near_field(window, (tiles0_ref, tiles1_ref), list_ref, sums, nrhs)
    image = image_of(basis, far, self_ref, (rows_high, rows_low), near)
    image_ref[...] = image
    state_ref[...] = jnp.concatenate([far, jnp.broadcast_to(beta, far.shape)], axis=0)
    dot = jnp.sum(basis * image, axis=1, keepdims=True)
    share = jnp.where(norm > 0, dot / jnp.where(norm > 0, norm, 1.0), 0.0)
    rest = image - share * basis
    rest = jnp.sum(rest * rest, axis=1, keepdims=True)
    columns = [norm, dot, share, rest]
    put_message(image, columns, (cols_high, cols_low), (couple_high, couple_low), masks_ref, sent_ref)


def step1_kernel(
    own_ref, other_ref, loads_ref, image_ref, window0_ref, state_ref, rows_high, rows_low, self_ref, tiles0_ref, tiles1_ref,
    list_vmem, sent_ref, basis_ref, coeff_ref, list_ref, sems, window, *sums,
):
    rank = rows_high.shape[0]
    nrhs, panels = loads_ref.shape
    span, rows = panels // LANES, CORES * nrhs
    (copy,) = fetch(((list_vmem, list_ref),), sems)
    beta = state_ref[nrhs:, :1]
    far0 = state_ref[:nrhs, :]
    for held in sums:
        held[...] = jnp.zeros_like(held)
    got = (own_ref, other_ref)
    terms, stats = message_parts(got, rank)
    summed = total(stats)
    h00 = stat_column(summed, 1, nrhs, rank)
    away = shifted(stats, 2) - shifted(summed, 1)
    rest = total(shifted(stats, 3) + stats * away * away)
    h10 = jnp.sqrt(stat_column(rest, 0, nrhs, rank))
    scale = 1.0 / h10
    both, both_h00 = (jnp.concatenate([a] * CORES, axis=0) for a in (scale, h00))
    for step, (inside, part, unit) in enumerate(window_parts(got, rank)):
        part = (part * unit - both_h00 * window0_ref[step * rows : (step + 1) * rows, :]) * both
        put_blocks(jnp.where(inside, part, 0.0), step * span, window)
    basis0 = loads_ref[...] * (1.0 / beta)
    basis1 = (image_ref[...] - h00 * basis0) * scale
    far = (far_sum_of(terms, nrhs, rank) - h00 * far0) * scale
    copy.wait()
    near = near_field(window, (tiles0_ref, tiles1_ref), list_ref, sums, nrhs)
    image = image_of(basis1, far, self_ref, (rows_high, rows_low), near)
    columns = [jnp.sum(a * image, axis=1, keepdims=True) for a in (basis0, basis1, image)]
    sent_ref[:, 0, :] = jnp.broadcast_to(stats_row(columns, rank), (sent_ref.shape[0], LANES))
    basis_ref[...] = jnp.concatenate([basis0, basis1], axis=0)
    coeff_ref[...] = jnp.concatenate([jnp.broadcast_to(v, (nrhs, LANES)) for v in (beta, h00, h10)], axis=0)


def finish_kernel(rank, got_ref, basis_ref, coeff_ref, out_ref):
    nrhs = out_ref.shape[0]
    row = total(got_ref[:, 0, :])
    h01, h11, gram11 = (stat_column(row, k, nrhs, rank) for k in range(3))
    beta, h00, h10 = (coeff_ref[k * nrhs : (k + 1) * nrhs, :1] for k in range(3))
    gram00 = h00 * h00 + h10 * h10
    gram01 = h00 * h01 + h10 * h11
    lower00 = jnp.sqrt(gram00)
    lower10 = gram01 / lower00
    lower11 = jnp.sqrt(gram11 - lower10 * lower10)
    middle0 = beta * h00 / lower00
    middle1 = (beta * h01 - lower10 * middle0) / lower11
    y1 = middle1 / lower11
    y0 = (middle0 - lower10 * y1) / lower00
    out_ref[...] = y0 * basis_ref[:nrhs, :] + y1 * basis_ref[nrhs:, :]


class Plain(jax.ShapeDtypeStruct):
    pass


def in_vmem_like(array):
    return pltpu.VMEM(array.shape, array.dtype)


def in_vmem(arrays):
    return [pltpu.with_memory_space_constraint(a, pltpu.VMEM) for a in arrays]


def call(kernel, args, outs, scratch=(), held=()):
    args = [pltpu.with_memory_space_constraint(a, pltpu.HBM) if i in held else a for i, a in enumerate(args)]
    moved = sum(a.size * a.dtype.itemsize for a in args)
    return pl.pallas_call(
        kernel,
        out_shape=[
            jax.ShapeDtypeStruct(out, F32) if isinstance(out, tuple) else out if isinstance(out, Plain) else in_vmem_like(out)
            for out in outs
        ],
        in_specs=[pl.BlockSpec(memory_space=pl.ANY if i in held else pltpu.VMEM) for i in range(len(args))],
        out_specs=[pl.BlockSpec(memory_space=pltpu.VMEM)] * len(outs),
        scratch_shapes=list(scratch),
        compiler_params=pltpu.CompilerParams(vmem_limit_bytes=24 * 2**20),
        cost_estimate=pl.CostEstimate(flops=0, bytes_accessed=moved, transcendentals=0),
    )(*args)


def exchanged(sent):
    got = lax.all_to_all(sent, "strip", 0, 0, tiled=True)
    return got, lax.ppermute(got, "clus", [(0, 1), (1, 0)])


def body(loads, self_term, near_tiles, near_list, far_rows, far_cols, coupling, ranks):
    nrhs, panels = loads.shape
    rank = far_cols.shape[0]
    blocks, tile = near_tiles.shape[:2]
    rows = panels // tile
    strips = coupling.shape[0] // CORES
    couple = coupling.reshape(CORES * strips * rank, rank)
    near_list = near_list.T
    ranks = ranks.reshape(1, CORES * strips)
    self_term = self_term.reshape(1, panels)
    groups = CORES * strips
    message = Plain((strips, nrhs, panels // 2 + LANES), jnp.int32)
    index = pltpu.SMEM(near_list.shape, jnp.int32)
    scratch = [index, pltpu.SemaphoreType.DMA((1,)), pltpu.VMEM((3 * rows, CORES * nrhs, tile), F32)]
    late = PIECE * (blocks * 3 // (10 * PIECE))
    tiles0, tiles1 = (jax.ShapeDtypeStruct((count, tile, tile), BF16) for count in (blocks - late, late))
    scratch += [pltpu.VMEM((CORES * rows, CORES * nrhs, tile), F32)] * 4

    def twice(array):
        return [jax.ShapeDtypeStruct(array.shape, BF16)] * 2

    sent, *held, loads, self_term, tiles0 = call(
        start_kernel,
        (loads, far_cols, couple, ranks, self_term, near_tiles),
        [
            message, *twice(far_cols), *twice(couple), jax.ShapeDtypeStruct((groups, CHUNK * rank), F32),
            loads, self_term, tiles0,
        ],
        [
            pltpu.VMEM(far_cols.shape, F32), pltpu.VMEM(couple.shape, F32), pltpu.SMEM(ranks.shape, jnp.int32),
            pltpu.SemaphoreType.DMA((5 + tiles0.shape[0] // PIECE,)),
        ],
        held=range(6),
    )
    loads, *held, self_term, tiles0 = in_vmem([loads, *held, self_term, tiles0])
    near_list, *far_rows, tiles1 = in_vmem(
        call(
            fetch_kernel,
            (loads, near_list, far_rows, near_tiles),
            [near_list, *twice(far_rows), tiles1],
            [
                pltpu.VMEM(near_list.shape, jnp.int32), pltpu.VMEM(far_rows.shape, F32),
                pltpu.SemaphoreType.DMA((2 + late // PIECE,)),
            ],
            held=range(1, 4),
        )
    )
    source_side, target_side = [loads, *held], [*far_rows, self_term, tiles0, tiles1, near_list]
    sent, image, window0, state = call(
        step0_kernel,
        (*exchanged(sent), *source_side, *target_side),
        [message, loads.shape, (3 * CORES * nrhs, panels), (CORES * nrhs, LANES)],
        scratch,
    )
    sent, basis, coeff = call(
        step1_kernel,
        (*exchanged(sent), loads, image, window0, state, *target_side),
        [(groups, 1, LANES), (2 * nrhs, panels), (3 * nrhs, LANES)],
        scratch,
    )
    got = lax.all_to_all(sent, GROUP, 0, 0, tiled=True)
    return call(functools.partial(finish_kernel, rank), (got, basis, coeff), [loads.shape])[0]


def solution(mesh):
    every = ("case",) + GROUP
    in_specs = (
        P(None, every),
        P(every),
        P(every, None, None),
        P(every, None),
        P(None, every),
        P(None, every),
        P(None, GROUP, None, None),
        P(None, GROUP),
    )
    return jax.shard_map(body, mesh=mesh, in_specs=in_specs, out_specs=P(None, every), check_vma=False)
```

```python
import functools

import jax
import jax.numpy as jnp
from jax import lax
from jax.experimental import pallas as pl
from jax.experimental.pallas import tpu as pltpu
from jax.sharding import PartitionSpec as P

GROUP = ("strip", "clus")
CORES = 2
LANES = 128
CHUNK = 16
PIECE = 8
F32 = jnp.float32
BF16 = jnp.bfloat16

STEP = 8
COLS_TOP = 0.1875
COUPLE_TOP = 0.375
TOP = 32767.0
ONE = float(2**30)


def lanes_of(shape):
    return lax.broadcasted_iota(jnp.int32, shape, 1)


def rows_of(shape):
    return lax.broadcasted_iota(jnp.int32, shape, 0)


def total(rows):
    return jnp.sum(rows, axis=0, keepdims=True)


def stats_row(columns, rank, step=None):
    shape = (columns[0].shape[0], LANES)
    first = lanes_of(shape) - rank * rows_of(shape)
    spread = sum(jnp.where(first == k, column, 0.0) for k, column in enumerate(columns))
    if step is not None:
        spread = jnp.where((first >= STEP) & (first < rank), step, spread)
    return total(spread)


def steps_of(stats, rank):
    inner = lax.rem(lanes_of(stats.shape), rank)
    return jnp.where(inner < STEP, shifted(stats, STEP), stats)


def term_unit(panels, rank):
    return panels * rank * COLS_TOP * COUPLE_TOP * TOP / ONE


def stat_column(row, k, nrhs, rank):
    shape = (nrhs, LANES)
    first = lanes_of(shape) - rank * rows_of(shape)
    return jnp.sum(jnp.where(first == k, row, 0.0), axis=1, keepdims=True)


def shifted(value, k):
    return pltpu.roll(value, LANES - k, 1)


def far_sum_of(row, nrhs, rank):
    shape = (nrhs, LANES)
    first = lanes_of(shape) - rank * rows_of(shape)
    own = jnp.where((first >= 0) & (first < rank), row, 0.0)
    return sum((pltpu.roll(own, k * rank, 1) for k in range(1, LANES // rank)), own)


def halves(value):
    high = value.astype(BF16)
    return high, (value - high.astype(F32)).astype(BF16)


def product(left, right_high, right_low, side=0):
    rows = left.shape[0]
    high, low = halves(left)
    dims = (((1,), (side,)), ((), ()))
    both = lax.dot_general(jnp.concatenate([high, low], axis=0), right_high, dims, preferred_element_type=F32)
    return both[:rows] + (both[rows:] + lax.dot_general(high, right_low, dims, preferred_element_type=F32))


def coded(value):
    exponent = jnp.ceil(jnp.log2(jnp.maximum(jnp.abs(value), 1e-30)))
    return (value * jnp.exp2(-exponent) * ONE).astype(jnp.int32), exponent.astype(jnp.int32)


def decoded(mantissa, exponent):
    return mantissa.astype(F32) * (1.0 / ONE) * jnp.exp2(exponent.astype(F32))


def packed(field):
    top = jnp.max(jnp.abs(field), axis=1, keepdims=True)
    step = jnp.maximum(top, 1e-30) * (1.0 / TOP)
    codes = jnp.floor(field * (1.0 / step) + 0.5).astype(jnp.int32)
    width = field.shape[1] // 2
    return (codes[:, :width] << 16) | (codes[:, width:] & 0xFFFF), step


def unpacked(words):
    return jnp.concatenate([words >> 16, (words << 16) >> 16], axis=1).astype(F32)


def fetch(pairs, sems):
    copies = [pltpu.make_async_copy(a, b, sems.at[i]) for i, (a, b) in enumerate(pairs)]
    for copy in copies:
        copy.start()
    return copies


def put_message(field, columns, cols, couple, masks_ref, sent_ref):
    nrhs, rank = field.shape[0], cols[0].shape[0]
    unit = term_unit(field.shape[1], rank)
    proj = product(field, cols[0][...], cols[1][...], 1)
    wide = jnp.concatenate([proj] * CHUNK, axis=1)
    words, step = packed(field)
    width = words.shape[1]
    row = stats_row(columns, rank, step)
    finer = 1.0 / (steps_of(row, rank) * unit)
    for i in range(sent_ref.shape[0]):
        sent_ref[i, :, :width] = words
    half = CHUNK // CORES
    stats = [jnp.broadcast_to(a, (half, LANES)) for a in coded(row)]
    for start in range(0, sent_ref.shape[0], half):
        mask = masks_ref[pl.ds(CORES * start, CHUNK), :]
        spread = jnp.concatenate([mask * wide[r : r + 1] for r in range(nrhs)], axis=0)
        here = pl.ds(CORES * start * rank, CHUNK * rank)
        terms = product(spread, couple[0][here, :], couple[1][here, :])
        terms = jnp.concatenate([terms[r * CHUNK : (r + 1) * CHUNK] for r in range(nrhs)], axis=1)
        terms = (terms * finer).astype(jnp.int32)
        here = pl.ds(start, half)
        for k, value in enumerate([terms[:half], terms[half:]] + stats):
            sent_ref[here, k, width:] = value


def message_parts(got, rank):
    width = got[0].shape[2] - LANES
    first, second, mantissa, exponent = (jnp.concatenate([ref[:, k, width:] for ref in got], axis=0) for k in range(4))
    stats = decoded(mantissa, exponent)
    terms = jnp.where(lax.axis_index("clus") == 0, first, second).astype(F32)
    return total(terms * (steps_of(stats, rank) * term_unit(2 * width, rank))), stats


def window_parts(got, rank):
    strips, nrhs, width = got[0].shape
    width -= LANES
    shape = (CORES * nrhs, LANES)
    for step in range(3):
        owner = lax.axis_index("strip") + (step - 1)
        inside = (owner >= 0) & (owner < strips)
        owner = jnp.clip(owner, 0, strips - 1)
        words = jnp.concatenate([ref[owner, :, :width] for ref in got], axis=0)
        tails = [ref[owner, :, width:] for ref in got]
        rows = [decoded(tail[2:3], tail[3:4]) for tail in tails]
        rows = jnp.where(rows_of(shape) < nrhs, rows[0], rows[1])
        wanted = lanes_of(shape) == rank * lax.rem(rows_of(shape), nrhs) + STEP
        yield inside, unpacked(words), jnp.sum(jnp.where(wanted, rows, 0.0), axis=1, keepdims=True)


def put_blocks(part, first, window):
    part = part.astype(BF16).astype(F32)
    for c in range(part.shape[1] // LANES):
        window[first + c] = part[:, c * LANES : (c + 1) * LANES]


def near_field(window, tiles, list_ref, sums, nrhs):
    n = 0
    for tiles_ref in tiles:
        for first in range(0, tiles_ref.shape[0], 2):
            left = jnp.concatenate([window[list_ref[1, n + i]] for i in range(2)], axis=0).astype(BF16)
            right = jnp.concatenate([tiles_ref[first + i] for i in range(2)], axis=1)
            both = jnp.dot(left, right, preferred_element_type=F32)
            rows = window.shape[1]
            for i in range(2):
                held = sums[(n + i) % len(sums)]
                held[list_ref[0, n + i]] += both[i * rows : (i + 1) * rows, i * LANES : (i + 1) * LANES]
            n += 2
    whole = sum((held[...] for held in sums[1:]), sums[0][...])
    rows = whole.shape[0] // CORES
    return jnp.concatenate([whole[b, :nrhs] + whole[rows + b, nrhs:] for b in range(rows)], axis=1)


def tile_pieces(tiles_hbm, first, tiles_ref):
    starts = range(0, tiles_ref.shape[0], PIECE)
    return tuple((tiles_hbm.at[pl.ds(first + i, PIECE)], tiles_ref.at[pl.ds(i, PIECE)]) for i in starts)


def fetch_kernel(
    loads_ref, list_hbm, rows_hbm, tiles_hbm, list_ref, rows_high, rows_low, tiles_ref, raw_ref, rows_ref, sems
):
    panels = loads_ref.shape[1]
    first = tiles_hbm.shape[0] - tiles_ref.shape[0]
    copies = fetch(((list_hbm, raw_ref), (rows_hbm, rows_ref)) + tile_pieces(tiles_hbm, first, tiles_ref), sems)
    copies[0].wait()
    count = panels // LANES
    target, source = raw_ref[0:1, :], raw_ref[1:2, :]
    group, block = lax.div(source, count), lax.rem(source, count)
    strip, core = lax.div(group, CORES), lax.rem(group, CORES)
    apart = jnp.where(core == lax.axis_index("clus"), 0, 1)
    list_ref[...] = jnp.concatenate([apart * count + target, strip * count + block], axis=0)
    copies[1].wait()
    rows_high[...], rows_low[...] = halves(rows_ref[...])
    for copy in copies[2:]:
        copy.wait()


def start_kernel(
    loads_hbm, cols_hbm, couple_hbm, ranks_hbm, self_hbm, tiles_hbm, sent_ref, cols_high, cols_low, couple_high,
    couple_low, masks_ref, loads_ref, self_ref, tiles_ref, cols_ref, couple_ref, ranks_ref, sems,
):
    rank, panels = cols_ref.shape
    pairs = (
        (loads_hbm, loads_ref), (cols_hbm, cols_ref), (couple_hbm, couple_ref), (ranks_hbm, ranks_ref),
        (self_hbm, self_ref),
    )
    copies = fetch(pairs + tile_pieces(tiles_hbm, 0, tiles_ref), sems)
    copies[0].wait()
    loads = loads_ref[...]
    square = jnp.sum(loads * loads, axis=1, keepdims=True)
    copies[3].wait()
    shape = (CHUNK, CHUNK * rank)
    owner = lax.div(lanes_of(shape), rank)
    inner = lax.rem(lanes_of(shape), rank)
    half = CHUNK // CORES
    number = CORES * lax.rem(rows_of(shape), half) + lax.div(rows_of(shape), half)
    for start in range(0, masks_ref.shape[0], CHUNK):
        limit = jnp.zeros((1, CHUNK * rank), jnp.int32)
        for i in range(CHUNK):
            limit = jnp.where(owner[:1] == i, ranks_ref[0, start + i], limit)
        masks_ref[pl.ds(start, CHUNK), :] = jnp.where((owner == number) & (inner < limit), 1.0, 0.0)
    copies[1].wait()
    cols_high[...], cols_low[...] = halves(cols_ref[...])
    copies[2].wait()
    couple_high[...], couple_low[...] = halves(couple_ref[...])
    put_message(loads, [square], (cols_high, cols_low), (couple_high, couple_low), masks_ref, sent_ref)
    for copy in copies[4:]:
        copy.wait()


def image_of(field, far, self_ref, far_rows, near):
    rank = far_rows[0].shape[0]
    return self_ref[...] * field + near + product(far[:, :rank], far_rows[0][...], far_rows[1][...])


def step0_kernel(
    own_ref, other_ref, loads_ref, cols_high, cols_low, couple_high, couple_low, masks_ref, rows_high, rows_low, self_ref,
    tiles0_ref, tiles1_ref, list_vmem, sent_ref, image_ref, window0_ref, state_ref, list_ref, sems, window, *sums,
):
    rank = rows_high.shape[0]
    nrhs, panels = loads_ref.shape
    span, rows = panels // LANES, CORES * nrhs
    (copy,) = fetch(((list_vmem, list_ref),), sems)
    for held in sums:
        held[...] = jnp.zeros_like(held)
    got = (own_ref, other_ref)
    terms, stats = message_parts(got, rank)
    beta = jnp.sqrt(stat_column(total(stats), 0, nrhs, rank))
    scale = 1.0 / beta
    both = jnp.concatenate([scale] * CORES, axis=0)
    for step, (inside, part, unit) in enumerate(window_parts(got, rank)):
        part = jnp.where(inside, part * (unit * both), 0.0)
        window0_ref[step * rows : (step + 1) * rows, :] = part
        put_blocks(part, step * span, window)
    basis = loads_ref[...] * scale
    far = far_sum_of(terms, nrhs, rank) * scale
    norm = jnp.sum(basis * basis, axis=1, keepdims=True)
    copy.wait()
    near = near_field(window, (tiles0_ref, tiles1_ref), list_ref, sums, nrhs)
    image = image_of(basis, far, self_ref, (rows_high, rows_low), near)
    image_ref[...] = image
    state_ref[...] = jnp.concatenate([far, jnp.broadcast_to(beta, far.shape)], axis=0)
    dot = jnp.sum(basis * image, axis=1, keepdims=True)
    share = jnp.where(norm > 0, dot / jnp.where(norm > 0, norm, 1.0), 0.0)
    rest = image - share * basis
    rest = jnp.sum(rest * rest, axis=1, keepdims=True)
    columns = [norm, dot, share, rest]
    put_message(image, columns, (cols_high, cols_low), (couple_high, couple_low), masks_ref, sent_ref)


def step1_kernel(
    own_ref, other_ref, loads_ref, image_ref, window0_ref, state_ref, rows_high, rows_low, self_ref, tiles0_ref, tiles1_ref,
    list_vmem, sent_ref, basis_ref, coeff_ref, list_ref, sems, window, *sums,
):
    rank = rows_high.shape[0]
    nrhs, panels = loads_ref.shape
    span, rows = panels // LANES, CORES * nrhs
    (copy,) = fetch(((list_vmem, list_ref),), sems)
    beta = state_ref[nrhs:, :1]
    far0 = state_ref[:nrhs, :]
    for held in sums:
        held[...] = jnp.zeros_like(held)
    got = (own_ref, other_ref)
    terms, stats = message_parts(got, rank)
    summed = total(stats)
    h00 = stat_column(summed, 1, nrhs, rank)
    away = shifted(stats, 2) - shifted(summed, 1)
    rest = total(shifted(stats, 3) + stats * away * away)
    h10 = jnp.sqrt(stat_column(rest, 0, nrhs, rank))
    scale = 1.0 / h10
    both, both_h00 = (jnp.concatenate([a] * CORES, axis=0) for a in (scale, h00))
    for step, (inside, part, unit) in enumerate(window_parts(got, rank)):
        part = (part * unit - both_h00 * window0_ref[step * rows : (step + 1) * rows, :]) * both
        put_blocks(jnp.where(inside, part, 0.0), step * span, window)
    basis0 = loads_ref[...] * (1.0 / beta)
    basis1 = (image_ref[...] - h00 * basis0) * scale
    far = (far_sum_of(terms, nrhs, rank) - h00 * far0) * scale
    copy.wait()
    near = near_field(window, (tiles0_ref, tiles1_ref), list_ref, sums, nrhs)
    image = image_of(basis1, far, self_ref, (rows_high, rows_low), near)
    columns = [jnp.sum(a * image, axis=1, keepdims=True) for a in (basis0, basis1, image)]
    sent_ref[:, 0, :] = jnp.broadcast_to(stats_row(columns, rank), (sent_ref.shape[0], LANES))
    basis_ref[...] = jnp.concatenate([basis0, basis1], axis=0)
    coeff_ref[...] = jnp.concatenate([jnp.broadcast_to(v, (nrhs, LANES)) for v in (beta, h00, h10)], axis=0)


def finish_kernel(rank, got_ref, basis_ref, coeff_ref, out_ref):
    nrhs = out_ref.shape[0]
    row = total(got_ref[:, 0, :])
    h01, h11, gram11 = (stat_column(row, k, nrhs, rank) for k in range(3))
    beta, h00, h10 = (coeff_ref[k * nrhs : (k + 1) * nrhs, :1] for k in range(3))
    gram00 = h00 * h00 + h10 * h10
    gram01 = h00 * h01 + h10 * h11
    lower00 = jnp.sqrt(gram00)
    lower10 = gram01 / lower00
    lower11 = jnp.sqrt(gram11 - lower10 * lower10)
    middle0 = beta * h00 / lower00
    middle1 = (beta * h01 - lower10 * middle0) / lower11
    y1 = middle1 / lower11
    y0 = (middle0 - lower10 * y1) / lower00
    out_ref[...] = y0 * basis_ref[:nrhs, :] + y1 * basis_ref[nrhs:, :]


class Plain(jax.ShapeDtypeStruct):
    pass


def in_vmem_like(array):
    return pltpu.VMEM(array.shape, array.dtype)


def in_vmem(arrays):
    return [pltpu.with_memory_space_constraint(a, pltpu.VMEM) for a in arrays]


def call(kernel, args, outs, scratch=(), held=()):
    args = [pltpu.with_memory_space_constraint(a, pltpu.HBM) if i in held else a for i, a in enumerate(args)]
    moved = sum(a.size * a.dtype.itemsize for a in args)
    return pl.pallas_call(
        kernel,
        out_shape=[
            jax.ShapeDtypeStruct(out, F32) if isinstance(out, tuple) else out if isinstance(out, Plain) else in_vmem_like(out)
            for out in outs
        ],
        in_specs=[pl.BlockSpec(memory_space=pl.ANY if i in held else pltpu.VMEM) for i in range(len(args))],
        out_specs=[pl.BlockSpec(memory_space=pltpu.VMEM)] * len(outs),
        scratch_shapes=list(scratch),
        compiler_params=pltpu.CompilerParams(vmem_limit_bytes=24 * 2**20),
        cost_estimate=pl.CostEstimate(flops=0, bytes_accessed=moved, transcendentals=0),
    )(*args)


def exchanged(sent):
    got = lax.all_to_all(sent, "strip", 0, 0, tiled=True)
    return got, lax.ppermute(got, "clus", [(0, 1), (1, 0)])


def body(loads, self_term, near_tiles, near_list, far_rows, far_cols, coupling, ranks):
    nrhs, panels = loads.shape
    rank = far_cols.shape[0]
    blocks, tile = near_tiles.shape[:2]
    rows = panels // tile
    strips = coupling.shape[0] // CORES
    couple = coupling.reshape(CORES * strips * rank, rank)
    near_list = near_list.T
    ranks = ranks.reshape(1, CORES * strips)
    self_term = self_term.reshape(1, panels)
    groups = CORES * strips
    message = Plain((strips, nrhs, panels // 2 + LANES), jnp.int32)
    index = pltpu.SMEM(near_list.shape, jnp.int32)
    scratch = [index, pltpu.SemaphoreType.DMA((1,)), pltpu.VMEM((3 * rows, CORES * nrhs, tile), F32)]
    late = PIECE * (blocks * 3 // (10 * PIECE))
    tiles0, tiles1 = (jax.ShapeDtypeStruct((count, tile, tile), BF16) for count in (blocks - late, late))
    scratch += [pltpu.VMEM((CORES * rows, CORES * nrhs, tile), F32)] * 4

    def twice(array):
        return [jax.ShapeDtypeStruct(array.shape, BF16)] * 2

    sent, *held, loads, self_term, tiles0 = call(
        start_kernel,
        (loads, far_cols, couple, ranks, self_term, near_tiles),
        [
            message, *twice(far_cols), *twice(couple), jax.ShapeDtypeStruct((groups, CHUNK * rank), F32),
            loads, self_term, tiles0,
        ],
        [
            pltpu.VMEM(far_cols.shape, F32), pltpu.VMEM(couple.shape, F32), pltpu.SMEM(ranks.shape, jnp.int32),
            pltpu.SemaphoreType.DMA((5 + tiles0.shape[0] // PIECE,)),
        ],
        held=range(6),
    )
    loads, *held, self_term, tiles0 = in_vmem([loads, *held, self_term, tiles0])
    near_list, *far_rows, tiles1 = in_vmem(
        call(
            fetch_kernel,
            (loads, near_list, far_rows, near_tiles),
            [near_list, *twice(far_rows), tiles1],
            [
                pltpu.VMEM(near_list.shape, jnp.int32), pltpu.VMEM(far_rows.shape, F32),
                pltpu.SemaphoreType.DMA((2 + late // PIECE,)),
            ],
            held=range(1, 4),
        )
    )
    source_side, target_side = [loads, *held], [*far_rows, self_term, tiles0, tiles1, near_list]
    sent, image, window0, state = call(
        step0_kernel,
        (*exchanged(sent), *source_side, *target_side),
        [message, loads.shape, (3 * CORES * nrhs, panels), (CORES * nrhs, LANES)],
        scratch,
    )
    sent, basis, coeff = call(
        step1_kernel,
        (*exchanged(sent), loads, image, window0, state, *target_side),
        [(groups, 1, LANES), (2 * nrhs, panels), (3 * nrhs, LANES)],
        scratch,
    )
    got = lax.all_to_all(sent, GROUP, 0, 0, tiled=True)
    return call(functools.partial(finish_kernel, rank), (got, basis, coeff), [loads.shape])[0]


def solution(mesh):
    every = ("case",) + GROUP
    in_specs = (
        P(None, every),
        P(every),
        P(every, None, None),
        P(every, None),
        P(None, every),
        P(None, every),
        P(None, GROUP, None, None),
        P(None, GROUP),
    )
    return jax.shard_map(body, mesh=mesh, in_specs=in_specs, out_specs=P(None, every), check_vma=False)
```

```python
import functools

import jax
import jax.numpy as jnp
from jax import lax
from jax.experimental import pallas as pl
from jax.experimental.pallas import tpu as pltpu
from jax.sharding import PartitionSpec as P

GROUP = ("strip", "clus")
CORES = 2
LANES = 128
CHUNK = 16
PIECE = 8
F32 = jnp.float32
BF16 = jnp.bfloat16

STEP = 8
COLS_TOP = 0.1875
COUPLE_TOP = 0.375
TOP = 32767.0
ONE = float(2**30)


def lanes_of(shape):
    return lax.broadcasted_iota(jnp.int32, shape, 1)


def rows_of(shape):
    return lax.broadcasted_iota(jnp.int32, shape, 0)


def total(rows):
    return jnp.sum(rows, axis=0, keepdims=True)


def stats_row(columns, rank, step=None):
    shape = (columns[0].shape[0], LANES)
    first = lanes_of(shape) - rank * rows_of(shape)
    spread = sum(jnp.where(first == k, column, 0.0) for k, column in enumerate(columns))
    if step is not None:
        spread = jnp.where((first >= STEP) & (first < rank), step, spread)
    return total(spread)


def steps_of(stats, rank):
    inner = lax.rem(lanes_of(stats.shape), rank)
    return jnp.where(inner < STEP, shifted(stats, STEP), stats)


def term_unit(panels, rank):
    return panels * rank * COLS_TOP * COUPLE_TOP * TOP / ONE


def stat_column(row, k, nrhs, rank):
    shape = (nrhs, LANES)
    first = lanes_of(shape) - rank * rows_of(shape)
    return jnp.sum(jnp.where(first == k, row, 0.0), axis=1, keepdims=True)


def shifted(value, k):
    return pltpu.roll(value, LANES - k, 1)


def far_sum_of(row, nrhs, rank):
    shape = (nrhs, LANES)
    first = lanes_of(shape) - rank * rows_of(shape)
    own = jnp.where((first >= 0) & (first < rank), row, 0.0)
    return sum((pltpu.roll(own, k * rank, 1) for k in range(1, LANES // rank)), own)


def halves(value):
    high = value.astype(BF16)
    return high, (value - high.astype(F32)).astype(BF16)


def product(left, right_high, right_low, side=0):
    rows = left.shape[0]
    high, low = halves(left)
    dims = (((1,), (side,)), ((), ()))
    both = lax.dot_general(jnp.concatenate([high, low], axis=0), right_high, dims, preferred_element_type=F32)
    return both[:rows] + (both[rows:] + lax.dot_general(high, right_low, dims, preferred_element_type=F32))


def coded(value):
    exponent = jnp.ceil(jnp.log2(jnp.maximum(jnp.abs(value), 1e-30)))
    return (value * jnp.exp2(-exponent) * ONE).astype(jnp.int32), exponent.astype(jnp.int32)


def decoded(mantissa, exponent):
    return mantissa.astype(F32) * (1.0 / ONE) * jnp.exp2(exponent.astype(F32))


def packed(field):
    top = jnp.max(jnp.abs(field), axis=1, keepdims=True)
    step = jnp.maximum(top, 1e-30) * (1.0 / TOP)
    codes = jnp.floor(field * (1.0 / step) + 0.5).astype(jnp.int32)
    width = field.shape[1] // 2
    return (codes[:, :width] << 16) | (codes[:, width:] & 0xFFFF), step


def unpacked(words):
    return jnp.concatenate([words >> 16, (words << 16) >> 16], axis=1).astype(F32)


def fetch(pairs, sems):
    copies = [pltpu.make_async_copy(a, b, sems.at[i]) for i, (a, b) in enumerate(pairs)]
    for copy in copies:
        copy.start()
    return copies


def put_message(field, columns, cols, couple, masks_ref, sent_ref):
    nrhs, rank = field.shape[0], cols[0].shape[0]
    unit = term_unit(field.shape[1], rank)
    proj = product(field, cols[0][...], cols[1][...], 1)
    wide = jnp.concatenate([proj] * CHUNK, axis=1)
    words, step = packed(field)
    width = words.shape[1]
    row = stats_row(columns, rank, step)
    finer = 1.0 / (steps_of(row, rank) * unit)
    for i in range(sent_ref.shape[0]):
        sent_ref[i, :, :width] = words
    half = CHUNK // CORES
    stats = [jnp.broadcast_to(a, (half, LANES)) for a in coded(row)]
    for start in range(0, sent_ref.shape[0], half):
        mask = masks_ref[pl.ds(CORES * start, CHUNK), :]
        spread = jnp.concatenate([mask * wide[r : r + 1] for r in range(nrhs)], axis=0)
        here = pl.ds(CORES * start * rank, CHUNK * rank)
        terms = product(spread, couple[0][here, :], couple[1][here, :])
        terms = jnp.concatenate([terms[r * CHUNK : (r + 1) * CHUNK] for r in range(nrhs)], axis=1)
        terms = (terms * finer).astype(jnp.int32)
        here = pl.ds(start, half)
        for k, value in enumerate([terms[:half], terms[half:]] + stats):
            sent_ref[here, k, width:] = value


def message_parts(got, rank):
    width = got[0].shape[2] - LANES
    first, second, mantissa, exponent = (jnp.concatenate([ref[:, k, width:] for ref in got], axis=0) for k in range(4))
    stats = decoded(mantissa, exponent)
    terms = jnp.where(lax.axis_index("clus") == 0, first, second).astype(F32)
    return total(terms * (steps_of(stats, rank) * term_unit(2 * width, rank))), stats


def window_parts(got, rank):
    strips, nrhs, width = got[0].shape
    width -= LANES
    shape = (CORES * nrhs, LANES)
    for step in range(3):
        owner = lax.axis_index("strip") + (step - 1)
        inside = (owner >= 0) & (owner < strips)
        owner = jnp.clip(owner, 0, strips - 1)
        words = jnp.concatenate([ref[owner, :, :width] for ref in got], axis=0)
        tails = [ref[owner, :, width:] for ref in got]
        rows = [decoded(tail[2:3], tail[3:4]) for tail in tails]
        rows = jnp.where(rows_of(shape) < nrhs, rows[0], rows[1])
        wanted = lanes_of(shape) == rank * lax.rem(rows_of(shape), nrhs) + STEP
        yield inside, unpacked(words), jnp.sum(jnp.where(wanted, rows, 0.0), axis=1, keepdims=True)


def put_blocks(part, first, window):
    part = part.astype(BF16).astype(F32)
    for c in range(part.shape[1] // LANES):
        window[first + c] = part[:, c * LANES : (c + 1) * LANES]


def near_field(window, tiles, list_ref, sums, nrhs):
    n = 0
    for tiles_ref in tiles:
        for first in range(0, tiles_ref.shape[0], 2):
            left = jnp.concatenate([window[list_ref[1, n + i]] for i in range(2)], axis=0).astype(BF16)
            right = jnp.concatenate([tiles_ref[first + i] for i in range(2)], axis=1)
            both = jnp.dot(left, right, preferred_element_type=F32)
            rows = window.shape[1]
            for i in range(2):
                held = sums[(n + i) % len(sums)]
                held[list_ref[0, n + i]] += both[i * rows : (i + 1) * rows, i * LANES : (i + 1) * LANES]
            n += 2
    whole = sum((held[...] for held in sums[1:]), sums[0][...])
    rows = whole.shape[0] // CORES
    return jnp.concatenate([whole[b, :nrhs] + whole[rows + b, nrhs:] for b in range(rows)], axis=1)


def tile_pieces(tiles_hbm, first, tiles_ref):
    starts = range(0, tiles_ref.shape[0], PIECE)
    return tuple((tiles_hbm.at[pl.ds(first + i, PIECE)], tiles_ref.at[pl.ds(i, PIECE)]) for i in starts)


def fetch_kernel(
    loads_ref, list_hbm, rows_hbm, tiles_hbm, list_ref, rows_high, rows_low, tiles_ref, raw_ref, rows_ref, sems
):
    panels = loads_ref.shape[1]
    first = tiles_hbm.shape[0] - tiles_ref.shape[0]
    copies = fetch(((list_hbm, raw_ref), (rows_hbm, rows_ref)) + tile_pieces(tiles_hbm, first, tiles_ref), sems)
    copies[0].wait()
    count = panels // LANES
    target, source = raw_ref[0:1, :], raw_ref[1:2, :]
    group, block = lax.div(source, count), lax.rem(source, count)
    strip, core = lax.div(group, CORES), lax.rem(group, CORES)
    apart = jnp.where(core == lax.axis_index("clus"), 0, 1)
    list_ref[...] = jnp.concatenate([apart * count + target, strip * count + block], axis=0)
    copies[1].wait()
    rows_high[...], rows_low[...] = halves(rows_ref[...])
    for copy in copies[2:]:
        copy.wait()


def start_kernel(
    loads_hbm, cols_hbm, couple_hbm, ranks_hbm, self_hbm, tiles_hbm, sent_ref, cols_high, cols_low, couple_high,
    couple_low, masks_ref, loads_ref, self_ref, tiles_ref, cols_ref, couple_ref, ranks_ref, sems,
):
    rank, panels = cols_ref.shape
    pairs = (
        (loads_hbm, loads_ref), (cols_hbm, cols_ref), (couple_hbm, couple_ref), (ranks_hbm, ranks_ref),
        (self_hbm, self_ref),
    )
    copies = fetch(pairs + tile_pieces(tiles_hbm, 0, tiles_ref), sems)
    copies[0].wait()
    loads = loads_ref[...]
    square = jnp.sum(loads * loads, axis=1, keepdims=True)
    copies[3].wait()
    shape = (CHUNK, CHUNK * rank)
    owner = lax.div(lanes_of(shape), rank)
    inner = lax.rem(lanes_of(shape), rank)
    half = CHUNK // CORES
    number = CORES * lax.rem(rows_of(shape), half) + lax.div(rows_of(shape), half)
    for start in range(0, masks_ref.shape[0], CHUNK):
        limit = jnp.zeros((1, CHUNK * rank), jnp.int32)
        for i in range(CHUNK):
            limit = jnp.where(owner[:1] == i, ranks_ref[0, start + i], limit)
        masks_ref[pl.ds(start, CHUNK), :] = jnp.where((owner == number) & (inner < limit), 1.0, 0.0)
    copies[1].wait()
    cols_high[...], cols_low[...] = halves(cols_ref[...])
    copies[2].wait()
    couple_high[...], couple_low[...] = halves(couple_ref[...])
    put_message(loads, [square], (cols_high, cols_low), (couple_high, couple_low), masks_ref, sent_ref)
    for copy in copies[4:]:
        copy.wait()


def image_of(field, far, self_ref, far_rows, near):
    rank = far_rows[0].shape[0]
    return self_ref[...] * field + near + product(far[:, :rank], far_rows[0][...], far_rows[1][...])


def step0_kernel(
    own_ref, other_ref, loads_ref, cols_high, cols_low, couple_high, couple_low, masks_ref, rows_high, rows_low, self_ref,
    tiles0_ref, tiles1_ref, list_vmem, sent_ref, image_ref, window0_ref, state_ref, list_ref, sems, window, *sums,
):
    rank = rows_high.shape[0]
    nrhs, panels = loads_ref.shape
    span, rows = panels // LANES, CORES * nrhs
    (copy,) = fetch(((list_vmem, list_ref),), sems)
    for held in sums:
        held[...] = jnp.zeros_like(held)
    got = (own_ref, other_ref)
    terms, stats = message_parts(got, rank)
    beta = jnp.sqrt(stat_column(total(stats), 0, nrhs, rank))
    scale = 1.0 / beta
    both = jnp.concatenate([scale] * CORES, axis=0)
    for step, (inside, part, unit) in enumerate(window_parts(got, rank)):
        part = jnp.where(inside, part * (unit * both), 0.0)
        window0_ref[step * rows : (step + 1) * rows, :] = part
        put_blocks(part, step * span, window)
    basis = loads_ref[...] * scale
    far = far_sum_of(terms, nrhs, rank) * scale
    norm = jnp.sum(basis * basis, axis=1, keepdims=True)
    copy.wait()
    near = near_field(window, (tiles0_ref, tiles1_ref), list_ref, sums, nrhs)
    image = image_of(basis, far, self_ref, (rows_high, rows_low), near)
    image_ref[...] = image
    state_ref[...] = jnp.concatenate([far, jnp.broadcast_to(beta, far.shape)], axis=0)
    dot = jnp.sum(basis * image, axis=1, keepdims=True)
    share = jnp.where(norm > 0, dot / jnp.where(norm > 0, norm, 1.0), 0.0)
    rest = image - share * basis
    rest = jnp.sum(rest * rest, axis=1, keepdims=True)
    columns = [norm, dot, share, rest]
    put_message(image, columns, (cols_high, cols_low), (couple_high, couple_low), masks_ref, sent_ref)


def step1_kernel(
    own_ref, other_ref, loads_ref, image_ref, window0_ref, state_ref, rows_high, rows_low, self_ref, tiles0_ref, tiles1_ref,
    list_vmem, sent_ref, basis_ref, coeff_ref, list_ref, sems, window, *sums,
):
    rank = rows_high.shape[0]
    nrhs, panels = loads_ref.shape
    span, rows = panels // LANES, CORES * nrhs
    (copy,) = fetch(((list_vmem, list_ref),), sems)
    beta = state_ref[nrhs:, :1]
    far0 = state_ref[:nrhs, :]
    for held in sums:
        held[...] = jnp.zeros_like(held)
    got = (own_ref, other_ref)
    terms, stats = message_parts(got, rank)
    summed = total(stats)
    h00 = stat_column(summed, 1, nrhs, rank)
    away = shifted(stats, 2) - shifted(summed, 1)
    rest = total(shifted(stats, 3) + stats * away * away)
    h10 = jnp.sqrt(stat_column(rest, 0, nrhs, rank))
    scale = 1.0 / h10
    both, both_h00 = (jnp.concatenate([a] * CORES, axis=0) for a in (scale, h00))
    for step, (inside, part, unit) in enumerate(window_parts(got, rank)):
        part = (part * unit - both_h00 * window0_ref[step * rows : (step + 1) * rows, :]) * both
        put_blocks(jnp.where(inside, part, 0.0), step * span, window)
    basis0 = loads_ref[...] * (1.0 / beta)
    basis1 = (image_ref[...] - h00 * basis0) * scale
    far = (far_sum_of(terms, nrhs, rank) - h00 * far0) * scale
    copy.wait()
    near = near_field(window, (tiles0_ref, tiles1_ref), list_ref, sums, nrhs)
    image = image_of(basis1, far, self_ref, (rows_high, rows_low), near)
    columns = [jnp.sum(a * image, axis=1, keepdims=True) for a in (basis0, basis1, image)]
    sent_ref[:, 0, :] = jnp.broadcast_to(stats_row(columns, rank), (sent_ref.shape[0], LANES))
    basis_ref[...] = jnp.concatenate([basis0, basis1], axis=0)
    coeff_ref[...] = jnp.concatenate([jnp.broadcast_to(v, (nrhs, LANES)) for v in (beta, h00, h10)], axis=0)


def finish_kernel(rank, got_ref, basis_ref, coeff_ref, out_ref):
    nrhs = out_ref.shape[0]
    row = total(got_ref[:, 0, :])
    h01, h11, gram11 = (stat_column(row, k, nrhs, rank) for k in range(3))
    beta, h00, h10 = (coeff_ref[k * nrhs : (k + 1) * nrhs, :1] for k in range(3))
    gram00 = h00 * h00 + h10 * h10
    gram01 = h00 * h01 + h10 * h11
    lower00 = jnp.sqrt(gram00)
    lower10 = gram01 / lower00
    lower11 = jnp.sqrt(gram11 - lower10 * lower10)
    middle0 = beta * h00 / lower00
    middle1 = (beta * h01 - lower10 * middle0) / lower11
    y1 = middle1 / lower11
    y0 = (middle0 - lower10 * y1) / lower00
    out_ref[...] = y0 * basis_ref[:nrhs, :] + y1 * basis_ref[nrhs:, :]


class Plain(jax.ShapeDtypeStruct):
    pass


def in_vmem_like(array):
    return pltpu.VMEM(array.shape, array.dtype)


def in_vmem(arrays):
    return [pltpu.with_memory_space_constraint(a, pltpu.VMEM) for a in arrays]


def call(kernel, args, outs, scratch=(), held=()):
    args = [pltpu.with_memory_space_constraint(a, pltpu.HBM) if i in held else a for i, a in enumerate(args)]
    moved = sum(a.size * a.dtype.itemsize for a in args)
    return pl.pallas_call(
        kernel,
        out_shape=[
            jax.ShapeDtypeStruct(out, F32) if isinstance(out, tuple) else out if isinstance(out, Plain) else in_vmem_like(out)
            for out in outs
        ],
        in_specs=[pl.BlockSpec(memory_space=pl.ANY if i in held else pltpu.VMEM) for i in range(len(args))],
        out_specs=[pl.BlockSpec(memory_space=pltpu.VMEM)] * len(outs),
        scratch_shapes=list(scratch),
        compiler_params=pltpu.CompilerParams(vmem_limit_bytes=24 * 2**20),
        cost_estimate=pl.CostEstimate(flops=0, bytes_accessed=moved, transcendentals=0),
    )(*args)


def exchanged(sent):
    got = lax.all_to_all(sent, "strip", 0, 0, tiled=True)
    return got, lax.ppermute(got, "clus", [(0, 1), (1, 0)])


def body(loads, self_term, near_tiles, near_list, far_rows, far_cols, coupling, ranks):
    nrhs, panels = loads.shape
    rank = far_cols.shape[0]
    blocks, tile = near_tiles.shape[:2]
    rows = panels // tile
    strips = coupling.shape[0] // CORES
    couple = coupling.reshape(CORES * strips * rank, rank)
    near_list = near_list.T
    ranks = ranks.reshape(1, CORES * strips)
    self_term = self_term.reshape(1, panels)
    groups = CORES * strips
    message = Plain((strips, nrhs, panels // 2 + LANES), jnp.int32)
    index = pltpu.SMEM(near_list.shape, jnp.int32)
    scratch = [index, pltpu.SemaphoreType.DMA((1,)), pltpu.VMEM((3 * rows, CORES * nrhs, tile), F32)]
    late = PIECE * (blocks // (5 * PIECE))
    tiles0, tiles1 = (jax.ShapeDtypeStruct((count, tile, tile), BF16) for count in (blocks - late, late))
    scratch += [pltpu.VMEM((CORES * rows, CORES * nrhs, tile), F32)] * 4

    def twice(array):
        return [jax.ShapeDtypeStruct(array.shape, BF16)] * 2

    sent, *held, loads, self_term, tiles0 = call(
        start_kernel,
        (loads, far_cols, couple, ranks, self_term, near_tiles),
        [
            message, *twice(far_cols), *twice(couple), jax.ShapeDtypeStruct((groups, CHUNK * rank), F32),
            loads, self_term, tiles0,
        ],
        [
            pltpu.VMEM(far_cols.shape, F32), pltpu.VMEM(couple.shape, F32), pltpu.SMEM(ranks.shape, jnp.int32),
            pltpu.SemaphoreType.DMA((5 + tiles0.shape[0] // PIECE,)),
        ],
        held=range(6),
    )
    loads, *held, self_term, tiles0 = in_vmem([loads, *held, self_term, tiles0])
    near_list, *far_rows, tiles1 = in_vmem(
        call(
            fetch_kernel,
            (loads, near_list, far_rows, near_tiles),
            [near_list, *twice(far_rows), tiles1],
            [
                pltpu.VMEM(near_list.shape, jnp.int32), pltpu.VMEM(far_rows.shape, F32),
                pltpu.SemaphoreType.DMA((2 + late // PIECE,)),
            ],
            held=range(1, 4),
        )
    )
    source_side, target_side = [loads, *held], [*far_rows, self_term, tiles0, tiles1, near_list]
    sent, image, window0, state = call(
        step0_kernel,
        (*exchanged(sent), *source_side, *target_side),
        [message, loads.shape, (3 * CORES * nrhs, panels), (CORES * nrhs, LANES)],
        scratch,
    )
    sent, basis, coeff = call(
        step1_kernel,
        (*exchanged(sent), loads, image, window0, state, *target_side),
        [(groups, 1, LANES), (2 * nrhs, panels), (3 * nrhs, LANES)],
        scratch,
    )
    got = lax.all_to_all(sent, GROUP, 0, 0, tiled=True)
    return call(functools.partial(finish_kernel, rank), (got, basis, coeff), [loads.shape])[0]


def solution(mesh):
    every = ("case",) + GROUP
    in_specs = (
        P(None, every),
        P(every),
        P(every, None, None),
        P(every, None),
        P(None, every),
        P(None, every),
        P(None, GROUP, None, None),
        P(None, GROUP),
    )
    return jax.shard_map(body, mesh=mesh, in_specs=in_specs, out_specs=P(None, every), check_vma=False)
```
